32 devices in a mesh: kgrp: 4 (over y, x), energy: 8 (over z, core).
Axes of the slice: x: 2, y: 2, z: 4, core: 2. Of those that a mesh axis runs over, the one named last changes fastest.
Arguments:
- greens: float32 [2, 2, 2, 256, 1024], P(None, None, None, 'kgrp', 'energy'), may hold values from -6 to 6
- current: float32 [2, 2, 2, 256, 1024], P(None, None, None, ('kgrp', 'energy')), may hold values from -6 to 6
- past_inputs: float32 [5, 2, 2, 2, 256, 1024], P(None, None, None, None, ('kgrp', 'energy')), may hold values from -6 to 6
- past_residuals: float32 [5, 2, 2, 2, 256, 1024], P(None, None, None, None, ('kgrp', 'energy')), may hold values from -40 to 40
- slot_order: int32 [5], replicated, may hold values from 0 to 4, each once
- neighbour: int32 [256, 5], P('kgrp'), may hold values from 0 to 255, as said below
- momentum_class: int32 [256], P('kgrp'), may hold values from 0 to 3
- stencil_weight: float32 [5], replicated, may hold values from 0.1 to 0.4
- acoustic_coupling: float32 [4], replicated, may hold values from 0.3 to 1.5
- optical_coupling: float32 [2], replicated, may hold values from 0.2 to 0.6
- occupation: float32 [2], replicated, may hold values from 0.1 to 1
- phonon_shift: int32 [2], replicated, may hold values from 32 to 96, as said below
Outputs:
- mixed: float32 [2, 2, 2, 256, 1024], P(None, None, None, ('kgrp', 'energy'))
The draws below stay inside these ranges and needn't reach their ends.
Inputs may be any that keep to these rules, and one draw needn't show every extreme that they name: `neighbour`: each index names a momentum of the row's own group of 64 consecutive momenta or of the group just before or after it, counted periodically over all groups. `phonon_shift`: the larger of the two shifts is exactly 96.
All inputs are finite; a program needn't handle non-finite values.
Results may differ from the reference program's by a relative error of at most 0.000053.
Values sent between devices are 32-bit elements; how exact they have to be, the bound alone decides.
No kernel may reach another device: no remote copies, remote signals or barrier semaphores. Data moves between devices by JAX's collectives and lax.ppermute only.
A program may use at most 64 MiB of HBM per device.

```python
import math
import jax
import jax.numpy as jnp
from jax import lax

POS = 2
K_GRP = 64
SHIFT_MAX = 96
NCLS = 4
HIST = 5
NK = 256
NE = 1024


def draw_past_residuals(key, part):
    shape = (HIST, 2, 2, POS, NK, NE)
    subkeys = jax.random.split(key, 3)
    row_log = jax.random.uniform(subkeys[1], (HIST, 1, 1, 1, NK, 1), jnp.float32)
    column_log = jax.random.uniform(subkeys[2], (1, 1, 1, 1, 1, NE), jnp.float32)
    position = jnp.arange(NK, dtype=jnp.float32).reshape(1, 1, 1, 1, NK, 1) / max(NK - 1, 1)
    values = jnp.clip(jax.random.normal(subkeys[0], shape, jnp.float32), -4.0, 4.0)
    slope_scale = jnp.exp(position * math.log(3.0))
    divisor = 30.0
    scales = jnp.exp(row_log * math.log(10.0)) * jnp.exp(column_log * math.log(10.0)) * slope_scale
    return (values * scales / divisor).astype(jnp.float32)


def draw_neighbour(key, part):
    subkeys = jax.random.split(key, 2)
    groups = NK // K_GRP
    row_ids = jnp.arange(NK, dtype=jnp.int32)[:, None]
    offset_group = jax.random.randint(subkeys[0], (NK, 5), -1, 2, dtype=jnp.int32)
    member = jax.random.randint(subkeys[1], (NK, 5), 0, K_GRP, dtype=jnp.int32)
    target = (row_ids // K_GRP + offset_group + groups) % groups * K_GRP + member
    target = target.at[0, 0].set(NK - 1).at[NK - 1, 0].set(0)
    return target.astype(jnp.int32)


def draw_phonon_shift(key, part):
    subkeys = jax.random.split(key, 2)
    smaller = jax.random.randint(subkeys[0], (1,), SHIFT_MAX // 3, SHIFT_MAX, dtype=jnp.int32)
    swapped = jax.random.randint(subkeys[1], (1,), 0, 2, dtype=jnp.int32)
    largest = jnp.full((1,), SHIFT_MAX, jnp.int32)
    shifts_pair = jnp.concatenate([largest, smaller])
    return jnp.where(swapped == 1, shifts_pair[::-1], shifts_pair).astype(jnp.int32)


def plant(result, stream_key, least, high):
    extent = result.shape
    index_at = [jax.random.randint(jax.random.fold_in(stream_key, axis), (), 0, extent[axis]) for axis in range(len(extent))]
    result = result.at[tuple(index_at)].set(least)
    longest = extent.index(max(extent))
    index_at[longest] = (index_at[longest] + 1) % extent[longest]
    return result.at[tuple(index_at)].set(high)


def block_scale(stream_key, dims, shards, low, top_value):
    gain, own = 1.0, jax.random.fold_in(stream_key, 6)
    for dim, blocks in shards:
        steps = jnp.exp(jax.random.uniform(jax.random.fold_in(own, dim), (blocks,), jnp.float32, low / len(shards), top_value / len(shards)))
        gain = gain * jnp.repeat(steps, dims[dim] // blocks).reshape([-1 if axis == dim else 1 for axis in range(len(dims))])
    return gain


def noise(rng, dims, scale, bound, shards=(), held_as=jnp.bfloat16):
    factor_of = block_scale(rng, dims, shards, -0.22, 0.18) if shards else 1.0
    result = jax.random.normal(rng, dims, jnp.float32) * scale * factor_of
    return jnp.minimum(jnp.maximum(result, -bound), bound).astype(held_as)


def setup_inputs(seed: int = 0) -> dict:
    arg_keys = jax.random.split(jax.random.key(seed), 13)
    return {
        "greens": noise(arg_keys[0], (2, 2, POS, NK, NE), 1.0, 6.0, ((3, 4), (4, 8)), jnp.float32),
        "current": noise(arg_keys[1], (2, 2, POS, NK, NE), 1.0, 6.0, ((3, 32),), jnp.float32),
        "past_inputs": noise(arg_keys[2], (HIST, 2, 2, POS, NK, NE), 1.0, 6.0, ((4, 32),), jnp.float32),
        "past_residuals": draw_past_residuals(jax.random.fold_in(arg_keys[12], 71), 0),
        "slot_order": jax.random.permutation(arg_keys[4], HIST).astype(jnp.int32),
        "neighbour": draw_neighbour(jax.random.fold_in(arg_keys[12], 71), 0),
        "momentum_class": plant(jax.random.randint(arg_keys[6], (NK,), 0, NCLS), jax.random.fold_in(arg_keys[6], 1), 0, NCLS - 1).astype(jnp.int32),
        "stencil_weight": jnp.clip(jax.random.uniform(arg_keys[7], (5,), jnp.float32, 0.1, 0.4), 0.1, 0.4),
        "acoustic_coupling": jnp.clip(jnp.exp(jax.random.uniform(arg_keys[8], (NCLS,), jnp.float32, math.log(0.3), math.log(1.5))), 0.3, 1.5),
        "optical_coupling": jnp.clip(jnp.exp(jax.random.uniform(arg_keys[9], (2,), jnp.float32, math.log(0.2), math.log(0.6))), 0.2, 0.6),
        "occupation": jnp.clip(jnp.exp(jax.random.uniform(arg_keys[10], (2,), jnp.float32, math.log(0.1), math.log(1.0))), 0.1, 1.0),
        "phonon_shift": draw_phonon_shift(jax.random.fold_in(arg_keys[12], 71), 0),
    }


mixing_share = 0.5
ridge_share = 0.1

def emit(padded, margin, length, coupling_row, optical, occupation, shifts):
    lesser = padded[0]
    greater = padded[1]

    def energy_view(source, offset):
        return lax.dynamic_slice_in_dim(source, margin + offset, length, axis=source.ndim - 1)
    sigma_less = coupling_row[:, None] * energy_view(lesser, 0)
    sigma_more = coupling_row[:, None] * energy_view(greater, 0)
    for column in range(2):
        strength = optical[column]
        number = occupation[column]
        offset = shifts[column]
        sigma_less = sigma_less + strength * ((number + 1.0) * energy_view(lesser, offset) + number * energy_view(lesser, -offset))
        sigma_more = sigma_more + strength * ((number + 1.0) * energy_view(greater, -offset) + number * energy_view(greater, offset))
    return jnp.stack([sigma_less, sigma_more])

def solve_spd(matrix, vector):
    factor = jnp.linalg.cholesky(matrix)
    size_n = matrix.shape[0]
    forward = []
    for column in range(size_n):
        summed = vector[column]
        for earlier in range(column):
            summed = summed - factor[column, earlier] * forward[earlier]
        forward.append(summed / factor[column, column])
    backward = [None] * size_n
    for column in range(size_n - 1, -1, -1):
        summed = forward[column]
        for earlier in range(column + 1, size_n):
            summed = summed - factor[earlier, column] * backward[earlier]
        backward[column] = summed / factor[column, column]
    return jnp.stack(backward)

def mix_weights(products):
    size_n = products.shape[0] - 1
    differ_rows = jnp.eye(size_n, size_n + 1, dtype=jnp.float32) - jnp.eye(size_n, size_n + 1, k=1, dtype=jnp.float32)
    system = jnp.dot(jnp.dot(differ_rows, products, precision=lax.Precision.HIGHEST), differ_rows.T, precision=lax.Precision.HIGHEST)
    target = jnp.dot(differ_rows, products[:, 0], precision=lax.Precision.HIGHEST)
    ridge = ridge_share * jnp.trace(system) / size_n + 1e-06
    gamma = solve_spd(system + ridge * jnp.eye(size_n, dtype=jnp.float32), target)
    unit = jnp.zeros((size_n + 1,), jnp.float32).at[0].set(1.0)
    return unit - jnp.dot(differ_rows.T, gamma, precision=lax.Precision.HIGHEST)

def reference(greens, current, past_inputs, past_residuals, slot_order, neighbour, momentum_class, stencil_weight, acoustic_coupling, optical_coupling, occupation, phonon_shift):
    smeared = jnp.zeros_like(greens)
    for column in range(5):
        smeared = smeared + stencil_weight[column] * jnp.take(greens, neighbour[:, column], axis=3)
    coupling_row = acoustic_coupling[momentum_class]
    padded = jnp.pad(smeared, [(0, 0)] * 4 + [(SHIFT_MAX, SHIFT_MAX)])
    sigma_new = emit(padded, SHIFT_MAX, NE, coupling_row, optical_coupling, occupation, phonon_shift)
    residual_now = sigma_new - current
    older_res = jnp.take(past_residuals, slot_order, axis=0)
    older_in = jnp.take(past_inputs, slot_order, axis=0)
    stacked = jnp.concatenate([residual_now.reshape(1, -1), older_res.reshape(HIST, -1)], axis=0)
    products = jnp.dot(stacked, stacked.T, precision=lax.Precision.HIGHEST) / stacked.shape[1]
    weights = mix_weights(products)
    mixed = weights[0] * (current + mixing_share * residual_now)
    for column in range(HIST):
        mixed = mixed + weights[column + 1] * (older_in[column] + mixing_share * older_res[column])
    return mixed
```

```python
import jax
import jax.numpy as jnp
from jax import lax
from jax.experimental import pallas as pl
from jax.experimental.pallas import tpu as pltpu
from jax.sharding import PartitionSpec as P

HIST = 5
LANES = 128

mixing_share = 0.5
ridge_share = 0.1

VMEM = pl.BlockSpec(memory_space=pltpu.VMEM)
SMEM = pl.BlockSpec(memory_space=pltpu.SMEM)
PARAMS = pltpu.CompilerParams(vmem_limit_bytes=16 * 1024 * 1024)

PAIRS = [(i, j) for i in range(1, HIST + 1) for j in range(i, HIST + 1)]
SPOTS = {pair: v for v, pair in enumerate(PAIRS)}
for _j in range(HIST + 1):
    SPOTS[(0, _j)] = 16 + _j


def smear_kernel(total_k, own, low, high, neighbour, weight, out):
    comps, group_len, slice_len = own.shape
    parts, _, _ = out.shape
    rows = group_len // parts
    group_id = lax.axis_index("kgrp")
    local = (neighbour[...] - group_id * group_len + (group_len + total_k)) % total_k
    span = 3 * group_len
    spot = lax.broadcasted_iota(jnp.int32, (group_len, span), 1)
    stencil = jnp.zeros((group_len, span), jnp.float32)
    for n in range(local.shape[1]):
        stencil = stencil + jnp.where(spot == local[:, n : n + 1], weight[n], 0.0)
    stencil_hi = stencil.astype(jnp.bfloat16)
    stencil_lo = (stencil - stencil_hi.astype(jnp.float32)).astype(jnp.bfloat16)
    pair = 2 if comps % 2 == 0 else 1
    for c in range(0, comps, pair):
        block = jnp.concatenate(
            [
                jnp.concatenate([source[c + p] for source in (low, own, high)], axis=0)
                for p in range(pair)
            ],
            axis=1,
        )
        block_hi = block.astype(jnp.bfloat16)
        block_lo = (block - block_hi.astype(jnp.float32)).astype(jnp.bfloat16)
        dot = lambda a, b: jnp.dot(a, b, preferred_element_type=jnp.float32)
        result = dot(stencil_hi, block_hi) + (
            dot(stencil_hi, block_lo) + dot(stencil_lo, block_hi)
        )
        for p in range(pair):
            for d in range(parts):
                out[d, (c + p) * rows : (c + p + 1) * rows, :] = result[
                    d * rows : (d + 1) * rows, p * slice_len : (p + 1) * slice_len
                ]


def smear(greens, low, high, neighbour, weight, parts, total_k):
    comps, group_len, slice_len = greens.shape
    return pl.pallas_call(
        lambda *refs: smear_kernel(total_k, *refs),
        out_shape=jax.ShapeDtypeStruct(
            (parts, comps * group_len // parts, slice_len), jnp.float32
        ),
        in_specs=[VMEM] * 4 + [SMEM],
        out_specs=VMEM,
        compiler_params=PARAMS,
        name="smear",
    )(greens, low, high, neighbour, weight)


def spread(values, shape):
    row = lax.broadcasted_iota(jnp.int32, shape, 0)
    lane = lax.broadcasted_iota(jnp.int32, shape, 1)
    tile = jnp.zeros(shape, jnp.float32)
    for spot, value in values:
        tile = jnp.where((row == spot % 8) & (lane == spot // 8), value, tile)
    return tile


def total(acc):
    return jnp.sum(jnp.sum(acc, axis=0, keepdims=True), axis=1, keepdims=True)


def history_kernel(past_inputs, past_residuals, slots, aged, tile):
    _, rows, width = past_inputs.shape
    acc = [jnp.zeros((8, LANES), jnp.float32) for _ in PAIRS]
    for top in range(0, rows, 8):
        def column(t, acc, top=top):
            at = pl.ds(pl.multiple_of(t * LANES, LANES), LANES)
            old = []
            for j in range(HIST):
                res = past_residuals[slots[j], top : top + 8, at]
                aged[j, top : top + 8, at] = (
                    past_inputs[slots[j], top : top + 8, at] + mixing_share * res
                )
                old.append(res)
            return [a + old[i - 1] * old[j - 1] for a, (i, j) in zip(acc, PAIRS)]
        acc = lax.fori_loop(0, width // LANES, column, acc, unroll=4)
    tile[...] = spread([(v, total(a)) for v, a in enumerate(acc)], tile.shape)


def history(past_inputs, past_residuals, slots):
    size = past_inputs.size
    return pl.pallas_call(
        history_kernel,
        out_shape=(
            jax.ShapeDtypeStruct(past_inputs.shape, jnp.float32),
            jax.ShapeDtypeStruct((8, LANES), jnp.float32),
        ),
        in_specs=[VMEM, VMEM, SMEM],
        out_specs=(VMEM, VMEM),
        compiler_params=PARAMS,
        cost_estimate=pl.CostEstimate(flops=8 * size, bytes_accessed=12 * size, transcendentals=0),
        name="history",
    )(past_inputs, past_residuals, slots)


def residual_kernel(
    rows, smeared, current, past_residuals, old_tile, slots, classes, acoustic, optical, number, shift,
    fresh, tile,
):
    parts, height, slice_len = smeared.shape
    first = lax.axis_index("energy") * rows
    row = lax.broadcasted_iota(jnp.int32, (8, slice_len), 0) % rows
    lane = lax.broadcasted_iota(jnp.int32, (8, slice_len), 1)
    coupling = jnp.zeros((8, slice_len), jnp.float32)
    for i in range(rows):
        coupling = jnp.where(row == i, acoustic[classes[first + i]], coupling)
    modes = []
    for m in range(2):
        s = shift[m]
        modes.append((s, lane < slice_len - s, lane >= s, optical[m] * (number[m] + 1.0), optical[m] * number[m]))
    zero = jnp.zeros((8, slice_len), jnp.float32)
    acc = [zero] * (HIST + 1)
    for top in range(0, height, 8):
        at = slice(top, top + 8)
        source = [smeared[e, at, :] for e in range(parts)]
        sigma = [coupling * x for x in source]
        lesser = top < height // 2
        for s, keep_up, keep_down, emitted, absorbed in modes:
            up = [pltpu.roll(x, slice_len - s, 1) for x in source] + [zero]
            down = [zero] + [pltpu.roll(x, s, 1) for x in source]
            gain_up, gain_down = (emitted, absorbed) if lesser else (absorbed, emitted)
            for e in range(parts):
                above = jnp.where(keep_up, up[e], up[e + 1])
                below = jnp.where(keep_down, down[e + 1], down[e])
                sigma[e] = sigma[e] + (gain_up * above + gain_down * below)
        for e in range(parts):
            where = (at, slice(e * slice_len, (e + 1) * slice_len))
            new = sigma[e] - current[where]
            fresh[where] = new
            acc[0] = acc[0] + new * new
            for j in range(HIST):
                acc[j + 1] = acc[j + 1] + new * past_residuals[(slots[j],) + where]
    mine = jnp.concatenate([jnp.sum(a, axis=0, keepdims=True) for a in acc] + [zero[: 8 - HIST - 1]], axis=0)
    mine = jnp.sum(mine, axis=1, keepdims=True)
    tile[...] = jnp.where(lax.broadcasted_iota(jnp.int32, tile.shape, 1) == 2, mine, old_tile[...])


def residual(smeared, current, past_residuals, old_tile, slots, classes, acoustic, optical, number, shift, rows):
    return pl.pallas_call(
        lambda *refs: residual_kernel(rows, *refs),
        out_shape=(
            jax.ShapeDtypeStruct(current.shape, jnp.float32),
            jax.ShapeDtypeStruct((8, LANES), jnp.float32),
        ),
        in_specs=[VMEM] * 4 + [SMEM] * 6,
        out_specs=(VMEM, VMEM),
        compiler_params=PARAMS,
        name="residual",
    )(smeared, current, past_residuals, old_tile, slots, classes, acoustic, optical, number, shift)


def solve(products):
    prod = lambda i, j: products[(min(i, j), max(i, j))]
    n = HIST
    system = [
        [prod(i, j) - prod(i, j + 1) - prod(i + 1, j) + prod(i + 1, j + 1) for j in range(n)]
        for i in range(n)
    ]
    target = [prod(i, 0) - prod(i + 1, 0) for i in range(n)]
    trace = system[0][0]
    for i in range(1, n):
        trace = trace + system[i][i]
    ridge = ridge_share * trace / n + 1e-06
    for i in range(n):
        system[i][i] = system[i][i] + ridge
    inverse = [None] * n
    for k in range(n):
        inverse[k] = 1.0 / system[k][k]
        for i in range(k + 1, n):
            factor = system[k][i] * inverse[k]
            for j in range(i, n):
                system[i][j] = system[i][j] - factor * system[k][j]
            target[i] = target[i] - factor * target[k]
    gamma = [None] * n
    for k in range(n - 1, -1, -1):
        value = target[k]
        for j in range(k + 1, n):
            value = value - system[k][j] * gamma[j]
        gamma[k] = value * inverse[k]
    weights = [1.0 - gamma[0]]
    for j in range(1, n):
        weights.append(gamma[j - 1] - gamma[j])
    weights.append(gamma[n - 1])
    return weights


def mix_kernel(entries, tiles, fresh, current, aged, out):
    count = tiles.shape[0]
    summed = tiles[0]
    for d in range(1, count):
        summed = summed + tiles[d]
    summed = summed / entries
    products = {
        pair: summed[spot % 8 : spot % 8 + 1, spot // 8 : spot // 8 + 1] for pair, spot in SPOTS.items()
    }
    weights = [jnp.broadcast_to(w, (8, LANES)) for w in solve(products)]
    rows, width = fresh.shape
    for top in range(0, rows, 8):
        for left in range(0, width, LANES):
            at = (slice(top, top + 8), slice(left, left + LANES))
            mixed = weights[0] * (current[at] + mixing_share * fresh[at])
            for j in range(HIST):
                mixed = mixed + weights[j + 1] * aged[(j,) + at]
            out[at] = mixed


def mix(tiles, fresh, current, aged, entries):
    return pl.pallas_call(
        lambda *refs: mix_kernel(entries, *refs),
        out_shape=jax.ShapeDtypeStruct(fresh.shape, jnp.float32),
        in_specs=[VMEM] * 4,
        out_specs=VMEM,
        compiler_params=PARAMS,
        name="mix",
    )(tiles, fresh, current, aged)


def per_device(
    greens,
    current,
    past_inputs,
    past_residuals,
    slot_order,
    neighbour,
    momentum_class,
    stencil_weight,
    acoustic_coupling,
    optical_coupling,
    occupation,
    phonon_shift,
):
    group_len, slice_len = greens.shape[3:]
    rows, width = current.shape[3:]
    groups = lax.axis_size("kgrp")
    parts = lax.axis_size("energy")
    own = greens.reshape(-1, group_len, slice_len)
    height = own.shape[0] * rows

    forward = [(i, (i + 1) % groups) for i in range(groups)]
    backward = [(target, source) for source, target in forward]
    low = lax.ppermute(own, "kgrp", forward)
    high = lax.ppermute(own, "kgrp", backward)

    flat = current.reshape(height, width)
    old_in = past_inputs.reshape(HIST, height, width)
    old_res = past_residuals.reshape(HIST, height, width)
    aged, old_tile = history(old_in, old_res, slot_order)

    smeared = smear(own, low, high, neighbour, stencil_weight, parts, groups * group_len)
    smeared = lax.all_to_all(smeared, "energy", split_axis=0, concat_axis=0, tiled=True)
    fresh, tile = residual(
        smeared, flat, old_res, old_tile, slot_order, momentum_class, acoustic_coupling,
        optical_coupling, occupation, phonon_shift, rows,
    )
    tiles = lax.all_gather(tile, ("kgrp", "energy"))
    entries = float(flat.size * groups * parts)
    return mix(tiles, fresh, flat, aged, entries).reshape(current.shape)


def solution(mesh):
    return jax.shard_map(
        per_device,
        mesh=mesh,
        in_specs=(
            P(None, None, None, "kgrp", "energy"),
            P(None, None, None, ("kgrp", "energy"), None),
            P(None, None, None, None, ("kgrp", "energy"), None),
            P(None, None, None, None, ("kgrp", "energy"), None),
            P(),
            P("kgrp", None),
            P("kgrp"),
            P(),
            P(),
            P(),
            P(),
            P(),
        ),
        out_specs=P(None, None, None, ("kgrp", "energy"), None),
        check_vma=False,
    )
```

```python
import jax
import jax.numpy as jnp
from jax import lax
from jax.experimental import pallas as pl
from jax.experimental.pallas import tpu as pltpu
from jax.sharding import PartitionSpec as P

HIST = 5
LANES = 128

mixing_share = 0.5
ridge_share = 0.1

VMEM = pl.BlockSpec(memory_space=pltpu.VMEM)
SMEM = pl.BlockSpec(memory_space=pltpu.SMEM)
PARAMS = pltpu.CompilerParams(vmem_limit_bytes=16 * 1024 * 1024)

PAIRS = [(i, j) for i in range(1, HIST + 1) for j in range(i, HIST + 1)]
SPOTS = {pair: v for v, pair in enumerate(PAIRS)}
for _j in range(HIST + 1):
    SPOTS[(0, _j)] = 16 + _j


def smear_kernel(total_k, own, low, high, neighbour, weight, out):
    comps, group_len, slice_len = own.shape
    parts, _, _ = out.shape
    rows = group_len // parts
    group_id = lax.axis_index("kgrp")
    local = (neighbour[...] - group_id * group_len + (group_len + total_k)) % total_k
    span = 3 * group_len
    spot = lax.broadcasted_iota(jnp.int32, (group_len, span), 1)
    stencil = jnp.zeros((group_len, span), jnp.float32)
    for n in range(local.shape[1]):
        stencil = stencil + jnp.where(spot == local[:, n : n + 1], weight[n], 0.0)
    stencil_hi = stencil.astype(jnp.bfloat16)
    stencil_lo = (stencil - stencil_hi.astype(jnp.float32)).astype(jnp.bfloat16)
    pair = 2 if comps % 2 == 0 else 1
    for c in range(0, comps, pair):
        block = jnp.concatenate(
            [
                jnp.concatenate([source[c + p] for source in (low, own, high)], axis=0)
                for p in range(pair)
            ],
            axis=1,
        )
        block_hi = block.astype(jnp.bfloat16)
        block_lo = (block - block_hi.astype(jnp.float32)).astype(jnp.bfloat16)
        dot = lambda a, b: jnp.dot(a, b, preferred_element_type=jnp.float32)
        result = dot(stencil_hi, block_hi) + (
            dot(stencil_hi, block_lo) + dot(stencil_lo, block_hi)
        )
        for p in range(pair):
            for d in range(parts):
                out[d, (c + p) * rows : (c + p + 1) * rows, :] = result[
                    d * rows : (d + 1) * rows, p * slice_len : (p + 1) * slice_len
                ]


def smear(greens, low, high, neighbour, weight, parts, total_k):
    comps, group_len, slice_len = greens.shape
    return pl.pallas_call(
        lambda *refs: smear_kernel(total_k, *refs),
        out_shape=jax.ShapeDtypeStruct(
            (parts, comps * group_len // parts, slice_len), jnp.float32
        ),
        in_specs=[VMEM] * 4 + [SMEM],
        out_specs=VMEM,
        compiler_params=PARAMS,
        name="smear",
    )(greens, low, high, neighbour, weight)


def spread(values, shape):
    row = lax.broadcasted_iota(jnp.int32, shape, 0)
    lane = lax.broadcasted_iota(jnp.int32, shape, 1)
    tile = jnp.zeros(shape, jnp.float32)
    for spot, value in values:
        tile = jnp.where((row == spot % 8) & (lane == spot // 8), value, tile)
    return tile


def total(acc):
    return jnp.sum(jnp.sum(acc, axis=0, keepdims=True), axis=1, keepdims=True)


def history_kernel(past_inputs, past_residuals, slots, aged, tile):
    _, rows, width = past_inputs.shape
    acc = [jnp.zeros((8, LANES), jnp.float32) for _ in PAIRS]
    for top in range(0, rows, 8):
        def column(t, acc, top=top):
            at = pl.ds(pl.multiple_of(t * LANES, LANES), LANES)
            old = []
            for j in range(HIST):
                res = past_residuals[slots[j], top : top + 8, at]
                aged[j, top : top + 8, at] = (
                    past_inputs[slots[j], top : top + 8, at] + mixing_share * res
                )
                old.append(res)
            return [a + old[i - 1] * old[j - 1] for a, (i, j) in zip(acc, PAIRS)]
        acc = lax.fori_loop(0, width // LANES, column, acc, unroll=4)
    tile[...] = spread([(v, total(a)) for v, a in enumerate(acc)], tile.shape)


def history(past_inputs, past_residuals, slots):
    size = past_inputs.size
    return pl.pallas_call(
        history_kernel,
        out_shape=(
            jax.ShapeDtypeStruct(past_inputs.shape, jnp.float32),
            jax.ShapeDtypeStruct((8, LANES), jnp.float32),
        ),
        in_specs=[VMEM, VMEM, SMEM],
        out_specs=(VMEM, VMEM),
        compiler_params=PARAMS,
        cost_estimate=pl.CostEstimate(flops=8 * size, bytes_accessed=12 * size, transcendentals=0),
        name="history",
    )(past_inputs, past_residuals, slots)


def residual_kernel(
    rows, smeared, current, past_residuals, old_tile, slots, classes, acoustic, optical, number, shift,
    fresh, tile,
):
    parts, height, slice_len = smeared.shape
    first = lax.axis_index("energy") * rows
    row = lax.broadcasted_iota(jnp.int32, (8, slice_len), 0) % rows
    lane = lax.broadcasted_iota(jnp.int32, (8, slice_len), 1)
    coupling = jnp.zeros((8, slice_len), jnp.float32)
    for i in range(rows):
        coupling = jnp.where(row == i, acoustic[classes[first + i]], coupling)
    modes = []
    for m in range(2):
        s = shift[m]
        modes.append((s, lane < slice_len - s, lane >= s, optical[m] * (number[m] + 1.0), optical[m] * number[m]))
    zero = jnp.zeros((8, slice_len), jnp.float32)
    acc = [zero] * (HIST + 1)
    for top in range(0, height, 8):
        at = slice(top, top + 8)
        source = [smeared[e, at, :] for e in range(parts)]
        sigma = [coupling * x for x in source]
        lesser = top < height // 2
        for s, keep_up, keep_down, emitted, absorbed in modes:
            up = [pltpu.roll(x, slice_len - s, 1) for x in source] + [zero]
            down = [zero] + [pltpu.roll(x, s, 1) for x in source]
            gain_up, gain_down = (emitted, absorbed) if lesser else (absorbed, emitted)
            for e in range(parts):
                above = jnp.where(keep_up, up[e], up[e + 1])
                below = jnp.where(keep_down, down[e + 1], down[e])
                sigma[e] = sigma[e] + (gain_up * above + gain_down * below)
        for e in range(parts):
            where = (at, slice(e * slice_len, (e + 1) * slice_len))
            new = sigma[e] - current[where]
            fresh[where] = new
            acc[0] = acc[0] + new * new
            for j in range(HIST):
                acc[j + 1] = acc[j + 1] + new * past_residuals[(slots[j],) + where]
    mine = jnp.concatenate([jnp.sum(a, axis=0, keepdims=True) for a in acc] + [zero[: 8 - HIST - 1]], axis=0)
    mine = jnp.sum(mine, axis=1, keepdims=True)
    tile[...] = jnp.where(lax.broadcasted_iota(jnp.int32, tile.shape, 1) == 2, mine, old_tile[...])


def residual(smeared, current, past_residuals, old_tile, slots, classes, acoustic, optical, number, shift, rows):
    return pl.pallas_call(
        lambda *refs: residual_kernel(rows, *refs),
        out_shape=(
            jax.ShapeDtypeStruct(current.shape, jnp.float32),
            jax.ShapeDtypeStruct((8, LANES), jnp.float32),
        ),
        in_specs=[VMEM] * 4 + [SMEM] * 6,
        out_specs=(VMEM, VMEM),
        compiler_params=PARAMS,
        name="residual",
    )(smeared, current, past_residuals, old_tile, slots, classes, acoustic, optical, number, shift)


def solve(products):
    prod = lambda i, j: products[(min(i, j), max(i, j))]
    n = HIST
    system = [
        [prod(i, j) - prod(i, j + 1) - prod(i + 1, j) + prod(i + 1, j + 1) for j in range(n)]
        for i in range(n)
    ]
    target = [prod(i, 0) - prod(i + 1, 0) for i in range(n)]
    trace = system[0][0]
    for i in range(1, n):
        trace = trace + system[i][i]
    ridge = ridge_share * trace / n + 1e-06
    for i in range(n):
        system[i][i] = system[i][i] + ridge
    inverse = [None] * n
    for k in range(n):
        inverse[k] = 1.0 / system[k][k]
        for i in range(k + 1, n):
            factor = system[k][i] * inverse[k]
            for j in range(i, n):
                system[i][j] = system[i][j] - factor * system[k][j]
            target[i] = target[i] - factor * target[k]
    gamma = [None] * n
    for k in range(n - 1, -1, -1):
        value = target[k]
        for j in range(k + 1, n):
            value = value - system[k][j] * gamma[j]
        gamma[k] = value * inverse[k]
    weights = [1.0 - gamma[0]]
    for j in range(1, n):
        weights.append(gamma[j - 1] - gamma[j])
    weights.append(gamma[n - 1])
    return weights


def mix_kernel(entries, *refs):
    *tiles, fresh, current, aged, out = refs
    summed = tiles[0][...]
    for tile in tiles[1:]:
        summed = summed + tile[...]
    summed = summed / entries
    products = {
        pair: summed[spot % 8 : spot % 8 + 1, spot // 8 : spot // 8 + 1] for pair, spot in SPOTS.items()
    }
    weights = [jnp.broadcast_to(w, (8, LANES)) for w in solve(products)]
    rows, width = fresh.shape
    for top in range(0, rows, 8):
        for left in range(0, width, LANES):
            at = (slice(top, top + 8), slice(left, left + LANES))
            mixed = weights[0] * (current[at] + mixing_share * fresh[at])
            for j in range(HIST):
                mixed = mixed + weights[j + 1] * aged[(j,) + at]
            out[at] = mixed


def mix(tiles, fresh, current, aged, entries):
    return pl.pallas_call(
        lambda *refs: mix_kernel(entries, *refs),
        out_shape=jax.ShapeDtypeStruct(fresh.shape, jnp.float32),
        in_specs=[VMEM] * (len(tiles) + 3),
        out_specs=VMEM,
        compiler_params=PARAMS,
        name="mix",
    )(*tiles, fresh, current, aged)


def from_all(block, axis):
    count = lax.axis_size(axis)
    return [block] + [
        lax.ppermute(block, axis, [(i, (i + step) % count) for i in range(count)])
        for step in range(1, count)
    ]


def per_device(
    greens,
    current,
    past_inputs,
    past_residuals,
    slot_order,
    neighbour,
    momentum_class,
    stencil_weight,
    acoustic_coupling,
    optical_coupling,
    occupation,
    phonon_shift,
):
    group_len, slice_len = greens.shape[3:]
    rows, width = current.shape[3:]
    groups = lax.axis_size("kgrp")
    parts = lax.axis_size("energy")
    own = greens.reshape(-1, group_len, slice_len)
    height = own.shape[0] * rows

    forward = [(i, (i + 1) % groups) for i in range(groups)]
    backward = [(target, source) for source, target in forward]
    low = lax.ppermute(own, "kgrp", forward)
    high = lax.ppermute(own, "kgrp", backward)

    flat = current.reshape(height, width)
    old_in = past_inputs.reshape(HIST, height, width)
    old_res = past_residuals.reshape(HIST, height, width)
    aged, old_tile = history(old_in, old_res, slot_order)

    smeared = smear(own, low, high, neighbour, stencil_weight, parts, groups * group_len)
    smeared = lax.all_to_all(smeared, "energy", split_axis=0, concat_axis=0, tiled=True)
    fresh, tile = residual(
        smeared, flat, old_res, old_tile, slot_order, momentum_class, acoustic_coupling,
        optical_coupling, occupation, phonon_shift, rows,
    )
    tile = sum(from_all(tile, "energy"))
    tiles = from_all(tile, "kgrp")
    entries = float(flat.size * groups * parts)
    return mix(tiles, fresh, flat, aged, entries).reshape(current.shape)


def solution(mesh):
    return jax.shard_map(
        per_device,
        mesh=mesh,
        in_specs=(
            P(None, None, None, "kgrp", "energy"),
            P(None, None, None, ("kgrp", "energy"), None),
            P(None, None, None, None, ("kgrp", "energy"), None),
            P(None, None, None, None, ("kgrp", "energy"), None),
            P(),
            P("kgrp", None),
            P("kgrp"),
            P(),
            P(),
            P(),
            P(),
            P(),
        ),
        out_specs=P(None, None, None, ("kgrp", "energy"), None),
        check_vma=False,
    )
```

```python
import jax
import jax.numpy as jnp
from jax import lax
from jax.experimental import pallas as pl
from jax.experimental.pallas import tpu as pltpu
from jax.sharding import PartitionSpec as P

HIST = 5
LANES = 128

mixing_share = 0.5
ridge_share = 0.1

VMEM = pl.BlockSpec(memory_space=pltpu.VMEM)
SMEM = pl.BlockSpec(memory_space=pltpu.SMEM)
PARAMS = pltpu.CompilerParams(vmem_limit_bytes=16 * 1024 * 1024)

PAIRS = [(i, j) for i in range(1, HIST + 1) for j in range(i, HIST + 1)]
SPOTS = {pair: v for v, pair in enumerate(PAIRS)}
for _j in range(HIST + 1):
    SPOTS[(0, _j)] = 16 + _j


def smear_kernel(total_k, own, low, high, neighbour, weight, out):
    comps, group_len, slice_len = own.shape
    parts, _, _ = out.shape
    rows = group_len // parts
    group_id = lax.axis_index("kgrp")
    local = (neighbour[...] - group_id * group_len + (group_len + total_k)) % total_k
    span = 3 * group_len
    spot = lax.broadcasted_iota(jnp.int32, (group_len, span), 1)
    stencil = jnp.zeros((group_len, span), jnp.float32)
    for n in range(local.shape[1]):
        stencil = stencil + jnp.where(spot == local[:, n : n + 1], weight[n], 0.0)
    stencil_hi = stencil.astype(jnp.bfloat16)
    stencil_lo = (stencil - stencil_hi.astype(jnp.float32)).astype(jnp.bfloat16)
    pair = 2 if comps % 2 == 0 else 1
    for c in range(0, comps, pair):
        block = jnp.concatenate(
            [
                jnp.concatenate([source[c + p] for source in (low, own, high)], axis=0)
                for p in range(pair)
            ],
            axis=1,
        )
        block_hi = block.astype(jnp.bfloat16)
        block_lo = (block - block_hi.astype(jnp.float32)).astype(jnp.bfloat16)
        dot = lambda a, b: jnp.dot(a, b, preferred_element_type=jnp.float32)
        result = dot(stencil_hi, block_hi) + (
            dot(stencil_hi, block_lo) + dot(stencil_lo, block_hi)
        )
        for p in range(pair):
            for d in range(parts):
                out[d, (c + p) * rows : (c + p + 1) * rows, :] = result[
                    d * rows : (d + 1) * rows, p * slice_len : (p + 1) * slice_len
                ]


def smear(greens, low, high, neighbour, weight, parts, total_k):
    comps, group_len, slice_len = greens.shape
    return pl.pallas_call(
        lambda *refs: smear_kernel(total_k, *refs),
        out_shape=jax.ShapeDtypeStruct(
            (parts, comps * group_len // parts, slice_len), jnp.float32
        ),
        in_specs=[VMEM] * 4 + [SMEM],
        out_specs=VMEM,
        compiler_params=PARAMS,
        name="smear",
    )(greens, low, high, neighbour, weight)


def spread(values, shape):
    row = lax.broadcasted_iota(jnp.int32, shape, 0)
    lane = lax.broadcasted_iota(jnp.int32, shape, 1)
    tile = jnp.zeros(shape, jnp.float32)
    for spot, value in values:
        tile = jnp.where((row == spot % 8) & (lane == spot // 8), value, tile)
    return tile


def total(acc):
    return jnp.sum(jnp.sum(acc, axis=0, keepdims=True), axis=1, keepdims=True)


def history_kernel(past_inputs, past_residuals, slots, aged, tile):
    _, rows, width = past_inputs.shape
    acc = [jnp.zeros((8, LANES), jnp.float32) for _ in PAIRS]
    for top in range(0, rows, 8):
        def column(t, acc, top=top):
            at = pl.ds(pl.multiple_of(t * LANES, LANES), LANES)
            old = []
            for j in range(HIST):
                res = past_residuals[slots[j], top : top + 8, at]
                aged[j, top : top + 8, at] = (
                    past_inputs[slots[j], top : top + 8, at] + mixing_share * res
                )
                old.append(res)
            return [a + old[i - 1] * old[j - 1] for a, (i, j) in zip(acc, PAIRS)]
        acc = lax.fori_loop(0, width // LANES, column, acc, unroll=4)
    tile[...] = spread([(v, total(a)) for v, a in enumerate(acc)], tile.shape)


def history(past_inputs, past_residuals, slots):
    size = past_inputs.size
    return pl.pallas_call(
        history_kernel,
        out_shape=(
            jax.ShapeDtypeStruct(past_inputs.shape, jnp.float32),
            jax.ShapeDtypeStruct((8, LANES), jnp.float32),
        ),
        in_specs=[VMEM, VMEM, SMEM],
        out_specs=(VMEM, VMEM),
        compiler_params=PARAMS,
        cost_estimate=pl.CostEstimate(flops=8 * size, bytes_accessed=12 * size, transcendentals=0),
        name="history",
    )(past_inputs, past_residuals, slots)


def residual_kernel(
    rows, smeared, current, past_residuals, old_tile, slots, classes, acoustic, optical, number, shift,
    fresh, tile,
):
    parts, height, slice_len = smeared.shape
    first = lax.axis_index("energy") * rows
    row = lax.broadcasted_iota(jnp.int32, (8, slice_len), 0) % rows
    lane = lax.broadcasted_iota(jnp.int32, (8, slice_len), 1)
    coupling = jnp.zeros((8, slice_len), jnp.float32)
    for i in range(rows):
        coupling = jnp.where(row == i, acoustic[classes[first + i]], coupling)
    modes = []
    for m in range(2):
        s = shift[m]
        modes.append((s, lane < slice_len - s, lane >= s, optical[m] * (number[m] + 1.0), optical[m] * number[m]))
    zero = jnp.zeros((8, slice_len), jnp.float32)
    acc = [zero] * (HIST + 1)
    for top in range(0, height, 8):
        at = slice(top, top + 8)
        source = [smeared[e, at, :] for e in range(parts)]
        sigma = [coupling * x for x in source]
        lesser = top < height // 2
        for s, keep_up, keep_down, emitted, absorbed in modes:
            up = [pltpu.roll(x, slice_len - s, 1) for x in source] + [zero]
            down = [zero] + [pltpu.roll(x, s, 1) for x in source]
            gain_up, gain_down = (emitted, absorbed) if lesser else (absorbed, emitted)
            for e in range(parts):
                above = jnp.where(keep_up, up[e], up[e + 1])
                below = jnp.where(keep_down, down[e + 1], down[e])
                sigma[e] = sigma[e] + (gain_up * above + gain_down * below)
        for e in range(parts):
            where = (at, slice(e * slice_len, (e + 1) * slice_len))
            new = sigma[e] - current[where]
            fresh[where] = new
            acc[0] = acc[0] + new * new
            for j in range(HIST):
                acc[j + 1] = acc[j + 1] + new * past_residuals[(slots[j],) + where]
    mine = jnp.concatenate([jnp.sum(a, axis=0, keepdims=True) for a in acc] + [zero[: 8 - HIST - 1]], axis=0)
    mine = jnp.sum(mine, axis=1, keepdims=True)
    lane = lax.broadcasted_iota(jnp.int32, old_tile.shape, 1)
    tile[...] = jnp.broadcast_to(jnp.where(lane == 2, mine, old_tile[...])[None], tile.shape)


def residual(smeared, current, past_residuals, old_tile, slots, classes, acoustic, optical, number, shift, rows, copies):
    return pl.pallas_call(
        lambda *refs: residual_kernel(rows, *refs),
        out_shape=(
            jax.ShapeDtypeStruct(current.shape, jnp.float32),
            jax.ShapeDtypeStruct((copies, 8, LANES), jnp.float32),
        ),
        in_specs=[VMEM] * 4 + [SMEM] * 6,
        out_specs=(VMEM, VMEM),
        compiler_params=PARAMS,
        name="residual",
    )(smeared, current, past_residuals, old_tile, slots, classes, acoustic, optical, number, shift)


def solve(products):
    prod = lambda i, j: products[(min(i, j), max(i, j))]
    n = HIST
    system = [
        [prod(i, j) - prod(i, j + 1) - prod(i + 1, j) + prod(i + 1, j + 1) for j in range(n)]
        for i in range(n)
    ]
    target = [prod(i, 0) - prod(i + 1, 0) for i in range(n)]
    trace = system[0][0]
    for i in range(1, n):
        trace = trace + system[i][i]
    ridge = ridge_share * trace / n + 1e-06
    for i in range(n):
        system[i][i] = system[i][i] + ridge
    inverse = [None] * n
    for k in range(n):
        inverse[k] = 1.0 / system[k][k]
        for i in range(k + 1, n):
            factor = system[k][i] * inverse[k]
            for j in range(i, n):
                system[i][j] = system[i][j] - factor * system[k][j]
            target[i] = target[i] - factor * target[k]
    gamma = [None] * n
    for k in range(n - 1, -1, -1):
        value = target[k]
        for j in range(k + 1, n):
            value = value - system[k][j] * gamma[j]
        gamma[k] = value * inverse[k]
    weights = [1.0 - gamma[0]]
    for j in range(1, n):
        weights.append(gamma[j - 1] - gamma[j])
    weights.append(gamma[n - 1])
    return weights


def mix_kernel(entries, tiles, fresh, current, aged, out):
    summed = jnp.sum(tiles[...], axis=0) / entries
    products = {
        pair: summed[spot % 8 : spot % 8 + 1, spot // 8 : spot // 8 + 1] for pair, spot in SPOTS.items()
    }
    weights = [jnp.broadcast_to(w, (8, LANES)) for w in solve(products)]
    rows, width = fresh.shape
    for top in range(0, rows, 8):
        for left in range(0, width, LANES):
            at = (slice(top, top + 8), slice(left, left + LANES))
            mixed = weights[0] * (current[at] + mixing_share * fresh[at])
            for j in range(HIST):
                mixed = mixed + weights[j + 1] * aged[(j,) + at]
            out[at] = mixed


def mix(tiles, fresh, current, aged, entries):
    return pl.pallas_call(
        lambda *refs: mix_kernel(entries, *refs),
        out_shape=jax.ShapeDtypeStruct(fresh.shape, jnp.float32),
        in_specs=[VMEM] * 4,
        out_specs=VMEM,
        compiler_params=PARAMS,
        name="mix",
    )(tiles, fresh, current, aged)


def per_device(
    greens,
    current,
    past_inputs,
    past_residuals,
    slot_order,
    neighbour,
    momentum_class,
    stencil_weight,
    acoustic_coupling,
    optical_coupling,
    occupation,
    phonon_shift,
):
    group_len, slice_len = greens.shape[3:]
    rows, width = current.shape[3:]
    groups = lax.axis_size("kgrp")
    parts = lax.axis_size("energy")
    own = greens.reshape(-1, group_len, slice_len)
    height = own.shape[0] * rows

    forward = [(i, (i + 1) % groups) for i in range(groups)]
    backward = [(target, source) for source, target in forward]
    low = lax.ppermute(own, "kgrp", forward)
    high = lax.ppermute(own, "kgrp", backward)

    flat = current.reshape(height, width)
    old_in = past_inputs.reshape(HIST, height, width)
    old_res = past_residuals.reshape(HIST, height, width)
    aged, old_tile = history(old_in, old_res, slot_order)

    smeared = smear(own, low, high, neighbour, stencil_weight, parts, groups * group_len)
    smeared = lax.all_to_all(smeared, "energy", split_axis=0, concat_axis=0, tiled=True)
    fresh, tile = residual(
        smeared, flat, old_res, old_tile, slot_order, momentum_class, acoustic_coupling,
        optical_coupling, occupation, phonon_shift, rows, groups * parts,
    )
    tiles = lax.all_to_all(tile, ("kgrp", "energy"), split_axis=0, concat_axis=0, tiled=True)
    entries = float(flat.size * groups * parts)
    return mix(tiles, fresh, flat, aged, entries).reshape(current.shape)


def solution(mesh):
    return jax.shard_map(
        per_device,
        mesh=mesh,
        in_specs=(
            P(None, None, None, "kgrp", "energy"),
            P(None, None, None, ("kgrp", "energy"), None),
            P(None, None, None, None, ("kgrp", "energy"), None),
            P(None, None, None, None, ("kgrp", "energy"), None),
            P(),
            P("kgrp", None),
            P("kgrp"),
            P(),
            P(),
            P(),
            P(),
            P(),
        ),
        out_specs=P(None, None, None, ("kgrp", "energy"), None),
        check_vma=False,
    )
```

```python
import jax
import jax.numpy as jnp
from jax import lax
from jax.experimental import pallas as pl
from jax.experimental.pallas import tpu as pltpu
from jax.sharding import PartitionSpec as P

HIST = 5
LANES = 128

mixing_share = 0.5
ridge_share = 0.1

VMEM = pl.BlockSpec(memory_space=pltpu.VMEM)
SMEM = pl.BlockSpec(memory_space=pltpu.SMEM)
PARAMS = pltpu.CompilerParams(vmem_limit_bytes=16 * 1024 * 1024)

PAIRS = [(i, j) for i in range(1, HIST + 1) for j in range(i, HIST + 1)]
SPOTS = {pair: v for v, pair in enumerate(PAIRS)}
for _j in range(HIST + 1):
    SPOTS[(0, _j)] = 16 + _j


def split(value):
    high = value.astype(jnp.bfloat16)
    return high, (value - high.astype(jnp.float32)).astype(jnp.bfloat16)


def product(left, right):
    dot = lambda a, b: jnp.dot(a, b, preferred_element_type=jnp.float32)
    return dot(left[0], right[0]) + (dot(left[0], right[1]) + dot(left[1], right[0]))


def prepare_kernel(total_k, own, neighbour, weight, stencil_hi, stencil_lo, part):
    comps, group_len, slice_len = own.shape
    group_id = lax.axis_index("kgrp")
    local = (neighbour[...] - group_id * group_len + (group_len + total_k)) % total_k
    spot = lax.broadcasted_iota(jnp.int32, (group_len, 3 * group_len), 1)
    stencil = jnp.zeros(spot.shape, jnp.float32)
    for n in range(local.shape[1]):
        stencil = stencil + jnp.where(spot == local[:, n : n + 1], weight[n], 0.0)
    sides = jnp.concatenate([stencil[:, :group_len], stencil[:, 2 * group_len :]], axis=1)
    stencil_hi[...], stencil_lo[...] = split(sides)
    centre = split(stencil[:, group_len : 2 * group_len])
    for c in range(0, comps, 2):
        result = product(centre, split(jnp.concatenate([own[c], own[c + 1]], axis=1)))
        part[c] = result[:, :slice_len]
        part[c + 1] = result[:, slice_len:]


def prepare(own, neighbour, weight, total_k):
    group_len = own.shape[1]
    sides = jax.ShapeDtypeStruct((group_len, 2 * group_len), jnp.bfloat16)
    return pl.pallas_call(
        lambda *refs: prepare_kernel(total_k, *refs),
        out_shape=(sides, sides, jax.ShapeDtypeStruct(own.shape, jnp.float32)),
        in_specs=[VMEM, VMEM, SMEM],
        out_specs=(VMEM, VMEM, VMEM),
        compiler_params=PARAMS,
        cost_estimate=pl.CostEstimate(
            flops=6 * own.size * group_len, bytes_accessed=8 * own.size, transcendentals=0
        ),
        name="prepare",
    )(own, neighbour, weight)


def smear_kernel(first, low, high, stencil_hi, stencil_lo, part, out):
    comps, group_len, slice_len = low.shape
    parts, _, _ = out.shape
    rows = group_len // parts
    stencil = (stencil_hi[...], stencil_lo[...])
    for c in range(0, comps, 2):
        block = jnp.concatenate(
            [
                jnp.concatenate([low[c], low[c + 1]], axis=1),
                jnp.concatenate([high[c], high[c + 1]], axis=1),
            ],
            axis=0,
        )
        result = product(stencil, split(block))
        for p in range(2):
            smeared = part[first + c + p] + result[:, p * slice_len : (p + 1) * slice_len]
            for d in range(parts):
                out[d, (c + p) * rows : (c + p + 1) * rows, :] = smeared[d * rows : (d + 1) * rows]


def smear(first, low, high, stencil_hi, stencil_lo, part, parts):
    comps, group_len, slice_len = low.shape
    return pl.pallas_call(
        lambda *refs: smear_kernel(first, *refs),
        out_shape=jax.ShapeDtypeStruct(
            (parts, comps * group_len // parts, slice_len), jnp.float32
        ),
        in_specs=[VMEM] * 5,
        out_specs=VMEM,
        compiler_params=PARAMS,
        name="smear",
    )(low, high, stencil_hi, stencil_lo, part)


def spread(values, shape):
    row = lax.broadcasted_iota(jnp.int32, shape, 0)
    lane = lax.broadcasted_iota(jnp.int32, shape, 1)
    tile = jnp.zeros(shape, jnp.float32)
    for spot, value in values:
        tile = jnp.where((row == spot % 8) & (lane == spot // 8), value, tile)
    return tile


def total(acc):
    return jnp.sum(jnp.sum(acc, axis=0, keepdims=True), axis=1, keepdims=True)


def history_kernel(past_inputs, past_residuals, slots, aged, tile):
    _, rows, width = past_inputs.shape
    acc = [jnp.zeros((8, LANES), jnp.float32) for _ in PAIRS]
    for top in range(0, rows, 8):
        def column(t, acc, top=top):
            at = pl.ds(pl.multiple_of(t * LANES, LANES), LANES)
            old = []
            for j in range(HIST):
                res = past_residuals[slots[j], top : top + 8, at]
                aged[j, top : top + 8, at] = (
                    past_inputs[slots[j], top : top + 8, at] + mixing_share * res
                )
                old.append(res)
            return [a + old[i - 1] * old[j - 1] for a, (i, j) in zip(acc, PAIRS)]
        acc = lax.fori_loop(0, width // LANES, column, acc, unroll=4)
    tile[...] = spread([(v, total(a)) for v, a in enumerate(acc)], tile.shape)


def history(past_inputs, past_residuals, slots):
    size = past_inputs.size
    return pl.pallas_call(
        history_kernel,
        out_shape=(
            jax.ShapeDtypeStruct(past_inputs.shape, jnp.float32),
            jax.ShapeDtypeStruct((8, LANES), jnp.float32),
        ),
        in_specs=[VMEM, VMEM, SMEM],
        out_specs=(VMEM, VMEM),
        compiler_params=PARAMS,
        cost_estimate=pl.CostEstimate(flops=8 * size, bytes_accessed=12 * size, transcendentals=0),
        name="history",
    )(past_inputs, past_residuals, slots)


def residual_kernel(
    rows, lesser, smeared, current, past_residuals, old_tile, slots, classes, acoustic, optical, number,
    shift, fresh, tile,
):
    parts, height, slice_len = smeared.shape
    base = 0 if lesser else height
    first = lax.axis_index("energy") * rows
    row = lax.broadcasted_iota(jnp.int32, (8, slice_len), 0) % rows
    lane = lax.broadcasted_iota(jnp.int32, (8, slice_len), 1)
    coupling = jnp.zeros((8, slice_len), jnp.float32)
    for i in range(rows):
        coupling = jnp.where(row == i, acoustic[classes[first + i]], coupling)
    modes = []
    for m in range(2):
        s = shift[m]
        modes.append((s, lane < slice_len - s, lane >= s, optical[m] * (number[m] + 1.0), optical[m] * number[m]))
    zero = jnp.zeros((8, slice_len), jnp.float32)
    acc = [zero] * (HIST + 1)
    for top in range(0, height, 8):
        source = [smeared[e, top : top + 8, :] for e in range(parts)]
        sigma = [coupling * x for x in source]
        for s, keep_up, keep_down, emitted, absorbed in modes:
            up = [pltpu.roll(x, slice_len - s, 1) for x in source] + [zero]
            down = [zero] + [pltpu.roll(x, s, 1) for x in source]
            gain_up, gain_down = (emitted, absorbed) if lesser else (absorbed, emitted)
            for e in range(parts):
                above = jnp.where(keep_up, up[e], up[e + 1])
                below = jnp.where(keep_down, down[e + 1], down[e])
                sigma[e] = sigma[e] + (gain_up * above + gain_down * below)
        for e in range(parts):
            across = slice(e * slice_len, (e + 1) * slice_len)
            where = (slice(base + top, base + top + 8), across)
            new = sigma[e] - current[where]
            fresh[top : top + 8, across] = new
            acc[0] = acc[0] + new * new
            for j in range(HIST):
                acc[j + 1] = acc[j + 1] + new * past_residuals[(slots[j],) + where]
    mine = jnp.concatenate([jnp.sum(a, axis=0, keepdims=True) for a in acc] + [zero[: 8 - HIST - 1]], axis=0)
    mine = jnp.sum(mine, axis=1, keepdims=True)
    mine = old_tile[...] + jnp.where(lax.broadcasted_iota(jnp.int32, old_tile.shape, 1) == 2, mine, 0.0)
    if lesser:
        tile[...] = mine
    else:
        tile[...] = jnp.broadcast_to(mine[None], tile.shape)


def residual(lesser, smeared, current, past_residuals, old_tile, scalars, rows, copies):
    return pl.pallas_call(
        lambda *refs: residual_kernel(rows, lesser, *refs),
        out_shape=(
            jax.ShapeDtypeStruct((current.shape[0] // 2, current.shape[1]), jnp.float32),
            jax.ShapeDtypeStruct((8, LANES) if lesser else (copies, 8, LANES), jnp.float32),
        ),
        in_specs=[VMEM] * 4 + [SMEM] * 6,
        out_specs=(VMEM, VMEM),
        compiler_params=PARAMS,
        name="residual",
    )(smeared, current, past_residuals, old_tile, *scalars)


def solve(products):
    prod = lambda i, j: products[(min(i, j), max(i, j))]
    n = HIST
    system = [
        [prod(i, j) - prod(i, j + 1) - prod(i + 1, j) + prod(i + 1, j + 1) for j in range(n)]
        for i in range(n)
    ]
    target = [prod(i, 0) - prod(i + 1, 0) for i in range(n)]
    trace = system[0][0]
    for i in range(1, n):
        trace = trace + system[i][i]
    ridge = ridge_share * trace / n + 1e-06
    for i in range(n):
        system[i][i] = system[i][i] + ridge
    inverse = [None] * n
    for k in range(n):
        inverse[k] = 1.0 / system[k][k]
        for i in range(k + 1, n):
            factor = system[k][i] * inverse[k]
            for j in range(i, n):
                system[i][j] = system[i][j] - factor * system[k][j]
            target[i] = target[i] - factor * target[k]
    gamma = [None] * n
    for k in range(n - 1, -1, -1):
        value = target[k]
        for j in range(k + 1, n):
            value = value - system[k][j] * gamma[j]
        gamma[k] = value * inverse[k]
    weights = [1.0 - gamma[0]]
    for j in range(1, n):
        weights.append(gamma[j - 1] - gamma[j])
    weights.append(gamma[n - 1])
    return weights


def mix_kernel(entries, tiles, fresh_lesser, fresh_greater, current, aged, out):
    summed = jnp.sum(tiles[...], axis=0) / entries
    products = {
        pair: summed[spot % 8 : spot % 8 + 1, spot // 8 : spot // 8 + 1] for pair, spot in SPOTS.items()
    }
    weights = [jnp.broadcast_to(w, (8, LANES)) for w in solve(products)]
    rows, width = current.shape
    half = rows // 2
    for top in range(0, rows, 8):
        fresh = fresh_lesser if top < half else fresh_greater
        for left in range(0, width, LANES):
            across = slice(left, left + LANES)
            at = (slice(top, top + 8), across)
            mixed = weights[0] * (current[at] + mixing_share * fresh[top % half : top % half + 8, across])
            for j in range(HIST):
                mixed = mixed + weights[j + 1] * aged[(j,) + at]
            out[at] = mixed


def mix(tiles, fresh_lesser, fresh_greater, current, aged, entries):
    return pl.pallas_call(
        lambda *refs: mix_kernel(entries, *refs),
        out_shape=jax.ShapeDtypeStruct(current.shape, jnp.float32),
        in_specs=[VMEM] * 5,
        out_specs=VMEM,
        compiler_params=PARAMS,
        name="mix",
    )(tiles, fresh_lesser, fresh_greater, current, aged)


def per_device(
    greens,
    current,
    past_inputs,
    past_residuals,
    slot_order,
    neighbour,
    momentum_class,
    stencil_weight,
    acoustic_coupling,
    optical_coupling,
    occupation,
    phonon_shift,
):
    group_len, slice_len = greens.shape[3:]
    rows, width = current.shape[3:]
    groups = lax.axis_size("kgrp")
    parts = lax.axis_size("energy")
    own = greens.reshape(-1, group_len, slice_len)
    comps = own.shape[0]
    height = comps * rows
    half = comps // 2

    forward = [(i, (i + 1) % groups) for i in range(groups)]
    backward = [(target, source) for source, target in forward]
    sides = []
    for chunk in range(2):
        block = own[chunk * half : (chunk + 1) * half]
        sides.append((lax.ppermute(block, "kgrp", forward), lax.ppermute(block, "kgrp", backward)))

    flat = current.reshape(height, width)
    old_in = past_inputs.reshape(HIST, height, width)
    old_res = past_residuals.reshape(HIST, height, width)
    stencil_hi, stencil_lo, part = prepare(own, neighbour, stencil_weight, groups * group_len)
    aged, tile = history(old_in, old_res, slot_order)

    scalars = (
        slot_order, momentum_class, acoustic_coupling, optical_coupling, occupation, phonon_shift
    )
    fresh = []
    for chunk, (low, high) in enumerate(sides):
        smeared = smear(chunk * half, low, high, stencil_hi, stencil_lo, part, parts)
        smeared = lax.all_to_all(smeared, "energy", split_axis=0, concat_axis=0, tiled=True)
        new, tile = residual(
            chunk == 0, smeared, flat, old_res, tile, scalars, rows, groups * parts
        )
        fresh.append(new)
    tiles = lax.all_to_all(tile, ("kgrp", "energy"), split_axis=0, concat_axis=0, tiled=True)
    entries = float(flat.size * groups * parts)
    return mix(tiles, *fresh, flat, aged, entries).reshape(current.shape)


def solution(mesh):
    return jax.shard_map(
        per_device,
        mesh=mesh,
        in_specs=(
            P(None, None, None, "kgrp", "energy"),
            P(None, None, None, ("kgrp", "energy"), None),
            P(None, None, None, None, ("kgrp", "energy"), None),
            P(None, None, None, None, ("kgrp", "energy"), None),
            P(),
            P("kgrp", None),
            P("kgrp"),
            P(),
            P(),
            P(),
            P(),
            P(),
        ),
        out_specs=P(None, None, None, ("kgrp", "energy"), None),
        check_vma=False,
    )
```

```python
import jax
import jax.numpy as jnp
from jax import lax
from jax.experimental import pallas as pl
from jax.experimental.pallas import tpu as pltpu
from jax.sharding import PartitionSpec as P

HIST = 5
LANES = 128

mixing_share = 0.5
ridge_share = 0.1

VMEM = pl.BlockSpec(memory_space=pltpu.VMEM)
SMEM = pl.BlockSpec(memory_space=pltpu.SMEM)
PARAMS = pltpu.CompilerParams(vmem_limit_bytes=16 * 1024 * 1024)

SMEAR_COST = pl.CostEstimate(flops=20_000_000_000, bytes_accessed=60_000_000, transcendentals=0)

PAIRS = [(i, j) for i in range(1, HIST + 1) for j in range(i, HIST + 1)]
SPOTS = {pair: v for v, pair in enumerate(PAIRS)}
for _j in range(HIST + 1):
    SPOTS[(0, _j)] = 16 + _j


def split(value):
    high = value.astype(jnp.bfloat16)
    return high, (value - high.astype(jnp.float32)).astype(jnp.bfloat16)


def product(left, right):
    dot = lambda a, b: jnp.dot(a, b, preferred_element_type=jnp.float32)
    return dot(left[0], right[0]) + (dot(left[0], right[1]) + dot(left[1], right[0]))


def prepare_kernel(total_k, own, neighbour, weight, stencil_hi, stencil_lo, part):
    comps, group_len, slice_len = own.shape
    group_id = lax.axis_index("kgrp")
    local = (neighbour[...] - group_id * group_len + (group_len + total_k)) % total_k
    spot = lax.broadcasted_iota(jnp.int32, (group_len, 3 * group_len), 1)
    stencil = jnp.zeros(spot.shape, jnp.float32)
    for n in range(local.shape[1]):
        stencil = stencil + jnp.where(spot == local[:, n : n + 1], weight[n], 0.0)
    sides = jnp.concatenate([stencil[:, :group_len], stencil[:, 2 * group_len :]], axis=1)
    stencil_hi[...], stencil_lo[...] = split(sides)
    centre = split(stencil[:, group_len : 2 * group_len])
    for c in range(0, comps, 2):
        result = product(centre, split(jnp.concatenate([own[c], own[c + 1]], axis=1)))
        part[c] = result[:, :slice_len]
        part[c + 1] = result[:, slice_len:]


def prepare(own, neighbour, weight, total_k):
    group_len = own.shape[1]
    sides = jax.ShapeDtypeStruct((group_len, 2 * group_len), jnp.bfloat16)
    return pl.pallas_call(
        lambda *refs: prepare_kernel(total_k, *refs),
        out_shape=(sides, sides, jax.ShapeDtypeStruct(own.shape, jnp.float32)),
        in_specs=[VMEM, VMEM, SMEM],
        out_specs=(VMEM, VMEM, VMEM),
        compiler_params=PARAMS,
        cost_estimate=pl.CostEstimate(
            flops=6 * own.size * group_len, bytes_accessed=8 * own.size, transcendentals=0
        ),
        name="prepare",
    )(own, neighbour, weight)


def smear_kernel(first, low, high, stencil_hi, stencil_lo, part, out):
    comps, group_len, slice_len = low.shape
    parts, _, _ = out.shape
    rows = group_len // parts
    stencil = (stencil_hi[...], stencil_lo[...])
    for c in range(0, comps, 2):
        block = jnp.concatenate(
            [
                jnp.concatenate([low[c], low[c + 1]], axis=1),
                jnp.concatenate([high[c], high[c + 1]], axis=1),
            ],
            axis=0,
        )
        result = product(stencil, split(block))
        for p in range(2):
            smeared = part[first + c + p] + result[:, p * slice_len : (p + 1) * slice_len]
            for d in range(parts):
                out[d, (c + p) * rows : (c + p + 1) * rows, :] = smeared[d * rows : (d + 1) * rows]


def smear(first, low, high, stencil_hi, stencil_lo, part, parts):
    comps, group_len, slice_len = low.shape
    return pl.pallas_call(
        lambda *refs: smear_kernel(first, *refs),
        out_shape=jax.ShapeDtypeStruct(
            (parts, comps * group_len // parts, slice_len), jnp.float32
        ),
        in_specs=[VMEM] * 5,
        out_specs=VMEM,
        compiler_params=PARAMS,
        cost_estimate=SMEAR_COST,
        name="smear",
    )(low, high, stencil_hi, stencil_lo, part)


def spread(values, shape):
    row = lax.broadcasted_iota(jnp.int32, shape, 0)
    lane = lax.broadcasted_iota(jnp.int32, shape, 1)
    tile = jnp.zeros(shape, jnp.float32)
    for spot, value in values:
        tile = jnp.where((row == spot % 8) & (lane == spot // 8), value, tile)
    return tile


def total(acc):
    return jnp.sum(jnp.sum(acc, axis=0, keepdims=True), axis=1, keepdims=True)


def history_kernel(past_inputs, past_residuals, slots, aged, tile):
    _, rows, width = past_inputs.shape
    acc = [jnp.zeros((8, LANES), jnp.float32) for _ in PAIRS]
    for top in range(0, rows, 8):
        def column(t, acc, top=top):
            at = pl.ds(pl.multiple_of(t * LANES, LANES), LANES)
            old = []
            for j in range(HIST):
                res = past_residuals[slots[j], top : top + 8, at]
                aged[j, top : top + 8, at] = (
                    past_inputs[slots[j], top : top + 8, at] + mixing_share * res
                )
                old.append(res)
            return [a + old[i - 1] * old[j - 1] for a, (i, j) in zip(acc, PAIRS)]
        acc = lax.fori_loop(0, width // LANES, column, acc, unroll=4)
    tile[...] = spread([(v, total(a)) for v, a in enumerate(acc)], tile.shape)


def history(past_inputs, past_residuals, slots):
    size = past_inputs.size
    return pl.pallas_call(
        history_kernel,
        out_shape=(
            jax.ShapeDtypeStruct(past_inputs.shape, jnp.float32),
            jax.ShapeDtypeStruct((8, LANES), jnp.float32),
        ),
        in_specs=[VMEM, VMEM, SMEM],
        out_specs=(VMEM, VMEM),
        compiler_params=PARAMS,
        cost_estimate=pl.CostEstimate(flops=8 * size, bytes_accessed=12 * size, transcendentals=0),
        name="history",
    )(past_inputs, past_residuals, slots)


def residual_kernel(
    rows, lesser, smeared, current, past_residuals, old_tile, slots, classes, acoustic, optical, number,
    shift, fresh, tile,
):
    parts, height, slice_len = smeared.shape
    base = 0 if lesser else height
    first = lax.axis_index("energy") * rows
    row = lax.broadcasted_iota(jnp.int32, (8, slice_len), 0) % rows
    lane = lax.broadcasted_iota(jnp.int32, (8, slice_len), 1)
    coupling = jnp.zeros((8, slice_len), jnp.float32)
    for i in range(rows):
        coupling = jnp.where(row == i, acoustic[classes[first + i]], coupling)
    modes = []
    for m in range(2):
        s = shift[m]
        modes.append((s, lane < slice_len - s, lane >= s, optical[m] * (number[m] + 1.0), optical[m] * number[m]))
    zero = jnp.zeros((8, slice_len), jnp.float32)
    acc = [zero] * (HIST + 1)
    for top in range(0, height, 8):
        source = [smeared[e, top : top + 8, :] for e in range(parts)]
        sigma = [coupling * x for x in source]
        for s, keep_up, keep_down, emitted, absorbed in modes:
            up = [pltpu.roll(x, slice_len - s, 1) for x in source] + [zero]
            down = [zero] + [pltpu.roll(x, s, 1) for x in source]
            gain_up, gain_down = (emitted, absorbed) if lesser else (absorbed, emitted)
            for e in range(parts):
                above = jnp.where(keep_up, up[e], up[e + 1])
                below = jnp.where(keep_down, down[e + 1], down[e])
                sigma[e] = sigma[e] + (gain_up * above + gain_down * below)
        for e in range(parts):
            across = slice(e * slice_len, (e + 1) * slice_len)
            where = (slice(base + top, base + top + 8), across)
            new = sigma[e] - current[where]
            fresh[top : top + 8, across] = new
            acc[0] = acc[0] + new * new
            for j in range(HIST):
                acc[j + 1] = acc[j + 1] + new * past_residuals[(slots[j],) + where]
    mine = jnp.concatenate([jnp.sum(a, axis=0, keepdims=True) for a in acc] + [zero[: 8 - HIST - 1]], axis=0)
    mine = jnp.sum(mine, axis=1, keepdims=True)
    mine = old_tile[...] + jnp.where(lax.broadcasted_iota(jnp.int32, old_tile.shape, 1) == 2, mine, 0.0)
    if lesser:
        tile[...] = mine
    else:
        tile[...] = jnp.broadcast_to(mine[None], tile.shape)


def residual(lesser, smeared, current, past_residuals, old_tile, scalars, rows, copies):
    return pl.pallas_call(
        lambda *refs: residual_kernel(rows, lesser, *refs),
        out_shape=(
            jax.ShapeDtypeStruct((current.shape[0] // 2, current.shape[1]), jnp.float32),
            jax.ShapeDtypeStruct((8, LANES) if lesser else (copies, 8, LANES), jnp.float32),
        ),
        in_specs=[VMEM] * 4 + [SMEM] * 6,
        out_specs=(VMEM, VMEM),
        compiler_params=PARAMS,
        name="residual",
    )(smeared, current, past_residuals, old_tile, *scalars)


def solve(products):
    prod = lambda i, j: products[(min(i, j), max(i, j))]
    n = HIST
    system = [
        [prod(i, j) - prod(i, j + 1) - prod(i + 1, j) + prod(i + 1, j + 1) for j in range(n)]
        for i in range(n)
    ]
    target = [prod(i, 0) - prod(i + 1, 0) for i in range(n)]
    trace = system[0][0]
    for i in range(1, n):
        trace = trace + system[i][i]
    ridge = ridge_share * trace / n + 1e-06
    for i in range(n):
        system[i][i] = system[i][i] + ridge
    inverse = [None] * n
    for k in range(n):
        inverse[k] = 1.0 / system[k][k]
        for i in range(k + 1, n):
            factor = system[k][i] * inverse[k]
            for j in range(i, n):
                system[i][j] = system[i][j] - factor * system[k][j]
            target[i] = target[i] - factor * target[k]
    gamma = [None] * n
    for k in range(n - 1, -1, -1):
        value = target[k]
        for j in range(k + 1, n):
            value = value - system[k][j] * gamma[j]
        gamma[k] = value * inverse[k]
    weights = [1.0 - gamma[0]]
    for j in range(1, n):
        weights.append(gamma[j - 1] - gamma[j])
    weights.append(gamma[n - 1])
    return weights


def mix_kernel(entries, tiles, fresh_lesser, fresh_greater, current, aged, out):
    summed = jnp.sum(tiles[...], axis=0) / entries
    products = {
        pair: summed[spot % 8 : spot % 8 + 1, spot // 8 : spot // 8 + 1] for pair, spot in SPOTS.items()
    }
    weights = [jnp.broadcast_to(w, (8, LANES)) for w in solve(products)]
    rows, width = current.shape
    half = rows // 2
    for top in range(0, rows, 8):
        fresh = fresh_lesser if top < half else fresh_greater
        for left in range(0, width, LANES):
            across = slice(left, left + LANES)
            at = (slice(top, top + 8), across)
            mixed = weights[0] * (current[at] + mixing_share * fresh[top % half : top % half + 8, across])
            for j in range(HIST):
                mixed = mixed + weights[j + 1] * aged[(j,) + at]
            out[at] = mixed


def mix(tiles, fresh_lesser, fresh_greater, current, aged, entries):
    return pl.pallas_call(
        lambda *refs: mix_kernel(entries, *refs),
        out_shape=jax.ShapeDtypeStruct(current.shape, jnp.float32),
        in_specs=[VMEM] * 5,
        out_specs=VMEM,
        compiler_params=PARAMS,
        name="mix",
    )(tiles, fresh_lesser, fresh_greater, current, aged)


def per_device(
    greens,
    current,
    past_inputs,
    past_residuals,
    slot_order,
    neighbour,
    momentum_class,
    stencil_weight,
    acoustic_coupling,
    optical_coupling,
    occupation,
    phonon_shift,
):
    group_len, slice_len = greens.shape[3:]
    rows, width = current.shape[3:]
    groups = lax.axis_size("kgrp")
    parts = lax.axis_size("energy")
    own = greens.reshape(-1, group_len, slice_len)
    comps = own.shape[0]
    height = comps * rows
    half = comps // 2

    forward = [(i, (i + 1) % groups) for i in range(groups)]
    backward = [(target, source) for source, target in forward]
    sides = []
    for chunk in range(2):
        block = own[chunk * half : (chunk + 1) * half]
        sides.append((lax.ppermute(block, "kgrp", forward), lax.ppermute(block, "kgrp", backward)))

    flat = current.reshape(height, width)
    old_in = past_inputs.reshape(HIST, height, width)
    old_res = past_residuals.reshape(HIST, height, width)
    stencil_hi, stencil_lo, part = prepare(own, neighbour, stencil_weight, groups * group_len)
    aged, tile = history(old_in, old_res, slot_order)

    scalars = (
        slot_order, momentum_class, acoustic_coupling, optical_coupling, occupation, phonon_shift
    )
    fresh = []
    for chunk, (low, high) in enumerate(sides):
        smeared = smear(chunk * half, low, high, stencil_hi, stencil_lo, part, parts)
        smeared = lax.all_to_all(smeared, "energy", split_axis=0, concat_axis=0, tiled=True)
        new, tile = residual(
            chunk == 0, smeared, flat, old_res, tile, scalars, rows, groups * parts
        )
        fresh.append(new)
    tiles = lax.all_to_all(tile, ("kgrp", "energy"), split_axis=0, concat_axis=0, tiled=True)
    entries = float(flat.size * groups * parts)
    return mix(tiles, *fresh, flat, aged, entries).reshape(current.shape)


def solution(mesh):
    return jax.shard_map(
        per_device,
        mesh=mesh,
        in_specs=(
            P(None, None, None, "kgrp", "energy"),
            P(None, None, None, ("kgrp", "energy"), None),
            P(None, None, None, None, ("kgrp", "energy"), None),
            P(None, None, None, None, ("kgrp", "energy"), None),
            P(),
            P("kgrp", None),
            P("kgrp"),
            P(),
            P(),
            P(),
            P(),
            P(),
        ),
        out_specs=P(None, None, None, ("kgrp", "energy"), None),
        check_vma=False,
    )
```

```python
import jax
import jax.numpy as jnp
from jax import lax
from jax.experimental import pallas as pl
from jax.experimental.pallas import tpu as pltpu
from jax.sharding import PartitionSpec as P

HIST = 5
LANES = 128

mixing_share = 0.5
ridge_share = 0.1

VMEM = pl.BlockSpec(memory_space=pltpu.VMEM)
SMEM = pl.BlockSpec(memory_space=pltpu.SMEM)
PARAMS = pltpu.CompilerParams(vmem_limit_bytes=16 * 1024 * 1024)

FIRST_SIDE = 1

PAIRS = [(i, j) for i in range(1, HIST + 1) for j in range(i, HIST + 1)]
SPOTS = {pair: v for v, pair in enumerate(PAIRS)}
for _j in range(HIST + 1):
    SPOTS[(0, _j)] = 16 + _j


def split(value):
    high = value.astype(jnp.bfloat16)
    return high, (value - high.astype(jnp.float32)).astype(jnp.bfloat16)


def product(left, right):
    dot = lambda a, b: jnp.dot(a, b, preferred_element_type=jnp.float32)
    return dot(left[0], right[0]) + (dot(left[0], right[1]) + dot(left[1], right[0]))


def prepare_kernel(total_k, own, neighbour, weight, stencil_hi, stencil_lo, part):
    comps, group_len, slice_len = own.shape
    group_id = lax.axis_index("kgrp")
    local = (neighbour[...] - group_id * group_len + (group_len + total_k)) % total_k
    spot = lax.broadcasted_iota(jnp.int32, (group_len, 3 * group_len), 1)
    stencil = jnp.zeros(spot.shape, jnp.float32)
    for n in range(local.shape[1]):
        stencil = stencil + jnp.where(spot == local[:, n : n + 1], weight[n], 0.0)
    sides = jnp.concatenate([stencil[:, :group_len], stencil[:, 2 * group_len :]], axis=1)
    stencil_hi[...], stencil_lo[...] = split(sides)
    centre = split(stencil[:, group_len : 2 * group_len])
    for c in range(0, comps, 2):
        result = product(centre, split(jnp.concatenate([own[c], own[c + 1]], axis=1)))
        part[c] = result[:, :slice_len]
        part[c + 1] = result[:, slice_len:]


def prepare(own, neighbour, weight, total_k):
    group_len = own.shape[1]
    sides = jax.ShapeDtypeStruct((group_len, 2 * group_len), jnp.bfloat16)
    return pl.pallas_call(
        lambda *refs: prepare_kernel(total_k, *refs),
        out_shape=(sides, sides, jax.ShapeDtypeStruct(own.shape, jnp.float32)),
        in_specs=[VMEM, VMEM, SMEM],
        out_specs=(VMEM, VMEM, VMEM),
        compiler_params=PARAMS,
        cost_estimate=pl.CostEstimate(
            flops=6 * own.size * group_len, bytes_accessed=8 * own.size, transcendentals=0
        ),
        name="prepare",
    )(own, neighbour, weight)


def smear_kernel(block_at, block, stencil_hi, stencil_lo, part, out):
    comps, group_len, slice_len = block.shape
    at = slice(block_at * group_len, (block_at + 1) * group_len)
    stencil = (stencil_hi[:, at], stencil_lo[:, at])
    for c in range(0, comps, 2):
        result = product(stencil, split(jnp.concatenate([block[c], block[c + 1]], axis=1)))
        for p in range(2):
            smeared = part[c + p] + result[:, p * slice_len : (p + 1) * slice_len]
            if block_at == FIRST_SIDE:
                out[c + p] = smeared
                continue
            rows = group_len // out.shape[0]
            for d in range(out.shape[0]):
                out[d, (c + p) * rows : (c + p + 1) * rows, :] = smeared[d * rows : (d + 1) * rows]


def smear(side, block, stencil_hi, stencil_lo, part, parts):
    comps, group_len, slice_len = block.shape
    shape = block.shape if side == FIRST_SIDE else (parts, comps * group_len // parts, slice_len)
    return pl.pallas_call(
        lambda *refs: smear_kernel(side, *refs),
        out_shape=jax.ShapeDtypeStruct(shape, jnp.float32),
        in_specs=[VMEM] * 4,
        out_specs=VMEM,
        compiler_params=PARAMS,
        cost_estimate=pl.CostEstimate(
            flops=6 * block.size * group_len, bytes_accessed=12 * block.size, transcendentals=0
        ),
        name="smear",
    )(block, stencil_hi, stencil_lo, part)


def spread(values, shape):
    row = lax.broadcasted_iota(jnp.int32, shape, 0)
    lane = lax.broadcasted_iota(jnp.int32, shape, 1)
    tile = jnp.zeros(shape, jnp.float32)
    for spot, value in values:
        tile = jnp.where((row == spot % 8) & (lane == spot // 8), value, tile)
    return tile


def total(acc):
    return jnp.sum(jnp.sum(acc, axis=0, keepdims=True), axis=1, keepdims=True)


def history_kernel(past_inputs, past_residuals, slots, aged, tile):
    _, rows, width = past_inputs.shape
    acc = [jnp.zeros((8, LANES), jnp.float32) for _ in PAIRS]
    for top in range(0, rows, 8):
        def column(t, acc, top=top):
            at = pl.ds(pl.multiple_of(t * LANES, LANES), LANES)
            old = []
            for j in range(HIST):
                res = past_residuals[slots[j], top : top + 8, at]
                aged[j, top : top + 8, at] = (
                    past_inputs[slots[j], top : top + 8, at] + mixing_share * res
                )
                old.append(res)
            return [a + old[i - 1] * old[j - 1] for a, (i, j) in zip(acc, PAIRS)]
        acc = lax.fori_loop(0, width // LANES, column, acc, unroll=4)
    tile[...] = spread([(v, total(a)) for v, a in enumerate(acc)], tile.shape)


def history(past_inputs, past_residuals, slots):
    size = past_inputs.size
    return pl.pallas_call(
        history_kernel,
        out_shape=(
            jax.ShapeDtypeStruct(past_inputs.shape, jnp.float32),
            jax.ShapeDtypeStruct((8, LANES), jnp.float32),
        ),
        in_specs=[VMEM, VMEM, SMEM],
        out_specs=(VMEM, VMEM),
        compiler_params=PARAMS,
        cost_estimate=pl.CostEstimate(flops=8 * size, bytes_accessed=12 * size, transcendentals=0),
        name="history",
    )(past_inputs, past_residuals, slots)


def residual_kernel(
    rows, smeared, current, past_residuals, old_tile, slots, classes, acoustic, optical, number, shift,
    fresh, tile,
):
    parts, height, slice_len = smeared.shape
    first = lax.axis_index("energy") * rows
    row = lax.broadcasted_iota(jnp.int32, (8, slice_len), 0) % rows
    lane = lax.broadcasted_iota(jnp.int32, (8, slice_len), 1)
    coupling = jnp.zeros((8, slice_len), jnp.float32)
    for i in range(rows):
        coupling = jnp.where(row == i, acoustic[classes[first + i]], coupling)
    modes = []
    for m in range(2):
        s = shift[m]
        modes.append((s, lane < slice_len - s, lane >= s, optical[m] * (number[m] + 1.0), optical[m] * number[m]))
    zero = jnp.zeros((8, slice_len), jnp.float32)
    acc = [zero] * (HIST + 1)
    for top in range(0, height, 8):
        at = slice(top, top + 8)
        source = [smeared[e, at, :] for e in range(parts)]
        sigma = [coupling * x for x in source]
        lesser = top < height // 2
        for s, keep_up, keep_down, emitted, absorbed in modes:
            up = [pltpu.roll(x, slice_len - s, 1) for x in source] + [zero]
            down = [zero] + [pltpu.roll(x, s, 1) for x in source]
            gain_up, gain_down = (emitted, absorbed) if lesser else (absorbed, emitted)
            for e in range(parts):
                above = jnp.where(keep_up, up[e], up[e + 1])
                below = jnp.where(keep_down, down[e + 1], down[e])
                sigma[e] = sigma[e] + (gain_up * above + gain_down * below)
        for e in range(parts):
            where = (at, slice(e * slice_len, (e + 1) * slice_len))
            new = sigma[e] - current[where]
            fresh[where] = new
            acc[0] = acc[0] + new * new
            for j in range(HIST):
                acc[j + 1] = acc[j + 1] + new * past_residuals[(slots[j],) + where]
    mine = jnp.concatenate([jnp.sum(a, axis=0, keepdims=True) for a in acc] + [zero[: 8 - HIST - 1]], axis=0)
    mine = jnp.sum(mine, axis=1, keepdims=True)
    lane = lax.broadcasted_iota(jnp.int32, old_tile.shape, 1)
    tile[...] = jnp.broadcast_to(jnp.where(lane == 2, mine, old_tile[...])[None], tile.shape)


def residual(smeared, current, past_residuals, old_tile, slots, classes, acoustic, optical, number, shift, rows, copies):
    return pl.pallas_call(
        lambda *refs: residual_kernel(rows, *refs),
        out_shape=(
            jax.ShapeDtypeStruct(current.shape, jnp.float32),
            jax.ShapeDtypeStruct((copies, 8, LANES), jnp.float32),
        ),
        in_specs=[VMEM] * 4 + [SMEM] * 6,
        out_specs=(VMEM, VMEM),
        compiler_params=PARAMS,
        name="residual",
    )(smeared, current, past_residuals, old_tile, slots, classes, acoustic, optical, number, shift)


def solve(products):
    prod = lambda i, j: products[(min(i, j), max(i, j))]
    n = HIST
    system = [
        [prod(i, j) - prod(i, j + 1) - prod(i + 1, j) + prod(i + 1, j + 1) for j in range(n)]
        for i in range(n)
    ]
    target = [prod(i, 0) - prod(i + 1, 0) for i in range(n)]
    trace = system[0][0]
    for i in range(1, n):
        trace = trace + system[i][i]
    ridge = ridge_share * trace / n + 1e-06
    for i in range(n):
        system[i][i] = system[i][i] + ridge
    inverse = [None] * n
    for k in range(n):
        inverse[k] = 1.0 / system[k][k]
        for i in range(k + 1, n):
            factor = system[k][i] * inverse[k]
            for j in range(i, n):
                system[i][j] = system[i][j] - factor * system[k][j]
            target[i] = target[i] - factor * target[k]
    gamma = [None] * n
    for k in range(n - 1, -1, -1):
        value = target[k]
        for j in range(k + 1, n):
            value = value - system[k][j] * gamma[j]
        gamma[k] = value * inverse[k]
    weights = [1.0 - gamma[0]]
    for j in range(1, n):
        weights.append(gamma[j - 1] - gamma[j])
    weights.append(gamma[n - 1])
    return weights


def mix_kernel(entries, tiles, fresh, current, aged, out, wide):
    summed = jnp.sum(tiles[...], axis=0) / entries
    for lane in range(wide.shape[0]):
        wide[lane] = jnp.broadcast_to(summed[:, lane : lane + 1], (8, LANES))
    products = {
        pair: jnp.broadcast_to(wide[spot // 8, spot % 8 : spot % 8 + 1, :], (8, LANES))
        for pair, spot in SPOTS.items()
    }
    weights = solve(products)
    rows, width = fresh.shape
    for top in range(0, rows, 8):
        for left in range(0, width, LANES):
            at = (slice(top, top + 8), slice(left, left + LANES))
            mixed = weights[0] * (current[at] + mixing_share * fresh[at])
            for j in range(HIST):
                mixed = mixed + weights[j + 1] * aged[(j,) + at]
            out[at] = mixed


def mix(tiles, fresh, current, aged, entries):
    return pl.pallas_call(
        lambda *refs: mix_kernel(entries, *refs),
        out_shape=jax.ShapeDtypeStruct(fresh.shape, jnp.float32),
        in_specs=[VMEM] * 4,
        out_specs=VMEM,
        scratch_shapes=[pltpu.VMEM((3, 8, LANES), jnp.float32)],
        compiler_params=PARAMS,
        name="mix",
    )(tiles, fresh, current, aged)


def per_device(
    greens,
    current,
    past_inputs,
    past_residuals,
    slot_order,
    neighbour,
    momentum_class,
    stencil_weight,
    acoustic_coupling,
    optical_coupling,
    occupation,
    phonon_shift,
):
    group_len, slice_len = greens.shape[3:]
    rows, width = current.shape[3:]
    groups = lax.axis_size("kgrp")
    parts = lax.axis_size("energy")
    own = greens.reshape(-1, group_len, slice_len)
    height = own.shape[0] * rows

    forward = [(i, (i + 1) % groups) for i in range(groups)]
    backward = [(target, source) for source, target in forward]
    sides = [lax.ppermute(own, "kgrp", forward), lax.ppermute(own, "kgrp", backward)]

    flat = current.reshape(height, width)
    old_in = past_inputs.reshape(HIST, height, width)
    old_res = past_residuals.reshape(HIST, height, width)
    stencil_hi, stencil_lo, smeared = prepare(own, neighbour, stencil_weight, groups * group_len)
    aged, old_tile = history(old_in, old_res, slot_order)
    for side in (FIRST_SIDE, 1 - FIRST_SIDE):
        smeared = smear(side, sides[side], stencil_hi, stencil_lo, smeared, parts)
    smeared = lax.all_to_all(smeared, "energy", split_axis=0, concat_axis=0, tiled=True)
    fresh, tile = residual(
        smeared, flat, old_res, old_tile, slot_order, momentum_class, acoustic_coupling,
        optical_coupling, occupation, phonon_shift, rows, groups * parts,
    )
    tiles = lax.all_to_all(tile, ("kgrp", "energy"), split_axis=0, concat_axis=0, tiled=True)
    entries = float(flat.size * groups * parts)
    return mix(tiles, fresh, flat, aged, entries).reshape(current.shape)


def solution(mesh):
    return jax.shard_map(
        per_device,
        mesh=mesh,
        in_specs=(
            P(None, None, None, "kgrp", "energy"),
            P(None, None, None, ("kgrp", "energy"), None),
            P(None, None, None, None, ("kgrp", "energy"), None),
            P(None, None, None, None, ("kgrp", "energy"), None),
            P(),
            P("kgrp", None),
            P("kgrp"),
            P(),
            P(),
            P(),
            P(),
            P(),
        ),
        out_specs=P(None, None, None, ("kgrp", "energy"), None),
        check_vma=False,
    )
```

```python
import jax
import jax.numpy as jnp
from jax import lax
from jax.experimental import pallas as pl
from jax.experimental.pallas import tpu as pltpu
from jax.sharding import PartitionSpec as P

HIST = 5
LANES = 128

mixing_share = 0.5
ridge_share = 0.1

VMEM = pl.BlockSpec(memory_space=pltpu.VMEM)
SMEM = pl.BlockSpec(memory_space=pltpu.SMEM)
PARAMS = pltpu.CompilerParams(vmem_limit_bytes=16 * 1024 * 1024)

NEAR, FAR = 0, 1

PAIRS = [(i, j) for i in range(1, HIST + 1) for j in range(i, HIST + 1)]
SPOTS = {pair: v for v, pair in enumerate(PAIRS)}
for _j in range(HIST + 1):
    SPOTS[(0, _j)] = 16 + _j


def split(value):
    high = value.astype(jnp.bfloat16)
    return high, (value - high.astype(jnp.float32)).astype(jnp.bfloat16)


def product(left, right):
    dot = lambda a, b: jnp.dot(a, b, preferred_element_type=jnp.float32)
    return dot(left[0], right[0]) + (dot(left[0], right[1]) + dot(left[1], right[0]))


def prepare_kernel(total_k, own, neighbour, weight, stencil_hi, stencil_lo, part):
    comps, group_len, slice_len = own.shape
    group_id = lax.axis_index("kgrp")
    local = (neighbour[...] - group_id * group_len + (group_len + total_k)) % total_k
    spot = lax.broadcasted_iota(jnp.int32, (group_len, 3 * group_len), 1)
    stencil = jnp.zeros(spot.shape, jnp.float32)
    for n in range(local.shape[1]):
        stencil = stencil + jnp.where(spot == local[:, n : n + 1], weight[n], 0.0)
    before, after = stencil[:, :group_len], stencil[:, 2 * group_len :]
    swapped = paired(total_k // group_len) & (group_id % 2 == 1)
    near, far = jnp.where(swapped, before, after), jnp.where(swapped, after, before)
    stencil_hi[...], stencil_lo[...] = split(jnp.concatenate([near, far], axis=1))
    centre = split(stencil[:, group_len : 2 * group_len])
    for c in range(0, comps, 2):
        result = product(centre, split(jnp.concatenate([own[c], own[c + 1]], axis=1)))
        part[c] = result[:, :slice_len]
        part[c + 1] = result[:, slice_len:]


def prepare(own, neighbour, weight, total_k):
    group_len = own.shape[1]
    sides = jax.ShapeDtypeStruct((group_len, 2 * group_len), jnp.bfloat16)
    return pl.pallas_call(
        lambda *refs: prepare_kernel(total_k, *refs),
        out_shape=(sides, sides, jax.ShapeDtypeStruct(own.shape, jnp.float32)),
        in_specs=[VMEM, VMEM, SMEM],
        out_specs=(VMEM, VMEM, VMEM),
        compiler_params=PARAMS,
        cost_estimate=pl.CostEstimate(
            flops=6 * own.size * group_len, bytes_accessed=8 * own.size, transcendentals=0
        ),
        name="prepare",
    )(own, neighbour, weight)


def smear_kernel(side, *refs):
    *blocks, stencil_hi, stencil_lo, part, out = refs
    _, group_len, slice_len = blocks[0].shape
    at = slice(side * group_len, (side + 1) * group_len)
    stencil = (stencil_hi[:, at], stencil_lo[:, at])
    rows = group_len // out.shape[0]
    first = 0
    for block in blocks:
        for c in range(0, block.shape[0], 2):
            result = product(stencil, split(jnp.concatenate([block[c], block[c + 1]], axis=1)))
            for p in range(2):
                at = first + c + p
                smeared = part[at] + result[:, p * slice_len : (p + 1) * slice_len]
                if side == NEAR:
                    out[at] = smeared
                    continue
                for d in range(out.shape[0]):
                    out[d, at * rows : (at + 1) * rows, :] = smeared[d * rows : (d + 1) * rows]
        first += block.shape[0]


def smear(side, blocks, stencil_hi, stencil_lo, part, parts):
    comps, group_len, slice_len = part.shape
    shape = part.shape if side == NEAR else (parts, comps * group_len // parts, slice_len)
    return pl.pallas_call(
        lambda *refs: smear_kernel(side, *refs),
        out_shape=jax.ShapeDtypeStruct(shape, jnp.float32),
        in_specs=[VMEM] * (len(blocks) + 3),
        out_specs=VMEM,
        compiler_params=PARAMS,
        cost_estimate=pl.CostEstimate(
            flops=6 * part.size * group_len, bytes_accessed=12 * part.size, transcendentals=0
        ),
        name="smear",
    )(*blocks, stencil_hi, stencil_lo, part)


def paired(groups):
    return groups == 4


def exchange(own, groups):
    if not paired(groups):
        forward = [(i, (i + 1) % groups) for i in range(groups)]
        backward = [(target, source) for source, target in forward]
        return [lax.ppermute(own, "kgrp", backward)], [lax.ppermute(own, "kgrp", forward)]
    half = own.shape[0] // 2
    across = lambda block, flip: lax.ppermute(block, "kgrp", [(i, i ^ flip) for i in range(groups)])
    near = [across(own[:half], 1), across(own[half:], 1)]
    return near, [across(near[0], 2), across(own[half:], 3)]


def spread(values, shape):
    row = lax.broadcasted_iota(jnp.int32, shape, 0)
    lane = lax.broadcasted_iota(jnp.int32, shape, 1)
    tile = jnp.zeros(shape, jnp.float32)
    for spot, value in values:
        tile = jnp.where((row == spot % 8) & (lane == spot // 8), value, tile)
    return tile


def total(acc):
    return jnp.sum(jnp.sum(acc, axis=0, keepdims=True), axis=1, keepdims=True)


def history_kernel(past_inputs, past_residuals, slots, aged, tile):
    _, rows, width = past_inputs.shape
    acc = [jnp.zeros((8, LANES), jnp.float32) for _ in PAIRS]
    for top in range(0, rows, 8):
        def column(t, acc, top=top):
            at = pl.ds(pl.multiple_of(t * LANES, LANES), LANES)
            old = []
            for j in range(HIST):
                res = past_residuals[slots[j], top : top + 8, at]
                aged[j, top : top + 8, at] = (
                    past_inputs[slots[j], top : top + 8, at] + mixing_share * res
                )
                old.append(res)
            return [a + old[i - 1] * old[j - 1] for a, (i, j) in zip(acc, PAIRS)]
        acc = lax.fori_loop(0, width // LANES, column, acc, unroll=4)
    tile[...] = spread([(v, total(a)) for v, a in enumerate(acc)], tile.shape)


def history(past_inputs, past_residuals, slots):
    size = past_inputs.size
    return pl.pallas_call(
        history_kernel,
        out_shape=(
            jax.ShapeDtypeStruct(past_inputs.shape, jnp.float32),
            jax.ShapeDtypeStruct((8, LANES), jnp.float32),
        ),
        in_specs=[VMEM, VMEM, SMEM],
        out_specs=(VMEM, VMEM),
        compiler_params=PARAMS,
        cost_estimate=pl.CostEstimate(flops=8 * size, bytes_accessed=12 * size, transcendentals=0),
        name="history",
    )(past_inputs, past_residuals, slots)


def residual_kernel(
    rows, smeared, current, past_residuals, old_tile, slots, classes, acoustic, optical, number, shift,
    fresh, tile,
):
    parts, height, slice_len = smeared.shape
    first = lax.axis_index("energy") * rows
    row = lax.broadcasted_iota(jnp.int32, (8, slice_len), 0) % rows
    lane = lax.broadcasted_iota(jnp.int32, (8, slice_len), 1)
    coupling = jnp.zeros((8, slice_len), jnp.float32)
    for i in range(rows):
        coupling = jnp.where(row == i, acoustic[classes[first + i]], coupling)
    modes = []
    for m in range(2):
        s = shift[m]
        modes.append((s, lane < slice_len - s, lane >= s, optical[m] * (number[m] + 1.0), optical[m] * number[m]))
    zero = jnp.zeros((8, slice_len), jnp.float32)
    acc = [zero] * (HIST + 1)
    for top in range(0, height, 8):
        at = slice(top, top + 8)
        source = [smeared[e, at, :] for e in range(parts)]
        sigma = [coupling * x for x in source]
        lesser = top < height // 2
        for s, keep_up, keep_down, emitted, absorbed in modes:
            up = [pltpu.roll(x, slice_len - s, 1) for x in source] + [zero]
            down = [zero] + [pltpu.roll(x, s, 1) for x in source]
            gain_up, gain_down = (emitted, absorbed) if lesser else (absorbed, emitted)
            for e in range(parts):
                above = jnp.where(keep_up, up[e], up[e + 1])
                below = jnp.where(keep_down, down[e + 1], down[e])
                sigma[e] = sigma[e] + (gain_up * above + gain_down * below)
        for e in range(parts):
            where = (at, slice(e * slice_len, (e + 1) * slice_len))
            new = sigma[e] - current[where]
            fresh[where] = new
            acc[0] = acc[0] + new * new
            for j in range(HIST):
                acc[j + 1] = acc[j + 1] + new * past_residuals[(slots[j],) + where]
    mine = jnp.concatenate([jnp.sum(a, axis=0, keepdims=True) for a in acc] + [zero[: 8 - HIST - 1]], axis=0)
    mine = jnp.sum(mine, axis=1, keepdims=True)
    lane = lax.broadcasted_iota(jnp.int32, old_tile.shape, 1)
    tile[...] = jnp.broadcast_to(jnp.where(lane == 2, mine, old_tile[...])[None], tile.shape)


def residual(smeared, current, past_residuals, old_tile, slots, classes, acoustic, optical, number, shift, rows, copies):
    return pl.pallas_call(
        lambda *refs: residual_kernel(rows, *refs),
        out_shape=(
            jax.ShapeDtypeStruct(current.shape, jnp.float32),
            jax.ShapeDtypeStruct((copies, 8, LANES), jnp.float32),
        ),
        in_specs=[VMEM] * 4 + [SMEM] * 6,
        out_specs=(VMEM, VMEM),
        compiler_params=PARAMS,
        name="residual",
    )(smeared, current, past_residuals, old_tile, slots, classes, acoustic, optical, number, shift)


def solve(products):
    prod = lambda i, j: products[(min(i, j), max(i, j))]
    n = HIST
    system = [
        [prod(i, j) - prod(i, j + 1) - prod(i + 1, j) + prod(i + 1, j + 1) for j in range(n)]
        for i in range(n)
    ]
    target = [prod(i, 0) - prod(i + 1, 0) for i in range(n)]
    trace = system[0][0]
    for i in range(1, n):
        trace = trace + system[i][i]
    ridge = ridge_share * trace / n + 1e-06
    for i in range(n):
        system[i][i] = system[i][i] + ridge
    inverse = [None] * n
    for k in range(n):
        inverse[k] = 1.0 / system[k][k]
        for i in range(k + 1, n):
            factor = system[k][i] * inverse[k]
            for j in range(i, n):
                system[i][j] = system[i][j] - factor * system[k][j]
            target[i] = target[i] - factor * target[k]
    gamma = [None] * n
    for k in range(n - 1, -1, -1):
        value = target[k]
        for j in range(k + 1, n):
            value = value - system[k][j] * gamma[j]
        gamma[k] = value * inverse[k]
    weights = [1.0 - gamma[0]]
    for j in range(1, n):
        weights.append(gamma[j - 1] - gamma[j])
    weights.append(gamma[n - 1])
    return weights


def mix_kernel(entries, tiles, fresh, current, aged, out, wide):
    summed = jnp.sum(tiles[...], axis=0) / entries
    for lane in range(wide.shape[0]):
        wide[lane] = jnp.broadcast_to(summed[:, lane : lane + 1], (8, LANES))
    products = {
        pair: jnp.broadcast_to(wide[spot // 8, spot % 8 : spot % 8 + 1, :], (8, LANES))
        for pair, spot in SPOTS.items()
    }
    weights = solve(products)
    rows, width = fresh.shape
    for top in range(0, rows, 8):
        for left in range(0, width, LANES):
            at = (slice(top, top + 8), slice(left, left + LANES))
            mixed = weights[0] * (current[at] + mixing_share * fresh[at])
            for j in range(HIST):
                mixed = mixed + weights[j + 1] * aged[(j,) + at]
            out[at] = mixed


def mix(tiles, fresh, current, aged, entries):
    return pl.pallas_call(
        lambda *refs: mix_kernel(entries, *refs),
        out_shape=jax.ShapeDtypeStruct(fresh.shape, jnp.float32),
        in_specs=[VMEM] * 4,
        out_specs=VMEM,
        scratch_shapes=[pltpu.VMEM((3, 8, LANES), jnp.float32)],
        compiler_params=PARAMS,
        name="mix",
    )(tiles, fresh, current, aged)


def per_device(
    greens,
    current,
    past_inputs,
    past_residuals,
    slot_order,
    neighbour,
    momentum_class,
    stencil_weight,
    acoustic_coupling,
    optical_coupling,
    occupation,
    phonon_shift,
):
    group_len, slice_len = greens.shape[3:]
    rows, width = current.shape[3:]
    groups = lax.axis_size("kgrp")
    parts = lax.axis_size("energy")
    own = greens.reshape(-1, group_len, slice_len)
    height = own.shape[0] * rows

    sides = exchange(own, groups)

    flat = current.reshape(height, width)
    old_in = past_inputs.reshape(HIST, height, width)
    old_res = past_residuals.reshape(HIST, height, width)
    stencil_hi, stencil_lo, smeared = prepare(own, neighbour, stencil_weight, groups * group_len)
    aged, old_tile = history(old_in, old_res, slot_order)
    for side in (NEAR, FAR):
        smeared = smear(side, sides[side], stencil_hi, stencil_lo, smeared, parts)
    smeared = lax.all_to_all(smeared, "energy", split_axis=0, concat_axis=0, tiled=True)
    fresh, tile = residual(
        smeared, flat, old_res, old_tile, slot_order, momentum_class, acoustic_coupling,
        optical_coupling, occupation, phonon_shift, rows, groups * parts,
    )
    tiles = lax.all_to_all(tile, ("kgrp", "energy"), split_axis=0, concat_axis=0, tiled=True)
    entries = float(flat.size * groups * parts)
    return mix(tiles, fresh, flat, aged, entries).reshape(current.shape)


def solution(mesh):
    return jax.shard_map(
        per_device,
        mesh=mesh,
        in_specs=(
            P(None, None, None, "kgrp", "energy"),
            P(None, None, None, ("kgrp", "energy"), None),
            P(None, None, None, None, ("kgrp", "energy"), None),
            P(None, None, None, None, ("kgrp", "energy"), None),
            P(),
            P("kgrp", None),
            P("kgrp"),
            P(),
            P(),
            P(),
            P(),
            P(),
        ),
        out_specs=P(None, None, None, ("kgrp", "energy"), None),
        check_vma=False,
    )
```

```python
import jax
import jax.numpy as jnp
from jax import lax
from jax.experimental import pallas as pl
from jax.experimental.pallas import tpu as pltpu
from jax.sharding import PartitionSpec as P

HIST = 5
LANES = 128

mixing_share = 0.5
ridge_share = 0.1

VMEM = pl.BlockSpec(memory_space=pltpu.VMEM)
SMEM = pl.BlockSpec(memory_space=pltpu.SMEM)
PARAMS = pltpu.CompilerParams(vmem_limit_bytes=16 * 1024 * 1024)

NEAR, FAR = 0, 1

PAIRS = [(i, j) for i in range(1, HIST + 1) for j in range(i, HIST + 1)]
SPOTS = {pair: v for v, pair in enumerate(PAIRS)}
for _j in range(HIST + 1):
    SPOTS[(0, _j)] = 16 + _j


def split(value):
    high = value.astype(jnp.bfloat16)
    return high, (value - high.astype(jnp.float32)).astype(jnp.bfloat16)


def product(left, right):
    dot = lambda a, b: jnp.dot(a, b, preferred_element_type=jnp.float32)
    return dot(left[0], right[0]) + (dot(left[0], right[1]) + dot(left[1], right[0]))


def prepare_kernel(total_k, own, neighbour, weight, stencil_hi, stencil_lo, part, tail):
    comps, group_len, slice_len = own.shape
    group_id = lax.axis_index("kgrp")
    local = (neighbour[...] - group_id * group_len + (group_len + total_k)) % total_k
    spot = lax.broadcasted_iota(jnp.int32, (group_len, 3 * group_len), 1)
    stencil = jnp.zeros(spot.shape, jnp.float32)
    for n in range(local.shape[1]):
        stencil = stencil + jnp.where(spot == local[:, n : n + 1], weight[n], 0.0)
    before, after = stencil[:, :group_len], stencil[:, 2 * group_len :]
    swapped = paired(total_k // group_len) & (group_id % 2 == 1)
    near, far = jnp.where(swapped, before, after), jnp.where(swapped, after, before)
    stencil_hi[...], stencil_lo[...] = split(jnp.concatenate([near, far], axis=1))
    centre = split(stencil[:, group_len : 2 * group_len])
    for c in range(0, comps, 2):
        result = product(centre, split(jnp.concatenate([own[c], own[c + 1]], axis=1)))
        if c >= comps - tail.shape[0]:
            at = c - comps + tail.shape[0]
            tail[at], tail[at + 1] = own[c], own[c + 1]
        part[c] = result[:, :slice_len]
        part[c + 1] = result[:, slice_len:]


def prepare(own, neighbour, weight, total_k):
    group_len = own.shape[1]
    sides = jax.ShapeDtypeStruct((group_len, 2 * group_len), jnp.bfloat16)
    tail = jax.ShapeDtypeStruct((own.shape[0] // 2,) + own.shape[1:], jnp.float32)
    return pl.pallas_call(
        lambda *refs: prepare_kernel(total_k, *refs),
        out_shape=(sides, sides, jax.ShapeDtypeStruct(own.shape, jnp.float32), tail),
        in_specs=[VMEM, VMEM, SMEM],
        out_specs=(VMEM,) * 4,
        compiler_params=PARAMS,
        cost_estimate=pl.CostEstimate(
            flops=6 * own.size * group_len, bytes_accessed=8 * own.size, transcendentals=0
        ),
        name="prepare",
    )(own, neighbour, weight)


def smear_kernel(side, *refs):
    *blocks, stencil_hi, stencil_lo, part, out = refs
    _, group_len, slice_len = blocks[0].shape
    at = slice(side * group_len, (side + 1) * group_len)
    stencil = (stencil_hi[:, at], stencil_lo[:, at])
    rows = group_len // out.shape[0]
    first = 0
    for block in blocks:
        for c in range(0, block.shape[0], 2):
            result = product(stencil, split(jnp.concatenate([block[c], block[c + 1]], axis=1)))
            for p in range(2):
                at = first + c + p
                smeared = part[at] + result[:, p * slice_len : (p + 1) * slice_len]
                if side == NEAR:
                    out[at] = smeared
                    continue
                for d in range(out.shape[0]):
                    out[d, at * rows : (at + 1) * rows, :] = smeared[d * rows : (d + 1) * rows]
        first += block.shape[0]


def smear(side, blocks, stencil_hi, stencil_lo, part, parts):
    comps, group_len, slice_len = part.shape
    shape = part.shape if side == NEAR else (parts, comps * group_len // parts, slice_len)
    return pl.pallas_call(
        lambda *refs: smear_kernel(side, *refs),
        out_shape=jax.ShapeDtypeStruct(shape, jnp.float32),
        in_specs=[VMEM] * (len(blocks) + 3),
        out_specs=VMEM,
        compiler_params=PARAMS,
        cost_estimate=pl.CostEstimate(
            flops=6 * part.size * group_len, bytes_accessed=12 * part.size, transcendentals=0
        ),
        name="smear",
    )(*blocks, stencil_hi, stencil_lo, part)


def paired(groups):
    return groups == 4


def exchange(own, tail, groups):
    if not paired(groups):
        forward = [(i, (i + 1) % groups) for i in range(groups)]
        backward = [(target, source) for source, target in forward]
        return [lax.ppermute(own, "kgrp", backward)], [lax.ppermute(own, "kgrp", forward)]
    across = lambda block, flip: lax.ppermute(block, "kgrp", [(i, i ^ flip) for i in range(groups)])
    near = across(own, 1)
    head = near[: near.shape[0] - tail.shape[0]]
    return [near], [across(head, 2), across(tail, 3)]


def spread(values, shape):
    row = lax.broadcasted_iota(jnp.int32, shape, 0)
    lane = lax.broadcasted_iota(jnp.int32, shape, 1)
    tile = jnp.zeros(shape, jnp.float32)
    for spot, value in values:
        tile = jnp.where((row == spot % 8) & (lane == spot // 8), value, tile)
    return tile


def total(acc):
    return jnp.sum(jnp.sum(acc, axis=0, keepdims=True), axis=1, keepdims=True)


def history_kernel(past_inputs, past_residuals, slots, aged, tile):
    _, rows, width = past_inputs.shape
    acc = [jnp.zeros((8, LANES), jnp.float32) for _ in PAIRS]
    for top in range(0, rows, 8):
        def column(t, acc, top=top):
            at = pl.ds(pl.multiple_of(t * LANES, LANES), LANES)
            old = []
            for j in range(HIST):
                res = past_residuals[slots[j], top : top + 8, at]
                aged[j, top : top + 8, at] = (
                    past_inputs[slots[j], top : top + 8, at] + mixing_share * res
                )
                old.append(res)
            return [a + old[i - 1] * old[j - 1] for a, (i, j) in zip(acc, PAIRS)]
        acc = lax.fori_loop(0, width // LANES, column, acc, unroll=4)
    tile[...] = spread([(v, total(a)) for v, a in enumerate(acc)], tile.shape)


def history(past_inputs, past_residuals, slots):
    size = past_inputs.size
    return pl.pallas_call(
        history_kernel,
        out_shape=(
            jax.ShapeDtypeStruct(past_inputs.shape, jnp.float32),
            jax.ShapeDtypeStruct((8, LANES), jnp.float32),
        ),
        in_specs=[VMEM, VMEM, SMEM],
        out_specs=(VMEM, VMEM),
        compiler_params=PARAMS,
        cost_estimate=pl.CostEstimate(flops=8 * size, bytes_accessed=12 * size, transcendentals=0),
        name="history",
    )(past_inputs, past_residuals, slots)


def residual_kernel(
    rows, smeared, current, past_residuals, old_tile, slots, classes, acoustic, optical, number, shift,
    fresh, tile,
):
    parts, height, slice_len = smeared.shape
    first = lax.axis_index("energy") * rows
    row = lax.broadcasted_iota(jnp.int32, (8, slice_len), 0) % rows
    lane = lax.broadcasted_iota(jnp.int32, (8, slice_len), 1)
    coupling = jnp.zeros((8, slice_len), jnp.float32)
    for i in range(rows):
        coupling = jnp.where(row == i, acoustic[classes[first + i]], coupling)
    modes = []
    for m in range(2):
        s = shift[m]
        modes.append((s, lane < slice_len - s, lane >= s, optical[m] * (number[m] + 1.0), optical[m] * number[m]))
    zero = jnp.zeros((8, slice_len), jnp.float32)
    acc = [zero] * (HIST + 1)
    for top in range(0, height, 8):
        at = slice(top, top + 8)
        source = [smeared[e, at, :] for e in range(parts)]
        sigma = [coupling * x for x in source]
        lesser = top < height // 2
        for s, keep_up, keep_down, emitted, absorbed in modes:
            up = [pltpu.roll(x, slice_len - s, 1) for x in source] + [zero]
            down = [zero] + [pltpu.roll(x, s, 1) for x in source]
            gain_up, gain_down = (emitted, absorbed) if lesser else (absorbed, emitted)
            for e in range(parts):
                above = jnp.where(keep_up, up[e], up[e + 1])
                below = jnp.where(keep_down, down[e + 1], down[e])
                sigma[e] = sigma[e] + (gain_up * above + gain_down * below)
        for e in range(parts):
            where = (at, slice(e * slice_len, (e + 1) * slice_len))
            new = sigma[e] - current[where]
            fresh[where] = new
            acc[0] = acc[0] + new * new
            for j in range(HIST):
                acc[j + 1] = acc[j + 1] + new * past_residuals[(slots[j],) + where]
    mine = jnp.concatenate([jnp.sum(a, axis=0, keepdims=True) for a in acc] + [zero[: 8 - HIST - 1]], axis=0)
    mine = jnp.sum(mine, axis=1, keepdims=True)
    lane = lax.broadcasted_iota(jnp.int32, old_tile.shape, 1)
    tile[...] = jnp.broadcast_to(jnp.where(lane == 2, mine, old_tile[...])[None], tile.shape)


def residual(smeared, current, past_residuals, old_tile, slots, classes, acoustic, optical, number, shift, rows, copies):
    return pl.pallas_call(
        lambda *refs: residual_kernel(rows, *refs),
        out_shape=(
            jax.ShapeDtypeStruct(current.shape, jnp.float32),
            jax.ShapeDtypeStruct((copies, 8, LANES), jnp.float32),
        ),
        in_specs=[VMEM] * 4 + [SMEM] * 6,
        out_specs=(VMEM, VMEM),
        compiler_params=PARAMS,
        name="residual",
    )(smeared, current, past_residuals, old_tile, slots, classes, acoustic, optical, number, shift)


def solve(products):
    prod = lambda i, j: products[(min(i, j), max(i, j))]
    n = HIST
    system = [
        [prod(i, j) - prod(i, j + 1) - prod(i + 1, j) + prod(i + 1, j + 1) for j in range(n)]
        for i in range(n)
    ]
    target = [prod(i, 0) - prod(i + 1, 0) for i in range(n)]
    trace = system[0][0]
    for i in range(1, n):
        trace = trace + system[i][i]
    ridge = ridge_share * trace / n + 1e-06
    for i in range(n):
        system[i][i] = system[i][i] + ridge
    inverse = [None] * n
    for k in range(n):
        inverse[k] = 1.0 / system[k][k]
        for i in range(k + 1, n):
            factor = system[k][i] * inverse[k]
            for j in range(i, n):
                system[i][j] = system[i][j] - factor * system[k][j]
            target[i] = target[i] - factor * target[k]
    gamma = [None] * n
    for k in range(n - 1, -1, -1):
        value = target[k]
        for j in range(k + 1, n):
            value = value - system[k][j] * gamma[j]
        gamma[k] = value * inverse[k]
    weights = [1.0 - gamma[0]]
    for j in range(1, n):
        weights.append(gamma[j - 1] - gamma[j])
    weights.append(gamma[n - 1])
    return weights


def mix_kernel(entries, tiles, fresh, current, aged, out, wide):
    summed = jnp.sum(tiles[...], axis=0) / entries
    for lane in range(wide.shape[0]):
        wide[lane] = jnp.broadcast_to(summed[:, lane : lane + 1], (8, LANES))
    products = {
        pair: jnp.broadcast_to(wide[spot // 8, spot % 8 : spot % 8 + 1, :], (8, LANES))
        for pair, spot in SPOTS.items()
    }
    weights = solve(products)
    rows, width = fresh.shape
    for top in range(0, rows, 8):
        for left in range(0, width, LANES):
            at = (slice(top, top + 8), slice(left, left + LANES))
            mixed = weights[0] * (current[at] + mixing_share * fresh[at])
            for j in range(HIST):
                mixed = mixed + weights[j + 1] * aged[(j,) + at]
            out[at] = mixed


def mix(tiles, fresh, current, aged, entries):
    return pl.pallas_call(
        lambda *refs: mix_kernel(entries, *refs),
        out_shape=jax.ShapeDtypeStruct(fresh.shape, jnp.float32),
        in_specs=[VMEM] * 4,
        out_specs=VMEM,
        scratch_shapes=[pltpu.VMEM((3, 8, LANES), jnp.float32)],
        compiler_params=PARAMS,
        name="mix",
    )(tiles, fresh, current, aged)


def per_device(
    greens,
    current,
    past_inputs,
    past_residuals,
    slot_order,
    neighbour,
    momentum_class,
    stencil_weight,
    acoustic_coupling,
    optical_coupling,
    occupation,
    phonon_shift,
):
    group_len, slice_len = greens.shape[3:]
    rows, width = current.shape[3:]
    groups = lax.axis_size("kgrp")
    parts = lax.axis_size("energy")
    own = greens.reshape(-1, group_len, slice_len)
    height = own.shape[0] * rows

    flat = current.reshape(height, width)
    old_in = past_inputs.reshape(HIST, height, width)
    old_res = past_residuals.reshape(HIST, height, width)
    stencil_hi, stencil_lo, smeared, tail = prepare(
        own, neighbour, stencil_weight, groups * group_len
    )
    sides = exchange(own, tail, groups)
    aged, old_tile = history(old_in, old_res, slot_order)
    for side in (NEAR, FAR):
        smeared = smear(side, sides[side], stencil_hi, stencil_lo, smeared, parts)
    smeared = lax.all_to_all(smeared, "energy", split_axis=0, concat_axis=0, tiled=True)
    fresh, tile = residual(
        smeared, flat, old_res, old_tile, slot_order, momentum_class, acoustic_coupling,
        optical_coupling, occupation, phonon_shift, rows, groups * parts,
    )
    tiles = lax.all_to_all(tile, ("kgrp", "energy"), split_axis=0, concat_axis=0, tiled=True)
    entries = float(flat.size * groups * parts)
    return mix(tiles, fresh, flat, aged, entries).reshape(current.shape)


def solution(mesh):
    return jax.shard_map(
        per_device,
        mesh=mesh,
        in_specs=(
            P(None, None, None, "kgrp", "energy"),
            P(None, None, None, ("kgrp", "energy"), None),
            P(None, None, None, None, ("kgrp", "energy"), None),
            P(None, None, None, None, ("kgrp", "energy"), None),
            P(),
            P("kgrp", None),
            P("kgrp"),
            P(),
            P(),
            P(),
            P(),
            P(),
        ),
        out_specs=P(None, None, None, ("kgrp", "energy"), None),
        check_vma=False,
    )
```

```python
import jax
import jax.numpy as jnp
from jax import lax
from jax.experimental import pallas as pl
from jax.experimental.pallas import tpu as pltpu
from jax.sharding import PartitionSpec as P

HIST = 5
LANES = 128

mixing_share = 0.5
ridge_share = 0.1

VMEM = pl.BlockSpec(memory_space=pltpu.VMEM)
SMEM = pl.BlockSpec(memory_space=pltpu.SMEM)
PARAMS = pltpu.CompilerParams(vmem_limit_bytes=16 * 1024 * 1024)

NEAR, FAR = 0, 1

PAIRS = [(i, j) for i in range(1, HIST + 1) for j in range(i, HIST + 1)]
SPOTS = {pair: v for v, pair in enumerate(PAIRS)}
for _j in range(HIST + 1):
    SPOTS[(0, _j)] = 16 + _j


def split(value):
    high = value.astype(jnp.bfloat16)
    return high, (value - high.astype(jnp.float32)).astype(jnp.bfloat16)


def product(left, right):
    dot = lambda a, b: jnp.dot(a, b, preferred_element_type=jnp.float32)
    return dot(left[0], right[0]) + (dot(left[0], right[1]) + dot(left[1], right[0]))


def prepare_kernel(total_k, own, neighbour, weight, stencil_hi, stencil_lo, part):
    comps, group_len, slice_len = own.shape
    group_id = lax.axis_index("kgrp")
    parts = lax.axis_size("energy")
    rows = group_len // parts
    targets = neighbour[...]
    place = lax.axis_index("energy")
    bit = 1
    while bit < parts:
        span = bit * rows
        blocks = [targets[at : at + span] for at in range(0, group_len, span)]
        flipped = [blocks[b ^ 1] for b in range(len(blocks))]
        targets = jnp.where(place & bit != 0, jnp.concatenate(flipped, axis=0), targets)
        bit *= 2
    local = (targets - group_id * group_len + (group_len + total_k)) % total_k
    spot = lax.broadcasted_iota(jnp.int32, (group_len, 3 * group_len), 1)
    stencil = jnp.zeros(spot.shape, jnp.float32)
    for n in range(local.shape[1]):
        stencil = stencil + jnp.where(spot == local[:, n : n + 1], weight[n], 0.0)
    before, after = stencil[:, :group_len], stencil[:, 2 * group_len :]
    swapped = paired(total_k // group_len) & (group_id % 2 == 1)
    near, far = jnp.where(swapped, before, after), jnp.where(swapped, after, before)
    stencil_hi[...], stencil_lo[...] = split(jnp.concatenate([near, far], axis=1))
    centre = split(stencil[:, group_len : 2 * group_len])
    for c in range(0, comps, 2):
        result = product(centre, split(jnp.concatenate([own[c], own[c + 1]], axis=1)))
        part[c] = result[:, :slice_len]
        part[c + 1] = result[:, slice_len:]


def prepare(own, neighbour, weight, total_k):
    group_len = own.shape[1]
    sides = jax.ShapeDtypeStruct((group_len, 2 * group_len), jnp.bfloat16)
    return pl.pallas_call(
        lambda *refs: prepare_kernel(total_k, *refs),
        out_shape=(sides, sides, jax.ShapeDtypeStruct(own.shape, jnp.float32)),
        in_specs=[VMEM, VMEM, SMEM],
        out_specs=(VMEM, VMEM, VMEM),
        compiler_params=PARAMS,
        cost_estimate=pl.CostEstimate(
            flops=6 * own.size * group_len, bytes_accessed=8 * own.size, transcendentals=0
        ),
        name="prepare",
    )(own, neighbour, weight)


def smear_kernel(side, count, *refs):
    blocks, (stencil_hi, stencil_lo, part), out = refs[:count], refs[count : count + 3], refs[count + 3 :]
    _, group_len, slice_len = blocks[0].shape
    at = slice(side * group_len, (side + 1) * group_len)
    stencil = (stencil_hi[:, at], stencil_lo[:, at])
    rows = group_len // len(out)
    first = 0
    for block in blocks:
        for c in range(0, block.shape[0], 2):
            result = product(stencil, split(jnp.concatenate([block[c], block[c + 1]], axis=1)))
            for p in range(2):
                at = first + c + p
                smeared = part[at] + result[:, p * slice_len : (p + 1) * slice_len]
                if side == NEAR:
                    out[0][at] = smeared
                    continue
                for m in range(len(out)):
                    out[m][at * rows : (at + 1) * rows, :] = smeared[m * rows : (m + 1) * rows]
        first += block.shape[0]


def smear(side, blocks, stencil_hi, stencil_lo, part, parts):
    comps, group_len, slice_len = part.shape
    if side == NEAR:
        out_shape = [jax.ShapeDtypeStruct(part.shape, jnp.float32)]
    else:
        out_shape = [jax.ShapeDtypeStruct((comps * group_len // parts, slice_len), jnp.float32)] * parts
    return pl.pallas_call(
        lambda *refs: smear_kernel(side, len(blocks), *refs),
        out_shape=out_shape,
        in_specs=[VMEM] * (len(blocks) + 3),
        out_specs=[VMEM] * len(out_shape),
        compiler_params=PARAMS,
        cost_estimate=pl.CostEstimate(
            flops=6 * part.size * group_len, bytes_accessed=12 * part.size, transcendentals=0
        ),
        name="smear",
    )(*blocks, stencil_hi, stencil_lo, part)


def paired(groups):
    return groups == 4


def exchange(own, groups):
    if not paired(groups):
        forward = [(i, (i + 1) % groups) for i in range(groups)]
        backward = [(target, source) for source, target in forward]
        return [lax.ppermute(own, "kgrp", backward)], [lax.ppermute(own, "kgrp", forward)]
    half = own.shape[0] // 2
    across = lambda block, flip: lax.ppermute(block, "kgrp", [(i, i ^ flip) for i in range(groups)])
    near = [across(own[:half], 1), across(own[half:], 1)]
    return near, [across(near[0], 2), across(own[half:], 3)]


def spread(values, shape):
    row = lax.broadcasted_iota(jnp.int32, shape, 0)
    lane = lax.broadcasted_iota(jnp.int32, shape, 1)
    tile = jnp.zeros(shape, jnp.float32)
    for spot, value in values:
        tile = jnp.where((row == spot % 8) & (lane == spot // 8), value, tile)
    return tile


def total(acc):
    return jnp.sum(jnp.sum(acc, axis=0, keepdims=True), axis=1, keepdims=True)


def history_kernel(past_inputs, past_residuals, slots, aged, tile):
    _, rows, width = past_inputs.shape
    acc = [jnp.zeros((8, LANES), jnp.float32) for _ in PAIRS]
    for top in range(0, rows, 8):
        def column(t, acc, top=top):
            at = pl.ds(pl.multiple_of(t * LANES, LANES), LANES)
            old = []
            for j in range(HIST):
                res = past_residuals[slots[j], top : top + 8, at]
                aged[j, top : top + 8, at] = (
                    past_inputs[slots[j], top : top + 8, at] + mixing_share * res
                )
                old.append(res)
            return [a + old[i - 1] * old[j - 1] for a, (i, j) in zip(acc, PAIRS)]
        acc = lax.fori_loop(0, width // LANES, column, acc, unroll=4)
    tile[...] = spread([(v, total(a)) for v, a in enumerate(acc)], tile.shape)


def history(past_inputs, past_residuals, slots):
    size = past_inputs.size
    return pl.pallas_call(
        history_kernel,
        out_shape=(
            jax.ShapeDtypeStruct(past_inputs.shape, jnp.float32),
            jax.ShapeDtypeStruct((8, LANES), jnp.float32),
        ),
        in_specs=[VMEM, VMEM, SMEM],
        out_specs=(VMEM, VMEM),
        compiler_params=PARAMS,
        cost_estimate=pl.CostEstimate(flops=8 * size, bytes_accessed=12 * size, transcendentals=0),
        name="history",
    )(past_inputs, past_residuals, slots)


def residual_kernel(rows, parts, *refs):
    received = refs[:parts]
    (current, past_residuals, old_tile, slots, classes, acoustic, optical, number, shift,
     fresh, tile, smeared) = refs[parts:]
    _, height, slice_len = smeared.shape
    place = lax.axis_index("energy")
    for m in range(parts):
        smeared[place ^ m] = received[m][...]
    first = place * rows
    row = lax.broadcasted_iota(jnp.int32, (8, slice_len), 0) % rows
    lane = lax.broadcasted_iota(jnp.int32, (8, slice_len), 1)
    coupling = jnp.zeros((8, slice_len), jnp.float32)
    for i in range(rows):
        coupling = jnp.where(row == i, acoustic[classes[first + i]], coupling)
    modes = []
    for m in range(2):
        s = shift[m]
        modes.append((s, lane < slice_len - s, lane >= s, optical[m] * (number[m] + 1.0), optical[m] * number[m]))
    zero = jnp.zeros((8, slice_len), jnp.float32)
    acc = [zero] * (HIST + 1)
    for top in range(0, height, 8):
        at = slice(top, top + 8)
        source = [smeared[e, at, :] for e in range(parts)]
        sigma = [coupling * x for x in source]
        lesser = top < height // 2
        for s, keep_up, keep_down, emitted, absorbed in modes:
            up = [pltpu.roll(x, slice_len - s, 1) for x in source] + [zero]
            down = [zero] + [pltpu.roll(x, s, 1) for x in source]
            gain_up, gain_down = (emitted, absorbed) if lesser else (absorbed, emitted)
            for e in range(parts):
                above = jnp.where(keep_up, up[e], up[e + 1])
                below = jnp.where(keep_down, down[e + 1], down[e])
                sigma[e] = sigma[e] + (gain_up * above + gain_down * below)
        for e in range(parts):
            where = (at, slice(e * slice_len, (e + 1) * slice_len))
            new = sigma[e] - current[where]
            fresh[where] = new
            acc[0] = acc[0] + new * new
            for j in range(HIST):
                acc[j + 1] = acc[j + 1] + new * past_residuals[(slots[j],) + where]
    mine = jnp.concatenate([jnp.sum(a, axis=0, keepdims=True) for a in acc] + [zero[: 8 - HIST - 1]], axis=0)
    mine = jnp.sum(mine, axis=1, keepdims=True)
    lane = lax.broadcasted_iota(jnp.int32, old_tile.shape, 1)
    tile[...] = jnp.broadcast_to(jnp.where(lane == 2, mine, old_tile[...])[None], tile.shape)


def residual(smeared, current, past_residuals, old_tile, slots, classes, acoustic, optical, number, shift, rows, copies):
    return pl.pallas_call(
        lambda *refs: residual_kernel(rows, len(smeared), *refs),
        out_shape=(
            jax.ShapeDtypeStruct(current.shape, jnp.float32),
            jax.ShapeDtypeStruct((copies, 8, LANES), jnp.float32),
        ),
        in_specs=[VMEM] * (len(smeared) + 3) + [SMEM] * 6,
        out_specs=(VMEM, VMEM),
        scratch_shapes=[pltpu.VMEM((len(smeared),) + smeared[0].shape, jnp.float32)],
        compiler_params=PARAMS,
        name="residual",
    )(*smeared, current, past_residuals, old_tile, slots, classes, acoustic, optical, number, shift)


def solve(products):
    prod = lambda i, j: products[(min(i, j), max(i, j))]
    n = HIST
    system = [
        [prod(i, j) - prod(i, j + 1) - prod(i + 1, j) + prod(i + 1, j + 1) for j in range(n)]
        for i in range(n)
    ]
    target = [prod(i, 0) - prod(i + 1, 0) for i in range(n)]
    trace = system[0][0]
    for i in range(1, n):
        trace = trace + system[i][i]
    ridge = ridge_share * trace / n + 1e-06
    for i in range(n):
        system[i][i] = system[i][i] + ridge
    inverse = [None] * n
    for k in range(n):
        inverse[k] = 1.0 / system[k][k]
        for i in range(k + 1, n):
            factor = system[k][i] * inverse[k]
            for j in range(i, n):
                system[i][j] = system[i][j] - factor * system[k][j]
            target[i] = target[i] - factor * target[k]
    gamma = [None] * n
    for k in range(n - 1, -1, -1):
        value = target[k]
        for j in range(k + 1, n):
            value = value - system[k][j] * gamma[j]
        gamma[k] = value * inverse[k]
    weights = [1.0 - gamma[0]]
    for j in range(1, n):
        weights.append(gamma[j - 1] - gamma[j])
    weights.append(gamma[n - 1])
    return weights


def mix_kernel(entries, tiles, fresh, current, aged, out, wide):
    summed = jnp.sum(tiles[...], axis=0) / entries
    for lane in range(wide.shape[0]):
        wide[lane] = jnp.broadcast_to(summed[:, lane : lane + 1], (8, LANES))
    products = {
        pair: jnp.broadcast_to(wide[spot // 8, spot % 8 : spot % 8 + 1, :], (8, LANES))
        for pair, spot in SPOTS.items()
    }
    weights = solve(products)
    rows, width = fresh.shape
    for top in range(0, rows, 8):
        for left in range(0, width, LANES):
            at = (slice(top, top + 8), slice(left, left + LANES))
            mixed = weights[0] * (current[at] + mixing_share * fresh[at])
            for j in range(HIST):
                mixed = mixed + weights[j + 1] * aged[(j,) + at]
            out[at] = mixed


def mix(tiles, fresh, current, aged, entries):
    return pl.pallas_call(
        lambda *refs: mix_kernel(entries, *refs),
        out_shape=jax.ShapeDtypeStruct(fresh.shape, jnp.float32),
        in_specs=[VMEM] * 4,
        out_specs=VMEM,
        scratch_shapes=[pltpu.VMEM((3, 8, LANES), jnp.float32)],
        compiler_params=PARAMS,
        name="mix",
    )(tiles, fresh, current, aged)


def per_device(
    greens,
    current,
    past_inputs,
    past_residuals,
    slot_order,
    neighbour,
    momentum_class,
    stencil_weight,
    acoustic_coupling,
    optical_coupling,
    occupation,
    phonon_shift,
):
    group_len, slice_len = greens.shape[3:]
    rows, width = current.shape[3:]
    groups = lax.axis_size("kgrp")
    parts = lax.axis_size("energy")
    own = greens.reshape(-1, group_len, slice_len)
    height = own.shape[0] * rows

    sides = exchange(own, groups)

    flat = current.reshape(height, width)
    old_in = past_inputs.reshape(HIST, height, width)
    old_res = past_residuals.reshape(HIST, height, width)
    stencil_hi, stencil_lo, smeared = prepare(own, neighbour, stencil_weight, groups * group_len)
    aged, old_tile = history(old_in, old_res, slot_order)
    (smeared,) = smear(NEAR, sides[NEAR], stencil_hi, stencil_lo, smeared, parts)
    smeared = list(smear(FAR, sides[FAR], stencil_hi, stencil_lo, smeared, parts))
    for m in range(parts - 1, 0, -1):
        smeared[m] = lax.ppermute(smeared[m], "energy", [(e, e ^ m) for e in range(parts)])
    fresh, tile = residual(
        smeared, flat, old_res, old_tile, slot_order, momentum_class, acoustic_coupling,
        optical_coupling, occupation, phonon_shift, rows, groups * parts,
    )
    tiles = lax.all_to_all(tile, ("kgrp", "energy"), split_axis=0, concat_axis=0, tiled=True)
    entries = float(flat.size * groups * parts)
    return mix(tiles, fresh, flat, aged, entries).reshape(current.shape)


def solution(mesh):
    return jax.shard_map(
        per_device,
        mesh=mesh,
        in_specs=(
            P(None, None, None, "kgrp", "energy"),
            P(None, None, None, ("kgrp", "energy"), None),
            P(None, None, None, None, ("kgrp", "energy"), None),
            P(None, None, None, None, ("kgrp", "energy"), None),
            P(),
            P("kgrp", None),
            P("kgrp"),
            P(),
            P(),
            P(),
            P(),
            P(),
        ),
        out_specs=P(None, None, None, ("kgrp", "energy"), None),
        check_vma=False,
    )
```

```python
import jax
import jax.numpy as jnp
from jax import lax
from jax.experimental import pallas as pl
from jax.experimental.pallas import tpu as pltpu
from jax.sharding import PartitionSpec as P

HIST = 5
LANES = 128

mixing_share = 0.5
ridge_share = 0.1

VMEM = pl.BlockSpec(memory_space=pltpu.VMEM)
SMEM = pl.BlockSpec(memory_space=pltpu.SMEM)
PARAMS = pltpu.CompilerParams(vmem_limit_bytes=16 * 1024 * 1024)

NEAR, FAR = 0, 1

PAIRS = [(i, j) for i in range(1, HIST + 1) for j in range(i, HIST + 1)]
SPOTS = {pair: v for v, pair in enumerate(PAIRS)}
for _j in range(HIST + 1):
    SPOTS[(0, _j)] = 16 + _j


def split(value):
    high = value.astype(jnp.bfloat16)
    return high, (value - high.astype(jnp.float32)).astype(jnp.bfloat16)


def product(left, right):
    dot = lambda a, b: jnp.dot(a, b, preferred_element_type=jnp.float32)
    return dot(left[0], right[0]) + (dot(left[0], right[1]) + dot(left[1], right[0]))


def prepare_kernel(total_k, own, neighbour, weight, stencil_hi, stencil_lo, part, tail):
    comps, group_len, slice_len = own.shape
    group_id = lax.axis_index("kgrp")
    parts = lax.axis_size("energy")
    rows = group_len // parts
    slots, _ = neighbour.shape
    padded = jnp.concatenate([neighbour[...], jnp.zeros((8 - slots, group_len), jnp.int32)], axis=0)
    targets = jnp.transpose(padded)
    place = lax.axis_index("energy")
    bit = 1
    while bit < parts:
        span = bit * rows
        blocks = [targets[at : at + span] for at in range(0, group_len, span)]
        flipped = [blocks[b ^ 1] for b in range(len(blocks))]
        targets = jnp.where(place & bit != 0, jnp.concatenate(flipped, axis=0), targets)
        bit *= 2
    local = (targets - group_id * group_len + (group_len + total_k)) % total_k
    spot = lax.broadcasted_iota(jnp.int32, (group_len, 3 * group_len), 1)
    stencil = jnp.zeros(spot.shape, jnp.float32)
    for n in range(slots):
        stencil = stencil + jnp.where(spot == local[:, n : n + 1], weight[n], 0.0)
    before, after = stencil[:, :group_len], stencil[:, 2 * group_len :]
    swapped = paired(total_k // group_len) & (group_id % 2 == 1)
    near, far = jnp.where(swapped, before, after), jnp.where(swapped, after, before)
    stencil_hi[...], stencil_lo[...] = split(jnp.concatenate([near, far], axis=1))
    centre = split(stencil[:, group_len : 2 * group_len])
    for c in range(0, comps, 2):
        result = product(centre, split(jnp.concatenate([own[c], own[c + 1]], axis=1)))
        if c >= comps - tail.shape[0]:
            at = c - comps + tail.shape[0]
            tail[at], tail[at + 1] = own[c], own[c + 1]
        part[c] = result[:, :slice_len]
        part[c + 1] = result[:, slice_len:]


def prepare(own, neighbour, weight, total_k):
    group_len = own.shape[1]
    sides = jax.ShapeDtypeStruct((group_len, 2 * group_len), jnp.bfloat16)
    tail = jax.ShapeDtypeStruct((own.shape[0] // 2,) + own.shape[1:], jnp.float32)
    return pl.pallas_call(
        lambda *refs: prepare_kernel(total_k, *refs),
        out_shape=(sides, sides, jax.ShapeDtypeStruct(own.shape, jnp.float32), tail),
        in_specs=[VMEM, VMEM, SMEM],
        out_specs=(VMEM,) * 4,
        compiler_params=PARAMS,
        cost_estimate=pl.CostEstimate(
            flops=6 * own.size * group_len, bytes_accessed=8 * own.size, transcendentals=0
        ),
        name="prepare",
    )(own, jnp.transpose(neighbour), weight)


def smear_kernel(side, count, *refs):
    blocks, (stencil_hi, stencil_lo, part, _) = refs[:count], refs[count : count + 4]
    out = refs[count + 4 :]
    _, group_len, slice_len = blocks[0].shape
    at = slice(side * group_len, (side + 1) * group_len)
    stencil = (stencil_hi[:, at], stencil_lo[:, at])
    rows = group_len // len(out)
    first = 0
    for block in blocks:
        for c in range(0, block.shape[0], 2):
            result = product(stencil, split(jnp.concatenate([block[c], block[c + 1]], axis=1)))
            for p in range(2):
                at = first + c + p
                smeared = part[at] + result[:, p * slice_len : (p + 1) * slice_len]
                if side == NEAR:
                    out[0][at] = smeared
                    continue
                for m in range(len(out)):
                    out[m][at * rows : (at + 1) * rows, :] = smeared[m * rows : (m + 1) * rows]
        first += block.shape[0]


def smear(side, blocks, stencil_hi, stencil_lo, part, after, parts):
    comps, group_len, slice_len = part.shape
    if side == NEAR:
        out_shape = [jax.ShapeDtypeStruct(part.shape, jnp.float32)]
    else:
        out_shape = [jax.ShapeDtypeStruct((comps * group_len // parts, slice_len), jnp.float32)] * parts
    return pl.pallas_call(
        lambda *refs: smear_kernel(side, len(blocks), *refs),
        out_shape=out_shape,
        in_specs=[VMEM] * (len(blocks) + 4),
        out_specs=[VMEM] * len(out_shape),
        compiler_params=PARAMS,
        cost_estimate=pl.CostEstimate(
            flops=6 * part.size * group_len, bytes_accessed=12 * part.size, transcendentals=0
        ),
        name="smear",
    )(*blocks, stencil_hi, stencil_lo, part, after)


def paired(groups):
    return groups == 4


def exchange(own, tail, groups):
    if not paired(groups):
        forward = [(i, (i + 1) % groups) for i in range(groups)]
        backward = [(target, source) for source, target in forward]
        return [lax.ppermute(own, "kgrp", backward)], [lax.ppermute(own, "kgrp", forward)]
    across = lambda block, flip: lax.ppermute(block, "kgrp", [(i, i ^ flip) for i in range(groups)])
    head = across(own[: own.shape[0] - tail.shape[0]], 1)
    return [head, across(tail, 1)], [across(head, 2), across(tail, 3)]


def spread(values, shape):
    row = lax.broadcasted_iota(jnp.int32, shape, 0)
    lane = lax.broadcasted_iota(jnp.int32, shape, 1)
    tile = jnp.zeros(shape, jnp.float32)
    for spot, value in values:
        tile = jnp.where((row == spot % 8) & (lane == spot // 8), value, tile)
    return tile


def total(acc):
    return jnp.sum(jnp.sum(acc, axis=0, keepdims=True), axis=1, keepdims=True)


def history_kernel(past_inputs, past_residuals, slots, aged, tile):
    _, rows, width = past_inputs.shape
    acc = [jnp.zeros((8, LANES), jnp.float32) for _ in PAIRS]
    for top in range(0, rows, 8):
        def column(t, acc, top=top):
            at = pl.ds(pl.multiple_of(t * LANES, LANES), LANES)
            old = []
            for j in range(HIST):
                res = past_residuals[slots[j], top : top + 8, at]
                aged[j, top : top + 8, at] = (
                    past_inputs[slots[j], top : top + 8, at] + mixing_share * res
                )
                old.append(res)
            return [a + old[i - 1] * old[j - 1] for a, (i, j) in zip(acc, PAIRS)]
        acc = lax.fori_loop(0, width // LANES, column, acc, unroll=4)
    tile[...] = spread([(v, total(a)) for v, a in enumerate(acc)], tile.shape)


def history(past_inputs, past_residuals, slots):
    size = past_inputs.size
    return pl.pallas_call(
        history_kernel,
        out_shape=(
            jax.ShapeDtypeStruct(past_inputs.shape, jnp.float32),
            jax.ShapeDtypeStruct((8, LANES), jnp.float32),
        ),
        in_specs=[VMEM, VMEM, SMEM],
        out_specs=(VMEM, VMEM),
        compiler_params=PARAMS,
        cost_estimate=pl.CostEstimate(flops=8 * size, bytes_accessed=12 * size, transcendentals=0),
        name="history",
    )(past_inputs, past_residuals, slots)


def residual_kernel(rows, parts, *refs):
    received = refs[:parts]
    (current, past_residuals, old_tile, slots, classes, acoustic, optical, number, shift,
     fresh, tile, smeared) = refs[parts:]
    _, height, slice_len = smeared.shape
    place = lax.axis_index("energy")
    for m in range(parts):
        smeared[place ^ m] = received[m][...]
    first = place * rows
    row = lax.broadcasted_iota(jnp.int32, (8, slice_len), 0) % rows
    lane = lax.broadcasted_iota(jnp.int32, (8, slice_len), 1)
    coupling = jnp.zeros((8, slice_len), jnp.float32)
    for i in range(rows):
        coupling = jnp.where(row == i, acoustic[classes[first + i]], coupling)
    modes = []
    for m in range(2):
        s = shift[m]
        modes.append((s, lane < slice_len - s, lane >= s, optical[m] * (number[m] + 1.0), optical[m] * number[m]))
    zero = jnp.zeros((8, slice_len), jnp.float32)
    acc = [zero] * (HIST + 1)
    for top in range(0, height, 8):
        at = slice(top, top + 8)
        source = [smeared[e, at, :] for e in range(parts)]
        sigma = [coupling * x for x in source]
        lesser = top < height // 2
        for s, keep_up, keep_down, emitted, absorbed in modes:
            up = [pltpu.roll(x, slice_len - s, 1) for x in source] + [zero]
            down = [zero] + [pltpu.roll(x, s, 1) for x in source]
            gain_up, gain_down = (emitted, absorbed) if lesser else (absorbed, emitted)
            for e in range(parts):
                above = jnp.where(keep_up, up[e], up[e + 1])
                below = jnp.where(keep_down, down[e + 1], down[e])
                sigma[e] = sigma[e] + (gain_up * above + gain_down * below)
        for e in range(parts):
            where = (at, slice(e * slice_len, (e + 1) * slice_len))
            new = sigma[e] - current[where]
            fresh[where] = new
            acc[0] = acc[0] + new * new
            for j in range(HIST):
                acc[j + 1] = acc[j + 1] + new * past_residuals[(slots[j],) + where]
    mine = jnp.concatenate([jnp.sum(a, axis=0, keepdims=True) for a in acc] + [zero[: 8 - HIST - 1]], axis=0)
    mine = jnp.sum(mine, axis=1, keepdims=True)
    lane = lax.broadcasted_iota(jnp.int32, old_tile.shape, 1)
    tile[...] = jnp.broadcast_to(jnp.where(lane == 2, mine, old_tile[...])[None], tile.shape)


def residual(smeared, current, past_residuals, old_tile, slots, classes, acoustic, optical, number, shift, rows, copies):
    return pl.pallas_call(
        lambda *refs: residual_kernel(rows, len(smeared), *refs),
        out_shape=(
            jax.ShapeDtypeStruct(current.shape, jnp.float32),
            jax.ShapeDtypeStruct((copies, 8, LANES), jnp.float32),
        ),
        in_specs=[VMEM] * (len(smeared) + 3) + [SMEM] * 6,
        out_specs=(VMEM, VMEM),
        scratch_shapes=[pltpu.VMEM((len(smeared),) + smeared[0].shape, jnp.float32)],
        compiler_params=PARAMS,
        name="residual",
    )(*smeared, current, past_residuals, old_tile, slots, classes, acoustic, optical, number, shift)


def solve(products):
    prod = lambda i, j: products[(min(i, j), max(i, j))]
    n = HIST
    system = [
        [prod(i, j) - prod(i, j + 1) - prod(i + 1, j) + prod(i + 1, j + 1) for j in range(n)]
        for i in range(n)
    ]
    target = [prod(i, 0) - prod(i + 1, 0) for i in range(n)]
    trace = system[0][0]
    for i in range(1, n):
        trace = trace + system[i][i]
    ridge = ridge_share * trace / n + 1e-06
    for i in range(n):
        system[i][i] = system[i][i] + ridge
    inverse = [None] * n
    for k in range(n):
        inverse[k] = 1.0 / system[k][k]
        for i in range(k + 1, n):
            factor = system[k][i] * inverse[k]
            for j in range(i, n):
                system[i][j] = system[i][j] - factor * system[k][j]
            target[i] = target[i] - factor * target[k]
    gamma = [None] * n
    for k in range(n - 1, -1, -1):
        value = target[k]
        for j in range(k + 1, n):
            value = value - system[k][j] * gamma[j]
        gamma[k] = value * inverse[k]
    weights = [1.0 - gamma[0]]
    for j in range(1, n):
        weights.append(gamma[j - 1] - gamma[j])
    weights.append(gamma[n - 1])
    return weights


def mix_kernel(entries, tiles, fresh, current, aged, out, wide):
    summed = jnp.sum(tiles[...], axis=0) / entries
    for lane in range(wide.shape[0]):
        wide[lane] = jnp.broadcast_to(summed[:, lane : lane + 1], (8, LANES))
    products = {
        pair: jnp.broadcast_to(wide[spot // 8, spot % 8 : spot % 8 + 1, :], (8, LANES))
        for pair, spot in SPOTS.items()
    }
    weights = solve(products)
    rows, width = fresh.shape
    for top in range(0, rows, 8):
        for left in range(0, width, LANES):
            at = (slice(top, top + 8), slice(left, left + LANES))
            mixed = weights[0] * (current[at] + mixing_share * fresh[at])
            for j in range(HIST):
                mixed = mixed + weights[j + 1] * aged[(j,) + at]
            out[at] = mixed


def mix(tiles, fresh, current, aged, entries):
    return pl.pallas_call(
        lambda *refs: mix_kernel(entries, *refs),
        out_shape=jax.ShapeDtypeStruct(fresh.shape, jnp.float32),
        in_specs=[VMEM] * 4,
        out_specs=VMEM,
        scratch_shapes=[pltpu.VMEM((3, 8, LANES), jnp.float32)],
        compiler_params=PARAMS,
        name="mix",
    )(tiles, fresh, current, aged)


def per_device(
    greens,
    current,
    past_inputs,
    past_residuals,
    slot_order,
    neighbour,
    momentum_class,
    stencil_weight,
    acoustic_coupling,
    optical_coupling,
    occupation,
    phonon_shift,
):
    group_len, slice_len = greens.shape[3:]
    rows, width = current.shape[3:]
    groups = lax.axis_size("kgrp")
    parts = lax.axis_size("energy")
    own = greens.reshape(-1, group_len, slice_len)
    height = own.shape[0] * rows

    flat = current.reshape(height, width)
    old_in = past_inputs.reshape(HIST, height, width)
    old_res = past_residuals.reshape(HIST, height, width)
    stencil_hi, stencil_lo, smeared, tail = prepare(
        own, neighbour, stencil_weight, groups * group_len
    )
    sides = exchange(own, tail, groups)
    aged, old_tile = history(old_in, old_res, slot_order)
    (smeared,) = smear(NEAR, sides[NEAR], stencil_hi, stencil_lo, smeared, old_tile, parts)
    smeared = list(smear(FAR, sides[FAR], stencil_hi, stencil_lo, smeared, old_tile, parts))
    for m in range(parts - 1, 0, -1):
        smeared[m] = lax.ppermute(smeared[m], "energy", [(e, e ^ m) for e in range(parts)])
    fresh, tile = residual(
        smeared, flat, old_res, old_tile, slot_order, momentum_class, acoustic_coupling,
        optical_coupling, occupation, phonon_shift, rows, groups * parts,
    )
    tiles = lax.all_to_all(tile, ("kgrp", "energy"), split_axis=0, concat_axis=0, tiled=True)
    entries = float(flat.size * groups * parts)
    return mix(tiles, fresh, flat, aged, entries).reshape(current.shape)


def solution(mesh):
    return jax.shard_map(
        per_device,
        mesh=mesh,
        in_specs=(
            P(None, None, None, "kgrp", "energy"),
            P(None, None, None, ("kgrp", "energy"), None),
            P(None, None, None, None, ("kgrp", "energy"), None),
            P(None, None, None, None, ("kgrp", "energy"), None),
            P(),
            P("kgrp", None),
            P("kgrp"),
            P(),
            P(),
            P(),
            P(),
            P(),
        ),
        out_specs=P(None, None, None, ("kgrp", "energy"), None),
        check_vma=False,
    )
```

```python
import jax
import jax.numpy as jnp
from jax import lax
from jax.experimental import pallas as pl
from jax.experimental.pallas import tpu as pltpu
from jax.sharding import PartitionSpec as P

HIST = 5
LANES = 128

mixing_share = 0.5
ridge_share = 0.1

VMEM = pl.BlockSpec(memory_space=pltpu.VMEM)
SMEM = pl.BlockSpec(memory_space=pltpu.SMEM)
PARAMS = pltpu.CompilerParams(vmem_limit_bytes=16 * 1024 * 1024)

NEAR, FAR = 0, 1

PAIRS = [(i, j) for i in range(1, HIST + 1) for j in range(i, HIST + 1)]
SPOTS = {pair: v for v, pair in enumerate(PAIRS)}
for _j in range(HIST + 1):
    SPOTS[(0, _j)] = 16 + _j


def split(value):
    high = value.astype(jnp.bfloat16)
    return high, (value - high.astype(jnp.float32)).astype(jnp.bfloat16)


def product(left, right):
    dot = lambda a, b: jnp.dot(a, b, preferred_element_type=jnp.float32)
    return dot(left[0], right[0]) + (dot(left[0], right[1]) + dot(left[1], right[0]))


def prepare_kernel(total_k, own, neighbour, weight, stencil_hi, stencil_lo, part):
    comps, group_len, slice_len = own.shape
    group_id = lax.axis_index("kgrp")
    parts = lax.axis_size("energy")
    rows = group_len // parts
    slots, _ = neighbour.shape
    padded = jnp.concatenate([neighbour[...], jnp.zeros((8 - slots, group_len), jnp.int32)], axis=0)
    targets = jnp.transpose(padded)
    place = lax.axis_index("energy")
    bit = 1
    while bit < parts:
        span = bit * rows
        blocks = [targets[at : at + span] for at in range(0, group_len, span)]
        flipped = [blocks[b ^ 1] for b in range(len(blocks))]
        targets = jnp.where(place & bit != 0, jnp.concatenate(flipped, axis=0), targets)
        bit *= 2
    local = (targets - group_id * group_len + (group_len + total_k)) % total_k
    spot = lax.broadcasted_iota(jnp.int32, (group_len, 3 * group_len), 1)
    stencil = jnp.zeros(spot.shape, jnp.float32)
    for n in range(slots):
        stencil = stencil + jnp.where(spot == local[:, n : n + 1], weight[n], 0.0)
    before, after = stencil[:, :group_len], stencil[:, 2 * group_len :]
    swapped = paired(total_k // group_len) & (group_id % 2 == 1)
    near, far = jnp.where(swapped, before, after), jnp.where(swapped, after, before)
    stencil_hi[...], stencil_lo[...] = split(jnp.concatenate([near, far], axis=1))
    centre = split(stencil[:, group_len : 2 * group_len])
    for c in range(0, comps, 2):
        result = product(centre, split(jnp.concatenate([own[c], own[c + 1]], axis=1)))
        part[c] = result[:, :slice_len]
        part[c + 1] = result[:, slice_len:]


def prepare(own, neighbour, weight, total_k):
    group_len = own.shape[1]
    sides = jax.ShapeDtypeStruct((group_len, 2 * group_len), jnp.bfloat16)
    return pl.pallas_call(
        lambda *refs: prepare_kernel(total_k, *refs),
        out_shape=(sides, sides, jax.ShapeDtypeStruct(own.shape, jnp.float32)),
        in_specs=[VMEM, VMEM, SMEM],
        out_specs=(VMEM,) * 3,
        compiler_params=PARAMS,
        cost_estimate=pl.CostEstimate(
            flops=6 * own.size * group_len, bytes_accessed=8 * own.size, transcendentals=0
        ),
        name="prepare",
    )(own, jnp.transpose(neighbour), weight)


def smear_kernel(side, count, *refs):
    blocks, (stencil_hi, stencil_lo, part, _) = refs[:count], refs[count : count + 4]
    out = refs[count + 4 :]
    _, group_len, slice_len = blocks[0].shape
    at = slice(side * group_len, (side + 1) * group_len)
    stencil = (stencil_hi[:, at], stencil_lo[:, at])
    first = 0
    for block in blocks:
        for c in range(0, block.shape[0], 2):
            result = product(stencil, split(jnp.concatenate([block[c], block[c + 1]], axis=1)))
            for p in range(2):
                at = first + c + p
                smeared = part[at] + result[:, p * slice_len : (p + 1) * slice_len]
                if side == NEAR:
                    out[0][at] = smeared
                    continue
                chips, height, _ = out[0].shape
                rows = height // part.shape[0]
                for m in range(2 * chips):
                    out[m % 2][m // 2, at * rows : (at + 1) * rows, :] = smeared[m * rows : (m + 1) * rows]
        first += block.shape[0]


def smear(side, blocks, stencil_hi, stencil_lo, part, after, parts):
    comps, group_len, slice_len = part.shape
    if side == NEAR:
        out_shape = [jax.ShapeDtypeStruct(part.shape, jnp.float32)]
    else:
        shape = (parts // 2, comps * group_len // parts, slice_len)
        out_shape = [jax.ShapeDtypeStruct(shape, jnp.float32)] * 2
    return pl.pallas_call(
        lambda *refs: smear_kernel(side, len(blocks), *refs),
        out_shape=out_shape,
        in_specs=[VMEM] * (len(blocks) + 4),
        out_specs=[VMEM] * len(out_shape),
        compiler_params=PARAMS,
        cost_estimate=pl.CostEstimate(
            flops=6 * part.size * group_len, bytes_accessed=12 * part.size, transcendentals=0
        ),
        name="smear",
    )(*blocks, stencil_hi, stencil_lo, part, after)


def join_kernel(own, swapped, *out):
    for chip, block in enumerate(out, 1):
        block[0], block[1] = own[chip], swapped[chip]


def join(own, swapped):
    chips, height, slice_len = own.shape
    shape = jax.ShapeDtypeStruct((2, height, slice_len), jnp.float32)
    return pl.pallas_call(
        join_kernel,
        out_shape=[shape] * (chips - 1),
        in_specs=[VMEM] * 2,
        out_specs=[VMEM] * (chips - 1),
        compiler_params=PARAMS,
        name="join",
    )(own, swapped)


def paired(groups):
    return groups == 4


def exchange(own, groups):
    if not paired(groups):
        forward = [(i, (i + 1) % groups) for i in range(groups)]
        backward = [(target, source) for source, target in forward]
        return [lax.ppermute(own, "kgrp", backward)], [lax.ppermute(own, "kgrp", forward)]
    across = lambda block, flip: lax.ppermute(block, "kgrp", [(i, i ^ flip) for i in range(groups)])
    half = own.shape[0] // 2
    near = [across(own[:half], 1), across(own[half:], 1)]
    return near, [across(near[0], 2), across(own[half:], 3)]


def spread(values, shape):
    row = lax.broadcasted_iota(jnp.int32, shape, 0)
    lane = lax.broadcasted_iota(jnp.int32, shape, 1)
    tile = jnp.zeros(shape, jnp.float32)
    for spot, value in values:
        tile = jnp.where((row == spot % 8) & (lane == spot // 8), value, tile)
    return tile


def total(acc):
    return jnp.sum(jnp.sum(acc, axis=0, keepdims=True), axis=1, keepdims=True)


def history_kernel(past_inputs, past_residuals, slots, aged, tile):
    _, rows, width = past_inputs.shape
    acc = [jnp.zeros((8, LANES), jnp.float32) for _ in PAIRS]
    for top in range(0, rows, 8):
        def column(t, acc, top=top):
            at = pl.ds(pl.multiple_of(t * LANES, LANES), LANES)
            old = []
            for j in range(HIST):
                res = past_residuals[slots[j], top : top + 8, at]
                aged[j, top : top + 8, at] = (
                    past_inputs[slots[j], top : top + 8, at] + mixing_share * res
                )
                old.append(res)
            return [a + old[i - 1] * old[j - 1] for a, (i, j) in zip(acc, PAIRS)]
        acc = lax.fori_loop(0, width // LANES, column, acc, unroll=4)
    tile[...] = spread([(v, total(a)) for v, a in enumerate(acc)], tile.shape)


def history(past_inputs, past_residuals, slots):
    size = past_inputs.size
    return pl.pallas_call(
        history_kernel,
        out_shape=(
            jax.ShapeDtypeStruct(past_inputs.shape, jnp.float32),
            jax.ShapeDtypeStruct((8, LANES), jnp.float32),
        ),
        in_specs=[VMEM, VMEM, SMEM],
        out_specs=(VMEM, VMEM),
        compiler_params=PARAMS,
        cost_estimate=pl.CostEstimate(flops=8 * size, bytes_accessed=12 * size, transcendentals=0),
        name="history",
    )(past_inputs, past_residuals, slots)


def residual_kernel(rows, count, own, swapped, *refs):
    received = refs[:count]
    (current, past_residuals, old_tile, slots, classes, acoustic, optical, number, shift,
     fresh, tile, smeared) = refs[count:]
    parts, height, slice_len = smeared.shape
    place = lax.axis_index("energy")
    smeared[place], smeared[place ^ 1] = own[0], swapped[0]
    for chip, block in enumerate(received, 1):
        smeared[place ^ (2 * chip)], smeared[place ^ (2 * chip + 1)] = block[0], block[1]
    first = place * rows
    row = lax.broadcasted_iota(jnp.int32, (8, slice_len), 0) % rows
    lane = lax.broadcasted_iota(jnp.int32, (8, slice_len), 1)
    coupling = jnp.zeros((8, slice_len), jnp.float32)
    for i in range(rows):
        coupling = jnp.where(row == i, acoustic[classes[first + i]], coupling)
    modes = []
    for m in range(2):
        s = shift[m]
        modes.append((s, lane < slice_len - s, lane >= s, optical[m] * (number[m] + 1.0), optical[m] * number[m]))
    zero = jnp.zeros((8, slice_len), jnp.float32)
    acc = [zero] * (HIST + 1)
    for top in range(0, height, 8):
        at = slice(top, top + 8)
        source = [smeared[e, at, :] for e in range(parts)]
        sigma = [coupling * x for x in source]
        lesser = top < height // 2
        for s, keep_up, keep_down, emitted, absorbed in modes:
            up = [pltpu.roll(x, slice_len - s, 1) for x in source] + [zero]
            down = [zero] + [pltpu.roll(x, s, 1) for x in source]
            gain_up, gain_down = (emitted, absorbed) if lesser else (absorbed, emitted)
            for e in range(parts):
                above = jnp.where(keep_up, up[e], up[e + 1])
                below = jnp.where(keep_down, down[e + 1], down[e])
                sigma[e] = sigma[e] + (gain_up * above + gain_down * below)
        for e in range(parts):
            where = (at, slice(e * slice_len, (e + 1) * slice_len))
            new = sigma[e] - current[where]
            fresh[where] = new
            acc[0] = acc[0] + new * new
            for j in range(HIST):
                acc[j + 1] = acc[j + 1] + new * past_residuals[(slots[j],) + where]
    mine = jnp.concatenate([jnp.sum(a, axis=0, keepdims=True) for a in acc] + [zero[: 8 - HIST - 1]], axis=0)
    mine = jnp.sum(mine, axis=1, keepdims=True)
    lane = lax.broadcasted_iota(jnp.int32, old_tile.shape, 1)
    tile[...] = jnp.broadcast_to(jnp.where(lane == 2, mine, old_tile[...])[None], tile.shape)


def residual(kept, swapped, smeared, current, past_residuals, old_tile, slots, classes, acoustic, optical, number, shift, rows, copies):
    return pl.pallas_call(
        lambda *refs: residual_kernel(rows, len(smeared), *refs),
        out_shape=(
            jax.ShapeDtypeStruct(current.shape, jnp.float32),
            jax.ShapeDtypeStruct((copies, 8, LANES), jnp.float32),
        ),
        in_specs=[VMEM] * (len(smeared) + 5) + [SMEM] * 6,
        out_specs=(VMEM, VMEM),
        scratch_shapes=[pltpu.VMEM((2 * kept.shape[0],) + kept.shape[1:], jnp.float32)],
        compiler_params=PARAMS,
        name="residual",
    )(kept, swapped, *smeared, current, past_residuals, old_tile, slots, classes, acoustic, optical, number, shift)


def solve(products):
    prod = lambda i, j: products[(min(i, j), max(i, j))]
    n = HIST
    system = [
        [prod(i, j) - prod(i, j + 1) - prod(i + 1, j) + prod(i + 1, j + 1) for j in range(n)]
        for i in range(n)
    ]
    target = [prod(i, 0) - prod(i + 1, 0) for i in range(n)]
    trace = system[0][0]
    for i in range(1, n):
        trace = trace + system[i][i]
    ridge = ridge_share * trace / n + 1e-06
    for i in range(n):
        system[i][i] = system[i][i] + ridge
    inverse = [None] * n
    for k in range(n):
        inverse[k] = 1.0 / system[k][k]
        for i in range(k + 1, n):
            factor = system[k][i] * inverse[k]
            for j in range(i, n):
                system[i][j] = system[i][j] - factor * system[k][j]
            target[i] = target[i] - factor * target[k]
    gamma = [None] * n
    for k in range(n - 1, -1, -1):
        value = target[k]
        for j in range(k + 1, n):
            value = value - system[k][j] * gamma[j]
        gamma[k] = value * inverse[k]
    weights = [1.0 - gamma[0]]
    for j in range(1, n):
        weights.append(gamma[j - 1] - gamma[j])
    weights.append(gamma[n - 1])
    return weights


def mix_kernel(entries, tiles, fresh, current, aged, out, wide):
    summed = jnp.sum(tiles[...], axis=0) / entries
    for lane in range(wide.shape[0]):
        wide[lane] = jnp.broadcast_to(summed[:, lane : lane + 1], (8, LANES))
    products = {
        pair: jnp.broadcast_to(wide[spot // 8, spot % 8 : spot % 8 + 1, :], (8, LANES))
        for pair, spot in SPOTS.items()
    }
    weights = solve(products)
    rows, width = fresh.shape
    for top in range(0, rows, 8):
        for left in range(0, width, LANES):
            at = (slice(top, top + 8), slice(left, left + LANES))
            mixed = weights[0] * (current[at] + mixing_share * fresh[at])
            for j in range(HIST):
                mixed = mixed + weights[j + 1] * aged[(j,) + at]
            out[at] = mixed


def mix(tiles, fresh, current, aged, entries):
    return pl.pallas_call(
        lambda *refs: mix_kernel(entries, *refs),
        out_shape=jax.ShapeDtypeStruct(fresh.shape, jnp.float32),
        in_specs=[VMEM] * 4,
        out_specs=VMEM,
        scratch_shapes=[pltpu.VMEM((3, 8, LANES), jnp.float32)],
        compiler_params=PARAMS,
        name="mix",
    )(tiles, fresh, current, aged)


def per_device(
    greens,
    current,
    past_inputs,
    past_residuals,
    slot_order,
    neighbour,
    momentum_class,
    stencil_weight,
    acoustic_coupling,
    optical_coupling,
    occupation,
    phonon_shift,
):
    group_len, slice_len = greens.shape[3:]
    rows, width = current.shape[3:]
    groups = lax.axis_size("kgrp")
    parts = lax.axis_size("energy")
    own = greens.reshape(-1, group_len, slice_len)
    height = own.shape[0] * rows

    flat = current.reshape(height, width)
    old_in = past_inputs.reshape(HIST, height, width)
    old_res = past_residuals.reshape(HIST, height, width)
    sides = exchange(own, groups)
    stencil_hi, stencil_lo, smeared = prepare(own, neighbour, stencil_weight, groups * group_len)
    aged, old_tile = history(old_in, old_res, slot_order)
    (smeared,) = smear(NEAR, sides[NEAR], stencil_hi, stencil_lo, smeared, old_tile, parts)
    kept, given = smear(FAR, sides[FAR], stencil_hi, stencil_lo, smeared, old_tile, parts)
    meet = lambda block, m: lax.ppermute(block, "energy", [(e, e ^ m) for e in range(parts)])
    swapped = meet(given, 1)
    smeared = [meet(block, 2 * chip) for chip, block in enumerate(join(kept, swapped), 1)]
    fresh, tile = residual(
        kept, swapped, smeared, flat, old_res, old_tile, slot_order, momentum_class, acoustic_coupling,
        optical_coupling, occupation, phonon_shift, rows, groups * parts,
    )
    tiles = lax.all_to_all(tile, ("kgrp", "energy"), split_axis=0, concat_axis=0, tiled=True)
    entries = float(flat.size * groups * parts)
    return mix(tiles, fresh, flat, aged, entries).reshape(current.shape)


def solution(mesh):
    return jax.shard_map(
        per_device,
        mesh=mesh,
        in_specs=(
            P(None, None, None, "kgrp", "energy"),
            P(None, None, None, ("kgrp", "energy"), None),
            P(None, None, None, None, ("kgrp", "energy"), None),
            P(None, None, None, None, ("kgrp", "energy"), None),
            P(),
            P("kgrp", None),
            P("kgrp"),
            P(),
            P(),
            P(),
            P(),
            P(),
        ),
        out_specs=P(None, None, None, ("kgrp", "energy"), None),
        check_vma=False,
    )
```

```python
import jax
import jax.numpy as jnp
from jax import lax
from jax.experimental import pallas as pl
from jax.experimental.pallas import tpu as pltpu
from jax.sharding import PartitionSpec as P

HIST = 5
LANES = 128

mixing_share = 0.5
ridge_share = 0.1

VMEM = pl.BlockSpec(memory_space=pltpu.VMEM)
SMEM = pl.BlockSpec(memory_space=pltpu.SMEM)
PARAMS = pltpu.CompilerParams(vmem_limit_bytes=16 * 1024 * 1024)

CHUNKS = 2

PAIRS = [(i, j) for i in range(1, HIST + 1) for j in range(i, HIST + 1)]
SPOTS = {pair: v for v, pair in enumerate(PAIRS)}
for _j in range(HIST + 1):
    SPOTS[(0, _j)] = 16 + _j


def split(value):
    high = value.astype(jnp.bfloat16)
    return high, (value - high.astype(jnp.float32)).astype(jnp.bfloat16)


def product(left, right):
    dot = lambda a, b: jnp.dot(a, b, preferred_element_type=jnp.float32)
    return dot(left[0], right[0]) + (dot(left[0], right[1]) + dot(left[1], right[0]))


def prepare_kernel(total_k, own, neighbour, weight, _, stencil_hi, stencil_lo, part):
    comps, group_len, slice_len = own.shape
    group_id = lax.axis_index("kgrp")
    parts = lax.axis_size("energy")
    rows = group_len // parts
    slots, _ = neighbour.shape
    padded = jnp.concatenate([neighbour[...], jnp.zeros((8 - slots, group_len), jnp.int32)], axis=0)
    targets = jnp.transpose(padded)
    place = lax.axis_index("energy")
    bit = 1
    while bit < parts:
        span = bit * rows
        blocks = [targets[at : at + span] for at in range(0, group_len, span)]
        flipped = [blocks[b ^ 1] for b in range(len(blocks))]
        targets = jnp.where(place & bit != 0, jnp.concatenate(flipped, axis=0), targets)
        bit *= 2
    local = (targets - group_id * group_len + (group_len + total_k)) % total_k
    spot = lax.broadcasted_iota(jnp.int32, (group_len, 3 * group_len), 1)
    stencil = jnp.zeros(spot.shape, jnp.float32)
    for n in range(slots):
        stencil = stencil + jnp.where(spot == local[:, n : n + 1], weight[n], 0.0)
    before, after = stencil[:, :group_len], stencil[:, 2 * group_len :]
    swapped = paired(total_k // group_len) & (group_id % 2 == 1)
    near, far = jnp.where(swapped, before, after), jnp.where(swapped, after, before)
    stencil_hi[...], stencil_lo[...] = split(jnp.concatenate([near, far], axis=1))
    centre = split(stencil[:, group_len : 2 * group_len])
    for c in range(0, comps, 2):
        result = product(centre, split(jnp.concatenate([own[c], own[c + 1]], axis=1)))
        part[c] = result[:, :slice_len]
        part[c + 1] = result[:, slice_len:]


def prepare(own, neighbour, weight, after, total_k):
    group_len = own.shape[1]
    sides = jax.ShapeDtypeStruct((group_len, 2 * group_len), jnp.bfloat16)
    return pl.pallas_call(
        lambda *refs: prepare_kernel(total_k, *refs),
        out_shape=(sides, sides, jax.ShapeDtypeStruct(own.shape, jnp.float32)),
        in_specs=[VMEM, VMEM, SMEM, VMEM],
        out_specs=(VMEM,) * 3,
        compiler_params=PARAMS,
        cost_estimate=pl.CostEstimate(
            flops=6 * own.size * group_len, bytes_accessed=8 * own.size, transcendentals=0
        ),
        name="prepare",
    )(own, jnp.transpose(neighbour), weight, after)


def smear_kernel(first, near, far, stencil_hi, stencil_lo, part, *refs):
    *_, kept, given = refs
    comps, _, slice_len = near.shape
    chips, height, _ = kept.shape
    rows = height // comps
    stencil = (stencil_hi[...], stencil_lo[...])
    for c in range(0, comps, 2):
        block = jnp.concatenate(
            [jnp.concatenate([side[c], side[c + 1]], axis=1) for side in (near, far)], axis=0
        )
        result = product(stencil, split(block))
        for p in range(2):
            smeared = part[first + c + p] + result[:, p * slice_len : (p + 1) * slice_len]
            at = slice((c + p) * rows, (c + p + 1) * rows)
            for m in range(2 * chips):
                out = given if m % 2 else kept
                out[m // 2, at, :] = smeared[m * rows : (m + 1) * rows]


def smear(first, near, far, stencil_hi, stencil_lo, part, after, parts):
    comps, group_len, slice_len = near.shape
    shape = (parts // 2, comps * group_len // parts, slice_len)
    return pl.pallas_call(
        lambda *refs: smear_kernel(first, *refs),
        out_shape=[jax.ShapeDtypeStruct(shape, jnp.float32)] * 2,
        in_specs=[VMEM] * 5 + [pl.BlockSpec(memory_space=pl.ANY)] * len(after),
        out_specs=[VMEM] * 2,
        compiler_params=PARAMS,
        cost_estimate=pl.CostEstimate(
            flops=12 * near.size * group_len, bytes_accessed=16 * near.size, transcendentals=0
        ),
        name="smear",
    )(near, far, stencil_hi, stencil_lo, part, *after)


def join_kernel(own, swapped, *out):
    for chip, block in enumerate(out, 1):
        block[0], block[1] = own[chip], swapped[chip]


def join(own, swapped):
    chips, height, slice_len = own.shape
    shape = jax.ShapeDtypeStruct((2, height, slice_len), jnp.float32)
    return pl.pallas_call(
        join_kernel,
        out_shape=[shape] * (chips - 1),
        in_specs=[VMEM] * 2,
        out_specs=[VMEM] * (chips - 1),
        compiler_params=PARAMS,
        name="join",
    )(own, swapped)


def paired(groups):
    return groups == 4


def exchange(block, groups):
    if paired(groups):
        near = [(i, i ^ 1) for i in range(groups)]
        far = [(i, i ^ 3) for i in range(groups)]
    else:
        far = [(i, (i + 1) % groups) for i in range(groups)]
        near = [(target, source) for source, target in far]
    return lax.ppermute(block, "kgrp", near), lax.ppermute(block, "kgrp", far)


def spread(values, shape):
    row = lax.broadcasted_iota(jnp.int32, shape, 0)
    lane = lax.broadcasted_iota(jnp.int32, shape, 1)
    tile = jnp.zeros(shape, jnp.float32)
    for spot, value in values:
        tile = jnp.where((row == spot % 8) & (lane == spot // 8), value, tile)
    return tile


def total(acc):
    return jnp.sum(jnp.sum(acc, axis=0, keepdims=True), axis=1, keepdims=True)


def history_kernel(past_inputs, past_residuals, slots, aged, tile):
    _, rows, width = past_inputs.shape
    acc = [jnp.zeros((8, LANES), jnp.float32) for _ in PAIRS]
    for top in range(0, rows, 8):
        def column(t, acc, top=top):
            at = pl.ds(pl.multiple_of(t * LANES, LANES), LANES)
            old = []
            for j in range(HIST):
                res = past_residuals[slots[j], top : top + 8, at]
                aged[j, top : top + 8, at] = (
                    past_inputs[slots[j], top : top + 8, at] + mixing_share * res
                )
                old.append(res)
            return [a + old[i - 1] * old[j - 1] for a, (i, j) in zip(acc, PAIRS)]
        acc = lax.fori_loop(0, width // LANES, column, acc, unroll=4)
    tile[...] = spread([(v, total(a)) for v, a in enumerate(acc)], tile.shape)


def history(past_inputs, past_residuals, slots):
    size = past_inputs.size
    return pl.pallas_call(
        history_kernel,
        out_shape=(
            jax.ShapeDtypeStruct(past_inputs.shape, jnp.float32),
            jax.ShapeDtypeStruct((8, LANES), jnp.float32),
        ),
        in_specs=[VMEM, VMEM, SMEM],
        out_specs=(VMEM, VMEM),
        compiler_params=PARAMS,
        cost_estimate=pl.CostEstimate(flops=8 * size, bytes_accessed=12 * size, transcendentals=0),
        name="history",
    )(past_inputs, past_residuals, slots)


def residual_kernel(rows, count, *refs):
    arrived = refs[: CHUNKS * count]
    (current, past_residuals, old_tile, slots, classes, acoustic, optical, number, shift,
     fresh, tile, smeared) = refs[CHUNKS * count :]
    parts, height, slice_len = smeared.shape
    span = height // CHUNKS
    place = lax.axis_index("energy")
    for chunk in range(CHUNKS):
        own, swapped, *received = arrived[chunk * count : (chunk + 1) * count]
        at = slice(chunk * span, (chunk + 1) * span)
        smeared[place, at], smeared[place ^ 1, at] = own[0], swapped[0]
        for chip, block in enumerate(received, 1):
            smeared[place ^ (2 * chip), at] = block[0]
            smeared[place ^ (2 * chip + 1), at] = block[1]
    first = place * rows
    row = lax.broadcasted_iota(jnp.int32, (8, slice_len), 0) % rows
    lane = lax.broadcasted_iota(jnp.int32, (8, slice_len), 1)
    coupling = jnp.zeros((8, slice_len), jnp.float32)
    for i in range(rows):
        coupling = jnp.where(row == i, acoustic[classes[first + i]], coupling)
    modes = []
    for m in range(2):
        s = shift[m]
        modes.append((s, lane < slice_len - s, lane >= s, optical[m] * (number[m] + 1.0), optical[m] * number[m]))
    zero = jnp.zeros((8, slice_len), jnp.float32)
    acc = [zero] * (HIST + 1)
    for top in range(0, height, 8):
        at = slice(top, top + 8)
        source = [smeared[e, at, :] for e in range(parts)]
        sigma = [coupling * x for x in source]
        lesser = top < height // 2
        for s, keep_up, keep_down, emitted, absorbed in modes:
            up = [pltpu.roll(x, slice_len - s, 1) for x in source] + [zero]
            down = [zero] + [pltpu.roll(x, s, 1) for x in source]
            gain_up, gain_down = (emitted, absorbed) if lesser else (absorbed, emitted)
            for e in range(parts):
                above = jnp.where(keep_up, up[e], up[e + 1])
                below = jnp.where(keep_down, down[e + 1], down[e])
                sigma[e] = sigma[e] + (gain_up * above + gain_down * below)
        for e in range(parts):
            where = (at, slice(e * slice_len, (e + 1) * slice_len))
            new = sigma[e] - current[where]
            fresh[where] = new
            acc[0] = acc[0] + new * new
            for j in range(HIST):
                acc[j + 1] = acc[j + 1] + new * past_residuals[(slots[j],) + where]
    mine = jnp.concatenate([jnp.sum(a, axis=0, keepdims=True) for a in acc] + [zero[: 8 - HIST - 1]], axis=0)
    mine = jnp.sum(mine, axis=1, keepdims=True)
    lane = lax.broadcasted_iota(jnp.int32, old_tile.shape, 1)
    tile[...] = jnp.broadcast_to(jnp.where(lane == 2, mine, old_tile[...])[None], tile.shape)


def residual(arrived, current, past_residuals, old_tile, slots, classes, acoustic, optical, number, shift, rows, copies):
    count = len(arrived) // CHUNKS
    chips, span, slice_len = arrived[0].shape
    return pl.pallas_call(
        lambda *refs: residual_kernel(rows, count, *refs),
        out_shape=(
            jax.ShapeDtypeStruct(current.shape, jnp.float32),
            jax.ShapeDtypeStruct((copies, 8, LANES), jnp.float32),
        ),
        in_specs=[VMEM] * (len(arrived) + 3) + [SMEM] * 6,
        out_specs=(VMEM, VMEM),
        scratch_shapes=[pltpu.VMEM((2 * chips, CHUNKS * span, slice_len), jnp.float32)],
        compiler_params=PARAMS,
        name="residual",
    )(*arrived, current, past_residuals, old_tile, slots, classes, acoustic, optical, number, shift)


def solve(products):
    prod = lambda i, j: products[(min(i, j), max(i, j))]
    n = HIST
    system = [
        [prod(i, j) - prod(i, j + 1) - prod(i + 1, j) + prod(i + 1, j + 1) for j in range(n)]
        for i in range(n)
    ]
    target = [prod(i, 0) - prod(i + 1, 0) for i in range(n)]
    trace = system[0][0]
    for i in range(1, n):
        trace = trace + system[i][i]
    ridge = ridge_share * trace / n + 1e-06
    for i in range(n):
        system[i][i] = system[i][i] + ridge
    inverse = [None] * n
    for k in range(n):
        inverse[k] = 1.0 / system[k][k]
        for i in range(k + 1, n):
            factor = system[k][i] * inverse[k]
            for j in range(i, n):
                system[i][j] = system[i][j] - factor * system[k][j]
            target[i] = target[i] - factor * target[k]
    gamma = [None] * n
    for k in range(n - 1, -1, -1):
        value = target[k]
        for j in range(k + 1, n):
            value = value - system[k][j] * gamma[j]
        gamma[k] = value * inverse[k]
    weights = [1.0 - gamma[0]]
    for j in range(1, n):
        weights.append(gamma[j - 1] - gamma[j])
    weights.append(gamma[n - 1])
    return weights


def mix_kernel(entries, tiles, fresh, current, aged, out, wide):
    summed = jnp.sum(tiles[...], axis=0) / entries
    for lane in range(wide.shape[0]):
        wide[lane] = jnp.broadcast_to(summed[:, lane : lane + 1], (8, LANES))
    products = {
        pair: jnp.broadcast_to(wide[spot // 8, spot % 8 : spot % 8 + 1, :], (8, LANES))
        for pair, spot in SPOTS.items()
    }
    weights = solve(products)
    rows, width = fresh.shape
    for top in range(0, rows, 8):
        for left in range(0, width, LANES):
            at = (slice(top, top + 8), slice(left, left + LANES))
            mixed = weights[0] * (current[at] + mixing_share * fresh[at])
            for j in range(HIST):
                mixed = mixed + weights[j + 1] * aged[(j,) + at]
            out[at] = mixed


def mix(tiles, fresh, current, aged, entries):
    return pl.pallas_call(
        lambda *refs: mix_kernel(entries, *refs),
        out_shape=jax.ShapeDtypeStruct(fresh.shape, jnp.float32),
        in_specs=[VMEM] * 4,
        out_specs=VMEM,
        scratch_shapes=[pltpu.VMEM((3, 8, LANES), jnp.float32)],
        compiler_params=PARAMS,
        name="mix",
    )(tiles, fresh, current, aged)


def per_device(
    greens,
    current,
    past_inputs,
    past_residuals,
    slot_order,
    neighbour,
    momentum_class,
    stencil_weight,
    acoustic_coupling,
    optical_coupling,
    occupation,
    phonon_shift,
):
    group_len, slice_len = greens.shape[3:]
    rows, width = current.shape[3:]
    groups = lax.axis_size("kgrp")
    parts = lax.axis_size("energy")
    own = greens.reshape(-1, group_len, slice_len)
    height = own.shape[0] * rows

    flat = current.reshape(height, width)
    old_in = past_inputs.reshape(HIST, height, width)
    old_res = past_residuals.reshape(HIST, height, width)
    span = own.shape[0] // CHUNKS
    sides = [exchange(own[c * span : (c + 1) * span], groups) for c in range(CHUNKS)]

    flat = current.reshape(height, width)
    old_in = past_inputs.reshape(HIST, height, width)
    old_res = past_residuals.reshape(HIST, height, width)
    aged, old_tile = history(old_in, old_res, slot_order)
    stencil_hi, stencil_lo, part = prepare(
        own, neighbour, stencil_weight, old_tile, groups * group_len
    )
    meet = lambda block, m: lax.ppermute(block, "energy", [(e, e ^ m) for e in range(parts)])
    arrived = []
    for chunk, (near, far) in enumerate(sides):
        after = arrived[2:]
        kept, given = smear(chunk * span, near, far, stencil_hi, stencil_lo, part, after, parts)
        swapped = meet(given, 1)
        joined = join(kept, swapped)
        arrived += [kept, swapped] + [meet(block, 2 * chip) for chip, block in enumerate(joined, 1)]
    fresh, tile = residual(
        arrived, flat, old_res, old_tile, slot_order, momentum_class, acoustic_coupling,
        optical_coupling, occupation, phonon_shift, rows, groups * parts,
    )
    tiles = lax.all_to_all(tile, ("kgrp", "energy"), split_axis=0, concat_axis=0, tiled=True)
    entries = float(flat.size * groups * parts)
    return mix(tiles, fresh, flat, aged, entries).reshape(current.shape)


def solution(mesh):
    return jax.shard_map(
        per_device,
        mesh=mesh,
        in_specs=(
            P(None, None, None, "kgrp", "energy"),
            P(None, None, None, ("kgrp", "energy"), None),
            P(None, None, None, None, ("kgrp", "energy"), None),
            P(None, None, None, None, ("kgrp", "energy"), None),
            P(),
            P("kgrp", None),
            P("kgrp"),
            P(),
            P(),
            P(),
            P(),
            P(),
        ),
        out_specs=P(None, None, None, ("kgrp", "energy"), None),
        check_vma=False,
    )
```

```python
import jax
import jax.numpy as jnp
from jax import lax
from jax.experimental import pallas as pl
from jax.experimental.pallas import tpu as pltpu
from jax.sharding import PartitionSpec as P

HIST = 5
LANES = 128

mixing_share = 0.5
ridge_share = 0.1

VMEM = pl.BlockSpec(memory_space=pltpu.VMEM)
SMEM = pl.BlockSpec(memory_space=pltpu.SMEM)
PARAMS = pltpu.CompilerParams(vmem_limit_bytes=16 * 1024 * 1024)

NEAR, FAR = 0, 1

PAIRS = [(i, j) for i in range(1, HIST + 1) for j in range(i, HIST + 1)]
SPOTS = {pair: v for v, pair in enumerate(PAIRS)}
for _j in range(HIST + 1):
    SPOTS[(0, _j)] = 16 + _j


def split(value):
    high = value.astype(jnp.bfloat16)
    return high, (value - high.astype(jnp.float32)).astype(jnp.bfloat16)


def product(left, right):
    dot = lambda a, b: jnp.dot(a, b, preferred_element_type=jnp.float32)
    return dot(left[0], right[0]) + (dot(left[0], right[1]) + dot(left[1], right[0]))


def prepare_kernel(total_k, own, neighbour, weight, stencil_hi, stencil_lo, part):
    comps, group_len, slice_len = own.shape
    group_id = lax.axis_index("kgrp")
    parts = lax.axis_size("energy")
    rows = group_len // parts
    slots, _ = neighbour.shape
    padded = jnp.concatenate([neighbour[...], jnp.zeros((8 - slots, group_len), jnp.int32)], axis=0)
    targets = jnp.transpose(padded)
    place = lax.axis_index("energy")
    bit = 1
    while bit < parts:
        span = bit * rows
        blocks = [targets[at : at + span] for at in range(0, group_len, span)]
        flipped = [blocks[b ^ 1] for b in range(len(blocks))]
        targets = jnp.where(place & bit != 0, jnp.concatenate(flipped, axis=0), targets)
        bit *= 2
    local = (targets - group_id * group_len + (group_len + total_k)) % total_k
    spot = lax.broadcasted_iota(jnp.int32, (group_len, 3 * group_len), 1)
    stencil = jnp.zeros(spot.shape, jnp.float32)
    for n in range(slots):
        stencil = stencil + jnp.where(spot == local[:, n : n + 1], weight[n], 0.0)
    before, after = stencil[:, :group_len], stencil[:, 2 * group_len :]
    swapped = paired(total_k // group_len) & (group_id % 2 == 1)
    near, far = jnp.where(swapped, before, after), jnp.where(swapped, after, before)
    stencil_hi[...], stencil_lo[...] = split(jnp.concatenate([near, far], axis=1))
    centre = split(stencil[:, group_len : 2 * group_len])
    for c in range(0, comps, 2):
        result = product(centre, split(jnp.concatenate([own[c], own[c + 1]], axis=1)))
        part[c] = result[:, :slice_len]
        part[c + 1] = result[:, slice_len:]


def prepare(own, neighbour, weight, total_k):
    group_len = own.shape[1]
    sides = jax.ShapeDtypeStruct((group_len, 2 * group_len), jnp.bfloat16)
    return pl.pallas_call(
        lambda *refs: prepare_kernel(total_k, *refs),
        out_shape=(sides, sides, jax.ShapeDtypeStruct(own.shape, jnp.float32)),
        in_specs=[VMEM, VMEM, SMEM],
        out_specs=(VMEM,) * 3,
        compiler_params=PARAMS,
        cost_estimate=pl.CostEstimate(
            flops=6 * own.size * group_len, bytes_accessed=8 * own.size, transcendentals=0
        ),
        name="prepare",
    )(own, jnp.transpose(neighbour), weight)


def smear_kernel(side, count, *refs):
    blocks, (stencil_hi, stencil_lo, part), out = refs[:count], refs[count : count + 3], refs[count + 3 :]
    _, group_len, slice_len = blocks[0].shape
    at = slice(side * group_len, (side + 1) * group_len)
    stencil = (stencil_hi[:, at], stencil_lo[:, at])
    first = 0
    for block in blocks:
        for c in range(0, block.shape[0], 2):
            result = product(stencil, split(jnp.concatenate([block[c], block[c + 1]], axis=1)))
            for p in range(2):
                at = first + c + p
                smeared = part[at] + result[:, p * slice_len : (p + 1) * slice_len]
                if side == NEAR:
                    out[0][at] = smeared
                    continue
                chips, height, _ = out[0].shape
                rows = height // part.shape[0]
                for m in range(2 * chips):
                    out[m % 2][m // 2, at * rows : (at + 1) * rows, :] = smeared[m * rows : (m + 1) * rows]
        first += block.shape[0]


def smear(side, blocks, stencil_hi, stencil_lo, part, parts):
    comps, group_len, slice_len = part.shape
    if side == NEAR:
        out_shape = [jax.ShapeDtypeStruct(part.shape, jnp.float32)]
    else:
        shape = (parts // 2, comps * group_len // parts, slice_len)
        out_shape = [jax.ShapeDtypeStruct(shape, jnp.float32)] * 2
    return pl.pallas_call(
        lambda *refs: smear_kernel(side, len(blocks), *refs),
        out_shape=out_shape,
        in_specs=[VMEM] * (len(blocks) + 3),
        out_specs=[VMEM] * len(out_shape),
        compiler_params=PARAMS,
        cost_estimate=pl.CostEstimate(
            flops=6 * part.size * group_len, bytes_accessed=12 * part.size, transcendentals=0
        ),
        name="smear",
    )(*blocks, stencil_hi, stencil_lo, part)


def join_kernel(own, swapped, *out):
    for chip, block in enumerate(out, 1):
        block[0], block[1] = own[chip], swapped[chip]


def join(own, swapped):
    chips, height, slice_len = own.shape
    shape = jax.ShapeDtypeStruct((2, height, slice_len), jnp.float32)
    return pl.pallas_call(
        join_kernel,
        out_shape=[shape] * (chips - 1),
        in_specs=[VMEM] * 2,
        out_specs=[VMEM] * (chips - 1),
        compiler_params=PARAMS,
        name="join",
    )(own, swapped)


def paired(groups):
    return groups == 4


def exchange(own, groups):
    if not paired(groups):
        forward = [(i, (i + 1) % groups) for i in range(groups)]
        backward = [(target, source) for source, target in forward]
        return [lax.ppermute(own, "kgrp", backward)], [lax.ppermute(own, "kgrp", forward)]
    across = lambda block, flip: lax.ppermute(block, "kgrp", [(i, i ^ flip) for i in range(groups)])
    half = own.shape[0] // 2
    near = [across(own[:half], 1), across(own[half:], 1)]
    return near, [across(near[0], 2), across(own[half:], 3)]


def spread(values, shape):
    lane = lax.broadcasted_iota(jnp.int32, shape, 1)
    row = jnp.zeros(shape, jnp.float32)
    for spot, value in values:
        row = jnp.where(lane == spot, value, row)
    return row


def total(acc):
    return jnp.sum(jnp.sum(acc, axis=0, keepdims=True), axis=1, keepdims=True)


def history_kernel(
    total_rows, past_inputs, past_residuals, slots, classes, acoustic, optical, number, aged, line, gains,
):
    first = lax.axis_index("energy") * total_rows
    row = lax.broadcasted_iota(jnp.int32, (8, LANES), 0) % total_rows
    coupling = jnp.zeros((8, LANES), jnp.float32)
    for i in range(total_rows):
        coupling = jnp.where(row == i, acoustic[classes[first + i]], coupling)
    gains[0] = coupling
    for m in range(2):
        gains[2 * m + 1] = jnp.full((8, LANES), optical[m] * (number[m] + 1.0))
        gains[2 * m + 2] = jnp.full((8, LANES), optical[m] * number[m])
    _, rows, width = past_inputs.shape
    acc = [jnp.zeros((8, LANES), jnp.float32) for _ in PAIRS]
    for top in range(0, rows, 8):
        def column(t, acc, top=top):
            at = pl.ds(pl.multiple_of(t * LANES, LANES), LANES)
            old = []
            for j in range(HIST):
                res = past_residuals[slots[j], top : top + 8, at]
                aged[j, top : top + 8, at] = (
                    past_inputs[slots[j], top : top + 8, at] + mixing_share * res
                )
                old.append(res)
            return [a + old[i - 1] * old[j - 1] for a, (i, j) in zip(acc, PAIRS)]
        acc = lax.fori_loop(0, width // LANES, column, acc, unroll=4)
    line[...] = spread([(v, total(a)) for v, a in enumerate(acc)], line.shape)


def history(past_inputs, past_residuals, scalars, rows):
    size = past_inputs.size
    return pl.pallas_call(
        lambda *refs: history_kernel(rows, *refs),
        out_shape=(
            jax.ShapeDtypeStruct(past_inputs.shape, jnp.float32),
            jax.ShapeDtypeStruct((1, LANES), jnp.float32),
            jax.ShapeDtypeStruct((5, 8, LANES), jnp.float32),
        ),
        in_specs=[VMEM, VMEM] + [SMEM] * 5,
        out_specs=(VMEM,) * 3,
        compiler_params=PARAMS,
        cost_estimate=pl.CostEstimate(flops=8 * size, bytes_accessed=12 * size, transcendentals=0),
        name="history",
    )(past_inputs, past_residuals, *scalars)


def residual_kernel(count, own, swapped, *refs):
    received = refs[:count]
    current, past_residuals, old_line, gains, slots, shift, fresh, lines, smeared = refs[count:]
    parts, height, slice_len = smeared.shape
    place = lax.axis_index("energy")
    smeared[place], smeared[place ^ 1] = own[0], swapped[0]
    for chip, block in enumerate(received, 1):
        smeared[place ^ (2 * chip)], smeared[place ^ (2 * chip + 1)] = block[0], block[1]
    lane = lax.broadcasted_iota(jnp.int32, (8, slice_len), 1)
    coupling = gains[0]
    modes = [
        (shift[m], lane < slice_len - shift[m], lane >= shift[m], gains[2 * m + 1], gains[2 * m + 2])
        for m in range(2)
    ]
    zero = jnp.zeros((8, slice_len), jnp.float32)
    acc = [zero] * (HIST + 1)
    for top in range(0, height, 8):
        at = slice(top, top + 8)
        source = [smeared[e, at, :] for e in range(parts)]
        sigma = [coupling * x for x in source]
        lesser = top < height // 2
        for s, keep_up, keep_down, emitted, absorbed in modes:
            up = [pltpu.roll(x, slice_len - s, 1) for x in source] + [zero]
            down = [zero] + [pltpu.roll(x, s, 1) for x in source]
            gain_up, gain_down = (emitted, absorbed) if lesser else (absorbed, emitted)
            for e in range(parts):
                above = jnp.where(keep_up, up[e], up[e + 1])
                below = jnp.where(keep_down, down[e + 1], down[e])
                sigma[e] = sigma[e] + (gain_up * above + gain_down * below)
        for e in range(parts):
            where = (at, slice(e * slice_len, (e + 1) * slice_len))
            new = sigma[e] - current[where]
            fresh[where] = new
            acc[0] = acc[0] + new * new
            for j in range(HIST):
                acc[j + 1] = acc[j + 1] + new * past_residuals[(slots[j],) + where]
    mine = jnp.concatenate([jnp.sum(a, axis=0, keepdims=True) for a in acc] + [zero[: 8 - HIST - 1]], axis=0)
    mine = jnp.sum(mine, axis=1, keepdims=True)
    spot = lax.broadcasted_iota(jnp.int32, (8, LANES), 0) + SPOTS[(0, 0)]
    mine = jnp.where(lax.broadcasted_iota(jnp.int32, (8, LANES), 1) == spot, mine, 0.0)
    mine = old_line[...] + jnp.sum(mine, axis=0, keepdims=True)
    lines[...] = jnp.broadcast_to(mine[None], lines.shape)


def residual(kept, swapped, smeared, current, past_residuals, old_line, gains, slots, shift, copies):
    return pl.pallas_call(
        lambda *refs: residual_kernel(len(smeared), *refs),
        out_shape=(
            jax.ShapeDtypeStruct(current.shape, jnp.float32),
            jax.ShapeDtypeStruct((copies, 1, LANES), jnp.float32),
        ),
        in_specs=[VMEM] * (len(smeared) + 6) + [SMEM] * 2,
        out_specs=(VMEM, VMEM),
        scratch_shapes=[pltpu.VMEM((2 * kept.shape[0],) + kept.shape[1:], jnp.float32)],
        compiler_params=PARAMS,
        name="residual",
    )(kept, swapped, *smeared, current, past_residuals, old_line, gains, slots, shift)


def solve(products):
    prod = lambda i, j: products[(min(i, j), max(i, j))]
    n = HIST
    system = [
        [prod(i, j) - prod(i, j + 1) - prod(i + 1, j) + prod(i + 1, j + 1) for j in range(n)]
        for i in range(n)
    ]
    target = [prod(i, 0) - prod(i + 1, 0) for i in range(n)]
    trace = system[0][0]
    for i in range(1, n):
        trace = trace + system[i][i]
    ridge = ridge_share * trace / n + 1e-06
    for i in range(n):
        system[i][i] = system[i][i] + ridge
    inverse = [None] * n
    for k in range(n):
        inverse[k] = 1.0 / system[k][k]
        for i in range(k + 1, n):
            factor = system[k][i] * inverse[k]
            for j in range(i, n):
                system[i][j] = system[i][j] - factor * system[k][j]
            target[i] = target[i] - factor * target[k]
    gamma = [None] * n
    for k in range(n - 1, -1, -1):
        value = target[k]
        for j in range(k + 1, n):
            value = value - system[k][j] * gamma[j]
        gamma[k] = value * inverse[k]
    weights = [1.0 - gamma[0]]
    for j in range(1, n):
        weights.append(gamma[j - 1] - gamma[j])
    weights.append(gamma[n - 1])
    return weights


def mix_kernel(entries, lines, fresh, current, aged, out, wide):
    summed = jnp.sum(lines[...], axis=0) / entries
    row = lax.broadcasted_iota(jnp.int32, (8, LANES), 0)
    lane = lax.broadcasted_iota(jnp.int32, (8, LANES), 1)
    for part in range(wide.shape[0]):
        own = jnp.where(lane == row + 8 * part, summed, 0.0)
        wide[part] = jnp.broadcast_to(jnp.sum(own, axis=1, keepdims=True), (8, LANES))
    products = {
        pair: jnp.broadcast_to(wide[spot // 8, spot % 8 : spot % 8 + 1, :], (8, LANES))
        for pair, spot in SPOTS.items()
    }
    weights = solve(products)
    rows, width = fresh.shape
    for top in range(0, rows, 8):
        for left in range(0, width, LANES):
            at = (slice(top, top + 8), slice(left, left + LANES))
            mixed = weights[0] * (current[at] + mixing_share * fresh[at])
            for j in range(HIST):
                mixed = mixed + weights[j + 1] * aged[(j,) + at]
            out[at] = mixed


def mix(lines, fresh, current, aged, entries):
    return pl.pallas_call(
        lambda *refs: mix_kernel(entries, *refs),
        out_shape=jax.ShapeDtypeStruct(fresh.shape, jnp.float32),
        in_specs=[VMEM] * 4,
        out_specs=VMEM,
        scratch_shapes=[pltpu.VMEM((3, 8, LANES), jnp.float32)],
        compiler_params=PARAMS,
        name="mix",
    )(lines, fresh, current, aged)


def per_device(
    greens,
    current,
    past_inputs,
    past_residuals,
    slot_order,
    neighbour,
    momentum_class,
    stencil_weight,
    acoustic_coupling,
    optical_coupling,
    occupation,
    phonon_shift,
):
    group_len, slice_len = greens.shape[3:]
    rows, width = current.shape[3:]
    groups = lax.axis_size("kgrp")
    parts = lax.axis_size("energy")
    own = greens.reshape(-1, group_len, slice_len)
    height = own.shape[0] * rows

    flat = current.reshape(height, width)
    old_in = past_inputs.reshape(HIST, height, width)
    old_res = past_residuals.reshape(HIST, height, width)
    sides = exchange(own, groups)
    stencil_hi, stencil_lo, smeared = prepare(own, neighbour, stencil_weight, groups * group_len)
    scalars = (slot_order, momentum_class, acoustic_coupling, optical_coupling, occupation)
    aged, old_line, gains = history(old_in, old_res, scalars, rows)
    (smeared,) = smear(NEAR, sides[NEAR], stencil_hi, stencil_lo, smeared, parts)
    kept, given = smear(FAR, sides[FAR], stencil_hi, stencil_lo, smeared, parts)
    meet = lambda block, m: lax.ppermute(block, "energy", [(e, e ^ m) for e in range(parts)])
    swapped = meet(given, 1)
    smeared = [meet(block, 2 * chip) for chip, block in enumerate(join(kept, swapped), 1)]
    fresh, lines = residual(
        kept, swapped, smeared, flat, old_res, old_line, gains, slot_order, phonon_shift, groups * parts
    )
    lines = lax.all_to_all(lines, ("kgrp", "energy"), split_axis=0, concat_axis=0, tiled=True)
    entries = float(flat.size * groups * parts)
    return mix(lines, fresh, flat, aged, entries).reshape(current.shape)


def solution(mesh):
    return jax.shard_map(
        per_device,
        mesh=mesh,
        in_specs=(
            P(None, None, None, "kgrp", "energy"),
            P(None, None, None, ("kgrp", "energy"), None),
            P(None, None, None, None, ("kgrp", "energy"), None),
            P(None, None, None, None, ("kgrp", "energy"), None),
            P(),
            P("kgrp", None),
            P("kgrp"),
            P(),
            P(),
            P(),
            P(),
            P(),
        ),
        out_specs=P(None, None, None, ("kgrp", "energy"), None),
        check_vma=False,
    )
```

```python
import jax
import jax.numpy as jnp
from jax import lax
from jax.experimental import pallas as pl
from jax.experimental.pallas import tpu as pltpu
from jax.sharding import PartitionSpec as P

HIST = 5
LANES = 128

mixing_share = 0.5
ridge_share = 0.1

VMEM = pl.BlockSpec(memory_space=pltpu.VMEM)
SMEM = pl.BlockSpec(memory_space=pltpu.SMEM)
PARAMS = pltpu.CompilerParams(vmem_limit_bytes=16 * 1024 * 1024)

NEAR, FAR = 0, 1

PAIRS = [(i, j) for i in range(1, HIST + 1) for j in range(i, HIST + 1)]
SPOTS = {pair: v for v, pair in enumerate(PAIRS)}
for _j in range(HIST + 1):
    SPOTS[(0, _j)] = 16 + _j


def split(value):
    high = value.astype(jnp.bfloat16)
    return high, (value - high.astype(jnp.float32)).astype(jnp.bfloat16)


def product(left, right):
    dot = lambda a, b: jnp.dot(a, b, preferred_element_type=jnp.float32)
    return dot(left[0], right[0]) + (dot(left[0], right[1]) + dot(left[1], right[0]))


def prepare_kernel(total_k, own, neighbour, weight, stencil_hi, stencil_lo, part):
    comps, group_len, slice_len = own.shape
    group_id = lax.axis_index("kgrp")
    parts = lax.axis_size("energy")
    rows = group_len // parts
    slots, _ = neighbour.shape
    padded = jnp.concatenate([neighbour[...], jnp.zeros((8 - slots, group_len), jnp.int32)], axis=0)
    targets = jnp.transpose(padded)
    place = lax.axis_index("energy")
    bit = 1
    while bit < parts:
        span = bit * rows
        blocks = [targets[at : at + span] for at in range(0, group_len, span)]
        flipped = [blocks[b ^ 1] for b in range(len(blocks))]
        targets = jnp.where(place & bit != 0, jnp.concatenate(flipped, axis=0), targets)
        bit *= 2
    local = (targets - group_id * group_len + (group_len + total_k)) % total_k
    spot = lax.broadcasted_iota(jnp.int32, (group_len, 3 * group_len), 1)
    stencil = jnp.zeros(spot.shape, jnp.float32)
    for n in range(slots):
        stencil = stencil + jnp.where(spot == local[:, n : n + 1], weight[n], 0.0)
    before, after = stencil[:, :group_len], stencil[:, 2 * group_len :]
    swapped = paired(total_k // group_len) & (group_id % 2 == 1)
    near, far = jnp.where(swapped, before, after), jnp.where(swapped, after, before)
    stencil_hi[...], stencil_lo[...] = split(jnp.concatenate([near, far], axis=1))
    centre = split(stencil[:, group_len : 2 * group_len])
    for c in range(0, comps, 2):
        result = product(centre, split(jnp.concatenate([own[c], own[c + 1]], axis=1)))
        part[c] = result[:, :slice_len]
        part[c + 1] = result[:, slice_len:]


def prepare(own, neighbour, weight, total_k):
    group_len = own.shape[1]
    sides = jax.ShapeDtypeStruct((group_len, 2 * group_len), jnp.bfloat16)
    return pl.pallas_call(
        lambda *refs: prepare_kernel(total_k, *refs),
        out_shape=(sides, sides, jax.ShapeDtypeStruct(own.shape, jnp.float32)),
        in_specs=[VMEM, VMEM, SMEM],
        out_specs=(VMEM,) * 3,
        compiler_params=PARAMS,
        cost_estimate=pl.CostEstimate(
            flops=6 * own.size * group_len, bytes_accessed=8 * own.size, transcendentals=0
        ),
        name="prepare",
    )(own, jnp.transpose(neighbour), weight)


def smeared_pairs(side, first, block, stencil_hi, stencil_lo, part):
    comps, group_len, slice_len = block.shape
    at = slice(side * group_len, (side + 1) * group_len)
    stencil = (stencil_hi[:, at], stencil_lo[:, at])
    for c in range(0, comps, 2):
        result = product(stencil, split(jnp.concatenate([block[c], block[c + 1]], axis=1)))
        for p in range(2):
            yield c + p, part[first + c + p] + result[:, p * slice_len : (p + 1) * slice_len]


def add_side_kernel(side, first, *refs):
    *blocks, stencil_hi, stencil_lo, part, out = refs
    done = 0
    for block in blocks:
        for c, smeared in smeared_pairs(side, first + done, block, stencil_hi, stencil_lo, part):
            out[done + c] = smeared
        done += block.shape[0]


def add_side(side, first, blocks, stencil_hi, stencil_lo, part):
    shape = (sum(block.shape[0] for block in blocks),) + part.shape[1:]
    return pl.pallas_call(
        lambda *refs: add_side_kernel(side, first, *refs),
        out_shape=jax.ShapeDtypeStruct(shape, jnp.float32),
        in_specs=[VMEM] * (len(blocks) + 3),
        out_specs=VMEM,
        compiler_params=PARAMS,
        cost_estimate=pl.CostEstimate(
            flops=6 * part.size * part.shape[1], bytes_accessed=12 * part.size, transcendentals=0
        ),
        name="add_side",
    )(*blocks, stencil_hi, stencil_lo, part)


def finish_kernel(side, block, stencil_hi, stencil_lo, part, *refs):
    *ready, kept, given = refs
    chips, height, _ = kept.shape
    comps = part.shape[0]
    rows = height // comps

    def place(c, smeared):
        for m in range(2 * chips):
            out = given if m % 2 else kept
            out[m // 2, c * rows : (c + 1) * rows, :] = smeared[m * rows : (m + 1) * rows]

    for c, smeared in smeared_pairs(side, 0, block, stencil_hi, stencil_lo, part):
        place(c, smeared)
    for c in range(block.shape[0], comps):
        place(c, ready[0][c - block.shape[0]])


def finish(side, block, stencil_hi, stencil_lo, part, ready, parts):
    comps, group_len, slice_len = part.shape
    shape = (parts // 2, comps * group_len // parts, slice_len)
    return pl.pallas_call(
        lambda *refs: finish_kernel(side, *refs),
        out_shape=[jax.ShapeDtypeStruct(shape, jnp.float32)] * 2,
        in_specs=[VMEM] * (len(ready) + 4),
        out_specs=[VMEM] * 2,
        compiler_params=PARAMS,
        cost_estimate=pl.CostEstimate(
            flops=6 * part.size * group_len, bytes_accessed=12 * part.size, transcendentals=0
        ),
        name="finish",
    )(block, stencil_hi, stencil_lo, part, *ready)


def join_kernel(own, swapped, *out):
    for chip, block in enumerate(out, 1):
        block[0], block[1] = own[chip], swapped[chip]


def join(own, swapped):
    chips, height, slice_len = own.shape
    shape = jax.ShapeDtypeStruct((2, height, slice_len), jnp.float32)
    return pl.pallas_call(
        join_kernel,
        out_shape=[shape] * (chips - 1),
        in_specs=[VMEM] * 2,
        out_specs=[VMEM] * (chips - 1),
        compiler_params=PARAMS,
        name="join",
    )(own, swapped)


def paired(groups):
    return groups == 4


def hold_kernel(block, _, out):
    out[...] = block[...]


def hold(block, until):
    return pl.pallas_call(
        hold_kernel,
        out_shape=jax.ShapeDtypeStruct(block.shape, jnp.float32),
        in_specs=[VMEM, pl.BlockSpec(memory_space=pl.ANY)],
        out_specs=VMEM,
        compiler_params=PARAMS,
        name="hold",
    )(block, until)


def exchange(own, groups):
    if not paired(groups):
        forward = [(i, (i + 1) % groups) for i in range(groups)]
        backward = [(target, source) for source, target in forward]
        return [lax.ppermute(own, "kgrp", backward)], [lax.ppermute(own, "kgrp", forward)]
    across = lambda block, flip: lax.ppermute(block, "kgrp", [(i, i ^ flip) for i in range(groups)])
    half = own.shape[0] // 2
    near = [across(own[:half], 1), across(own[half:], 1)]
    return near, [across(hold(own[:half], near[1]), 3), across(near[1], 2)]


def spread(values, shape):
    lane = lax.broadcasted_iota(jnp.int32, shape, 1)
    row = jnp.zeros(shape, jnp.float32)
    for spot, value in values:
        row = jnp.where(lane == spot, value, row)
    return row


def total(acc):
    return jnp.sum(jnp.sum(acc, axis=0, keepdims=True), axis=1, keepdims=True)


def history_kernel(
    total_rows, past_inputs, past_residuals, slots, classes, acoustic, optical, number, aged, line, gains,
):
    first = lax.axis_index("energy") * total_rows
    row = lax.broadcasted_iota(jnp.int32, (8, LANES), 0) % total_rows
    coupling = jnp.zeros((8, LANES), jnp.float32)
    for i in range(total_rows):
        coupling = jnp.where(row == i, acoustic[classes[first + i]], coupling)
    gains[0] = coupling
    for m in range(2):
        gains[2 * m + 1] = jnp.full((8, LANES), optical[m] * (number[m] + 1.0))
        gains[2 * m + 2] = jnp.full((8, LANES), optical[m] * number[m])
    _, rows, width = past_inputs.shape
    acc = [jnp.zeros((8, LANES), jnp.float32) for _ in PAIRS]
    for top in range(0, rows, 8):
        def column(t, acc, top=top):
            at = pl.ds(pl.multiple_of(t * LANES, LANES), LANES)
            old = []
            for j in range(HIST):
                res = past_residuals[slots[j], top : top + 8, at]
                aged[j, top : top + 8, at] = (
                    past_inputs[slots[j], top : top + 8, at] + mixing_share * res
                )
                old.append(res)
            return [a + old[i - 1] * old[j - 1] for a, (i, j) in zip(acc, PAIRS)]
        acc = lax.fori_loop(0, width // LANES, column, acc, unroll=4)
    line[...] = spread([(v, total(a)) for v, a in enumerate(acc)], line.shape)


def history(past_inputs, past_residuals, scalars, rows):
    size = past_inputs.size
    return pl.pallas_call(
        lambda *refs: history_kernel(rows, *refs),
        out_shape=(
            jax.ShapeDtypeStruct(past_inputs.shape, jnp.float32),
            jax.ShapeDtypeStruct((1, LANES), jnp.float32),
            jax.ShapeDtypeStruct((5, 8, LANES), jnp.float32),
        ),
        in_specs=[VMEM, VMEM] + [SMEM] * 5,
        out_specs=(VMEM,) * 3,
        compiler_params=PARAMS,
        cost_estimate=pl.CostEstimate(flops=8 * size, bytes_accessed=12 * size, transcendentals=0),
        name="history",
    )(past_inputs, past_residuals, *scalars)


def residual_kernel(count, own, swapped, *refs):
    received = refs[:count]
    current, past_residuals, old_line, gains, slots, shift, fresh, lines, smeared = refs[count:]
    parts, height, slice_len = smeared.shape
    place = lax.axis_index("energy")
    smeared[place], smeared[place ^ 1] = own[0], swapped[0]
    for chip, block in enumerate(received, 1):
        smeared[place ^ (2 * chip)], smeared[place ^ (2 * chip + 1)] = block[0], block[1]
    lane = lax.broadcasted_iota(jnp.int32, (8, slice_len), 1)
    coupling = gains[0]
    modes = [
        (shift[m], lane < slice_len - shift[m], lane >= shift[m], gains[2 * m + 1], gains[2 * m + 2])
        for m in range(2)
    ]
    zero = jnp.zeros((8, slice_len), jnp.float32)
    acc = [zero] * (HIST + 1)
    for top in range(0, height, 8):
        at = slice(top, top + 8)
        source = [smeared[e, at, :] for e in range(parts)]
        sigma = [coupling * x for x in source]
        lesser = top < height // 2
        for s, keep_up, keep_down, emitted, absorbed in modes:
            up = [pltpu.roll(x, slice_len - s, 1) for x in source] + [zero]
            down = [zero] + [pltpu.roll(x, s, 1) for x in source]
            gain_up, gain_down = (emitted, absorbed) if lesser else (absorbed, emitted)
            for e in range(parts):
                above = jnp.where(keep_up, up[e], up[e + 1])
                below = jnp.where(keep_down, down[e + 1], down[e])
                sigma[e] = sigma[e] + (gain_up * above + gain_down * below)
        for e in range(parts):
            where = (at, slice(e * slice_len, (e + 1) * slice_len))
            new = sigma[e] - current[where]
            fresh[where] = new
            acc[0] = acc[0] + new * new
            for j in range(HIST):
                acc[j + 1] = acc[j + 1] + new * past_residuals[(slots[j],) + where]
    mine = jnp.concatenate([jnp.sum(a, axis=0, keepdims=True) for a in acc] + [zero[: 8 - HIST - 1]], axis=0)
    mine = jnp.sum(mine, axis=1, keepdims=True)
    spot = lax.broadcasted_iota(jnp.int32, (8, LANES), 0) + SPOTS[(0, 0)]
    mine = jnp.where(lax.broadcasted_iota(jnp.int32, (8, LANES), 1) == spot, mine, 0.0)
    mine = old_line[...] + jnp.sum(mine, axis=0, keepdims=True)
    lines[...] = jnp.broadcast_to(mine[None], lines.shape)


def residual(kept, swapped, smeared, current, past_residuals, old_line, gains, slots, shift, copies):
    return pl.pallas_call(
        lambda *refs: residual_kernel(len(smeared), *refs),
        out_shape=(
            jax.ShapeDtypeStruct(current.shape, jnp.float32),
            jax.ShapeDtypeStruct((copies, 1, LANES), jnp.float32),
        ),
        in_specs=[VMEM] * (len(smeared) + 6) + [SMEM] * 2,
        out_specs=(VMEM, VMEM),
        scratch_shapes=[pltpu.VMEM((2 * kept.shape[0],) + kept.shape[1:], jnp.float32)],
        compiler_params=PARAMS,
        name="residual",
    )(kept, swapped, *smeared, current, past_residuals, old_line, gains, slots, shift)


def solve(products):
    prod = lambda i, j: products[(min(i, j), max(i, j))]
    n = HIST
    system = [
        [prod(i, j) - prod(i, j + 1) - prod(i + 1, j) + prod(i + 1, j + 1) for j in range(n)]
        for i in range(n)
    ]
    target = [prod(i, 0) - prod(i + 1, 0) for i in range(n)]
    trace = system[0][0]
    for i in range(1, n):
        trace = trace + system[i][i]
    ridge = ridge_share * trace / n + 1e-06
    for i in range(n):
        system[i][i] = system[i][i] + ridge
    inverse = [None] * n
    for k in range(n):
        inverse[k] = 1.0 / system[k][k]
        for i in range(k + 1, n):
            factor = system[k][i] * inverse[k]
            for j in range(i, n):
                system[i][j] = system[i][j] - factor * system[k][j]
            target[i] = target[i] - factor * target[k]
    gamma = [None] * n
    for k in range(n - 1, -1, -1):
        value = target[k]
        for j in range(k + 1, n):
            value = value - system[k][j] * gamma[j]
        gamma[k] = value * inverse[k]
    weights = [1.0 - gamma[0]]
    for j in range(1, n):
        weights.append(gamma[j - 1] - gamma[j])
    weights.append(gamma[n - 1])
    return weights


def mix_kernel(entries, lines, fresh, current, aged, out, wide):
    summed = jnp.sum(lines[...], axis=0) / entries
    row = lax.broadcasted_iota(jnp.int32, (8, LANES), 0)
    lane = lax.broadcasted_iota(jnp.int32, (8, LANES), 1)
    for part in range(wide.shape[0]):
        own = jnp.where(lane == row + 8 * part, summed, 0.0)
        wide[part] = jnp.broadcast_to(jnp.sum(own, axis=1, keepdims=True), (8, LANES))
    products = {
        pair: jnp.broadcast_to(wide[spot // 8, spot % 8 : spot % 8 + 1, :], (8, LANES))
        for pair, spot in SPOTS.items()
    }
    weights = solve(products)
    rows, width = fresh.shape
    for top in range(0, rows, 8):
        for left in range(0, width, LANES):
            at = (slice(top, top + 8), slice(left, left + LANES))
            mixed = weights[0] * (current[at] + mixing_share * fresh[at])
            for j in range(HIST):
                mixed = mixed + weights[j + 1] * aged[(j,) + at]
            out[at] = mixed


def mix(lines, fresh, current, aged, entries):
    return pl.pallas_call(
        lambda *refs: mix_kernel(entries, *refs),
        out_shape=jax.ShapeDtypeStruct(fresh.shape, jnp.float32),
        in_specs=[VMEM] * 4,
        out_specs=VMEM,
        scratch_shapes=[pltpu.VMEM((3, 8, LANES), jnp.float32)],
        compiler_params=PARAMS,
        name="mix",
    )(lines, fresh, current, aged)


def per_device(
    greens,
    current,
    past_inputs,
    past_residuals,
    slot_order,
    neighbour,
    momentum_class,
    stencil_weight,
    acoustic_coupling,
    optical_coupling,
    occupation,
    phonon_shift,
):
    group_len, slice_len = greens.shape[3:]
    rows, width = current.shape[3:]
    groups = lax.axis_size("kgrp")
    parts = lax.axis_size("energy")
    own = greens.reshape(-1, group_len, slice_len)
    height = own.shape[0] * rows

    flat = current.reshape(height, width)
    old_in = past_inputs.reshape(HIST, height, width)
    old_res = past_residuals.reshape(HIST, height, width)
    near, far = exchange(own, groups)
    stencil_hi, stencil_lo, smeared = prepare(own, neighbour, stencil_weight, groups * group_len)
    scalars = (slot_order, momentum_class, acoustic_coupling, optical_coupling, occupation)
    aged, old_line, gains = history(old_in, old_res, scalars, rows)
    smeared = add_side(NEAR, 0, near, stencil_hi, stencil_lo, smeared)
    direct, *forwarded = far
    ready = [add_side(FAR, direct.shape[0], forwarded, stencil_hi, stencil_lo, smeared)] if forwarded else []
    kept, given = finish(FAR, direct, stencil_hi, stencil_lo, smeared, ready, parts)
    meet = lambda block, m: lax.ppermute(block, "energy", [(e, e ^ m) for e in range(parts)])
    swapped = meet(given, 1)
    smeared = [meet(block, 2 * chip) for chip, block in enumerate(join(kept, swapped), 1)]
    fresh, lines = residual(
        kept, swapped, smeared, flat, old_res, old_line, gains, slot_order, phonon_shift, groups * parts
    )
    lines = lax.all_to_all(lines, ("kgrp", "energy"), split_axis=0, concat_axis=0, tiled=True)
    entries = float(flat.size * groups * parts)
    return mix(lines, fresh, flat, aged, entries).reshape(current.shape)


def solution(mesh):
    return jax.shard_map(
        per_device,
        mesh=mesh,
        in_specs=(
            P(None, None, None, "kgrp", "energy"),
            P(None, None, None, ("kgrp", "energy"), None),
            P(None, None, None, None, ("kgrp", "energy"), None),
            P(None, None, None, None, ("kgrp", "energy"), None),
            P(),
            P("kgrp", None),
            P("kgrp"),
            P(),
            P(),
            P(),
            P(),
            P(),
        ),
        out_specs=P(None, None, None, ("kgrp", "energy"), None),
        check_vma=False,
    )
```

```python
import jax
import jax.numpy as jnp
from jax import lax
from jax.experimental import pallas as pl
from jax.experimental.pallas import tpu as pltpu
from jax.sharding import PartitionSpec as P

HIST = 5
LANES = 128

mixing_share = 0.5
ridge_share = 0.1

VMEM = pl.BlockSpec(memory_space=pltpu.VMEM)
SMEM = pl.BlockSpec(memory_space=pltpu.SMEM)
PARAMS = pltpu.CompilerParams(vmem_limit_bytes=16 * 1024 * 1024)

NEAR, FAR = 0, 1

PAIRS = [(i, j) for i in range(1, HIST + 1) for j in range(i, HIST + 1)]
SPOTS = {pair: v for v, pair in enumerate(PAIRS)}
for _j in range(HIST + 1):
    SPOTS[(0, _j)] = 16 + _j


def split(value):
    high = value.astype(jnp.bfloat16)
    return high, (value - high.astype(jnp.float32)).astype(jnp.bfloat16)


def product(left, right):
    dot = lambda a, b: jnp.dot(a, b, preferred_element_type=jnp.float32)
    return dot(left[0], right[0]) + (dot(left[0], right[1]) + dot(left[1], right[0]))


def prepare_kernel(total_k, *refs):
    *blocks, neighbour_hbm, weight_hbm, stencil_hi, stencil_lo, part, late, neighbour, weight, done = refs
    fetches = [
        pltpu.make_async_copy(neighbour_hbm, neighbour, done.at[0]),
        pltpu.make_async_copy(weight_hbm, weight, done.at[1]),
    ]
    for fetch in fetches:
        fetch.start()
    late[...] = blocks[0][...]
    _, group_len, slice_len = blocks[0].shape
    group_id = lax.axis_index("kgrp")
    parts = lax.axis_size("energy")
    rows = group_len // parts
    for fetch in fetches:
        fetch.wait()
    slots, _ = neighbour.shape
    padded = jnp.concatenate([neighbour[...], jnp.zeros((8 - slots, group_len), jnp.int32)], axis=0)
    targets = jnp.transpose(padded)
    place = lax.axis_index("energy")
    bit = 1
    while bit < parts:
        span = bit * rows
        pieces = [targets[at : at + span] for at in range(0, group_len, span)]
        flipped = [pieces[b ^ 1] for b in range(len(pieces))]
        targets = jnp.where(place & bit != 0, jnp.concatenate(flipped, axis=0), targets)
        bit *= 2
    local = targets - group_id * group_len + group_len
    local = jnp.where(local < 0, local + total_k, jnp.where(local >= total_k, local - total_k, local))
    spot = lax.broadcasted_iota(jnp.int32, (group_len, 3 * group_len), 1)
    stencil = jnp.zeros(spot.shape, jnp.float32)
    for n in range(slots):
        stencil = stencil + jnp.where(spot == local[:, n : n + 1], weight[n], 0.0)
    before, after = stencil[:, :group_len], stencil[:, 2 * group_len :]
    swapped = paired(total_k // group_len) & (group_id % 2 == 1)
    near, far = jnp.where(swapped, before, after), jnp.where(swapped, after, before)
    stencil_hi[...], stencil_lo[...] = split(jnp.concatenate([near, far], axis=1))
    centre = split(stencil[:, group_len : 2 * group_len])
    first = 0
    for own in blocks:
        for c in range(0, own.shape[0], 2):
            result = product(centre, split(jnp.concatenate([own[c], own[c + 1]], axis=1)))
            part[first + c] = result[:, :slice_len]
            part[first + c + 1] = result[:, slice_len:]
        first += own.shape[0]


def prepare(blocks, neighbour, weight, total_k):
    comps = sum(block.shape[0] for block in blocks)
    _, group_len, slice_len = blocks[0].shape
    sides = jax.ShapeDtypeStruct((group_len, 2 * group_len), jnp.bfloat16)
    size = comps * group_len * slice_len
    return pl.pallas_call(
        lambda *refs: prepare_kernel(total_k, *refs),
        out_shape=(
            sides,
            sides,
            jax.ShapeDtypeStruct((comps, group_len, slice_len), jnp.float32),
            jax.ShapeDtypeStruct(blocks[0].shape, jnp.float32),
        ),
        in_specs=[VMEM] * len(blocks) + [pl.BlockSpec(memory_space=pltpu.HBM)] * 2,
        out_specs=(VMEM,) * 4,
        scratch_shapes=[
            pltpu.VMEM(neighbour.shape[::-1], jnp.int32),
            pltpu.SMEM(weight.shape, jnp.float32),
            pltpu.SemaphoreType.DMA((2,)),
        ],
        compiler_params=PARAMS,
        cost_estimate=pl.CostEstimate(
            flops=6 * size * group_len, bytes_accessed=8 * size, transcendentals=0
        ),
        name="prepare",
    )(*blocks, jnp.transpose(neighbour), weight)


def smeared_pairs(side, first, block, stencil_hi, stencil_lo, part):
    comps, group_len, slice_len = block.shape
    at = slice(side * group_len, (side + 1) * group_len)
    stencil = (stencil_hi[:, at], stencil_lo[:, at])
    for c in range(0, comps, 2):
        result = product(stencil, split(jnp.concatenate([block[c], block[c + 1]], axis=1)))
        for p in range(2):
            yield c + p, part[first + c + p] + result[:, p * slice_len : (p + 1) * slice_len]


def add_side_kernel(side, first, *refs):
    *blocks, stencil_hi, stencil_lo, part, out = refs
    done = 0
    for block in blocks:
        for c, smeared in smeared_pairs(side, first + done, block, stencil_hi, stencil_lo, part):
            out[done + c] = smeared
        done += block.shape[0]


def add_side(side, first, blocks, stencil_hi, stencil_lo, part):
    shape = (sum(block.shape[0] for block in blocks),) + part.shape[1:]
    return pl.pallas_call(
        lambda *refs: add_side_kernel(side, first, *refs),
        out_shape=jax.ShapeDtypeStruct(shape, jnp.float32),
        in_specs=[VMEM] * (len(blocks) + 3),
        out_specs=VMEM,
        compiler_params=PARAMS,
        cost_estimate=pl.CostEstimate(
            flops=6 * part.size * part.shape[1], bytes_accessed=12 * part.size, transcendentals=0
        ),
        name="add_side",
    )(*blocks, stencil_hi, stencil_lo, part)


def finish_kernel(side, block, stencil_hi, stencil_lo, part, *refs):
    *ready, kept, given = refs
    chips, height, _ = kept.shape
    comps = part.shape[0]
    rows = height // comps

    def place(c, smeared):
        for m in range(2 * chips):
            out = given if m % 2 else kept
            out[m // 2, c * rows : (c + 1) * rows, :] = smeared[m * rows : (m + 1) * rows]

    for c, smeared in smeared_pairs(side, 0, block, stencil_hi, stencil_lo, part):
        place(c, smeared)
    for c in range(block.shape[0], comps):
        place(c, ready[0][c - block.shape[0]])


def finish(side, block, stencil_hi, stencil_lo, part, ready, parts):
    comps, group_len, slice_len = part.shape
    shape = (parts // 2, comps * group_len // parts, slice_len)
    return pl.pallas_call(
        lambda *refs: finish_kernel(side, *refs),
        out_shape=[jax.ShapeDtypeStruct(shape, jnp.float32)] * 2,
        in_specs=[VMEM] * (len(ready) + 4),
        out_specs=[VMEM] * 2,
        compiler_params=PARAMS,
        cost_estimate=pl.CostEstimate(
            flops=6 * part.size * group_len, bytes_accessed=12 * part.size, transcendentals=0
        ),
        name="finish",
    )(block, stencil_hi, stencil_lo, part, *ready)


def join_kernel(own, swapped, *out):
    for chip, block in enumerate(out, 1):
        block[0], block[1] = own[chip], swapped[chip]


def join(own, swapped):
    chips, height, slice_len = own.shape
    shape = jax.ShapeDtypeStruct((2, height, slice_len), jnp.float32)
    return pl.pallas_call(
        join_kernel,
        out_shape=[shape] * (chips - 1),
        in_specs=[VMEM] * 2,
        out_specs=[VMEM] * (chips - 1),
        compiler_params=PARAMS,
        name="join",
    )(own, swapped)


def paired(groups):
    return groups == 4


def hold_kernel(block, _, out):
    out[...] = block[...]


def hold(block, until):
    return pl.pallas_call(
        hold_kernel,
        out_shape=jax.ShapeDtypeStruct(block.shape, jnp.float32),
        in_specs=[VMEM, pl.BlockSpec(memory_space=pl.ANY)],
        out_specs=VMEM,
        compiler_params=PARAMS,
        name="hold",
    )(block, until)


def exchange(own, neighbour, weight, groups):
    total_k = groups * own.shape[1]
    if not paired(groups):
        forward = [(i, (i + 1) % groups) for i in range(groups)]
        backward = [(target, source) for source, target in forward]
        near, far = lax.ppermute(own, "kgrp", backward), lax.ppermute(own, "kgrp", forward)
        return [near], [far], prepare([own], neighbour, weight, total_k)[:3]
    across = lambda block, flip: lax.ppermute(block, "kgrp", [(i, i ^ flip) for i in range(groups)])
    half = own.shape[0] // 2
    blocks = own[:half], own[half:]
    head = across(blocks[1], 1)
    *made, late = prepare(blocks, neighbour, weight, total_k)
    return [across(late, 1), head], [across(hold(late, head), 3), across(head, 2)], made


def spread(values, shape):
    lane = lax.broadcasted_iota(jnp.int32, shape, 1)
    row = jnp.zeros(shape, jnp.float32)
    for spot, value in values:
        row = jnp.where(lane == spot, value, row)
    return row


def total(acc):
    return jnp.sum(jnp.sum(acc, axis=0, keepdims=True), axis=1, keepdims=True)


def history_kernel(
    total_rows, past_inputs, past_residuals, slots, classes, acoustic, optical, number, aged, line, gains,
):
    first = lax.axis_index("energy") * total_rows
    row = lax.broadcasted_iota(jnp.int32, (8, LANES), 0) % total_rows
    coupling = jnp.zeros((8, LANES), jnp.float32)
    for i in range(total_rows):
        coupling = jnp.where(row == i, acoustic[classes[first + i]], coupling)
    gains[0] = coupling
    for m in range(2):
        gains[2 * m + 1] = jnp.full((8, LANES), optical[m] * (number[m] + 1.0))
        gains[2 * m + 2] = jnp.full((8, LANES), optical[m] * number[m])
    _, rows, width = past_inputs.shape
    acc = [jnp.zeros((8, LANES), jnp.float32) for _ in PAIRS]
    for top in range(0, rows, 8):
        def column(t, acc, top=top):
            at = pl.ds(pl.multiple_of(t * LANES, LANES), LANES)
            old = []
            for j in range(HIST):
                res = past_residuals[slots[j], top : top + 8, at]
                aged[j, top : top + 8, at] = (
                    past_inputs[slots[j], top : top + 8, at] + mixing_share * res
                )
                old.append(res)
            return [a + old[i - 1] * old[j - 1] for a, (i, j) in zip(acc, PAIRS)]
        acc = lax.fori_loop(0, width // LANES, column, acc, unroll=4)
    line[...] = spread([(v, total(a)) for v, a in enumerate(acc)], line.shape)


def history(past_inputs, past_residuals, scalars, rows):
    size = past_inputs.size
    return pl.pallas_call(
        lambda *refs: history_kernel(rows, *refs),
        out_shape=(
            jax.ShapeDtypeStruct(past_inputs.shape, jnp.float32),
            jax.ShapeDtypeStruct((1, LANES), jnp.float32),
            jax.ShapeDtypeStruct((5, 8, LANES), jnp.float32),
        ),
        in_specs=[VMEM, VMEM] + [SMEM] * 5,
        out_specs=(VMEM,) * 3,
        compiler_params=PARAMS,
        cost_estimate=pl.CostEstimate(flops=8 * size, bytes_accessed=12 * size, transcendentals=0),
        name="history",
    )(past_inputs, past_residuals, *scalars)


def residual_kernel(count, own, swapped, *refs):
    received = refs[:count]
    current, past_residuals, old_line, gains, slots, shift, fresh, lines, smeared = refs[count:]
    parts, height, slice_len = smeared.shape
    place = lax.axis_index("energy")
    smeared[place], smeared[place ^ 1] = own[0], swapped[0]
    for chip, block in enumerate(received, 1):
        smeared[place ^ (2 * chip)], smeared[place ^ (2 * chip + 1)] = block[0], block[1]
    lane = lax.broadcasted_iota(jnp.int32, (8, slice_len), 1)
    coupling = gains[0]
    modes = [
        (shift[m], lane < slice_len - shift[m], lane >= shift[m], gains[2 * m + 1], gains[2 * m + 2])
        for m in range(2)
    ]
    zero = jnp.zeros((8, slice_len), jnp.float32)
    acc = [zero] * (HIST + 1)
    for top in range(0, height, 8):
        at = slice(top, top + 8)
        source = [smeared[e, at, :] for e in range(parts)]
        sigma = [coupling * x for x in source]
        lesser = top < height // 2
        for s, keep_up, keep_down, emitted, absorbed in modes:
            up = [pltpu.roll(x, slice_len - s, 1) for x in source] + [zero]
            down = [zero] + [pltpu.roll(x, s, 1) for x in source]
            gain_up, gain_down = (emitted, absorbed) if lesser else (absorbed, emitted)
            for e in range(parts):
                above = jnp.where(keep_up, up[e], up[e + 1])
                below = jnp.where(keep_down, down[e + 1], down[e])
                sigma[e] = sigma[e] + (gain_up * above + gain_down * below)
        for e in range(parts):
            where = (at, slice(e * slice_len, (e + 1) * slice_len))
            new = sigma[e] - current[where]
            fresh[where] = new
            acc[0] = acc[0] + new * new
            for j in range(HIST):
                acc[j + 1] = acc[j + 1] + new * past_residuals[(slots[j],) + where]
    mine = jnp.concatenate([jnp.sum(a, axis=0, keepdims=True) for a in acc] + [zero[: 8 - HIST - 1]], axis=0)
    mine = jnp.sum(mine, axis=1, keepdims=True)
    spot = lax.broadcasted_iota(jnp.int32, (8, LANES), 0) + SPOTS[(0, 0)]
    mine = jnp.where(lax.broadcasted_iota(jnp.int32, (8, LANES), 1) == spot, mine, 0.0)
    mine = old_line[...] + jnp.sum(mine, axis=0, keepdims=True)
    lines[...] = jnp.broadcast_to(mine[None], lines.shape)


def residual(kept, swapped, smeared, current, past_residuals, old_line, gains, slots, shift, copies):
    return pl.pallas_call(
        lambda *refs: residual_kernel(len(smeared), *refs),
        out_shape=(
            jax.ShapeDtypeStruct(current.shape, jnp.float32),
            jax.ShapeDtypeStruct((copies, 1, LANES), jnp.float32),
        ),
        in_specs=[VMEM] * (len(smeared) + 6) + [SMEM] * 2,
        out_specs=(VMEM, VMEM),
        scratch_shapes=[pltpu.VMEM((2 * kept.shape[0],) + kept.shape[1:], jnp.float32)],
        compiler_params=PARAMS,
        name="residual",
    )(kept, swapped, *smeared, current, past_residuals, old_line, gains, slots, shift)


def solve(products):
    prod = lambda i, j: products[(min(i, j), max(i, j))]
    n = HIST
    system = [
        [prod(i, j) - prod(i, j + 1) - prod(i + 1, j) + prod(i + 1, j + 1) for j in range(n)]
        for i in range(n)
    ]
    target = [prod(i, 0) - prod(i + 1, 0) for i in range(n)]
    trace = system[0][0]
    for i in range(1, n):
        trace = trace + system[i][i]
    ridge = ridge_share * trace / n + 1e-06
    for i in range(n):
        system[i][i] = system[i][i] + ridge
    inverse = [None] * n
    for k in range(n):
        inverse[k] = 1.0 / system[k][k]
        for i in range(k + 1, n):
            factor = system[k][i] * inverse[k]
            for j in range(i, n):
                system[i][j] = system[i][j] - factor * system[k][j]
            target[i] = target[i] - factor * target[k]
    gamma = [None] * n
    for k in range(n - 1, -1, -1):
        value = target[k]
        for j in range(k + 1, n):
            value = value - system[k][j] * gamma[j]
        gamma[k] = value * inverse[k]
    weights = [1.0 - gamma[0]]
    for j in range(1, n):
        weights.append(gamma[j - 1] - gamma[j])
    weights.append(gamma[n - 1])
    return weights


def mix_kernel(entries, lines, fresh, current, aged, out, wide):
    summed = jnp.sum(lines[...], axis=0) / entries
    row = lax.broadcasted_iota(jnp.int32, (8, LANES), 0)
    lane = lax.broadcasted_iota(jnp.int32, (8, LANES), 1)
    for part in range(wide.shape[0]):
        own = jnp.where(lane == row + 8 * part, summed, 0.0)
        wide[part] = jnp.broadcast_to(jnp.sum(own, axis=1, keepdims=True), (8, LANES))
    products = {
        pair: jnp.broadcast_to(wide[spot // 8, spot % 8 : spot % 8 + 1, :], (8, LANES))
        for pair, spot in SPOTS.items()
    }
    weights = solve(products)
    rows, width = fresh.shape
    for top in range(0, rows, 8):
        for left in range(0, width, LANES):
            at = (slice(top, top + 8), slice(left, left + LANES))
            mixed = weights[0] * (current[at] + mixing_share * fresh[at])
            for j in range(HIST):
                mixed = mixed + weights[j + 1] * aged[(j,) + at]
            out[at] = mixed


def mix(lines, fresh, current, aged, entries):
    return pl.pallas_call(
        lambda *refs: mix_kernel(entries, *refs),
        out_shape=jax.ShapeDtypeStruct(fresh.shape, jnp.float32),
        in_specs=[VMEM] * 4,
        out_specs=VMEM,
        scratch_shapes=[pltpu.VMEM((3, 8, LANES), jnp.float32)],
        compiler_params=PARAMS,
        name="mix",
    )(lines, fresh, current, aged)


def per_device(
    greens,
    current,
    past_inputs,
    past_residuals,
    slot_order,
    neighbour,
    momentum_class,
    stencil_weight,
    acoustic_coupling,
    optical_coupling,
    occupation,
    phonon_shift,
):
    group_len, slice_len = greens.shape[3:]
    rows, width = current.shape[3:]
    groups = lax.axis_size("kgrp")
    parts = lax.axis_size("energy")
    own = greens.reshape(-1, group_len, slice_len)
    height = own.shape[0] * rows

    flat = current.reshape(height, width)
    old_in = past_inputs.reshape(HIST, height, width)
    old_res = past_residuals.reshape(HIST, height, width)
    scalars = (slot_order, momentum_class, acoustic_coupling, optical_coupling, occupation)
    aged, old_line, gains = history(old_in, old_res, scalars, rows)
    near, far, (stencil_hi, stencil_lo, smeared) = exchange(own, neighbour, stencil_weight, groups)
    smeared = add_side(NEAR, 0, near, stencil_hi, stencil_lo, smeared)
    direct, *forwarded = far
    ready = [add_side(FAR, direct.shape[0], forwarded, stencil_hi, stencil_lo, smeared)] if forwarded else []
    kept, given = finish(FAR, direct, stencil_hi, stencil_lo, smeared, ready, parts)
    meet = lambda block, m: lax.ppermute(block, "energy", [(e, e ^ m) for e in range(parts)])
    swapped = meet(given, 1)
    smeared = [meet(block, 2 * chip) for chip, block in enumerate(join(kept, swapped), 1)]
    fresh, lines = residual(
        kept, swapped, smeared, flat, old_res, old_line, gains, slot_order, phonon_shift, groups * parts
    )
    lines = lax.all_to_all(lines, ("kgrp", "energy"), split_axis=0, concat_axis=0, tiled=True)
    entries = float(flat.size * groups * parts)
    return mix(lines, fresh, flat, aged, entries).reshape(current.shape)


def solution(mesh):
    return jax.shard_map(
        per_device,
        mesh=mesh,
        in_specs=(
            P(None, None, None, "kgrp", "energy"),
            P(None, None, None, ("kgrp", "energy"), None),
            P(None, None, None, None, ("kgrp", "energy"), None),
            P(None, None, None, None, ("kgrp", "energy"), None),
            P(),
            P("kgrp", None),
            P("kgrp"),
            P(),
            P(),
            P(),
            P(),
            P(),
        ),
        out_specs=P(None, None, None, ("kgrp", "energy"), None),
        check_vma=False,
    )
```

```python
import jax
import jax.numpy as jnp
from jax import lax
from jax.experimental import pallas as pl
from jax.experimental.pallas import tpu as pltpu
from jax.sharding import PartitionSpec as P

HIST = 5
LANES = 128

mixing_share = 0.5
ridge_share = 0.1

VMEM = pl.BlockSpec(memory_space=pltpu.VMEM)
SMEM = pl.BlockSpec(memory_space=pltpu.SMEM)
PARAMS = pltpu.CompilerParams(vmem_limit_bytes=16 * 1024 * 1024)

PAIRS = [(i, j) for i in range(1, HIST + 1) for j in range(i, HIST + 1)]
SPOTS = {pair: v for v, pair in enumerate(PAIRS)}
for _j in range(HIST + 1):
    SPOTS[(0, _j)] = 16 + _j


def split(value):
    high = value.astype(jnp.bfloat16)
    return high, (value - high.astype(jnp.float32)).astype(jnp.bfloat16)


def product(left, right):
    dot = lambda a, b: jnp.dot(a, b, preferred_element_type=jnp.float32)
    return dot(left[0], right[0]) + (dot(left[0], right[1]) + dot(left[1], right[0]))


def prepare_kernel(total_k, *refs):
    *blocks, neighbour_hbm, weight_hbm, stencil_hi, stencil_lo, part, neighbour, weight, done = refs
    fetches = [
        pltpu.make_async_copy(neighbour_hbm, neighbour, done.at[0]),
        pltpu.make_async_copy(weight_hbm, weight, done.at[1]),
    ]
    for fetch in fetches:
        fetch.start()
    _, group_len, slice_len = blocks[0].shape
    group_id = lax.axis_index("kgrp")
    parts = lax.axis_size("energy")
    rows = group_len // parts
    for fetch in fetches:
        fetch.wait()
    slots, _ = neighbour.shape
    padded = jnp.concatenate([neighbour[...], jnp.zeros((8 - slots, group_len), jnp.int32)], axis=0)
    targets = jnp.transpose(padded)
    place = lax.axis_index("energy")
    bit = 1
    while bit < parts:
        span = bit * rows
        pieces = [targets[at : at + span] for at in range(0, group_len, span)]
        flipped = [pieces[b ^ 1] for b in range(len(pieces))]
        targets = jnp.where(place & bit != 0, jnp.concatenate(flipped, axis=0), targets)
        bit *= 2
    local = targets - group_id * group_len + group_len
    local = jnp.where(local < 0, local + total_k, jnp.where(local >= total_k, local - total_k, local))
    spot = lax.broadcasted_iota(jnp.int32, (group_len, 3 * group_len), 1)
    stencil = jnp.zeros(spot.shape, jnp.float32)
    for n in range(slots):
        stencil = stencil + jnp.where(spot == local[:, n : n + 1], weight[n], 0.0)
    before, after = stencil[:, :group_len], stencil[:, 2 * group_len :]
    swapped = paired(total_k // group_len) & (group_id % 2 == 1)
    near, far = jnp.where(swapped, before, after), jnp.where(swapped, after, before)
    stencil_hi[...], stencil_lo[...] = split(jnp.concatenate([near, far], axis=1))
    centre = split(stencil[:, group_len : 2 * group_len])
    first = 0
    for own in blocks:
        for c in range(0, own.shape[0], 2):
            result = product(centre, split(jnp.concatenate([own[c], own[c + 1]], axis=1)))
            part[first + c] = result[:, :slice_len]
            part[first + c + 1] = result[:, slice_len:]
        first += own.shape[0]


def prepare(blocks, neighbour, weight, total_k):
    comps = sum(block.shape[0] for block in blocks)
    _, group_len, slice_len = blocks[0].shape
    sides = jax.ShapeDtypeStruct((group_len, 2 * group_len), jnp.bfloat16)
    size = comps * group_len * slice_len
    return pl.pallas_call(
        lambda *refs: prepare_kernel(total_k, *refs),
        out_shape=(
            sides,
            sides,
            jax.ShapeDtypeStruct((comps, group_len, slice_len), jnp.float32),
        ),
        in_specs=[VMEM] * len(blocks) + [pl.BlockSpec(memory_space=pltpu.HBM)] * 2,
        out_specs=(VMEM,) * 3,
        scratch_shapes=[
            pltpu.VMEM(neighbour.shape[::-1], jnp.int32),
            pltpu.SMEM(weight.shape, jnp.float32),
            pltpu.SemaphoreType.DMA((2,)),
        ],
        compiler_params=PARAMS,
        cost_estimate=pl.CostEstimate(
            flops=6 * size * group_len, bytes_accessed=8 * size, transcendentals=0
        ),
        name="prepare",
    )(*blocks, jnp.transpose(neighbour), weight)


def smeared_pairs(first, sides, stencil_hi, stencil_lo, part):
    blocks = [block for block in sides if block is not None]
    comps, group_len, slice_len = blocks[0].shape
    start = 0 if sides[0] is not None else group_len
    at = slice(start, start + len(blocks) * group_len)
    stencil = (stencil_hi[:, at], stencil_lo[:, at])
    for c in range(0, comps, 2):
        stacked = [jnp.concatenate([block[c], block[c + 1]], axis=1) for block in blocks]
        result = product(stencil, split(jnp.concatenate(stacked, axis=0)))
        for p in range(2):
            yield c + p, part[first + c + p] + result[:, p * slice_len : (p + 1) * slice_len]


def with_sides(kernel, sides):
    def body(*refs):
        refs = list(refs)
        kernel([None if side is None else refs.pop(0) for side in sides], *refs)

    return body


def smear_cost(blocks):
    size = sum(block.size for block in blocks)
    return pl.CostEstimate(
        flops=6 * size * blocks[0].shape[1], bytes_accessed=12 * size, transcendentals=0
    )


def add_sides(first, sides, stencil_hi, stencil_lo, part, after):
    def kernel(sides, stencil_hi, stencil_lo, part, *refs):
        for c, smeared in smeared_pairs(first, sides, stencil_hi, stencil_lo, part):
            refs[-1][c] = smeared

    blocks = [block for block in sides if block is not None]
    return pl.pallas_call(
        with_sides(kernel, sides),
        out_shape=jax.ShapeDtypeStruct(blocks[0].shape, jnp.float32),
        in_specs=[VMEM] * (len(blocks) + 3) + [pl.BlockSpec(memory_space=pl.ANY)] * len(after),
        out_specs=VMEM,
        compiler_params=PARAMS,
        cost_estimate=smear_cost(blocks),
        name="add_sides",
    )(*blocks, stencil_hi, stencil_lo, part, *after)


def finish_kernel(sides, stencil_hi, stencil_lo, part, *refs):
    *ready, kept, given = refs
    chips, height, _ = kept.shape
    comps = part.shape[0] + sum(block.shape[0] for block in ready)
    rows = height // comps

    def place(c, smeared):
        for m in range(2 * chips):
            out = given if m % 2 else kept
            out[m // 2, c * rows : (c + 1) * rows, :] = smeared[m * rows : (m + 1) * rows]

    for c, smeared in smeared_pairs(0, sides, stencil_hi, stencil_lo, part):
        place(c, smeared)
    for c in range(part.shape[0], comps):
        place(c, ready[0][c - part.shape[0]])


def finish(sides, stencil_hi, stencil_lo, part, ready, parts):
    blocks = [block for block in sides if block is not None]
    _, group_len, slice_len = part.shape
    comps = part.shape[0] + sum(block.shape[0] for block in ready)
    shape = (parts // 2, comps * group_len // parts, slice_len)
    return pl.pallas_call(
        with_sides(finish_kernel, sides),
        out_shape=[jax.ShapeDtypeStruct(shape, jnp.float32)] * 2,
        in_specs=[VMEM] * (len(blocks) + len(ready) + 3),
        out_specs=[VMEM] * 2,
        compiler_params=PARAMS,
        cost_estimate=smear_cost(blocks),
        name="finish",
    )(*blocks, stencil_hi, stencil_lo, part, *ready)


def join_kernel(own, swapped, *out):
    for chip, block in enumerate(out, 1):
        block[0], block[1] = own[chip], swapped[chip]


def join(own, swapped):
    chips, height, slice_len = own.shape
    shape = jax.ShapeDtypeStruct((2, height, slice_len), jnp.float32)
    return pl.pallas_call(
        join_kernel,
        out_shape=[shape] * (chips - 1),
        in_specs=[VMEM] * 2,
        out_specs=[VMEM] * (chips - 1),
        compiler_params=PARAMS,
        name="join",
    )(own, swapped)


def paired(groups):
    return groups == 4


def hold_kernel(block, _, out):
    out[...] = block[...]


def hold(block, until):
    return pl.pallas_call(
        hold_kernel,
        out_shape=jax.ShapeDtypeStruct(block.shape, jnp.float32),
        in_specs=[VMEM, pl.BlockSpec(memory_space=pl.ANY)],
        out_specs=VMEM,
        compiler_params=PARAMS,
        name="hold",
    )(block, until)


def smear(own, neighbour, weight, groups, parts):
    total_k = groups * own.shape[1]
    if not paired(groups):
        forward = [(i, (i + 1) % groups) for i in range(groups)]
        backward = [(target, source) for source, target in forward]
        near, far = lax.ppermute(own, "kgrp", backward), lax.ppermute(own, "kgrp", forward)
        return finish((near, far), *prepare([own], neighbour, weight, total_k), [], parts)
    across = lambda block, flip: lax.ppermute(block, "kgrp", [(i, i ^ flip) for i in range(groups)])
    half = own.shape[0] // 2
    tail, head = own[:half], own[half:]
    near_head, far_tail = across(head, 1), across(tail, 3)
    far_head, near_tail = across(near_head, 2), across(hold(tail, near_head), 1)
    hi, lo, part = prepare([tail, head], neighbour, weight, total_k)
    tail_part = add_sides(0, (None, far_tail), hi, lo, part, [])
    head_part = add_sides(half, (near_head, far_head), hi, lo, part, [tail_part])
    return finish((near_tail, None), hi, lo, tail_part, [head_part], parts)


def spread(values, shape):
    lane = lax.broadcasted_iota(jnp.int32, shape, 1)
    row = jnp.zeros(shape, jnp.float32)
    for spot, value in values:
        row = jnp.where(lane == spot, value, row)
    return row


def total(acc):
    return jnp.sum(jnp.sum(acc, axis=0, keepdims=True), axis=1, keepdims=True)


def history_kernel(
    total_rows, past_inputs, past_residuals, slots, classes, acoustic, optical, number, aged, line, gains,
):
    first = lax.axis_index("energy") * total_rows
    row = lax.broadcasted_iota(jnp.int32, (8, LANES), 0) % total_rows
    coupling = jnp.zeros((8, LANES), jnp.float32)
    for i in range(total_rows):
        coupling = jnp.where(row == i, acoustic[classes[first + i]], coupling)
    gains[0] = coupling
    for m in range(2):
        gains[2 * m + 1] = jnp.full((8, LANES), optical[m] * (number[m] + 1.0))
        gains[2 * m + 2] = jnp.full((8, LANES), optical[m] * number[m])
    _, rows, width = past_inputs.shape
    acc = [jnp.zeros((8, LANES), jnp.float32) for _ in PAIRS]
    for top in range(0, rows, 8):
        def column(t, acc, top=top):
            at = pl.ds(pl.multiple_of(t * LANES, LANES), LANES)
            old = []
            for j in range(HIST):
                res = past_residuals[slots[j], top : top + 8, at]
                aged[j, top : top + 8, at] = (
                    past_inputs[slots[j], top : top + 8, at] + mixing_share * res
                )
                old.append(res)
            return [a + old[i - 1] * old[j - 1] for a, (i, j) in zip(acc, PAIRS)]
        acc = lax.fori_loop(0, width // LANES, column, acc, unroll=4)
    line[...] = spread([(v, total(a)) for v, a in enumerate(acc)], line.shape)


def history(past_inputs, past_residuals, scalars, rows):
    size = past_inputs.size
    return pl.pallas_call(
        lambda *refs: history_kernel(rows, *refs),
        out_shape=(
            jax.ShapeDtypeStruct(past_inputs.shape, jnp.float32),
            jax.ShapeDtypeStruct((1, LANES), jnp.float32),
            jax.ShapeDtypeStruct((5, 8, LANES), jnp.float32),
        ),
        in_specs=[VMEM, VMEM] + [SMEM] * 5,
        out_specs=(VMEM,) * 3,
        compiler_params=PARAMS,
        cost_estimate=pl.CostEstimate(flops=8 * size, bytes_accessed=12 * size, transcendentals=0),
        name="history",
    )(past_inputs, past_residuals, *scalars)


def residual_kernel(count, own, swapped, *refs):
    received = refs[:count]
    current, past_residuals, old_line, gains, slots, shift, fresh, lines, smeared = refs[count:]
    parts, height, slice_len = smeared.shape
    place = lax.axis_index("energy")
    smeared[place], smeared[place ^ 1] = own[0], swapped[0]
    for chip, block in enumerate(received, 1):
        smeared[place ^ (2 * chip)], smeared[place ^ (2 * chip + 1)] = block[0], block[1]
    lane = lax.broadcasted_iota(jnp.int32, (8, slice_len), 1)
    coupling = gains[0]
    modes = [
        (shift[m], lane < slice_len - shift[m], lane >= shift[m], gains[2 * m + 1], gains[2 * m + 2])
        for m in range(2)
    ]
    zero = jnp.zeros((8, slice_len), jnp.float32)
    acc = [zero] * (HIST + 1)
    for top in range(0, height, 8):
        at = slice(top, top + 8)
        source = [smeared[e, at, :] for e in range(parts)]
        sigma = [coupling * x for x in source]
        lesser = top < height // 2
        for s, keep_up, keep_down, emitted, absorbed in modes:
            up = [pltpu.roll(x, slice_len - s, 1) for x in source] + [zero]
            down = [zero] + [pltpu.roll(x, s, 1) for x in source]
            gain_up, gain_down = (emitted, absorbed) if lesser else (absorbed, emitted)
            for e in range(parts):
                above = jnp.where(keep_up, up[e], up[e + 1])
                below = jnp.where(keep_down, down[e + 1], down[e])
                sigma[e] = sigma[e] + (gain_up * above + gain_down * below)
        for e in range(parts):
            where = (at, slice(e * slice_len, (e + 1) * slice_len))
            new = sigma[e] - current[where]
            fresh[where] = new
            acc[0] = acc[0] + new * new
            for j in range(HIST):
                acc[j + 1] = acc[j + 1] + new * past_residuals[(slots[j],) + where]
    mine = jnp.concatenate([jnp.sum(a, axis=0, keepdims=True) for a in acc] + [zero[: 8 - HIST - 1]], axis=0)
    mine = jnp.sum(mine, axis=1, keepdims=True)
    spot = lax.broadcasted_iota(jnp.int32, (8, LANES), 0) + SPOTS[(0, 0)]
    mine = jnp.where(lax.broadcasted_iota(jnp.int32, (8, LANES), 1) == spot, mine, 0.0)
    mine = old_line[...] + jnp.sum(mine, axis=0, keepdims=True)
    lines[...] = jnp.broadcast_to(mine[None], lines.shape)


def residual(kept, swapped, smeared, current, past_residuals, old_line, gains, slots, shift, copies):
    return pl.pallas_call(
        lambda *refs: residual_kernel(len(smeared), *refs),
        out_shape=(
            jax.ShapeDtypeStruct(current.shape, jnp.float32),
            jax.ShapeDtypeStruct((copies, 1, LANES), jnp.float32),
        ),
        in_specs=[VMEM] * (len(smeared) + 6) + [SMEM] * 2,
        out_specs=(VMEM, VMEM),
        scratch_shapes=[pltpu.VMEM((2 * kept.shape[0],) + kept.shape[1:], jnp.float32)],
        compiler_params=PARAMS,
        name="residual",
    )(kept, swapped, *smeared, current, past_residuals, old_line, gains, slots, shift)


def solve(products):
    prod = lambda i, j: products[(min(i, j), max(i, j))]
    n = HIST
    system = [
        [prod(i, j) - prod(i, j + 1) - prod(i + 1, j) + prod(i + 1, j + 1) for j in range(n)]
        for i in range(n)
    ]
    target = [prod(i, 0) - prod(i + 1, 0) for i in range(n)]
    trace = system[0][0]
    for i in range(1, n):
        trace = trace + system[i][i]
    ridge = ridge_share * trace / n + 1e-06
    for i in range(n):
        system[i][i] = system[i][i] + ridge
    inverse = [None] * n
    for k in range(n):
        inverse[k] = 1.0 / system[k][k]
        for i in range(k + 1, n):
            factor = system[k][i] * inverse[k]
            for j in range(i, n):
                system[i][j] = system[i][j] - factor * system[k][j]
            target[i] = target[i] - factor * target[k]
    gamma = [None] * n
    for k in range(n - 1, -1, -1):
        value = target[k]
        for j in range(k + 1, n):
            value = value - system[k][j] * gamma[j]
        gamma[k] = value * inverse[k]
    weights = [1.0 - gamma[0]]
    for j in range(1, n):
        weights.append(gamma[j - 1] - gamma[j])
    weights.append(gamma[n - 1])
    return weights


def mix_kernel(entries, lines, fresh, current, aged, out, wide):
    summed = jnp.sum(lines[...], axis=0) / entries
    row = lax.broadcasted_iota(jnp.int32, (8, LANES), 0)
    lane = lax.broadcasted_iota(jnp.int32, (8, LANES), 1)
    for part in range(wide.shape[0]):
        own = jnp.where(lane == row + 8 * part, summed, 0.0)
        wide[part] = jnp.broadcast_to(jnp.sum(own, axis=1, keepdims=True), (8, LANES))
    products = {
        pair: jnp.broadcast_to(wide[spot // 8, spot % 8 : spot % 8 + 1, :], (8, LANES))
        for pair, spot in SPOTS.items()
    }
    weights = solve(products)
    rows, width = fresh.shape
    for top in range(0, rows, 8):
        for left in range(0, width, LANES):
            at = (slice(top, top + 8), slice(left, left + LANES))
            mixed = weights[0] * (current[at] + mixing_share * fresh[at])
            for j in range(HIST):
                mixed = mixed + weights[j + 1] * aged[(j,) + at]
            out[at] = mixed


def mix(lines, fresh, current, aged, entries):
    return pl.pallas_call(
        lambda *refs: mix_kernel(entries, *refs),
        out_shape=jax.ShapeDtypeStruct(fresh.shape, jnp.float32),
        in_specs=[VMEM] * 4,
        out_specs=VMEM,
        scratch_shapes=[pltpu.VMEM((3, 8, LANES), jnp.float32)],
        compiler_params=PARAMS,
        name="mix",
    )(lines, fresh, current, aged)


def per_device(
    greens,
    current,
    past_inputs,
    past_residuals,
    slot_order,
    neighbour,
    momentum_class,
    stencil_weight,
    acoustic_coupling,
    optical_coupling,
    occupation,
    phonon_shift,
):
    group_len, slice_len = greens.shape[3:]
    rows, width = current.shape[3:]
    groups = lax.axis_size("kgrp")
    parts = lax.axis_size("energy")
    own = greens.reshape(-1, group_len, slice_len)
    height = own.shape[0] * rows

    flat = current.reshape(height, width)
    old_in = past_inputs.reshape(HIST, height, width)
    old_res = past_residuals.reshape(HIST, height, width)
    scalars = (slot_order, momentum_class, acoustic_coupling, optical_coupling, occupation)
    aged, old_line, gains = history(old_in, old_res, scalars, rows)
    kept, given = smear(own, neighbour, stencil_weight, groups, parts)
    meet = lambda block, m: lax.ppermute(block, "energy", [(e, e ^ m) for e in range(parts)])
    swapped = meet(given, 1)
    smeared = [meet(block, 2 * chip) for chip, block in enumerate(join(kept, swapped), 1)]
    fresh, lines = residual(
        kept, swapped, smeared, flat, old_res, old_line, gains, slot_order, phonon_shift, groups * parts
    )
    lines = lax.all_to_all(lines, ("kgrp", "energy"), split_axis=0, concat_axis=0, tiled=True)
    entries = float(flat.size * groups * parts)
    return mix(lines, fresh, flat, aged, entries).reshape(current.shape)


def solution(mesh):
    return jax.shard_map(
        per_device,
        mesh=mesh,
        in_specs=(
            P(None, None, None, "kgrp", "energy"),
            P(None, None, None, ("kgrp", "energy"), None),
            P(None, None, None, None, ("kgrp", "energy"), None),
            P(None, None, None, None, ("kgrp", "energy"), None),
            P(),
            P("kgrp", None),
            P("kgrp"),
            P(),
            P(),
            P(),
            P(),
            P(),
        ),
        out_specs=P(None, None, None, ("kgrp", "energy"), None),
        check_vma=False,
    )
```

```python
import jax
import jax.numpy as jnp
from jax import lax
from jax.experimental import pallas as pl
from jax.experimental.pallas import tpu as pltpu
from jax.sharding import PartitionSpec as P

HIST = 5
LANES = 128

mixing_share = 0.5
ridge_share = 0.1

VMEM = pl.BlockSpec(memory_space=pltpu.VMEM)
SMEM = pl.BlockSpec(memory_space=pltpu.SMEM)
PARAMS = pltpu.CompilerParams(vmem_limit_bytes=16 * 1024 * 1024)

PAIRS = [(i, j) for i in range(1, HIST + 1) for j in range(i, HIST + 1)]
SPOTS = {pair: v for v, pair in enumerate(PAIRS)}
for _j in range(HIST + 1):
    SPOTS[(0, _j)] = 16 + _j


def split(value):
    high = value.astype(jnp.bfloat16)
    return high, (value - high.astype(jnp.float32)).astype(jnp.bfloat16)


def product(left, right):
    dot = lambda a, b: jnp.dot(a, b, preferred_element_type=jnp.float32)
    return dot(left[0], right[0]) + (dot(left[0], right[1]) + dot(left[1], right[0]))


def prepare_kernel(total_k, *refs):
    *blocks, neighbour_hbm, weight_hbm, stencil_hi, stencil_lo, part, late, neighbour, weight, done = refs
    fetches = [
        pltpu.make_async_copy(neighbour_hbm, neighbour, done.at[0]),
        pltpu.make_async_copy(weight_hbm, weight, done.at[1]),
    ]
    for fetch in fetches:
        fetch.start()
    late[...] = blocks[-1][...]
    _, group_len, slice_len = blocks[0].shape
    group_id = lax.axis_index("kgrp")
    parts = lax.axis_size("energy")
    rows = group_len // parts
    for fetch in fetches:
        fetch.wait()
    slots, _ = neighbour.shape
    padded = jnp.concatenate([neighbour[...], jnp.zeros((8 - slots, group_len), jnp.int32)], axis=0)
    targets = jnp.transpose(padded)
    place = lax.axis_index("energy")
    bit = 1
    while bit < parts:
        span = bit * rows
        pieces = [targets[at : at + span] for at in range(0, group_len, span)]
        flipped = [pieces[b ^ 1] for b in range(len(pieces))]
        targets = jnp.where(place & bit != 0, jnp.concatenate(flipped, axis=0), targets)
        bit *= 2
    local = targets - group_id * group_len + group_len
    local = jnp.where(local < 0, local + total_k, jnp.where(local >= total_k, local - total_k, local))
    spot = lax.broadcasted_iota(jnp.int32, (group_len, 3 * group_len), 1)
    stencil = jnp.zeros(spot.shape, jnp.float32)
    for n in range(slots):
        stencil = stencil + jnp.where(spot == local[:, n : n + 1], weight[n], 0.0)
    before, after = stencil[:, :group_len], stencil[:, 2 * group_len :]
    swapped = paired(total_k // group_len) & (group_id % 2 == 1)
    near, far = jnp.where(swapped, before, after), jnp.where(swapped, after, before)
    stencil_hi[...], stencil_lo[...] = split(jnp.concatenate([near, far], axis=1))
    centre = split(stencil[:, group_len : 2 * group_len])
    first = 0
    for own in blocks:
        for c in range(0, own.shape[0], 2):
            result = product(centre, split(jnp.concatenate([own[c], own[c + 1]], axis=1)))
            part[first + c] = result[:, :slice_len]
            part[first + c + 1] = result[:, slice_len:]
        first += own.shape[0]


def prepare(blocks, neighbour, weight, total_k):
    comps = sum(block.shape[0] for block in blocks)
    _, group_len, slice_len = blocks[0].shape
    sides = jax.ShapeDtypeStruct((group_len, 2 * group_len), jnp.bfloat16)
    size = comps * group_len * slice_len
    return pl.pallas_call(
        lambda *refs: prepare_kernel(total_k, *refs),
        out_shape=(
            sides,
            sides,
            jax.ShapeDtypeStruct((comps, group_len, slice_len), jnp.float32),
            jax.ShapeDtypeStruct(blocks[-1].shape, jnp.float32),
        ),
        in_specs=[VMEM] * len(blocks) + [pl.BlockSpec(memory_space=pltpu.HBM)] * 2,
        out_specs=(VMEM,) * 4,
        scratch_shapes=[
            pltpu.VMEM(neighbour.shape[::-1], jnp.int32),
            pltpu.SMEM(weight.shape, jnp.float32),
            pltpu.SemaphoreType.DMA((2,)),
        ],
        compiler_params=PARAMS,
        cost_estimate=pl.CostEstimate(
            flops=6 * size * group_len, bytes_accessed=8 * size, transcendentals=0
        ),
        name="prepare",
    )(*blocks, jnp.transpose(neighbour), weight)


def smeared_pairs(first, sides, stencil_hi, stencil_lo, part):
    blocks = [block for block in sides if block is not None]
    comps, group_len, slice_len = blocks[0].shape
    start = 0 if sides[0] is not None else group_len
    at = slice(start, start + len(blocks) * group_len)
    stencil = (stencil_hi[:, at], stencil_lo[:, at])
    for c in range(0, comps, 2):
        stacked = [jnp.concatenate([block[c], block[c + 1]], axis=1) for block in blocks]
        result = product(stencil, split(jnp.concatenate(stacked, axis=0)))
        for p in range(2):
            yield c + p, part[first + c + p] + result[:, p * slice_len : (p + 1) * slice_len]


def with_sides(kernel, sides):
    def body(*refs):
        refs = list(refs)
        kernel([None if side is None else refs.pop(0) for side in sides], *refs)

    return body


def smear_cost(blocks):
    size = sum(block.size for block in blocks)
    return pl.CostEstimate(
        flops=6 * size * blocks[0].shape[1], bytes_accessed=12 * size, transcendentals=0
    )


def add_sides(first, sides, stencil_hi, stencil_lo, part, after):
    def kernel(sides, stencil_hi, stencil_lo, part, *refs):
        for c, smeared in smeared_pairs(first, sides, stencil_hi, stencil_lo, part):
            refs[-1][c] = smeared

    blocks = [block for block in sides if block is not None]
    return pl.pallas_call(
        with_sides(kernel, sides),
        out_shape=jax.ShapeDtypeStruct(blocks[0].shape, jnp.float32),
        in_specs=[VMEM] * (len(blocks) + 3) + [pl.BlockSpec(memory_space=pl.ANY)] * len(after),
        out_specs=VMEM,
        compiler_params=PARAMS,
        cost_estimate=smear_cost(blocks),
        name="add_sides",
    )(*blocks, stencil_hi, stencil_lo, part, *after)


def finish_kernel(sides, stencil_hi, stencil_lo, part, *refs):
    *ready, kept, given = refs
    chips, height, _ = kept.shape
    comps = part.shape[0]
    rows = height // comps

    def place(c, smeared):
        for m in range(2 * chips):
            out = given if m % 2 else kept
            out[m // 2, c * rows : (c + 1) * rows, :] = smeared[m * rows : (m + 1) * rows]

    first = 0
    for c, smeared in smeared_pairs(0, sides, stencil_hi, stencil_lo, part):
        place(c, smeared)
        first = c + 1
    for block in ready:
        for c in range(block.shape[0]):
            place(first + c, block[c])


def finish(sides, stencil_hi, stencil_lo, part, ready, parts):
    blocks = [block for block in sides if block is not None]
    comps, group_len, slice_len = part.shape
    shape = (parts // 2, comps * group_len // parts, slice_len)
    return pl.pallas_call(
        with_sides(finish_kernel, sides),
        out_shape=[jax.ShapeDtypeStruct(shape, jnp.float32)] * 2,
        in_specs=[VMEM] * (len(blocks) + len(ready) + 3),
        out_specs=[VMEM] * 2,
        compiler_params=PARAMS,
        cost_estimate=smear_cost(blocks),
        name="finish",
    )(*blocks, stencil_hi, stencil_lo, part, *ready)


def join_kernel(own, swapped, *out):
    for chip, block in enumerate(out, 1):
        block[0], block[1] = own[chip], swapped[chip]


def join(own, swapped):
    chips, height, slice_len = own.shape
    shape = jax.ShapeDtypeStruct((2, height, slice_len), jnp.float32)
    return pl.pallas_call(
        join_kernel,
        out_shape=[shape] * (chips - 1),
        in_specs=[VMEM] * 2,
        out_specs=[VMEM] * (chips - 1),
        compiler_params=PARAMS,
        name="join",
    )(own, swapped)


def paired(groups):
    return groups == 4


def hold_kernel(block, _, out):
    out[...] = block[...]


def hold(block, until):
    return pl.pallas_call(
        hold_kernel,
        out_shape=jax.ShapeDtypeStruct(block.shape, jnp.float32),
        in_specs=[VMEM, pl.BlockSpec(memory_space=pl.ANY)],
        out_specs=VMEM,
        compiler_params=PARAMS,
        name="hold",
    )(block, until)


def smear(own, neighbour, weight, groups, parts):
    total_k = groups * own.shape[1]
    if not paired(groups):
        forward = [(i, (i + 1) % groups) for i in range(groups)]
        backward = [(target, source) for source, target in forward]
        near, far = lax.ppermute(own, "kgrp", backward), lax.ppermute(own, "kgrp", forward)
        return finish((near, far), *prepare([own], neighbour, weight, total_k)[:3], [], parts)
    across = lambda block, flip: lax.ppermute(block, "kgrp", [(i, i ^ flip) for i in range(groups)])
    half = own.shape[0] // 2
    head, tail = own[:half], own[half:]
    near_head, far_tail = across(head, 1), across(tail, 3)
    hi, lo, part, late = prepare([head, tail], neighbour, weight, total_k)
    near_tail, far_head = across(late, 1), across(hold(near_head, late), 2)
    tail_part = add_sides(half, (near_tail, far_tail), hi, lo, part, [])
    return finish((near_head, far_head), hi, lo, part, [tail_part], parts)


def spread(values, shape):
    lane = lax.broadcasted_iota(jnp.int32, shape, 1)
    row = jnp.zeros(shape, jnp.float32)
    for spot, value in values:
        row = jnp.where(lane == spot, value, row)
    return row


def total(acc):
    return jnp.sum(jnp.sum(acc, axis=0, keepdims=True), axis=1, keepdims=True)


def history_kernel(
    total_rows, past_inputs, past_residuals, slots, classes, acoustic, optical, number, aged, line, gains,
):
    first = lax.axis_index("energy") * total_rows
    row = lax.broadcasted_iota(jnp.int32, (8, LANES), 0) % total_rows
    coupling = jnp.zeros((8, LANES), jnp.float32)
    for i in range(total_rows):
        coupling = jnp.where(row == i, acoustic[classes[first + i]], coupling)
    gains[0] = coupling
    for m in range(2):
        gains[2 * m + 1] = jnp.full((8, LANES), optical[m] * (number[m] + 1.0))
        gains[2 * m + 2] = jnp.full((8, LANES), optical[m] * number[m])
    _, rows, width = past_inputs.shape
    acc = [jnp.zeros((8, LANES), jnp.float32) for _ in PAIRS]
    for top in range(0, rows, 8):
        def column(t, acc, top=top):
            at = pl.ds(pl.multiple_of(t * LANES, LANES), LANES)
            old = []
            for j in range(HIST):
                res = past_residuals[slots[j], top : top + 8, at]
                aged[j, top : top + 8, at] = (
                    past_inputs[slots[j], top : top + 8, at] + mixing_share * res
                )
                old.append(res)
            return [a + old[i - 1] * old[j - 1] for a, (i, j) in zip(acc, PAIRS)]
        acc = lax.fori_loop(0, width // LANES, column, acc, unroll=4)
    line[...] = spread([(v, total(a)) for v, a in enumerate(acc)], line.shape)


def history(past_inputs, past_residuals, scalars, rows):
    size = past_inputs.size
    return pl.pallas_call(
        lambda *refs: history_kernel(rows, *refs),
        out_shape=(
            jax.ShapeDtypeStruct(past_inputs.shape, jnp.float32),
            jax.ShapeDtypeStruct((1, LANES), jnp.float32),
            jax.ShapeDtypeStruct((5, 8, LANES), jnp.float32),
        ),
        in_specs=[VMEM, VMEM] + [SMEM] * 5,
        out_specs=(VMEM,) * 3,
        compiler_params=PARAMS,
        cost_estimate=pl.CostEstimate(flops=8 * size, bytes_accessed=12 * size, transcendentals=0),
        name="history",
    )(past_inputs, past_residuals, *scalars)


def residual_kernel(count, own, swapped, *refs):
    received = refs[:count]
    current, past_residuals, old_line, gains, slots, shift, fresh, lines, smeared = refs[count:]
    parts, height, slice_len = smeared.shape
    place = lax.axis_index("energy")
    smeared[place], smeared[place ^ 1] = own[0], swapped[0]
    for chip, block in enumerate(received, 1):
        smeared[place ^ (2 * chip)], smeared[place ^ (2 * chip + 1)] = block[0], block[1]
    lane = lax.broadcasted_iota(jnp.int32, (8, slice_len), 1)
    coupling = gains[0]
    modes = [
        (shift[m], lane < slice_len - shift[m], lane >= shift[m], gains[2 * m + 1], gains[2 * m + 2])
        for m in range(2)
    ]
    zero = jnp.zeros((8, slice_len), jnp.float32)
    acc = [zero] * (HIST + 1)
    for top in range(0, height, 8):
        at = slice(top, top + 8)
        source = [smeared[e, at, :] for e in range(parts)]
        sigma = [coupling * x for x in source]
        lesser = top < height // 2
        for s, keep_up, keep_down, emitted, absorbed in modes:
            up = [pltpu.roll(x, slice_len - s, 1) for x in source] + [zero]
            down = [zero] + [pltpu.roll(x, s, 1) for x in source]
            gain_up, gain_down = (emitted, absorbed) if lesser else (absorbed, emitted)
            for e in range(parts):
                above = jnp.where(keep_up, up[e], up[e + 1])
                below = jnp.where(keep_down, down[e + 1], down[e])
                sigma[e] = sigma[e] + (gain_up * above + gain_down * below)
        for e in range(parts):
            where = (at, slice(e * slice_len, (e + 1) * slice_len))
            new = sigma[e] - current[where]
            fresh[where] = new
            acc[0] = acc[0] + new * new
            for j in range(HIST):
                acc[j + 1] = acc[j + 1] + new * past_residuals[(slots[j],) + where]
    mine = jnp.concatenate([jnp.sum(a, axis=0, keepdims=True) for a in acc] + [zero[: 8 - HIST - 1]], axis=0)
    mine = jnp.sum(mine, axis=1, keepdims=True)
    spot = lax.broadcasted_iota(jnp.int32, (8, LANES), 0) + SPOTS[(0, 0)]
    mine = jnp.where(lax.broadcasted_iota(jnp.int32, (8, LANES), 1) == spot, mine, 0.0)
    mine = old_line[...] + jnp.sum(mine, axis=0, keepdims=True)
    lines[...] = jnp.broadcast_to(mine[None], lines.shape)


def residual(kept, swapped, smeared, current, past_residuals, old_line, gains, slots, shift, copies):
    return pl.pallas_call(
        lambda *refs: residual_kernel(len(smeared), *refs),
        out_shape=(
            jax.ShapeDtypeStruct(current.shape, jnp.float32),
            jax.ShapeDtypeStruct((copies, 1, LANES), jnp.float32),
        ),
        in_specs=[VMEM] * (len(smeared) + 6) + [SMEM] * 2,
        out_specs=(VMEM, VMEM),
        scratch_shapes=[pltpu.VMEM((2 * kept.shape[0],) + kept.shape[1:], jnp.float32)],
        compiler_params=PARAMS,
        name="residual",
    )(kept, swapped, *smeared, current, past_residuals, old_line, gains, slots, shift)


def solve(products):
    prod = lambda i, j: products[(min(i, j), max(i, j))]
    n = HIST
    system = [
        [prod(i, j) - prod(i, j + 1) - prod(i + 1, j) + prod(i + 1, j + 1) for j in range(n)]
        for i in range(n)
    ]
    target = [prod(i, 0) - prod(i + 1, 0) for i in range(n)]
    trace = system[0][0]
    for i in range(1, n):
        trace = trace + system[i][i]
    ridge = ridge_share * trace / n + 1e-06
    for i in range(n):
        system[i][i] = system[i][i] + ridge
    inverse = [None] * n
    for k in range(n):
        inverse[k] = 1.0 / system[k][k]
        for i in range(k + 1, n):
            factor = system[k][i] * inverse[k]
            for j in range(i, n):
                system[i][j] = system[i][j] - factor * system[k][j]
            target[i] = target[i] - factor * target[k]
    gamma = [None] * n
    for k in range(n - 1, -1, -1):
        value = target[k]
        for j in range(k + 1, n):
            value = value - system[k][j] * gamma[j]
        gamma[k] = value * inverse[k]
    weights = [1.0 - gamma[0]]
    for j in range(1, n):
        weights.append(gamma[j - 1] - gamma[j])
    weights.append(gamma[n - 1])
    return weights


def mix_kernel(entries, lines, fresh, current, aged, out, wide):
    summed = jnp.sum(lines[...], axis=0) / entries
    row = lax.broadcasted_iota(jnp.int32, (8, LANES), 0)
    lane = lax.broadcasted_iota(jnp.int32, (8, LANES), 1)
    for part in range(wide.shape[0]):
        own = jnp.where(lane == row + 8 * part, summed, 0.0)
        wide[part] = jnp.broadcast_to(jnp.sum(own, axis=1, keepdims=True), (8, LANES))
    products = {
        pair: jnp.broadcast_to(wide[spot // 8, spot % 8 : spot % 8 + 1, :], (8, LANES))
        for pair, spot in SPOTS.items()
    }
    weights = solve(products)
    rows, width = fresh.shape
    for top in range(0, rows, 8):
        for left in range(0, width, LANES):
            at = (slice(top, top + 8), slice(left, left + LANES))
            mixed = weights[0] * (current[at] + mixing_share * fresh[at])
            for j in range(HIST):
                mixed = mixed + weights[j + 1] * aged[(j,) + at]
            out[at] = mixed


def mix(lines, fresh, current, aged, entries):
    return pl.pallas_call(
        lambda *refs: mix_kernel(entries, *refs),
        out_shape=jax.ShapeDtypeStruct(fresh.shape, jnp.float32),
        in_specs=[VMEM] * 4,
        out_specs=VMEM,
        scratch_shapes=[pltpu.VMEM((3, 8, LANES), jnp.float32)],
        compiler_params=PARAMS,
        name="mix",
    )(lines, fresh, current, aged)


def per_device(
    greens,
    current,
    past_inputs,
    past_residuals,
    slot_order,
    neighbour,
    momentum_class,
    stencil_weight,
    acoustic_coupling,
    optical_coupling,
    occupation,
    phonon_shift,
):
    group_len, slice_len = greens.shape[3:]
    rows, width = current.shape[3:]
    groups = lax.axis_size("kgrp")
    parts = lax.axis_size("energy")
    own = greens.reshape(-1, group_len, slice_len)
    height = own.shape[0] * rows

    flat = current.reshape(height, width)
    old_in = past_inputs.reshape(HIST, height, width)
    old_res = past_residuals.reshape(HIST, height, width)
    scalars = (slot_order, momentum_class, acoustic_coupling, optical_coupling, occupation)
    aged, old_line, gains = history(old_in, old_res, scalars, rows)
    kept, given = smear(own, neighbour, stencil_weight, groups, parts)
    meet = lambda block, m: lax.ppermute(block, "energy", [(e, e ^ m) for e in range(parts)])
    swapped = meet(given, 1)
    smeared = [meet(block, 2 * chip) for chip, block in enumerate(join(kept, swapped), 1)]
    fresh, lines = residual(
        kept, swapped, smeared, flat, old_res, old_line, gains, slot_order, phonon_shift, groups * parts
    )
    lines = lax.all_to_all(lines, ("kgrp", "energy"), split_axis=0, concat_axis=0, tiled=True)
    entries = float(flat.size * groups * parts)
    return mix(lines, fresh, flat, aged, entries).reshape(current.shape)


def solution(mesh):
    return jax.shard_map(
        per_device,
        mesh=mesh,
        in_specs=(
            P(None, None, None, "kgrp", "energy"),
            P(None, None, None, ("kgrp", "energy"), None),
            P(None, None, None, None, ("kgrp", "energy"), None),
            P(None, None, None, None, ("kgrp", "energy"), None),
            P(),
            P("kgrp", None),
            P("kgrp"),
            P(),
            P(),
            P(),
            P(),
            P(),
        ),
        out_specs=P(None, None, None, ("kgrp", "energy"), None),
        check_vma=False,
    )
```

```python
import jax
import jax.numpy as jnp
from jax import lax
from jax.experimental import pallas as pl
from jax.experimental.pallas import tpu as pltpu
from jax.sharding import PartitionSpec as P

HIST = 5
LANES = 128

mixing_share = 0.5
ridge_share = 0.1

VMEM = pl.BlockSpec(memory_space=pltpu.VMEM)
SMEM = pl.BlockSpec(memory_space=pltpu.SMEM)
PARAMS = pltpu.CompilerParams(vmem_limit_bytes=16 * 1024 * 1024)

PAIRS = [(i, j) for i in range(1, HIST + 1) for j in range(i, HIST + 1)]
SPOTS = {pair: v for v, pair in enumerate(PAIRS)}
for _j in range(HIST + 1):
    SPOTS[(0, _j)] = 16 + _j


def split(value):
    high = value.astype(jnp.bfloat16)
    return high, (value - high.astype(jnp.float32)).astype(jnp.bfloat16)


def product(left, right):
    dot = lambda a, b: jnp.dot(a, b, preferred_element_type=jnp.float32)
    return dot(left[0], right[0]) + (dot(left[0], right[1]) + dot(left[1], right[0]))


def prepare_kernel(total_k, *refs):
    *blocks, neighbour_hbm, weight_hbm, stencil_hi, stencil_lo, part, late, neighbour, weight, done = refs
    fetches = [
        pltpu.make_async_copy(neighbour_hbm, neighbour, done.at[0]),
        pltpu.make_async_copy(weight_hbm, weight, done.at[1]),
    ]
    for fetch in fetches:
        fetch.start()
    late[...] = blocks[-1][...]
    _, group_len, slice_len = blocks[0].shape
    group_id = lax.axis_index("kgrp")
    parts = lax.axis_size("energy")
    rows = group_len // parts
    for fetch in fetches:
        fetch.wait()
    slots, _ = neighbour.shape
    padded = jnp.concatenate([neighbour[...], jnp.zeros((8 - slots, group_len), jnp.int32)], axis=0)
    targets = jnp.transpose(padded)
    place = lax.axis_index("energy")
    bit = 1
    while bit < parts:
        span = bit * rows
        pieces = [targets[at : at + span] for at in range(0, group_len, span)]
        flipped = [pieces[b ^ 1] for b in range(len(pieces))]
        targets = jnp.where(place & bit != 0, jnp.concatenate(flipped, axis=0), targets)
        bit *= 2
    local = targets - group_id * group_len + group_len
    local = jnp.where(local < 0, local + total_k, jnp.where(local >= total_k, local - total_k, local))
    spot = lax.broadcasted_iota(jnp.int32, (group_len, 3 * group_len), 1)
    stencil = jnp.zeros(spot.shape, jnp.float32)
    for n in range(slots):
        stencil = stencil + jnp.where(spot == local[:, n : n + 1], weight[n], 0.0)
    before, after = stencil[:, :group_len], stencil[:, 2 * group_len :]
    swapped = paired(total_k // group_len) & (group_id % 2 == 1)
    near, far = jnp.where(swapped, before, after), jnp.where(swapped, after, before)
    stencil_hi[...], stencil_lo[...] = split(jnp.concatenate([near, far], axis=1))
    centre = split(stencil[:, group_len : 2 * group_len])
    first = 0
    for own in blocks:
        for c in range(0, own.shape[0], 2):
            result = product(centre, split(jnp.concatenate([own[c], own[c + 1]], axis=1)))
            part[first + c] = result[:, :slice_len]
            part[first + c + 1] = result[:, slice_len:]
        first += own.shape[0]


def prepare(blocks, neighbour, weight, total_k):
    comps = sum(block.shape[0] for block in blocks)
    _, group_len, slice_len = blocks[0].shape
    sides = jax.ShapeDtypeStruct((group_len, 2 * group_len), jnp.bfloat16)
    size = comps * group_len * slice_len
    return pl.pallas_call(
        lambda *refs: prepare_kernel(total_k, *refs),
        out_shape=(
            sides,
            sides,
            jax.ShapeDtypeStruct((comps, group_len, slice_len), jnp.float32),
            jax.ShapeDtypeStruct(blocks[-1].shape, jnp.float32),
        ),
        in_specs=[VMEM] * len(blocks) + [pl.BlockSpec(memory_space=pltpu.HBM)] * 2,
        out_specs=(VMEM,) * 4,
        scratch_shapes=[
            pltpu.VMEM(neighbour.shape[::-1], jnp.int32),
            pltpu.SMEM(weight.shape, jnp.float32),
            pltpu.SemaphoreType.DMA((2,)),
        ],
        compiler_params=PARAMS,
        cost_estimate=pl.CostEstimate(
            flops=6 * size * group_len, bytes_accessed=8 * size, transcendentals=0
        ),
        name="prepare",
    )(*blocks, jnp.transpose(neighbour), weight)


def smeared_pairs(first, sides, stencil_hi, stencil_lo, part):
    blocks = [block for block in sides if block is not None]
    comps, group_len, slice_len = blocks[0].shape
    start = 0 if sides[0] is not None else group_len
    at = slice(start, start + len(blocks) * group_len)
    stencil = (stencil_hi[:, at], stencil_lo[:, at])
    for c in range(0, comps, 2):
        stacked = [jnp.concatenate([block[c], block[c + 1]], axis=1) for block in blocks]
        result = product(stencil, split(jnp.concatenate(stacked, axis=0)))
        for p in range(2):
            yield c + p, part[first + c + p] + result[:, p * slice_len : (p + 1) * slice_len]


def with_sides(kernel, sides):
    def body(*refs):
        refs = list(refs)
        kernel([None if side is None else refs.pop(0) for side in sides], *refs)

    return body


def smear_cost(blocks):
    size = sum(block.size for block in blocks)
    return pl.CostEstimate(
        flops=6 * size * blocks[0].shape[1], bytes_accessed=12 * size, transcendentals=0
    )


def add_sides(first, sides, stencil_hi, stencil_lo, part, after):
    def kernel(sides, stencil_hi, stencil_lo, part, *refs):
        for c, smeared in smeared_pairs(first, sides, stencil_hi, stencil_lo, part):
            refs[-1][c] = smeared

    blocks = [block for block in sides if block is not None]
    return pl.pallas_call(
        with_sides(kernel, sides),
        out_shape=jax.ShapeDtypeStruct(blocks[0].shape, jnp.float32),
        in_specs=[VMEM] * (len(blocks) + 3) + [pl.BlockSpec(memory_space=pl.ANY)] * len(after),
        out_specs=VMEM,
        compiler_params=PARAMS,
        cost_estimate=smear_cost(blocks),
        name="add_sides",
    )(*blocks, stencil_hi, stencil_lo, part, *after)


def finish_kernel(sides, stencil_hi, stencil_lo, part, *refs):
    *ready, kept, given = refs
    chips, height, _ = kept.shape
    comps = part.shape[0]
    rows = height // comps

    def place(c, smeared):
        for m in range(2 * chips):
            out = given if m % 2 else kept
            out[m // 2, c * rows : (c + 1) * rows, :] = smeared[m * rows : (m + 1) * rows]

    first = 0
    for c, smeared in smeared_pairs(0, sides, stencil_hi, stencil_lo, part):
        place(c, smeared)
        first = c + 1
    for block in ready:
        for c in range(block.shape[0]):
            place(first + c, block[c])


def finish(sides, stencil_hi, stencil_lo, part, ready, parts):
    blocks = [block for block in sides if block is not None]
    comps, group_len, slice_len = part.shape
    shape = (parts // 2, comps * group_len // parts, slice_len)
    return pl.pallas_call(
        with_sides(finish_kernel, sides),
        out_shape=[jax.ShapeDtypeStruct(shape, jnp.float32)] * 2,
        in_specs=[VMEM] * (len(blocks) + len(ready) + 3),
        out_specs=[VMEM] * 2,
        compiler_params=PARAMS,
        cost_estimate=smear_cost(blocks),
        name="finish",
    )(*blocks, stencil_hi, stencil_lo, part, *ready)


def chip_order(parts):
    chips = parts // 2
    return [*range(chips // 2, chips), *range(1, chips // 2)] if chips > 1 else []


def join_kernel(own, swapped, *out):
    for chip, block in zip(chip_order(2 * own.shape[0]), out):
        block[0], block[1] = own[chip], swapped[chip]


def join(own, swapped):
    chips, height, slice_len = own.shape
    shape = jax.ShapeDtypeStruct((2, height, slice_len), jnp.float32)
    return pl.pallas_call(
        join_kernel,
        out_shape=[shape] * (chips - 1),
        in_specs=[VMEM] * 2,
        out_specs=[VMEM] * (chips - 1),
        compiler_params=PARAMS,
        name="join",
    )(own, swapped)


def paired(groups):
    return groups == 4


def hold_kernel(block, _, out):
    out[...] = block[...]


def hold(block, until):
    return pl.pallas_call(
        hold_kernel,
        out_shape=jax.ShapeDtypeStruct(block.shape, jnp.float32),
        in_specs=[VMEM, pl.BlockSpec(memory_space=pl.ANY)],
        out_specs=VMEM,
        compiler_params=PARAMS,
        name="hold",
    )(block, until)


def smear(own, neighbour, weight, groups, parts):
    total_k = groups * own.shape[1]
    if not paired(groups):
        forward = [(i, (i + 1) % groups) for i in range(groups)]
        backward = [(target, source) for source, target in forward]
        near, far = lax.ppermute(own, "kgrp", backward), lax.ppermute(own, "kgrp", forward)
        return finish((near, far), *prepare([own], neighbour, weight, total_k)[:3], [], parts)
    across = lambda block, flip: lax.ppermute(block, "kgrp", [(i, i ^ flip) for i in range(groups)])
    half = own.shape[0] // 2
    head, tail = own[:half], own[half:]
    near_head, far_tail = across(head, 1), across(tail, 3)
    hi, lo, part, late = prepare([head, tail], neighbour, weight, total_k)
    near_tail, far_head = across(late, 1), across(hold(near_head, late), 2)
    tail_part = add_sides(half, (near_tail, far_tail), hi, lo, part, [])
    return finish((near_head, far_head), hi, lo, part, [tail_part], parts)


def spread(values, shape):
    lane = lax.broadcasted_iota(jnp.int32, shape, 1)
    row = jnp.zeros(shape, jnp.float32)
    for spot, value in values:
        row = jnp.where(lane == spot, value, row)
    return row


def total(acc):
    return jnp.sum(jnp.sum(acc, axis=0, keepdims=True), axis=1, keepdims=True)


def history_kernel(
    total_rows, past_inputs, past_residuals, slots, classes, acoustic, optical, number, shift,
    aged, residuals, line, gains, shifts,
):
    first = lax.axis_index("energy") * total_rows
    row = lax.broadcasted_iota(jnp.int32, (8, LANES), 0) % total_rows
    coupling = jnp.zeros((8, LANES), jnp.float32)
    for i in range(total_rows):
        coupling = jnp.where(row == i, acoustic[classes[first + i]], coupling)
    gains[0] = coupling
    for m in range(2):
        gains[2 * m + 1] = jnp.full((8, LANES), optical[m] * (number[m] + 1.0))
        gains[2 * m + 2] = jnp.full((8, LANES), optical[m] * number[m])
        shifts[m] = jnp.full((8, LANES), shift[m], jnp.int32)
    _, rows, width = past_inputs.shape
    acc = [jnp.zeros((8, LANES), jnp.float32) for _ in PAIRS]
    for top in range(0, rows, 8):
        def column(t, acc, top=top):
            at = pl.ds(pl.multiple_of(t * LANES, LANES), LANES)
            old = []
            for j in range(HIST):
                res = past_residuals[slots[j], top : top + 8, at]
                aged[j, top : top + 8, at] = (
                    past_inputs[slots[j], top : top + 8, at] + mixing_share * res
                )
                residuals[j, top : top + 8, at] = res
                old.append(res)
            return [a + old[i - 1] * old[j - 1] for a, (i, j) in zip(acc, PAIRS)]
        acc = lax.fori_loop(0, width // LANES, column, acc, unroll=4)
    line[...] = spread([(v, total(a)) for v, a in enumerate(acc)], line.shape)


def history(past_inputs, past_residuals, scalars, rows):
    size = past_inputs.size
    return pl.pallas_call(
        lambda *refs: history_kernel(rows, *refs),
        out_shape=(
            jax.ShapeDtypeStruct(past_inputs.shape, jnp.float32),
            jax.ShapeDtypeStruct(past_inputs.shape, jnp.float32),
            jax.ShapeDtypeStruct((1, LANES), jnp.float32),
            jax.ShapeDtypeStruct((5, 8, LANES), jnp.float32),
            jax.ShapeDtypeStruct((2, 8, LANES), jnp.int32),
        ),
        in_specs=[VMEM, VMEM] + [SMEM] * 6,
        out_specs=(VMEM,) * 5,
        compiler_params=PARAMS,
        cost_estimate=pl.CostEstimate(flops=8 * size, bytes_accessed=12 * size, transcendentals=0),
        name="history",
    )(past_inputs, past_residuals, *scalars)


def residual_kernel(count, own, swapped, *refs):
    received = refs[:count]
    current, residuals, old_line, gains, shifts, fresh, lines, smeared = refs[count:]
    parts, height, slice_len = smeared.shape
    place = lax.axis_index("energy")
    smeared[place], smeared[place ^ 1] = own[0], swapped[0]
    for chip, block in zip(chip_order(parts), received):
        smeared[place ^ (2 * chip)], smeared[place ^ (2 * chip + 1)] = block[0], block[1]
    lane = lax.broadcasted_iota(jnp.int32, (8, slice_len), 1)
    coupling = gains[0]
    modes = []
    for m in range(2):
        wide = shifts[m]
        keeps = lane < slice_len - wide, lane >= wide
        modes.append((jnp.max(wide), *keeps, gains[2 * m + 1], gains[2 * m + 2]))
    zero = jnp.zeros((8, slice_len), jnp.float32)
    acc = [zero] * (HIST + 1)
    for top in range(0, height, 8):
        at = slice(top, top + 8)
        source = [smeared[e, at, :] for e in range(parts)]
        sigma = [coupling * x for x in source]
        lesser = top < height // 2
        for s, keep_up, keep_down, emitted, absorbed in modes:
            up = [pltpu.roll(x, slice_len - s, 1) for x in source] + [zero]
            down = [zero] + [pltpu.roll(x, s, 1) for x in source]
            gain_up, gain_down = (emitted, absorbed) if lesser else (absorbed, emitted)
            for e in range(parts):
                above = jnp.where(keep_up, up[e], up[e + 1])
                below = jnp.where(keep_down, down[e + 1], down[e])
                sigma[e] = sigma[e] + (gain_up * above + gain_down * below)
        for e in range(parts):
            where = (at, slice(e * slice_len, (e + 1) * slice_len))
            new = sigma[e] - current[where]
            fresh[where] = new
            acc[0] = acc[0] + new * new
            for j in range(HIST):
                acc[j + 1] = acc[j + 1] + new * residuals[(j,) + where]
    mine = jnp.concatenate([jnp.sum(a, axis=0, keepdims=True) for a in acc] + [zero[: 8 - HIST - 1]], axis=0)
    mine = jnp.sum(mine, axis=1, keepdims=True)
    spot = lax.broadcasted_iota(jnp.int32, (8, LANES), 0) + SPOTS[(0, 0)]
    mine = jnp.where(lax.broadcasted_iota(jnp.int32, (8, LANES), 1) == spot, mine, 0.0)
    mine = old_line[...] + jnp.sum(mine, axis=0, keepdims=True)
    lines[...] = jnp.broadcast_to(mine[None], lines.shape)


def residual(kept, swapped, smeared, current, residuals, old_line, gains, shifts, copies):
    return pl.pallas_call(
        lambda *refs: residual_kernel(len(smeared), *refs),
        out_shape=(
            jax.ShapeDtypeStruct(current.shape, jnp.float32),
            jax.ShapeDtypeStruct((copies, 1, LANES), jnp.float32),
        ),
        in_specs=[VMEM] * (len(smeared) + 7),
        out_specs=(VMEM, VMEM),
        scratch_shapes=[pltpu.VMEM((2 * kept.shape[0],) + kept.shape[1:], jnp.float32)],
        compiler_params=PARAMS,
        name="residual",
    )(kept, swapped, *smeared, current, residuals, old_line, gains, shifts)


def solve(products):
    prod = lambda i, j: products[(min(i, j), max(i, j))]
    n = HIST
    system = [
        [prod(i, j) - prod(i, j + 1) - prod(i + 1, j) + prod(i + 1, j + 1) for j in range(n)]
        for i in range(n)
    ]
    target = [prod(i, 0) - prod(i + 1, 0) for i in range(n)]
    trace = system[0][0]
    for i in range(1, n):
        trace = trace + system[i][i]
    ridge = ridge_share * trace / n + 1e-06
    for i in range(n):
        system[i][i] = system[i][i] + ridge
    inverse = [None] * n
    for k in range(n):
        inverse[k] = 1.0 / system[k][k]
        for i in range(k + 1, n):
            factor = system[k][i] * inverse[k]
            for j in range(i, n):
                system[i][j] = system[i][j] - factor * system[k][j]
            target[i] = target[i] - factor * target[k]
    gamma = [None] * n
    for k in range(n - 1, -1, -1):
        value = target[k]
        for j in range(k + 1, n):
            value = value - system[k][j] * gamma[j]
        gamma[k] = value * inverse[k]
    weights = [1.0 - gamma[0]]
    for j in range(1, n):
        weights.append(gamma[j - 1] - gamma[j])
    weights.append(gamma[n - 1])
    return weights


def mix_kernel(entries, lines, fresh, current, aged, out, wide, mixed_rows, done):
    summed = jnp.sum(lines[...], axis=0) / entries
    row = lax.broadcasted_iota(jnp.int32, (8, LANES), 0)
    lane = lax.broadcasted_iota(jnp.int32, (8, LANES), 1)
    for part in range(wide.shape[0]):
        own = jnp.where(lane == row + 8 * part, summed, 0.0)
        wide[part] = jnp.broadcast_to(jnp.sum(own, axis=1, keepdims=True), (8, LANES))
    products = {
        pair: jnp.broadcast_to(wide[spot // 8, spot % 8 : spot % 8 + 1, :], (8, LANES))
        for pair, spot in SPOTS.items()
    }
    weights = solve(products)
    rows, width = fresh.shape
    span = rows // done.shape[0]
    writes = []
    for part in range(done.shape[0]):
        for top in range(part * span, (part + 1) * span, 8):
            for left in range(0, width, LANES):
                at = (slice(top, top + 8), slice(left, left + LANES))
                mixed = weights[0] * (current[at] + mixing_share * fresh[at])
                for j in range(HIST):
                    mixed = mixed + weights[j + 1] * aged[(j,) + at]
                mixed_rows[at] = mixed
        at = pl.ds(part * span, span)
        writes.append(pltpu.make_async_copy(mixed_rows.at[at], out.at[at], done.at[part]))
        writes[-1].start()
    for write in writes:
        write.wait()


def mix(lines, fresh, current, aged, entries):
    return pl.pallas_call(
        lambda *refs: mix_kernel(entries, *refs),
        out_shape=jax.ShapeDtypeStruct(fresh.shape, jnp.float32),
        in_specs=[VMEM] * 4,
        out_specs=pl.BlockSpec(memory_space=pltpu.HBM),
        scratch_shapes=[
            pltpu.VMEM((3, 8, LANES), jnp.float32),
            pltpu.VMEM(fresh.shape, jnp.float32),
            pltpu.SemaphoreType.DMA((2,)),
        ],
        compiler_params=PARAMS,
        name="mix",
    )(lines, fresh, current, aged)


def per_device(
    greens,
    current,
    past_inputs,
    past_residuals,
    slot_order,
    neighbour,
    momentum_class,
    stencil_weight,
    acoustic_coupling,
    optical_coupling,
    occupation,
    phonon_shift,
):
    group_len, slice_len = greens.shape[3:]
    rows, width = current.shape[3:]
    groups = lax.axis_size("kgrp")
    parts = lax.axis_size("energy")
    own = greens.reshape(-1, group_len, slice_len)
    height = own.shape[0] * rows

    flat = current.reshape(height, width)
    old_in = past_inputs.reshape(HIST, height, width)
    old_res = past_residuals.reshape(HIST, height, width)
    scalars = (
        slot_order, momentum_class, acoustic_coupling, optical_coupling, occupation, phonon_shift
    )
    aged, residuals, old_line, gains, shifts = history(old_in, old_res, scalars, rows)
    kept, given = smear(own, neighbour, stencil_weight, groups, parts)
    meet = lambda block, m: lax.ppermute(block, "energy", [(e, e ^ m) for e in range(parts)])
    swapped = meet(given, 1)
    smeared = [meet(block, 2 * chip) for chip, block in zip(chip_order(parts), join(kept, swapped))]
    fresh, lines = residual(
        kept, swapped, smeared, flat, residuals, old_line, gains, shifts, groups * parts
    )
    lines = lax.all_to_all(lines, ("kgrp", "energy"), split_axis=0, concat_axis=0, tiled=True)
    entries = float(flat.size * groups * parts)
    return mix(lines, fresh, flat, aged, entries).reshape(current.shape)


def solution(mesh):
    return jax.shard_map(
        per_device,
        mesh=mesh,
        in_specs=(
            P(None, None, None, "kgrp", "energy"),
            P(None, None, None, ("kgrp", "energy"), None),
            P(None, None, None, None, ("kgrp", "energy"), None),
            P(None, None, None, None, ("kgrp", "energy"), None),
            P(),
            P("kgrp", None),
            P("kgrp"),
            P(),
            P(),
            P(),
            P(),
            P(),
        ),
        out_specs=P(None, None, None, ("kgrp", "energy"), None),
        check_vma=False,
    )
```

```python
import jax
import jax.numpy as jnp
from jax import lax
from jax.experimental import pallas as pl
from jax.experimental.pallas import tpu as pltpu
from jax.sharding import PartitionSpec as P

HIST = 5
LANES = 128

mixing_share = 0.5
ridge_share = 0.1

VMEM = pl.BlockSpec(memory_space=pltpu.VMEM)
SMEM = pl.BlockSpec(memory_space=pltpu.SMEM)
PARAMS = pltpu.CompilerParams(vmem_limit_bytes=16 * 1024 * 1024)

PAIRS = [(i, j) for i in range(1, HIST + 1) for j in range(i, HIST + 1)]
SPOTS = {pair: v for v, pair in enumerate(PAIRS)}
for _j in range(HIST + 1):
    SPOTS[(0, _j)] = 16 + _j


def split(value):
    high = value.astype(jnp.bfloat16)
    return high, (value - high.astype(jnp.float32)).astype(jnp.bfloat16)


def product(left, right):
    dot = lambda a, b: jnp.dot(a, b, preferred_element_type=jnp.float32)
    return dot(left[0], right[0]) + (dot(left[0], right[1]) + dot(left[1], right[0]))


def prepare_kernel(total_k, *refs):
    *blocks, neighbour_hbm, weight_hbm, stencil_hi, stencil_lo, part, late, neighbour, weight, done = refs
    fetches = [
        pltpu.make_async_copy(neighbour_hbm, neighbour, done.at[0]),
        pltpu.make_async_copy(weight_hbm, weight, done.at[1]),
    ]
    for fetch in fetches:
        fetch.start()
    late[...] = blocks[-1][...]
    _, group_len, slice_len = blocks[0].shape
    group_id = lax.axis_index("kgrp")
    parts = lax.axis_size("energy")
    rows = group_len // parts
    for fetch in fetches:
        fetch.wait()
    slots, _ = neighbour.shape
    padded = jnp.concatenate([neighbour[...], jnp.zeros((8 - slots, group_len), jnp.int32)], axis=0)
    targets = jnp.transpose(padded)
    place = lax.axis_index("energy")
    bit = 1
    while bit < parts:
        span = bit * rows
        pieces = [targets[at : at + span] for at in range(0, group_len, span)]
        flipped = [pieces[b ^ 1] for b in range(len(pieces))]
        targets = jnp.where(place & bit != 0, jnp.concatenate(flipped, axis=0), targets)
        bit *= 2
    local = targets - group_id * group_len + group_len
    local = jnp.where(local < 0, local + total_k, jnp.where(local >= total_k, local - total_k, local))
    spot = lax.broadcasted_iota(jnp.int32, (group_len, 3 * group_len), 1)
    stencil = jnp.zeros(spot.shape, jnp.float32)
    for n in range(slots):
        stencil = stencil + jnp.where(spot == local[:, n : n + 1], weight[n], 0.0)
    before, after = stencil[:, :group_len], stencil[:, 2 * group_len :]
    swapped = paired(total_k // group_len) & (group_id % 2 == 1)
    near, far = jnp.where(swapped, before, after), jnp.where(swapped, after, before)
    stencil_hi[...], stencil_lo[...] = split(jnp.concatenate([near, far], axis=1))
    centre = split(stencil[:, group_len : 2 * group_len])
    first = 0
    for own in blocks:
        for c in range(0, own.shape[0], 2):
            result = product(centre, split(jnp.concatenate([own[c], own[c + 1]], axis=1)))
            part[first + c] = result[:, :slice_len]
            part[first + c + 1] = result[:, slice_len:]
        first += own.shape[0]


def prepare(blocks, neighbour, weight, total_k):
    comps = sum(block.shape[0] for block in blocks)
    _, group_len, slice_len = blocks[0].shape
    sides = jax.ShapeDtypeStruct((group_len, 2 * group_len), jnp.bfloat16)
    size = comps * group_len * slice_len
    return pl.pallas_call(
        lambda *refs: prepare_kernel(total_k, *refs),
        out_shape=(
            sides,
            sides,
            jax.ShapeDtypeStruct((comps, group_len, slice_len), jnp.float32),
            jax.ShapeDtypeStruct(blocks[-1].shape, jnp.float32),
        ),
        in_specs=[VMEM] * len(blocks) + [pl.BlockSpec(memory_space=pltpu.HBM)] * 2,
        out_specs=(VMEM,) * 4,
        scratch_shapes=[
            pltpu.VMEM(neighbour.shape[::-1], jnp.int32),
            pltpu.SMEM(weight.shape, jnp.float32),
            pltpu.SemaphoreType.DMA((2,)),
        ],
        compiler_params=PARAMS,
        cost_estimate=pl.CostEstimate(
            flops=6 * size * group_len, bytes_accessed=8 * size, transcendentals=0
        ),
        name="prepare",
    )(*blocks, jnp.transpose(neighbour), weight)


def smeared_pairs(first, sides, stencil_hi, stencil_lo, part):
    blocks = [block for block in sides if block is not None]
    comps, group_len, slice_len = blocks[0].shape
    start = 0 if sides[0] is not None else group_len
    at = slice(start, start + len(blocks) * group_len)
    stencil = (stencil_hi[:, at], stencil_lo[:, at])
    for c in range(0, comps, 2):
        stacked = [jnp.concatenate([block[c], block[c + 1]], axis=1) for block in blocks]
        result = product(stencil, split(jnp.concatenate(stacked, axis=0)))
        for p in range(2):
            yield c + p, part[first + c + p] + result[:, p * slice_len : (p + 1) * slice_len]


def with_sides(kernel, sides):
    def body(*refs):
        refs = list(refs)
        kernel([None if side is None else refs.pop(0) for side in sides], *refs)

    return body


def smear_cost(blocks):
    size = sum(block.size for block in blocks)
    return pl.CostEstimate(
        flops=6 * size * blocks[0].shape[1], bytes_accessed=12 * size, transcendentals=0
    )


def add_sides(first, sides, stencil_hi, stencil_lo, part, after):
    def kernel(sides, stencil_hi, stencil_lo, part, *refs):
        for c, smeared in smeared_pairs(first, sides, stencil_hi, stencil_lo, part):
            refs[-1][c] = smeared

    blocks = [block for block in sides if block is not None]
    return pl.pallas_call(
        with_sides(kernel, sides),
        out_shape=jax.ShapeDtypeStruct(blocks[0].shape, jnp.float32),
        in_specs=[VMEM] * (len(blocks) + 3) + [pl.BlockSpec(memory_space=pl.ANY)] * len(after),
        out_specs=VMEM,
        compiler_params=PARAMS,
        cost_estimate=smear_cost(blocks),
        name="add_sides",
    )(*blocks, stencil_hi, stencil_lo, part, *after)


def finish_kernel(sides, stencil_hi, stencil_lo, part, *refs):
    *ready, kept, given = refs
    chips, height, _ = kept.shape
    comps = part.shape[0]
    rows = height // comps

    def place(c, smeared):
        for m in range(2 * chips):
            out = given if m % 2 else kept
            out[m // 2, c * rows : (c + 1) * rows, :] = smeared[m * rows : (m + 1) * rows]

    first = 0
    for c, smeared in smeared_pairs(0, sides, stencil_hi, stencil_lo, part):
        place(c, smeared)
        first = c + 1
    for block in ready:
        for c in range(block.shape[0]):
            place(first + c, block[c])


def finish(sides, stencil_hi, stencil_lo, part, ready, parts):
    blocks = [block for block in sides if block is not None]
    comps, group_len, slice_len = part.shape
    shape = (parts // 2, comps * group_len // parts, slice_len)
    return pl.pallas_call(
        with_sides(finish_kernel, sides),
        out_shape=[jax.ShapeDtypeStruct(shape, jnp.float32)] * 2,
        in_specs=[VMEM] * (len(blocks) + len(ready) + 3),
        out_specs=[VMEM] * 2,
        compiler_params=PARAMS,
        cost_estimate=smear_cost(blocks),
        name="finish",
    )(*blocks, stencil_hi, stencil_lo, part, *ready)


def chip_order(parts):
    chips = parts // 2
    return [*range(chips // 2, chips), *range(1, chips // 2)] if chips > 1 else []


def join_kernel(own, swapped, *out):
    for chip, block in zip(chip_order(2 * own.shape[0]), out):
        block[0], block[1] = own[chip], swapped[chip]


def join(own, swapped):
    chips, height, slice_len = own.shape
    shape = jax.ShapeDtypeStruct((2, height, slice_len), jnp.float32)
    return pl.pallas_call(
        join_kernel,
        out_shape=[shape] * (chips - 1),
        in_specs=[VMEM] * 2,
        out_specs=[VMEM] * (chips - 1),
        compiler_params=PARAMS,
        name="join",
    )(own, swapped)


def paired(groups):
    return groups == 4


def hold_kernel(block, _, out):
    out[...] = block[...]


def hold(block, until):
    return pl.pallas_call(
        hold_kernel,
        out_shape=jax.ShapeDtypeStruct(block.shape, jnp.float32),
        in_specs=[VMEM, pl.BlockSpec(memory_space=pl.ANY)],
        out_specs=VMEM,
        compiler_params=PARAMS,
        name="hold",
    )(block, until)


def smear(own, neighbour, weight, groups, parts):
    total_k = groups * own.shape[1]
    if not paired(groups):
        forward = [(i, (i + 1) % groups) for i in range(groups)]
        backward = [(target, source) for source, target in forward]
        near, far = lax.ppermute(own, "kgrp", backward), lax.ppermute(own, "kgrp", forward)
        return finish((near, far), *prepare([own], neighbour, weight, total_k)[:3], [], parts)
    across = lambda block, flip: lax.ppermute(block, "kgrp", [(i, i ^ flip) for i in range(groups)])
    half = own.shape[0] // 2
    head, tail = own[:half], own[half:]
    near_head, far_tail = across(head, 1), across(tail, 3)
    hi, lo, part, late = prepare([head, tail], neighbour, weight, total_k)
    near_tail, far_head = across(late, 1), across(hold(near_head, late), 2)
    tail_part = add_sides(half, (near_tail, far_tail), hi, lo, part, [])
    return finish((near_head, far_head), hi, lo, part, [tail_part], parts)


def spread(values, shape):
    lane = lax.broadcasted_iota(jnp.int32, shape, 1)
    row = jnp.zeros(shape, jnp.float32)
    for spot, value in values:
        row = jnp.where(lane == spot, value, row)
    return row


def total(acc):
    return jnp.sum(jnp.sum(acc, axis=0, keepdims=True), axis=1, keepdims=True)


def history_kernel(
    total_rows, past_inputs, past_residuals, slots, classes, acoustic, optical, number, shift,
    aged, residuals, line, gains, shifts,
):
    first = lax.axis_index("energy") * total_rows
    row = lax.broadcasted_iota(jnp.int32, (8, LANES), 0) % total_rows
    coupling = jnp.zeros((8, LANES), jnp.float32)
    for i in range(total_rows):
        coupling = jnp.where(row == i, acoustic[classes[first + i]], coupling)
    gains[0] = coupling
    for m in range(2):
        gains[2 * m + 1] = jnp.full((8, LANES), optical[m] * (number[m] + 1.0))
        gains[2 * m + 2] = jnp.full((8, LANES), optical[m] * number[m])
        shifts[m] = jnp.full((8, LANES), shift[m], jnp.int32)
    _, rows, width = past_inputs.shape
    acc = [jnp.zeros((8, LANES), jnp.float32) for _ in PAIRS]
    for top in range(0, rows, 8):
        def column(t, acc, top=top):
            at = pl.ds(pl.multiple_of(t * LANES, LANES), LANES)
            old = []
            for j in range(HIST):
                res = past_residuals[slots[j], top : top + 8, at]
                aged[j, top : top + 8, at] = (
                    past_inputs[slots[j], top : top + 8, at] + mixing_share * res
                )
                residuals[j, top : top + 8, at] = res
                old.append(res)
            return [a + old[i - 1] * old[j - 1] for a, (i, j) in zip(acc, PAIRS)]
        acc = lax.fori_loop(0, width // LANES, column, acc, unroll=4)
    line[...] = spread([(v, total(a)) for v, a in enumerate(acc)], line.shape)


def history(past_inputs, past_residuals, scalars, rows):
    size = past_inputs.size
    return pl.pallas_call(
        lambda *refs: history_kernel(rows, *refs),
        out_shape=(
            jax.ShapeDtypeStruct(past_inputs.shape, jnp.float32),
            jax.ShapeDtypeStruct(past_inputs.shape, jnp.float32),
            jax.ShapeDtypeStruct((1, LANES), jnp.float32),
            jax.ShapeDtypeStruct((5, 8, LANES), jnp.float32),
            jax.ShapeDtypeStruct((2, 8, LANES), jnp.int32),
        ),
        in_specs=[VMEM, VMEM] + [SMEM] * 6,
        out_specs=(VMEM,) * 5,
        compiler_params=PARAMS,
        cost_estimate=pl.CostEstimate(flops=8 * size, bytes_accessed=12 * size, transcendentals=0),
        name="history",
    )(past_inputs, past_residuals, *scalars)


def residual_kernel(count, own, swapped, *refs):
    received = refs[:count]
    current, residuals, old_line, gains, shifts, fresh, line, smeared = refs[count:]
    parts, height, slice_len = smeared.shape
    place = lax.axis_index("energy")
    smeared[place], smeared[place ^ 1] = own[0], swapped[0]
    for chip, block in zip(chip_order(parts), received):
        smeared[place ^ (2 * chip)], smeared[place ^ (2 * chip + 1)] = block[0], block[1]
    lane = lax.broadcasted_iota(jnp.int32, (8, slice_len), 1)
    coupling = gains[0]
    modes = []
    for m in range(2):
        wide = shifts[m]
        keeps = lane < slice_len - wide, lane >= wide
        modes.append((jnp.max(wide), *keeps, gains[2 * m + 1], gains[2 * m + 2]))
    zero = jnp.zeros((8, slice_len), jnp.float32)
    acc = [zero] * (HIST + 1)
    for top in range(0, height, 8):
        at = slice(top, top + 8)
        source = [smeared[e, at, :] for e in range(parts)]
        sigma = [coupling * x for x in source]
        lesser = top < height // 2
        for s, keep_up, keep_down, emitted, absorbed in modes:
            up = [pltpu.roll(x, slice_len - s, 1) for x in source] + [zero]
            down = [zero] + [pltpu.roll(x, s, 1) for x in source]
            gain_up, gain_down = (emitted, absorbed) if lesser else (absorbed, emitted)
            for e in range(parts):
                above = jnp.where(keep_up, up[e], up[e + 1])
                below = jnp.where(keep_down, down[e + 1], down[e])
                sigma[e] = sigma[e] + (gain_up * above + gain_down * below)
        for e in range(parts):
            where = (at, slice(e * slice_len, (e + 1) * slice_len))
            new = sigma[e] - current[where]
            fresh[where] = new
            acc[0] = acc[0] + new * new
            for j in range(HIST):
                acc[j + 1] = acc[j + 1] + new * residuals[(j,) + where]
    mine = jnp.concatenate([jnp.sum(a, axis=0, keepdims=True) for a in acc] + [zero[: 8 - HIST - 1]], axis=0)
    mine = jnp.sum(mine, axis=1, keepdims=True)
    spot = lax.broadcasted_iota(jnp.int32, (8, LANES), 0) + SPOTS[(0, 0)]
    mine = jnp.where(lax.broadcasted_iota(jnp.int32, (8, LANES), 1) == spot, mine, 0.0)
    mine = old_line[...] + jnp.sum(mine, axis=0, keepdims=True)
    line[...] = mine


def residual(kept, swapped, smeared, current, residuals, old_line, gains, shifts):
    return pl.pallas_call(
        lambda *refs: residual_kernel(len(smeared), *refs),
        out_shape=(
            jax.ShapeDtypeStruct(current.shape, jnp.float32),
            jax.ShapeDtypeStruct((1, LANES), jnp.float32),
        ),
        in_specs=[VMEM] * (len(smeared) + 7),
        out_specs=(VMEM, VMEM),
        scratch_shapes=[pltpu.VMEM((2 * kept.shape[0],) + kept.shape[1:], jnp.float32)],
        compiler_params=PARAMS,
        name="residual",
    )(kept, swapped, *smeared, current, residuals, old_line, gains, shifts)


def solve(products):
    prod = lambda i, j: products[(min(i, j), max(i, j))]
    n = HIST
    system = [
        [prod(i, j) - prod(i, j + 1) - prod(i + 1, j) + prod(i + 1, j + 1) for j in range(n)]
        for i in range(n)
    ]
    target = [prod(i, 0) - prod(i + 1, 0) for i in range(n)]
    trace = system[0][0]
    for i in range(1, n):
        trace = trace + system[i][i]
    ridge = ridge_share * trace / n + 1e-06
    for i in range(n):
        system[i][i] = system[i][i] + ridge
    inverse = [None] * n
    for k in range(n):
        inverse[k] = 1.0 / system[k][k]
        for i in range(k + 1, n):
            factor = system[k][i] * inverse[k]
            for j in range(i, n):
                system[i][j] = system[i][j] - factor * system[k][j]
            target[i] = target[i] - factor * target[k]
    gamma = [None] * n
    for k in range(n - 1, -1, -1):
        value = target[k]
        for j in range(k + 1, n):
            value = value - system[k][j] * gamma[j]
        gamma[k] = value * inverse[k]
    weights = [1.0 - gamma[0]]
    for j in range(1, n):
        weights.append(gamma[j - 1] - gamma[j])
    weights.append(gamma[n - 1])
    return weights


def mix_kernel(entries, count, *refs):
    lines, (fresh, current, aged, out, wide, mixed_rows, done) = refs[:count], refs[count:]
    summed = lines[0][...]
    for line in lines[1:]:
        summed = summed + line[...]
    summed = summed / entries
    row = lax.broadcasted_iota(jnp.int32, (8, LANES), 0)
    lane = lax.broadcasted_iota(jnp.int32, (8, LANES), 1)
    for part in range(wide.shape[0]):
        own = jnp.where(lane == row + 8 * part, summed, 0.0)
        wide[part] = jnp.broadcast_to(jnp.sum(own, axis=1, keepdims=True), (8, LANES))
    products = {
        pair: jnp.broadcast_to(wide[spot // 8, spot % 8 : spot % 8 + 1, :], (8, LANES))
        for pair, spot in SPOTS.items()
    }
    weights = solve(products)
    rows, width = fresh.shape
    span = rows // done.shape[0]
    writes = []
    for part in range(done.shape[0]):
        for top in range(part * span, (part + 1) * span, 8):
            for left in range(0, width, LANES):
                at = (slice(top, top + 8), slice(left, left + LANES))
                mixed = weights[0] * (current[at] + mixing_share * fresh[at])
                for j in range(HIST):
                    mixed = mixed + weights[j + 1] * aged[(j,) + at]
                mixed_rows[at] = mixed
        at = pl.ds(part * span, span)
        writes.append(pltpu.make_async_copy(mixed_rows.at[at], out.at[at], done.at[part]))
        writes[-1].start()
    for write in writes:
        write.wait()


def mix(lines, fresh, current, aged, entries):
    return pl.pallas_call(
        lambda *refs: mix_kernel(entries, len(lines), *refs),
        out_shape=jax.ShapeDtypeStruct(fresh.shape, jnp.float32),
        in_specs=[VMEM] * (len(lines) + 3),
        out_specs=pl.BlockSpec(memory_space=pltpu.HBM),
        scratch_shapes=[
            pltpu.VMEM((3, 8, LANES), jnp.float32),
            pltpu.VMEM(fresh.shape, jnp.float32),
            pltpu.SemaphoreType.DMA((2,)),
        ],
        compiler_params=PARAMS,
        name="mix",
    )(*lines, fresh, current, aged)


def per_device(
    greens,
    current,
    past_inputs,
    past_residuals,
    slot_order,
    neighbour,
    momentum_class,
    stencil_weight,
    acoustic_coupling,
    optical_coupling,
    occupation,
    phonon_shift,
):
    group_len, slice_len = greens.shape[3:]
    rows, width = current.shape[3:]
    groups = lax.axis_size("kgrp")
    parts = lax.axis_size("energy")
    own = greens.reshape(-1, group_len, slice_len)
    height = own.shape[0] * rows

    flat = current.reshape(height, width)
    old_in = past_inputs.reshape(HIST, height, width)
    old_res = past_residuals.reshape(HIST, height, width)
    scalars = (
        slot_order, momentum_class, acoustic_coupling, optical_coupling, occupation, phonon_shift
    )
    aged, residuals, old_line, gains, shifts = history(old_in, old_res, scalars, rows)
    kept, given = smear(own, neighbour, stencil_weight, groups, parts)
    meet = lambda block, m: lax.ppermute(block, "energy", [(e, e ^ m) for e in range(parts)])
    swapped = meet(given, 1)
    smeared = [meet(block, 2 * chip) for chip, block in zip(chip_order(parts), join(kept, swapped))]
    fresh, line = residual(
        kept, swapped, smeared, flat, residuals, old_line, gains, shifts
    )
    line = line + meet(line, 1)
    line = sum((meet(line, 2 * chip) for chip in chip_order(parts)), line)
    lines = [line] + [
        lax.ppermute(line, "kgrp", [(g, g ^ m) for g in range(groups)]) for m in range(1, groups)
    ]
    entries = float(flat.size * groups * parts)
    return mix(lines, fresh, flat, aged, entries).reshape(current.shape)


def solution(mesh):
    return jax.shard_map(
        per_device,
        mesh=mesh,
        in_specs=(
            P(None, None, None, "kgrp", "energy"),
            P(None, None, None, ("kgrp", "energy"), None),
            P(None, None, None, None, ("kgrp", "energy"), None),
            P(None, None, None, None, ("kgrp", "energy"), None),
            P(),
            P("kgrp", None),
            P("kgrp"),
            P(),
            P(),
            P(),
            P(),
            P(),
        ),
        out_specs=P(None, None, None, ("kgrp", "energy"), None),
        check_vma=False,
    )
```

```python
import jax
import jax.numpy as jnp
from jax import lax
from jax.experimental import pallas as pl
from jax.experimental.pallas import tpu as pltpu
from jax.sharding import PartitionSpec as P

HIST = 5
LANES = 128

mixing_share = 0.5
ridge_share = 0.1

VMEM = pl.BlockSpec(memory_space=pltpu.VMEM)
SMEM = pl.BlockSpec(memory_space=pltpu.SMEM)
PARAMS = pltpu.CompilerParams(vmem_limit_bytes=16 * 1024 * 1024)

PAIRS = [(i, j) for i in range(1, HIST + 1) for j in range(i, HIST + 1)]
SPOTS = {pair: v for v, pair in enumerate(PAIRS)}
for _j in range(HIST + 1):
    SPOTS[(0, _j)] = 16 + _j


def split(value):
    high = value.astype(jnp.bfloat16)
    return high, (value - high.astype(jnp.float32)).astype(jnp.bfloat16)


def product(left, right):
    dot = lambda a, b: jnp.dot(a, b, preferred_element_type=jnp.float32)
    return dot(left[0], right[0]) + (dot(left[0], right[1]) + dot(left[1], right[0]))


def prepare_kernel(total_k, *refs):
    *blocks, neighbour_hbm, weight_hbm, stencil_hi, stencil_lo, part, late, neighbour, weight, done = refs
    fetches = [
        pltpu.make_async_copy(neighbour_hbm, neighbour, done.at[0]),
        pltpu.make_async_copy(weight_hbm, weight, done.at[1]),
    ]
    for fetch in fetches:
        fetch.start()
    late[...] = blocks[-1][...]
    _, group_len, slice_len = blocks[0].shape
    group_id = lax.axis_index("kgrp")
    parts = lax.axis_size("energy")
    rows = group_len // parts
    for fetch in fetches:
        fetch.wait()
    slots, _ = neighbour.shape
    padded = jnp.concatenate([neighbour[...], jnp.zeros((8 - slots, group_len), jnp.int32)], axis=0)
    targets = jnp.transpose(padded)
    place = lax.axis_index("energy")
    bit = 1
    while bit < parts:
        span = bit * rows
        pieces = [targets[at : at + span] for at in range(0, group_len, span)]
        flipped = [pieces[b ^ 1] for b in range(len(pieces))]
        targets = jnp.where(place & bit != 0, jnp.concatenate(flipped, axis=0), targets)
        bit *= 2
    local = targets - group_id * group_len + group_len
    local = jnp.where(local < 0, local + total_k, jnp.where(local >= total_k, local - total_k, local))
    spot = lax.broadcasted_iota(jnp.int32, (group_len, 3 * group_len), 1)
    stencil = jnp.zeros(spot.shape, jnp.float32)
    for n in range(slots):
        stencil = stencil + jnp.where(spot == local[:, n : n + 1], weight[n], 0.0)
    before, after = stencil[:, :group_len], stencil[:, 2 * group_len :]
    swapped = paired(total_k // group_len) & (group_id % 2 == 1)
    near, far = jnp.where(swapped, before, after), jnp.where(swapped, after, before)
    stencil_hi[...], stencil_lo[...] = split(jnp.concatenate([near, far], axis=1))
    centre = split(stencil[:, group_len : 2 * group_len])
    first = 0
    for own in blocks:
        for c in range(0, own.shape[0], 2):
            result = product(centre, split(jnp.concatenate([own[c], own[c + 1]], axis=1)))
            part[first + c] = result[:, :slice_len]
            part[first + c + 1] = result[:, slice_len:]
        first += own.shape[0]


def prepare(blocks, neighbour, weight, total_k):
    comps = sum(block.shape[0] for block in blocks)
    _, group_len, slice_len = blocks[0].shape
    sides = jax.ShapeDtypeStruct((group_len, 2 * group_len), jnp.bfloat16)
    size = comps * group_len * slice_len
    return pl.pallas_call(
        lambda *refs: prepare_kernel(total_k, *refs),
        out_shape=(
            sides,
            sides,
            jax.ShapeDtypeStruct((comps, group_len, slice_len), jnp.float32),
            jax.ShapeDtypeStruct(blocks[-1].shape, jnp.float32),
        ),
        in_specs=[VMEM] * len(blocks) + [pl.BlockSpec(memory_space=pltpu.HBM)] * 2,
        out_specs=(VMEM,) * 4,
        scratch_shapes=[
            pltpu.VMEM(neighbour.shape[::-1], jnp.int32),
            pltpu.SMEM(weight.shape, jnp.float32),
            pltpu.SemaphoreType.DMA((2,)),
        ],
        compiler_params=PARAMS,
        cost_estimate=pl.CostEstimate(
            flops=6 * size * group_len, bytes_accessed=8 * size, transcendentals=0
        ),
        name="prepare",
    )(*blocks, jnp.transpose(neighbour), weight)


def smeared_pairs(first, sides, stencil_hi, stencil_lo, part):
    blocks = [block for block in sides if block is not None]
    comps, group_len, slice_len = blocks[0].shape
    start = 0 if sides[0] is not None else group_len
    at = slice(start, start + len(blocks) * group_len)
    stencil = (stencil_hi[:, at], stencil_lo[:, at])
    for c in range(0, comps, 2):
        stacked = [jnp.concatenate([block[c], block[c + 1]], axis=1) for block in blocks]
        result = product(stencil, split(jnp.concatenate(stacked, axis=0)))
        for p in range(2):
            yield c + p, part[first + c + p] + result[:, p * slice_len : (p + 1) * slice_len]


def with_sides(kernel, sides):
    def body(*refs):
        refs = list(refs)
        kernel([None if side is None else refs.pop(0) for side in sides], *refs)

    return body


def smear_cost(blocks):
    size = sum(block.size for block in blocks)
    return pl.CostEstimate(
        flops=6 * size * blocks[0].shape[1], bytes_accessed=12 * size, transcendentals=0
    )


def add_sides(first, sides, stencil_hi, stencil_lo, part, after):
    def kernel(sides, stencil_hi, stencil_lo, part, *refs):
        for c, smeared in smeared_pairs(first, sides, stencil_hi, stencil_lo, part):
            refs[-1][c] = smeared

    blocks = [block for block in sides if block is not None]
    return pl.pallas_call(
        with_sides(kernel, sides),
        out_shape=jax.ShapeDtypeStruct(blocks[0].shape, jnp.float32),
        in_specs=[VMEM] * (len(blocks) + 3) + [pl.BlockSpec(memory_space=pl.ANY)] * len(after),
        out_specs=VMEM,
        compiler_params=PARAMS,
        cost_estimate=smear_cost(blocks),
        name="add_sides",
    )(*blocks, stencil_hi, stencil_lo, part, *after)


def finish_kernel(sides, stencil_hi, stencil_lo, part, *refs):
    *ready, kept, given = refs
    chips, height, _ = kept.shape
    comps = part.shape[0]
    rows = height // comps

    def place(c, smeared):
        for m in range(2 * chips):
            out = given if m % 2 else kept
            out[m // 2, c * rows : (c + 1) * rows, :] = smeared[m * rows : (m + 1) * rows]

    first = 0
    for c, smeared in smeared_pairs(0, sides, stencil_hi, stencil_lo, part):
        place(c, smeared)
        first = c + 1
    for block in ready:
        for c in range(block.shape[0]):
            place(first + c, block[c])


def finish(sides, stencil_hi, stencil_lo, part, ready, parts):
    blocks = [block for block in sides if block is not None]
    comps, group_len, slice_len = part.shape
    shape = (parts // 2, comps * group_len // parts, slice_len)
    return pl.pallas_call(
        with_sides(finish_kernel, sides),
        out_shape=[jax.ShapeDtypeStruct(shape, jnp.float32)] * 2,
        in_specs=[VMEM] * (len(blocks) + len(ready) + 3),
        out_specs=[VMEM] * 2,
        compiler_params=PARAMS,
        cost_estimate=smear_cost(blocks),
        name="finish",
    )(*blocks, stencil_hi, stencil_lo, part, *ready)


def chip_order(parts):
    chips = parts // 2
    return [*range(chips // 2, chips), *range(1, chips // 2)] if chips > 1 else []


def join_kernel(own, swapped, *out):
    for chip, block in zip(chip_order(2 * own.shape[0]), out):
        block[0], block[1] = own[chip], swapped[chip]


def join(own, swapped):
    chips, height, slice_len = own.shape
    shape = jax.ShapeDtypeStruct((2, height, slice_len), jnp.float32)
    return pl.pallas_call(
        join_kernel,
        out_shape=[shape] * (chips - 1),
        in_specs=[VMEM] * 2,
        out_specs=[VMEM] * (chips - 1),
        compiler_params=PARAMS,
        name="join",
    )(own, swapped)


def paired(groups):
    return groups == 4


def hold_kernel(block, _, out):
    out[...] = block[...]


def hold(block, until):
    return pl.pallas_call(
        hold_kernel,
        out_shape=jax.ShapeDtypeStruct(block.shape, jnp.float32),
        in_specs=[VMEM, pl.BlockSpec(memory_space=pl.ANY)],
        out_specs=VMEM,
        compiler_params=PARAMS,
        name="hold",
    )(block, until)


def smear(own, neighbour, weight, groups, parts):
    total_k = groups * own.shape[1]
    if not paired(groups):
        forward = [(i, (i + 1) % groups) for i in range(groups)]
        backward = [(target, source) for source, target in forward]
        near, far = lax.ppermute(own, "kgrp", backward), lax.ppermute(own, "kgrp", forward)
        return finish((near, far), *prepare([own], neighbour, weight, total_k)[:3], [], parts)
    across = lambda block, flip: lax.ppermute(block, "kgrp", [(i, i ^ flip) for i in range(groups)])
    half = own.shape[0] // 2
    head, tail = own[:half], own[half:]
    near_head, far_tail = across(head, 1), across(tail, 3)
    hi, lo, part, late = prepare([head, tail], neighbour, weight, total_k)
    near_tail, far_head = across(late, 1), across(hold(near_head, late), 2)
    tail_part = add_sides(half, (near_tail, far_tail), hi, lo, part, [])
    return finish((near_head, far_head), hi, lo, part, [tail_part], parts)


def spread(values, shape):
    lane = lax.broadcasted_iota(jnp.int32, shape, 1)
    row = jnp.zeros(shape, jnp.float32)
    for spot, value in values:
        row = jnp.where(lane == spot, value, row)
    return row


def total(acc):
    return jnp.sum(jnp.sum(acc, axis=0, keepdims=True), axis=1, keepdims=True)


def history_kernel(
    total_rows, past_inputs, past_residuals, slots, classes, acoustic, optical, number, shift,
    aged, residuals, line, gains, shifts,
):
    first = lax.axis_index("energy") * total_rows
    row = lax.broadcasted_iota(jnp.int32, (8, LANES), 0) % total_rows
    coupling = jnp.zeros((8, LANES), jnp.float32)
    for i in range(total_rows):
        coupling = jnp.where(row == i, acoustic[classes[first + i]], coupling)
    gains[0] = coupling
    for m in range(2):
        gains[2 * m + 1] = jnp.full((8, LANES), optical[m] * (number[m] + 1.0))
        gains[2 * m + 2] = jnp.full((8, LANES), optical[m] * number[m])
        shifts[m] = jnp.full((8, LANES), shift[m], jnp.int32)
    _, rows, width = past_inputs.shape
    acc = [jnp.zeros((8, LANES), jnp.float32) for _ in PAIRS]
    for top in range(0, rows, 8):
        def column(t, acc, top=top):
            at = pl.ds(pl.multiple_of(t * LANES, LANES), LANES)
            old = []
            for j in range(HIST):
                res = past_residuals[slots[j], top : top + 8, at]
                aged[j, top : top + 8, at] = (
                    past_inputs[slots[j], top : top + 8, at] + mixing_share * res
                )
                residuals[j, top : top + 8, at] = res
                old.append(res)
            return [a + old[i - 1] * old[j - 1] for a, (i, j) in zip(acc, PAIRS)]
        acc = lax.fori_loop(0, width // LANES, column, acc, unroll=4)
    line[...] = spread([(v, total(a)) for v, a in enumerate(acc)], line.shape)


def history(past_inputs, past_residuals, scalars, rows):
    size = past_inputs.size
    return pl.pallas_call(
        lambda *refs: history_kernel(rows, *refs),
        out_shape=(
            jax.ShapeDtypeStruct(past_inputs.shape, jnp.float32),
            jax.ShapeDtypeStruct(past_inputs.shape, jnp.float32),
            jax.ShapeDtypeStruct((1, LANES), jnp.float32),
            jax.ShapeDtypeStruct((5, 8, LANES), jnp.float32),
            jax.ShapeDtypeStruct((2, 8, LANES), jnp.int32),
        ),
        in_specs=[VMEM, VMEM] + [SMEM] * 6,
        out_specs=(VMEM,) * 5,
        compiler_params=PARAMS,
        cost_estimate=pl.CostEstimate(flops=8 * size, bytes_accessed=12 * size, transcendentals=0),
        name="history",
    )(past_inputs, past_residuals, *scalars)


def residual_kernel(count, own, swapped, *refs):
    received = refs[:count]
    current, residuals, old_line, gains, shifts, fresh, lines, smeared = refs[count:]
    parts, height, slice_len = smeared.shape
    place = lax.axis_index("energy")
    smeared[place], smeared[place ^ 1] = own[0], swapped[0]
    for chip, block in zip(chip_order(parts), received):
        smeared[place ^ (2 * chip)], smeared[place ^ (2 * chip + 1)] = block[0], block[1]
    lane = lax.broadcasted_iota(jnp.int32, (8, slice_len), 1)
    coupling = gains[0]
    modes = []
    for m in range(2):
        wide = shifts[m]
        keeps = lane < slice_len - wide, lane >= wide
        modes.append((jnp.max(wide), *keeps, gains[2 * m + 1], gains[2 * m + 2]))
    zero = jnp.zeros((8, slice_len), jnp.float32)
    acc = [zero] * (HIST + 1)
    for top in range(0, height, 8):
        at = slice(top, top + 8)
        source = [smeared[e, at, :] for e in range(parts)]
        sigma = [coupling * x for x in source]
        lesser = top < height // 2
        for s, keep_up, keep_down, emitted, absorbed in modes:
            up = [pltpu.roll(x, slice_len - s, 1) for x in source] + [zero]
            down = [zero] + [pltpu.roll(x, s, 1) for x in source]
            gain_up, gain_down = (emitted, absorbed) if lesser else (absorbed, emitted)
            for e in range(parts):
                above = jnp.where(keep_up, up[e], up[e + 1])
                below = jnp.where(keep_down, down[e + 1], down[e])
                sigma[e] = sigma[e] + (gain_up * above + gain_down * below)
        for e in range(parts):
            where = (at, slice(e * slice_len, (e + 1) * slice_len))
            new = sigma[e] - current[where]
            fresh[where] = new
            acc[0] = acc[0] + new * new
            for j in range(HIST):
                acc[j + 1] = acc[j + 1] + new * residuals[(j,) + where]
    mine = jnp.concatenate([jnp.sum(a, axis=0, keepdims=True) for a in acc] + [zero[: 8 - HIST - 1]], axis=0)
    mine = jnp.sum(mine, axis=1, keepdims=True)
    spot = lax.broadcasted_iota(jnp.int32, (8, LANES), 0) + SPOTS[(0, 0)]
    mine = jnp.where(lax.broadcasted_iota(jnp.int32, (8, LANES), 1) == spot, mine, 0.0)
    mine = old_line[...] + jnp.sum(mine, axis=0, keepdims=True)
    lines[...] = jnp.broadcast_to(mine[None], lines.shape)


def residual(kept, swapped, smeared, current, residuals, old_line, gains, shifts, copies):
    return pl.pallas_call(
        lambda *refs: residual_kernel(len(smeared), *refs),
        out_shape=(
            jax.ShapeDtypeStruct(current.shape, jnp.float32),
            jax.ShapeDtypeStruct((copies, 1, LANES), jnp.float32),
        ),
        in_specs=[VMEM] * (len(smeared) + 7),
        out_specs=(VMEM, VMEM),
        scratch_shapes=[pltpu.VMEM((2 * kept.shape[0],) + kept.shape[1:], jnp.float32)],
        compiler_params=PARAMS,
        name="residual",
    )(kept, swapped, *smeared, current, residuals, old_line, gains, shifts)


def solve(products):
    prod = lambda i, j: products[(min(i, j), max(i, j))]
    n = HIST
    system = [
        [prod(i, j) - prod(i, j + 1) - prod(i + 1, j) + prod(i + 1, j + 1) for j in range(n)]
        for i in range(n)
    ]
    target = [prod(i, 0) - prod(i + 1, 0) for i in range(n)]
    trace = system[0][0]
    for i in range(1, n):
        trace = trace + system[i][i]
    ridge = ridge_share * trace / n + 1e-06
    for i in range(n):
        system[i][i] = system[i][i] + ridge
    inverse = [None] * n
    for k in range(n):
        inverse[k] = 1.0 / system[k][k]
        for i in range(k + 1, n):
            factor = system[k][i] * inverse[k]
            for j in range(i, n):
                system[i][j] = system[i][j] - factor * system[k][j]
            target[i] = target[i] - factor * target[k]
    gamma = [None] * n
    for k in range(n - 1, -1, -1):
        value = target[k]
        for j in range(k + 1, n):
            value = value - system[k][j] * gamma[j]
        gamma[k] = value * inverse[k]
    weights = [1.0 - gamma[0]]
    for j in range(1, n):
        weights.append(gamma[j - 1] - gamma[j])
    weights.append(gamma[n - 1])
    return weights


def mix_kernel(entries, lines, fresh, current, aged, out, wide, mixed_rows, done):
    summed = jnp.sum(lines[...], axis=0) / entries
    row = lax.broadcasted_iota(jnp.int32, (8, LANES), 0)
    lane = lax.broadcasted_iota(jnp.int32, (8, LANES), 1)
    for part in range(wide.shape[0]):
        own = jnp.where(lane == row + 8 * part, summed, 0.0)
        wide[part] = jnp.broadcast_to(jnp.sum(own, axis=1, keepdims=True), (8, LANES))
    products = {
        pair: jnp.broadcast_to(wide[spot // 8, spot % 8 : spot % 8 + 1, :], (8, LANES))
        for pair, spot in SPOTS.items()
    }
    weights = solve(products)
    rows, width = fresh.shape
    span = rows // done.shape[0]
    writes = []
    for part in range(done.shape[0]):
        for top in range(part * span, (part + 1) * span, 8):
            for left in range(0, width, LANES):
                at = (slice(top, top + 8), slice(left, left + LANES))
                mixed = weights[0] * (current[at] + mixing_share * fresh[at])
                for j in range(HIST):
                    mixed = mixed + weights[j + 1] * aged[(j,) + at]
                mixed_rows[at] = mixed
        at = pl.ds(part * span, span)
        writes.append(pltpu.make_async_copy(mixed_rows.at[at], out.at[at], done.at[part]))
        writes[-1].start()
    for write in writes:
        write.wait()


def mix(lines, fresh, current, aged, entries):
    return pl.pallas_call(
        lambda *refs: mix_kernel(entries, *refs),
        out_shape=jax.ShapeDtypeStruct(fresh.shape, jnp.float32),
        in_specs=[VMEM] * 4,
        out_specs=pl.BlockSpec(memory_space=pltpu.HBM),
        scratch_shapes=[
            pltpu.VMEM((3, 8, LANES), jnp.float32),
            pltpu.VMEM(fresh.shape, jnp.float32),
            pltpu.SemaphoreType.DMA((2,)),
        ],
        compiler_params=PARAMS,
        name="mix",
    )(lines, fresh, current, aged)


def per_device(
    greens,
    current,
    past_inputs,
    past_residuals,
    slot_order,
    neighbour,
    momentum_class,
    stencil_weight,
    acoustic_coupling,
    optical_coupling,
    occupation,
    phonon_shift,
):
    group_len, slice_len = greens.shape[3:]
    rows, width = current.shape[3:]
    groups = lax.axis_size("kgrp")
    parts = lax.axis_size("energy")
    own = greens.reshape(-1, group_len, slice_len)
    height = own.shape[0] * rows

    flat = current.reshape(height, width)
    old_in = past_inputs.reshape(HIST, height, width)
    old_res = past_residuals.reshape(HIST, height, width)
    scalars = (
        slot_order, momentum_class, acoustic_coupling, optical_coupling, occupation, phonon_shift
    )
    aged, residuals, old_line, gains, shifts = history(old_in, old_res, scalars, rows)
    kept, given = smear(own, neighbour, stencil_weight, groups, parts)
    meet = lambda block, m: lax.ppermute(block, "energy", [(e, e ^ m) for e in range(parts)])
    swapped = meet(given, 1)
    smeared = [meet(block, 2 * chip) for chip, block in zip(chip_order(parts), join(kept, swapped))]
    fresh, lines = residual(
        kept, swapped, smeared, flat, residuals, old_line, gains, shifts, groups * parts
    )
    lines = lax.all_to_all(lines, ("energy", "kgrp"), split_axis=0, concat_axis=0, tiled=True)
    entries = float(flat.size * groups * parts)
    return mix(lines, fresh, flat, aged, entries).reshape(current.shape)


def solution(mesh):
    return jax.shard_map(
        per_device,
        mesh=mesh,
        in_specs=(
            P(None, None, None, "kgrp", "energy"),
            P(None, None, None, ("kgrp", "energy"), None),
            P(None, None, None, None, ("kgrp", "energy"), None),
            P(None, None, None, None, ("kgrp", "energy"), None),
            P(),
            P("kgrp", None),
            P("kgrp"),
            P(),
            P(),
            P(),
            P(),
            P(),
        ),
        out_specs=P(None, None, None, ("kgrp", "energy"), None),
        check_vma=False,
    )
```

```python
import jax
import jax.numpy as jnp
from jax import lax
from jax.experimental import pallas as pl
from jax.experimental.pallas import tpu as pltpu
from jax.sharding import PartitionSpec as P

HIST = 5
LANES = 128

mixing_share = 0.5
ridge_share = 0.1

VMEM = pl.BlockSpec(memory_space=pltpu.VMEM)
SMEM = pl.BlockSpec(memory_space=pltpu.SMEM)
PARAMS = pltpu.CompilerParams(vmem_limit_bytes=16 * 1024 * 1024)

PAIRS = [(i, j) for i in range(1, HIST + 1) for j in range(i, HIST + 1)]
SPOTS = {pair: v for v, pair in enumerate(PAIRS)}
for _j in range(HIST + 1):
    SPOTS[(0, _j)] = 16 + _j


def split(value):
    high = value.astype(jnp.bfloat16)
    return high, (value - high.astype(jnp.float32)).astype(jnp.bfloat16)


def product(left, right):
    dot = lambda a, b: jnp.dot(a, b, preferred_element_type=jnp.float32)
    return dot(left[0], right[0]) + (dot(left[0], right[1]) + dot(left[1], right[0]))


def prepare_kernel(total_k, *refs):
    *blocks, neighbour_hbm, weight_hbm, stencil_hi, stencil_lo, part, late, neighbour, weight, done = refs
    fetches = [
        pltpu.make_async_copy(neighbour_hbm, neighbour, done.at[0]),
        pltpu.make_async_copy(weight_hbm, weight, done.at[1]),
    ]
    for fetch in fetches:
        fetch.start()
    late[...] = blocks[-1][...]
    _, group_len, slice_len = blocks[0].shape
    group_id = lax.axis_index("kgrp")
    parts = lax.axis_size("energy")
    rows = group_len // parts
    for fetch in fetches:
        fetch.wait()
    slots, _ = neighbour.shape
    padded = jnp.concatenate([neighbour[...], jnp.zeros((8 - slots, group_len), jnp.int32)], axis=0)
    targets = jnp.transpose(padded)
    place = lax.axis_index("energy")
    bit = 1
    while bit < parts:
        span = bit * rows
        pieces = [targets[at : at + span] for at in range(0, group_len, span)]
        flipped = [pieces[b ^ 1] for b in range(len(pieces))]
        targets = jnp.where(place & bit != 0, jnp.concatenate(flipped, axis=0), targets)
        bit *= 2
    local = targets - group_id * group_len + group_len
    local = jnp.where(local < 0, local + total_k, jnp.where(local >= total_k, local - total_k, local))
    spot = lax.broadcasted_iota(jnp.int32, (group_len, 3 * group_len), 1)
    stencil = jnp.zeros(spot.shape, jnp.float32)
    for n in range(slots):
        stencil = stencil + jnp.where(spot == local[:, n : n + 1], weight[n], 0.0)
    before, after = stencil[:, :group_len], stencil[:, 2 * group_len :]
    swapped = paired(total_k // group_len) & (group_id % 2 == 1)
    near, far = jnp.where(swapped, before, after), jnp.where(swapped, after, before)
    stencil_hi[...], stencil_lo[...] = split(jnp.concatenate([near, far], axis=1))
    centre = split(stencil[:, group_len : 2 * group_len])
    first = 0
    for own in blocks:
        for c in range(0, own.shape[0], 2):
            result = product(centre, split(jnp.concatenate([own[c], own[c + 1]], axis=1)))
            part[first + c] = result[:, :slice_len]
            part[first + c + 1] = result[:, slice_len:]
        first += own.shape[0]


def prepare(blocks, neighbour, weight, total_k):
    comps = sum(block.shape[0] for block in blocks)
    _, group_len, slice_len = blocks[0].shape
    sides = jax.ShapeDtypeStruct((group_len, 2 * group_len), jnp.bfloat16)
    size = comps * group_len * slice_len
    return pl.pallas_call(
        lambda *refs: prepare_kernel(total_k, *refs),
        out_shape=(
            sides,
            sides,
            jax.ShapeDtypeStruct((comps, group_len, slice_len), jnp.float32),
            jax.ShapeDtypeStruct(blocks[-1].shape, jnp.float32),
        ),
        in_specs=[VMEM] * len(blocks) + [pl.BlockSpec(memory_space=pltpu.HBM)] * 2,
        out_specs=(VMEM,) * 4,
        scratch_shapes=[
            pltpu.VMEM(neighbour.shape[::-1], jnp.int32),
            pltpu.SMEM(weight.shape, jnp.float32),
            pltpu.SemaphoreType.DMA((2,)),
        ],
        compiler_params=PARAMS,
        cost_estimate=pl.CostEstimate(
            flops=6 * size * group_len, bytes_accessed=8 * size, transcendentals=0
        ),
        name="prepare",
    )(*blocks, jnp.transpose(neighbour), weight)


def smeared_pairs(first, sides, stencil_hi, stencil_lo, part):
    blocks = [block for block in sides if block is not None]
    comps, group_len, slice_len = blocks[0].shape
    start = 0 if sides[0] is not None else group_len
    at = slice(start, start + len(blocks) * group_len)
    stencil = (stencil_hi[:, at], stencil_lo[:, at])
    for c in range(0, comps, 2):
        stacked = [jnp.concatenate([block[c], block[c + 1]], axis=1) for block in blocks]
        result = product(stencil, split(jnp.concatenate(stacked, axis=0)))
        for p in range(2):
            yield c + p, part[first + c + p] + result[:, p * slice_len : (p + 1) * slice_len]


def with_sides(kernel, sides):
    def body(*refs):
        refs = list(refs)
        kernel([None if side is None else refs.pop(0) for side in sides], *refs)

    return body


def smear_cost(blocks):
    size = sum(block.size for block in blocks)
    return pl.CostEstimate(
        flops=6 * size * blocks[0].shape[1], bytes_accessed=12 * size, transcendentals=0
    )


def add_sides(first, sides, stencil_hi, stencil_lo, part, after):
    def kernel(sides, stencil_hi, stencil_lo, part, *refs):
        for c, smeared in smeared_pairs(first, sides, stencil_hi, stencil_lo, part):
            refs[-1][c] = smeared

    blocks = [block for block in sides if block is not None]
    return pl.pallas_call(
        with_sides(kernel, sides),
        out_shape=jax.ShapeDtypeStruct(blocks[0].shape, jnp.float32),
        in_specs=[VMEM] * (len(blocks) + 3) + [pl.BlockSpec(memory_space=pl.ANY)] * len(after),
        out_specs=VMEM,
        compiler_params=PARAMS,
        cost_estimate=smear_cost(blocks),
        name="add_sides",
    )(*blocks, stencil_hi, stencil_lo, part, *after)


def finish_kernel(sides, stencil_hi, stencil_lo, part, *refs):
    *ready, kept, given = refs
    chips, height, _ = kept.shape
    comps = part.shape[0]
    rows = height // comps

    def place(c, smeared):
        for m in range(2 * chips):
            out = given if m % 2 else kept
            out[m // 2, c * rows : (c + 1) * rows, :] = smeared[m * rows : (m + 1) * rows]

    first = 0
    for c, smeared in smeared_pairs(0, sides, stencil_hi, stencil_lo, part):
        place(c, smeared)
        first = c + 1
    for block in ready:
        for c in range(block.shape[0]):
            place(first + c, block[c])


def finish(sides, stencil_hi, stencil_lo, part, ready, parts):
    blocks = [block for block in sides if block is not None]
    comps, group_len, slice_len = part.shape
    shape = (parts // 2, comps * group_len // parts, slice_len)
    return pl.pallas_call(
        with_sides(finish_kernel, sides),
        out_shape=[jax.ShapeDtypeStruct(shape, jnp.float32)] * 2,
        in_specs=[VMEM] * (len(blocks) + len(ready) + 3),
        out_specs=[VMEM] * 2,
        compiler_params=PARAMS,
        cost_estimate=smear_cost(blocks),
        name="finish",
    )(*blocks, stencil_hi, stencil_lo, part, *ready)


def chip_order(parts):
    chips = parts // 2
    half = chips // 2
    return [half, *range(1, half), *range(half + 1, chips)] if chips > 1 else []


def join_kernel(own, swapped, *out):
    for chip, block in zip(chip_order(2 * own.shape[0]), out):
        block[0], block[1] = own[chip], swapped[chip]


def join(own, swapped):
    chips, height, slice_len = own.shape
    shape = jax.ShapeDtypeStruct((2, height, slice_len), jnp.float32)
    return pl.pallas_call(
        join_kernel,
        out_shape=[shape] * (chips - 1),
        in_specs=[VMEM] * 2,
        out_specs=[VMEM] * (chips - 1),
        compiler_params=PARAMS,
        name="join",
    )(own, swapped)


def paired(groups):
    return groups == 4


def hold_kernel(block, _, out):
    out[...] = block[...]


def hold(block, until):
    return pl.pallas_call(
        hold_kernel,
        out_shape=jax.ShapeDtypeStruct(block.shape, jnp.float32),
        in_specs=[VMEM, pl.BlockSpec(memory_space=pl.ANY)],
        out_specs=VMEM,
        compiler_params=PARAMS,
        name="hold",
    )(block, until)


def smear(own, neighbour, weight, groups, parts):
    total_k = groups * own.shape[1]
    if not paired(groups):
        forward = [(i, (i + 1) % groups) for i in range(groups)]
        backward = [(target, source) for source, target in forward]
        near, far = lax.ppermute(own, "kgrp", backward), lax.ppermute(own, "kgrp", forward)
        return finish((near, far), *prepare([own], neighbour, weight, total_k)[:3], [], parts)
    across = lambda block, flip: lax.ppermute(block, "kgrp", [(i, i ^ flip) for i in range(groups)])
    half = own.shape[0] // 2
    head, tail = own[:half], own[half:]
    near_head, far_tail = across(head, 1), across(tail, 3)
    hi, lo, part, late = prepare([head, tail], neighbour, weight, total_k)
    near_tail, far_head = across(late, 1), across(hold(near_head, late), 2)
    tail_part = add_sides(half, (near_tail, far_tail), hi, lo, part, [])
    return finish((near_head, far_head), hi, lo, part, [tail_part], parts)


def spread(values, shape):
    lane = lax.broadcasted_iota(jnp.int32, shape, 1)
    row = jnp.zeros(shape, jnp.float32)
    for spot, value in values:
        row = jnp.where(lane == spot, value, row)
    return row


def total(acc):
    return jnp.sum(jnp.sum(acc, axis=0, keepdims=True), axis=1, keepdims=True)


def history_kernel(
    total_rows, past_inputs, past_residuals, slots, classes, acoustic, optical, number, shift,
    aged, residuals, line, gains, shifts,
):
    first = lax.axis_index("energy") * total_rows
    row = lax.broadcasted_iota(jnp.int32, (8, LANES), 0) % total_rows
    coupling = jnp.zeros((8, LANES), jnp.float32)
    for i in range(total_rows):
        coupling = jnp.where(row == i, acoustic[classes[first + i]], coupling)
    gains[0] = coupling
    for m in range(2):
        gains[2 * m + 1] = jnp.full((8, LANES), optical[m] * (number[m] + 1.0))
        gains[2 * m + 2] = jnp.full((8, LANES), optical[m] * number[m])
        shifts[m] = jnp.full((8, LANES), shift[m], jnp.int32)
    _, rows, width = past_inputs.shape
    acc = [jnp.zeros((8, LANES), jnp.float32) for _ in PAIRS]
    for top in range(0, rows, 8):
        def column(t, acc, top=top):
            at = pl.ds(pl.multiple_of(t * LANES, LANES), LANES)
            old = []
            for j in range(HIST):
                res = past_residuals[slots[j], top : top + 8, at]
                aged[j, top : top + 8, at] = (
                    past_inputs[slots[j], top : top + 8, at] + mixing_share * res
                )
                residuals[j, top : top + 8, at] = res
                old.append(res)
            return [a + old[i - 1] * old[j - 1] for a, (i, j) in zip(acc, PAIRS)]
        acc = lax.fori_loop(0, width // LANES, column, acc, unroll=4)
    line[...] = spread([(v, total(a)) for v, a in enumerate(acc)], line.shape)


def history(past_inputs, past_residuals, scalars, rows):
    size = past_inputs.size
    return pl.pallas_call(
        lambda *refs: history_kernel(rows, *refs),
        out_shape=(
            jax.ShapeDtypeStruct(past_inputs.shape, jnp.float32),
            jax.ShapeDtypeStruct(past_inputs.shape, jnp.float32),
            jax.ShapeDtypeStruct((1, LANES), jnp.float32),
            jax.ShapeDtypeStruct((5, 8, LANES), jnp.float32),
            jax.ShapeDtypeStruct((2, 8, LANES), jnp.int32),
        ),
        in_specs=[VMEM, VMEM] + [SMEM] * 6,
        out_specs=(VMEM,) * 5,
        compiler_params=PARAMS,
        cost_estimate=pl.CostEstimate(flops=8 * size, bytes_accessed=12 * size, transcendentals=0),
        name="history",
    )(past_inputs, past_residuals, *scalars)


def residual_kernel(count, own, swapped, *refs):
    received = refs[:count]
    current, residuals, old_line, gains, shifts, fresh, lines, smeared = refs[count:]
    parts, height, slice_len = smeared.shape
    place = lax.axis_index("energy")
    smeared[place], smeared[place ^ 1] = own[0], swapped[0]
    for chip, block in zip(chip_order(parts), received):
        smeared[place ^ (2 * chip)], smeared[place ^ (2 * chip + 1)] = block[0], block[1]
    lane = lax.broadcasted_iota(jnp.int32, (8, slice_len), 1)
    coupling = gains[0]
    modes = []
    for m in range(2):
        wide = shifts[m]
        keeps = lane < slice_len - wide, lane >= wide
        modes.append((jnp.max(wide), *keeps, gains[2 * m + 1], gains[2 * m + 2]))
    zero = jnp.zeros((8, slice_len), jnp.float32)
    acc = [zero] * (HIST + 1)
    for top in range(0, height, 8):
        at = slice(top, top + 8)
        source = [smeared[e, at, :] for e in range(parts)]
        sigma = [coupling * x for x in source]
        lesser = top < height // 2
        for s, keep_up, keep_down, emitted, absorbed in modes:
            up = [pltpu.roll(x, slice_len - s, 1) for x in source] + [zero]
            down = [zero] + [pltpu.roll(x, s, 1) for x in source]
            gain_up, gain_down = (emitted, absorbed) if lesser else (absorbed, emitted)
            for e in range(parts):
                above = jnp.where(keep_up, up[e], up[e + 1])
                below = jnp.where(keep_down, down[e + 1], down[e])
                sigma[e] = sigma[e] + (gain_up * above + gain_down * below)
        for e in range(parts):
            where = (at, slice(e * slice_len, (e + 1) * slice_len))
            new = sigma[e] - current[where]
            fresh[where] = new
            acc[0] = acc[0] + new * new
            for j in range(HIST):
                acc[j + 1] = acc[j + 1] + new * residuals[(j,) + where]
    mine = jnp.concatenate([jnp.sum(a, axis=0, keepdims=True) for a in acc] + [zero[: 8 - HIST - 1]], axis=0)
    mine = jnp.sum(mine, axis=1, keepdims=True)
    spot = lax.broadcasted_iota(jnp.int32, (8, LANES), 0) + SPOTS[(0, 0)]
    mine = jnp.where(lax.broadcasted_iota(jnp.int32, (8, LANES), 1) == spot, mine, 0.0)
    mine = old_line[...] + jnp.sum(mine, axis=0, keepdims=True)
    lines[...] = jnp.broadcast_to(mine[None], lines.shape)


def residual(kept, swapped, smeared, current, residuals, old_line, gains, shifts, copies):
    return pl.pallas_call(
        lambda *refs: residual_kernel(len(smeared), *refs),
        out_shape=(
            jax.ShapeDtypeStruct(current.shape, jnp.float32),
            jax.ShapeDtypeStruct((copies, 1, LANES), jnp.float32),
        ),
        in_specs=[VMEM] * (len(smeared) + 7),
        out_specs=(VMEM, VMEM),
        scratch_shapes=[pltpu.VMEM((2 * kept.shape[0],) + kept.shape[1:], jnp.float32)],
        compiler_params=PARAMS,
        name="residual",
    )(kept, swapped, *smeared, current, residuals, old_line, gains, shifts)


def solve(products):
    prod = lambda i, j: products[(min(i, j), max(i, j))]
    n = HIST
    system = [
        [prod(i, j) - prod(i, j + 1) - prod(i + 1, j) + prod(i + 1, j + 1) for j in range(n)]
        for i in range(n)
    ]
    target = [prod(i, 0) - prod(i + 1, 0) for i in range(n)]
    trace = system[0][0]
    for i in range(1, n):
        trace = trace + system[i][i]
    ridge = ridge_share * trace / n + 1e-06
    for i in range(n):
        system[i][i] = system[i][i] + ridge
    inverse = [None] * n
    for k in range(n):
        inverse[k] = 1.0 / system[k][k]
        for i in range(k + 1, n):
            factor = system[k][i] * inverse[k]
            for j in range(i, n):
                system[i][j] = system[i][j] - factor * system[k][j]
            target[i] = target[i] - factor * target[k]
    gamma = [None] * n
    for k in range(n - 1, -1, -1):
        value = target[k]
        for j in range(k + 1, n):
            value = value - system[k][j] * gamma[j]
        gamma[k] = value * inverse[k]
    weights = [1.0 - gamma[0]]
    for j in range(1, n):
        weights.append(gamma[j - 1] - gamma[j])
    weights.append(gamma[n - 1])
    return weights


def mix_kernel(entries, lines, fresh, current, aged, out, wide, mixed_rows, done):
    summed = jnp.sum(lines[...], axis=0) / entries
    row = lax.broadcasted_iota(jnp.int32, (8, LANES), 0)
    lane = lax.broadcasted_iota(jnp.int32, (8, LANES), 1)
    for part in range(wide.shape[0]):
        own = jnp.where(lane == row + 8 * part, summed, 0.0)
        wide[part] = jnp.broadcast_to(jnp.sum(own, axis=1, keepdims=True), (8, LANES))
    products = {
        pair: jnp.broadcast_to(wide[spot // 8, spot % 8 : spot % 8 + 1, :], (8, LANES))
        for pair, spot in SPOTS.items()
    }
    weights = solve(products)
    rows, width = fresh.shape
    span = rows // done.shape[0]
    writes = []
    for part in range(done.shape[0]):
        for top in range(part * span, (part + 1) * span, 8):
            for left in range(0, width, LANES):
                at = (slice(top, top + 8), slice(left, left + LANES))
                mixed = weights[0] * (current[at] + mixing_share * fresh[at])
                for j in range(HIST):
                    mixed = mixed + weights[j + 1] * aged[(j,) + at]
                mixed_rows[at] = mixed
        at = pl.ds(part * span, span)
        writes.append(pltpu.make_async_copy(mixed_rows.at[at], out.at[at], done.at[part]))
        writes[-1].start()
    for write in writes:
        write.wait()


def mix(lines, fresh, current, aged, entries):
    return pl.pallas_call(
        lambda *refs: mix_kernel(entries, *refs),
        out_shape=jax.ShapeDtypeStruct(fresh.shape, jnp.float32),
        in_specs=[VMEM] * 4,
        out_specs=pl.BlockSpec(memory_space=pltpu.HBM),
        scratch_shapes=[
            pltpu.VMEM((3, 8, LANES), jnp.float32),
            pltpu.VMEM(fresh.shape, jnp.float32),
            pltpu.SemaphoreType.DMA((2,)),
        ],
        compiler_params=PARAMS,
        name="mix",
    )(lines, fresh, current, aged)


def per_device(
    greens,
    current,
    past_inputs,
    past_residuals,
    slot_order,
    neighbour,
    momentum_class,
    stencil_weight,
    acoustic_coupling,
    optical_coupling,
    occupation,
    phonon_shift,
):
    group_len, slice_len = greens.shape[3:]
    rows, width = current.shape[3:]
    groups = lax.axis_size("kgrp")
    parts = lax.axis_size("energy")
    own = greens.reshape(-1, group_len, slice_len)
    height = own.shape[0] * rows

    flat = current.reshape(height, width)
    old_in = past_inputs.reshape(HIST, height, width)
    old_res = past_residuals.reshape(HIST, height, width)
    scalars = (
        slot_order, momentum_class, acoustic_coupling, optical_coupling, occupation, phonon_shift
    )
    aged, residuals, old_line, gains, shifts = history(old_in, old_res, scalars, rows)
    kept, given = smear(own, neighbour, stencil_weight, groups, parts)
    meet = lambda block, m: lax.ppermute(block, "energy", [(e, e ^ m) for e in range(parts)])
    swapped = meet(given, 1)
    smeared = [meet(block, 2 * chip) for chip, block in zip(chip_order(parts), join(kept, swapped))]
    fresh, lines = residual(
        kept, swapped, smeared, flat, residuals, old_line, gains, shifts, groups * parts
    )
    lines = lax.all_to_all(lines, ("energy", "kgrp"), split_axis=0, concat_axis=0, tiled=True)
    entries = float(flat.size * groups * parts)
    return mix(lines, fresh, flat, aged, entries).reshape(current.shape)


def solution(mesh):
    return jax.shard_map(
        per_device,
        mesh=mesh,
        in_specs=(
            P(None, None, None, "kgrp", "energy"),
            P(None, None, None, ("kgrp", "energy"), None),
            P(None, None, None, None, ("kgrp", "energy"), None),
            P(None, None, None, None, ("kgrp", "energy"), None),
            P(),
            P("kgrp", None),
            P("kgrp"),
            P(),
            P(),
            P(),
            P(),
            P(),
        ),
        out_specs=P(None, None, None, ("kgrp", "energy"), None),
        check_vma=False,
    )
```

```python
import jax
import jax.numpy as jnp
from jax import lax
from jax.experimental import pallas as pl
from jax.experimental.pallas import tpu as pltpu
from jax.sharding import PartitionSpec as P

HIST = 5
LANES = 128

mixing_share = 0.5
ridge_share = 0.1

VMEM = pl.BlockSpec(memory_space=pltpu.VMEM)
SMEM = pl.BlockSpec(memory_space=pltpu.SMEM)
PARAMS = pltpu.CompilerParams(vmem_limit_bytes=16 * 1024 * 1024)

PAIRS = [(i, j) for i in range(1, HIST + 1) for j in range(i, HIST + 1)]
SPOTS = {pair: v for v, pair in enumerate(PAIRS)}
for _j in range(HIST + 1):
    SPOTS[(0, _j)] = 16 + _j


def split(value):
    high = value.astype(jnp.bfloat16)
    return high, (value - high.astype(jnp.float32)).astype(jnp.bfloat16)


def product(left, right):
    dot = lambda a, b: jnp.dot(a, b, preferred_element_type=jnp.float32)
    return dot(left[0], right[0]) + (dot(left[0], right[1]) + dot(left[1], right[0]))


def prepare_kernel(total_k, *refs):
    *blocks, neighbour_hbm, weight_hbm, stencil_hi, stencil_lo, part, late, neighbour, weight, done = refs
    fetches = [
        pltpu.make_async_copy(neighbour_hbm, neighbour, done.at[0]),
        pltpu.make_async_copy(weight_hbm, weight, done.at[1]),
    ]
    for fetch in fetches:
        fetch.start()
    late[...] = blocks[-1][...]
    _, group_len, slice_len = blocks[0].shape
    group_id = lax.axis_index("kgrp")
    parts = lax.axis_size("energy")
    rows = group_len // parts
    for fetch in fetches:
        fetch.wait()
    slots, _ = neighbour.shape
    padded = jnp.concatenate([neighbour[...], jnp.zeros((8 - slots, group_len), jnp.int32)], axis=0)
    targets = jnp.transpose(padded)
    place = lax.axis_index("energy")
    bit = 1
    while bit < parts:
        span = bit * rows
        pieces = [targets[at : at + span] for at in range(0, group_len, span)]
        flipped = [pieces[b ^ 1] for b in range(len(pieces))]
        targets = jnp.where(place & bit != 0, jnp.concatenate(flipped, axis=0), targets)
        bit *= 2
    local = targets - group_id * group_len + group_len
    local = jnp.where(local < 0, local + total_k, jnp.where(local >= total_k, local - total_k, local))
    spot = lax.broadcasted_iota(jnp.int32, (group_len, 3 * group_len), 1)
    stencil = jnp.zeros(spot.shape, jnp.float32)
    for n in range(slots):
        stencil = stencil + jnp.where(spot == local[:, n : n + 1], weight[n], 0.0)
    before, after = stencil[:, :group_len], stencil[:, 2 * group_len :]
    swapped = paired(total_k // group_len) & (group_id % 2 == 1)
    near, far = jnp.where(swapped, before, after), jnp.where(swapped, after, before)
    stencil_hi[...], stencil_lo[...] = split(jnp.concatenate([near, far], axis=1))
    centre = split(stencil[:, group_len : 2 * group_len])
    first = 0
    for own in blocks:
        for c in range(0, own.shape[0], 2):
            result = product(centre, split(jnp.concatenate([own[c], own[c + 1]], axis=1)))
            part[first + c] = result[:, :slice_len]
            part[first + c + 1] = result[:, slice_len:]
        first += own.shape[0]


def prepare(blocks, neighbour, weight, total_k):
    comps = sum(block.shape[0] for block in blocks)
    _, group_len, slice_len = blocks[0].shape
    sides = jax.ShapeDtypeStruct((group_len, 2 * group_len), jnp.bfloat16)
    size = comps * group_len * slice_len
    return pl.pallas_call(
        lambda *refs: prepare_kernel(total_k, *refs),
        out_shape=(
            sides,
            sides,
            jax.ShapeDtypeStruct((comps, group_len, slice_len), jnp.float32),
            jax.ShapeDtypeStruct(blocks[-1].shape, jnp.float32),
        ),
        in_specs=[VMEM] * len(blocks) + [pl.BlockSpec(memory_space=pltpu.HBM)] * 2,
        out_specs=(VMEM,) * 4,
        scratch_shapes=[
            pltpu.VMEM(neighbour.shape[::-1], jnp.int32),
            pltpu.SMEM(weight.shape, jnp.float32),
            pltpu.SemaphoreType.DMA((2,)),
        ],
        compiler_params=PARAMS,
        cost_estimate=pl.CostEstimate(
            flops=6 * size * group_len, bytes_accessed=8 * size, transcendentals=0
        ),
        name="prepare",
    )(*blocks, jnp.transpose(neighbour), weight)


def smeared_pairs(first, sides, stencil_hi, stencil_lo, part):
    blocks = [block for block in sides if block is not None]
    comps, group_len, slice_len = blocks[0].shape
    start = 0 if sides[0] is not None else group_len
    at = slice(start, start + len(blocks) * group_len)
    stencil = (stencil_hi[:, at], stencil_lo[:, at])
    for c in range(0, comps, 2):
        stacked = [jnp.concatenate([block[c], block[c + 1]], axis=1) for block in blocks]
        result = product(stencil, split(jnp.concatenate(stacked, axis=0)))
        for p in range(2):
            yield c + p, part[first + c + p] + result[:, p * slice_len : (p + 1) * slice_len]


def with_sides(kernel, sides):
    def body(*refs):
        refs = list(refs)
        kernel([None if side is None else refs.pop(0) for side in sides], *refs)

    return body


def smear_cost(blocks):
    size = sum(block.size for block in blocks)
    return pl.CostEstimate(
        flops=6 * size * blocks[0].shape[1], bytes_accessed=12 * size, transcendentals=0
    )


def add_sides(first, sides, stencil_hi, stencil_lo, part, after):
    def kernel(sides, stencil_hi, stencil_lo, part, *refs):
        for c, smeared in smeared_pairs(first, sides, stencil_hi, stencil_lo, part):
            refs[-1][c] = smeared

    blocks = [block for block in sides if block is not None]
    return pl.pallas_call(
        with_sides(kernel, sides),
        out_shape=jax.ShapeDtypeStruct(blocks[0].shape, jnp.float32),
        in_specs=[VMEM] * (len(blocks) + 3) + [pl.BlockSpec(memory_space=pl.ANY)] * len(after),
        out_specs=VMEM,
        compiler_params=PARAMS,
        cost_estimate=smear_cost(blocks),
        name="add_sides",
    )(*blocks, stencil_hi, stencil_lo, part, *after)


def finish_kernel(sides, stencil_hi, stencil_lo, part, *refs):
    *ready, kept, given = refs
    chips, height, _ = kept.shape
    comps = part.shape[0]
    rows = height // comps

    def place(c, smeared):
        for m in range(2 * chips):
            out = given if m % 2 else kept
            out[m // 2, c * rows : (c + 1) * rows, :] = smeared[m * rows : (m + 1) * rows]

    first = 0
    for c, smeared in smeared_pairs(0, sides, stencil_hi, stencil_lo, part):
        place(c, smeared)
        first = c + 1
    for block in ready:
        for c in range(block.shape[0]):
            place(first + c, block[c])


def finish(sides, stencil_hi, stencil_lo, part, ready, parts):
    blocks = [block for block in sides if block is not None]
    comps, group_len, slice_len = part.shape
    shape = (parts // 2, comps * group_len // parts, slice_len)
    return pl.pallas_call(
        with_sides(finish_kernel, sides),
        out_shape=[jax.ShapeDtypeStruct(shape, jnp.float32)] * 2,
        in_specs=[VMEM] * (len(blocks) + len(ready) + 3),
        out_specs=[VMEM] * 2,
        compiler_params=PARAMS,
        cost_estimate=smear_cost(blocks),
        name="finish",
    )(*blocks, stencil_hi, stencil_lo, part, *ready)


def chip_order(parts):
    chips = parts // 2
    half = chips // 2
    return [half, *range(1, half), *range(half + 1, chips)] if chips > 1 else []


def join_kernel(own, swapped, *out):
    for chip, block in zip(chip_order(2 * own.shape[0]), out):
        block[0], block[1] = own[chip], swapped[chip]


def join(own, swapped):
    chips, height, slice_len = own.shape
    shape = jax.ShapeDtypeStruct((2, height, slice_len), jnp.float32)
    return pl.pallas_call(
        join_kernel,
        out_shape=[shape] * (chips - 1),
        in_specs=[VMEM] * 2,
        out_specs=[VMEM] * (chips - 1),
        compiler_params=PARAMS,
        name="join",
    )(own, swapped)


def paired(groups):
    return groups == 4


def hold_kernel(block, _, out):
    out[...] = block[...]


def hold(block, until):
    return pl.pallas_call(
        hold_kernel,
        out_shape=jax.ShapeDtypeStruct(block.shape, jnp.float32),
        in_specs=[VMEM, pl.BlockSpec(memory_space=pl.ANY)],
        out_specs=VMEM,
        compiler_params=PARAMS,
        name="hold",
    )(block, until)


def smear(own, neighbour, weight, groups, parts):
    total_k = groups * own.shape[1]
    if not paired(groups):
        forward = [(i, (i + 1) % groups) for i in range(groups)]
        backward = [(target, source) for source, target in forward]
        near, far = lax.ppermute(own, "kgrp", backward), lax.ppermute(own, "kgrp", forward)
        return finish((near, far), *prepare([own], neighbour, weight, total_k)[:3], [], parts)
    across = lambda block, flip: lax.ppermute(block, "kgrp", [(i, i ^ flip) for i in range(groups)])
    half = own.shape[0] // 2
    head, tail = own[:half], own[half:]
    near_head = across(head, 1)
    hi, lo, part, late = prepare([head, tail], neighbour, weight, total_k)
    far_tail, near_tail, far_head = across(late, 3), across(late, 1), across(hold(near_head, late), 2)
    tail_part = add_sides(half, (near_tail, far_tail), hi, lo, part, [])
    return finish((near_head, far_head), hi, lo, part, [tail_part], parts)


def spread(values, shape):
    lane = lax.broadcasted_iota(jnp.int32, shape, 1)
    row = jnp.zeros(shape, jnp.float32)
    for spot, value in values:
        row = jnp.where(lane == spot, value, row)
    return row


def total(acc):
    return jnp.sum(jnp.sum(acc, axis=0, keepdims=True), axis=1, keepdims=True)


def history_kernel(
    total_rows, past_inputs, past_residuals, slots, classes, acoustic, optical, number, shift,
    aged, residuals, line, gains, shifts,
):
    first = lax.axis_index("energy") * total_rows
    row = lax.broadcasted_iota(jnp.int32, (8, LANES), 0) % total_rows
    coupling = jnp.zeros((8, LANES), jnp.float32)
    for i in range(total_rows):
        coupling = jnp.where(row == i, acoustic[classes[first + i]], coupling)
    gains[0] = coupling
    for m in range(2):
        gains[2 * m + 1] = jnp.full((8, LANES), optical[m] * (number[m] + 1.0))
        gains[2 * m + 2] = jnp.full((8, LANES), optical[m] * number[m])
        shifts[m] = jnp.full((8, LANES), shift[m], jnp.int32)
    _, rows, width = past_inputs.shape
    acc = [jnp.zeros((8, LANES), jnp.float32) for _ in PAIRS]
    for top in range(0, rows, 8):
        def column(t, acc, top=top):
            at = pl.ds(pl.multiple_of(t * LANES, LANES), LANES)
            old = []
            for j in range(HIST):
                res = past_residuals[slots[j], top : top + 8, at]
                aged[j, top : top + 8, at] = (
                    past_inputs[slots[j], top : top + 8, at] + mixing_share * res
                )
                residuals[j, top : top + 8, at] = res
                old.append(res)
            return [a + old[i - 1] * old[j - 1] for a, (i, j) in zip(acc, PAIRS)]
        acc = lax.fori_loop(0, width // LANES, column, acc, unroll=4)
    line[...] = spread([(v, total(a)) for v, a in enumerate(acc)], line.shape)


def history(past_inputs, past_residuals, scalars, rows):
    size = past_inputs.size
    return pl.pallas_call(
        lambda *refs: history_kernel(rows, *refs),
        out_shape=(
            jax.ShapeDtypeStruct(past_inputs.shape, jnp.float32),
            jax.ShapeDtypeStruct(past_inputs.shape, jnp.float32),
            jax.ShapeDtypeStruct((1, LANES), jnp.float32),
            jax.ShapeDtypeStruct((5, 8, LANES), jnp.float32),
            jax.ShapeDtypeStruct((2, 8, LANES), jnp.int32),
        ),
        in_specs=[VMEM, VMEM] + [SMEM] * 6,
        out_specs=(VMEM,) * 5,
        compiler_params=PARAMS,
        cost_estimate=pl.CostEstimate(flops=8 * size, bytes_accessed=12 * size, transcendentals=0),
        name="history",
    )(past_inputs, past_residuals, *scalars)


def residual_kernel(count, own, swapped, *refs):
    received = refs[:count]
    current, residuals, old_line, gains, shifts, fresh, lines, smeared = refs[count:]
    parts, height, slice_len = smeared.shape
    place = lax.axis_index("energy")
    smeared[place], smeared[place ^ 1] = own[0], swapped[0]
    for chip, block in zip(chip_order(parts), received):
        smeared[place ^ (2 * chip)], smeared[place ^ (2 * chip + 1)] = block[0], block[1]
    lane = lax.broadcasted_iota(jnp.int32, (8, slice_len), 1)
    coupling = gains[0]
    modes = []
    for m in range(2):
        wide = shifts[m]
        keeps = lane < slice_len - wide, lane >= wide
        modes.append((jnp.max(wide), *keeps, gains[2 * m + 1], gains[2 * m + 2]))
    zero = jnp.zeros((8, slice_len), jnp.float32)
    acc = [zero] * (HIST + 1)
    for top in range(0, height, 8):
        at = slice(top, top + 8)
        source = [smeared[e, at, :] for e in range(parts)]
        sigma = [coupling * x for x in source]
        lesser = top < height // 2
        for s, keep_up, keep_down, emitted, absorbed in modes:
            up = [pltpu.roll(x, slice_len - s, 1) for x in source] + [zero]
            down = [zero] + [pltpu.roll(x, s, 1) for x in source]
            gain_up, gain_down = (emitted, absorbed) if lesser else (absorbed, emitted)
            for e in range(parts):
                above = jnp.where(keep_up, up[e], up[e + 1])
                below = jnp.where(keep_down, down[e + 1], down[e])
                sigma[e] = sigma[e] + (gain_up * above + gain_down * below)
        for e in range(parts):
            where = (at, slice(e * slice_len, (e + 1) * slice_len))
            new = sigma[e] - current[where]
            fresh[where] = new
            acc[0] = acc[0] + new * new
            for j in range(HIST):
                acc[j + 1] = acc[j + 1] + new * residuals[(j,) + where]
    mine = jnp.concatenate([jnp.sum(a, axis=0, keepdims=True) for a in acc] + [zero[: 8 - HIST - 1]], axis=0)
    mine = jnp.sum(mine, axis=1, keepdims=True)
    spot = lax.broadcasted_iota(jnp.int32, (8, LANES), 0) + SPOTS[(0, 0)]
    mine = jnp.where(lax.broadcasted_iota(jnp.int32, (8, LANES), 1) == spot, mine, 0.0)
    mine = old_line[...] + jnp.sum(mine, axis=0, keepdims=True)
    lines[...] = jnp.broadcast_to(mine[None], lines.shape)


def residual(kept, swapped, smeared, current, residuals, old_line, gains, shifts, copies):
    return pl.pallas_call(
        lambda *refs: residual_kernel(len(smeared), *refs),
        out_shape=(
            jax.ShapeDtypeStruct(current.shape, jnp.float32),
            jax.ShapeDtypeStruct((copies, 1, LANES), jnp.float32),
        ),
        in_specs=[VMEM] * (len(smeared) + 7),
        out_specs=(VMEM, VMEM),
        scratch_shapes=[pltpu.VMEM((2 * kept.shape[0],) + kept.shape[1:], jnp.float32)],
        compiler_params=PARAMS,
        name="residual",
    )(kept, swapped, *smeared, current, residuals, old_line, gains, shifts)


def solve(products):
    prod = lambda i, j: products[(min(i, j), max(i, j))]
    n = HIST
    system = [
        [prod(i, j) - prod(i, j + 1) - prod(i + 1, j) + prod(i + 1, j + 1) for j in range(n)]
        for i in range(n)
    ]
    target = [prod(i, 0) - prod(i + 1, 0) for i in range(n)]
    trace = system[0][0]
    for i in range(1, n):
        trace = trace + system[i][i]
    ridge = ridge_share * trace / n + 1e-06
    for i in range(n):
        system[i][i] = system[i][i] + ridge
    inverse = [None] * n
    for k in range(n):
        inverse[k] = 1.0 / system[k][k]
        for i in range(k + 1, n):
            factor = system[k][i] * inverse[k]
            for j in range(i, n):
                system[i][j] = system[i][j] - factor * system[k][j]
            target[i] = target[i] - factor * target[k]
    gamma = [None] * n
    for k in range(n - 1, -1, -1):
        value = target[k]
        for j in range(k + 1, n):
            value = value - system[k][j] * gamma[j]
        gamma[k] = value * inverse[k]
    weights = [1.0 - gamma[0]]
    for j in range(1, n):
        weights.append(gamma[j - 1] - gamma[j])
    weights.append(gamma[n - 1])
    return weights


def mix_kernel(entries, lines, fresh, current, aged, out, wide, mixed_rows, done):
    summed = jnp.sum(lines[...], axis=0) / entries
    row = lax.broadcasted_iota(jnp.int32, (8, LANES), 0)
    lane = lax.broadcasted_iota(jnp.int32, (8, LANES), 1)
    for part in range(wide.shape[0]):
        own = jnp.where(lane == row + 8 * part, summed, 0.0)
        wide[part] = jnp.broadcast_to(jnp.sum(own, axis=1, keepdims=True), (8, LANES))
    products = {
        pair: jnp.broadcast_to(wide[spot // 8, spot % 8 : spot % 8 + 1, :], (8, LANES))
        for pair, spot in SPOTS.items()
    }
    weights = solve(products)
    rows, width = fresh.shape
    span = rows // done.shape[0]
    writes = []
    for part in range(done.shape[0]):
        for top in range(part * span, (part + 1) * span, 8):
            for left in range(0, width, LANES):
                at = (slice(top, top + 8), slice(left, left + LANES))
                mixed = weights[0] * (current[at] + mixing_share * fresh[at])
                for j in range(HIST):
                    mixed = mixed + weights[j + 1] * aged[(j,) + at]
                mixed_rows[at] = mixed
        at = pl.ds(part * span, span)
        writes.append(pltpu.make_async_copy(mixed_rows.at[at], out.at[at], done.at[part]))
        writes[-1].start()
    for write in writes:
        write.wait()


def mix(lines, fresh, current, aged, entries):
    return pl.pallas_call(
        lambda *refs: mix_kernel(entries, *refs),
        out_shape=jax.ShapeDtypeStruct(fresh.shape, jnp.float32),
        in_specs=[VMEM] * 4,
        out_specs=pl.BlockSpec(memory_space=pltpu.HBM),
        scratch_shapes=[
            pltpu.VMEM((3, 8, LANES), jnp.float32),
            pltpu.VMEM(fresh.shape, jnp.float32),
            pltpu.SemaphoreType.DMA((2,)),
        ],
        compiler_params=PARAMS,
        name="mix",
    )(lines, fresh, current, aged)


def per_device(
    greens,
    current,
    past_inputs,
    past_residuals,
    slot_order,
    neighbour,
    momentum_class,
    stencil_weight,
    acoustic_coupling,
    optical_coupling,
    occupation,
    phonon_shift,
):
    group_len, slice_len = greens.shape[3:]
    rows, width = current.shape[3:]
    groups = lax.axis_size("kgrp")
    parts = lax.axis_size("energy")
    own = greens.reshape(-1, group_len, slice_len)
    height = own.shape[0] * rows

    flat = current.reshape(height, width)
    old_in = past_inputs.reshape(HIST, height, width)
    old_res = past_residuals.reshape(HIST, height, width)
    scalars = (
        slot_order, momentum_class, acoustic_coupling, optical_coupling, occupation, phonon_shift
    )
    aged, residuals, old_line, gains, shifts = history(old_in, old_res, scalars, rows)
    kept, given = smear(own, neighbour, stencil_weight, groups, parts)
    meet = lambda block, m: lax.ppermute(block, "energy", [(e, e ^ m) for e in range(parts)])
    swapped = meet(given, 1)
    smeared = [meet(block, 2 * chip) for chip, block in zip(chip_order(parts), join(kept, swapped))]
    fresh, lines = residual(
        kept, swapped, smeared, flat, residuals, old_line, gains, shifts, groups * parts
    )
    lines = lax.all_to_all(lines, ("energy", "kgrp"), split_axis=0, concat_axis=0, tiled=True)
    entries = float(flat.size * groups * parts)
    return mix(lines, fresh, flat, aged, entries).reshape(current.shape)


def solution(mesh):
    return jax.shard_map(
        per_device,
        mesh=mesh,
        in_specs=(
            P(None, None, None, "kgrp", "energy"),
            P(None, None, None, ("kgrp", "energy"), None),
            P(None, None, None, None, ("kgrp", "energy"), None),
            P(None, None, None, None, ("kgrp", "energy"), None),
            P(),
            P("kgrp", None),
            P("kgrp"),
            P(),
            P(),
            P(),
            P(),
            P(),
        ),
        out_specs=P(None, None, None, ("kgrp", "energy"), None),
        check_vma=False,
    )
```

```python
import jax
import jax.numpy as jnp
from jax import lax
from jax.experimental import pallas as pl
from jax.experimental.pallas import tpu as pltpu
from jax.sharding import PartitionSpec as P

HIST = 5
LANES = 128

mixing_share = 0.5
ridge_share = 0.1

VMEM = pl.BlockSpec(memory_space=pltpu.VMEM)
SMEM = pl.BlockSpec(memory_space=pltpu.SMEM)
PARAMS = pltpu.CompilerParams(vmem_limit_bytes=16 * 1024 * 1024)

PAIRS = [(i, j) for i in range(1, HIST + 1) for j in range(i, HIST + 1)]
SPOTS = {pair: v for v, pair in enumerate(PAIRS)}
for _j in range(HIST + 1):
    SPOTS[(0, _j)] = 16 + _j


def split(value):
    high = value.astype(jnp.bfloat16)
    return high, (value - high.astype(jnp.float32)).astype(jnp.bfloat16)


def product(left, right):
    dot = lambda a, b: jnp.dot(a, b, preferred_element_type=jnp.float32)
    return dot(left[0], right[0]) + (dot(left[0], right[1]) + dot(left[1], right[0]))


def prepare_kernel(total_k, *refs):
    *blocks, neighbour_hbm, weight_hbm, stencil_hi, stencil_lo, part, late, neighbour, weight, done = refs
    fetches = [
        pltpu.make_async_copy(neighbour_hbm, neighbour, done.at[0]),
        pltpu.make_async_copy(weight_hbm, weight, done.at[1]),
    ]
    for fetch in fetches:
        fetch.start()
    late[...] = blocks[-1][...]
    _, group_len, slice_len = blocks[0].shape
    group_id = lax.axis_index("kgrp")
    parts = lax.axis_size("energy")
    rows = group_len // parts
    for fetch in fetches:
        fetch.wait()
    slots, _ = neighbour.shape
    padded = jnp.concatenate([neighbour[...], jnp.zeros((8 - slots, group_len), jnp.int32)], axis=0)
    targets = jnp.transpose(padded)
    place = lax.axis_index("energy")
    bit = 1
    while bit < parts:
        span = bit * rows
        pieces = [targets[at : at + span] for at in range(0, group_len, span)]
        flipped = [pieces[b ^ 1] for b in range(len(pieces))]
        targets = jnp.where(place & bit != 0, jnp.concatenate(flipped, axis=0), targets)
        bit *= 2
    local = targets - group_id * group_len + group_len
    local = jnp.where(local < 0, local + total_k, jnp.where(local >= total_k, local - total_k, local))
    spot = lax.broadcasted_iota(jnp.int32, (group_len, 3 * group_len), 1)
    stencil = jnp.zeros(spot.shape, jnp.float32)
    for n in range(slots):
        stencil = stencil + jnp.where(spot == local[:, n : n + 1], weight[n], 0.0)
    before, after = stencil[:, :group_len], stencil[:, 2 * group_len :]
    swapped = paired(total_k // group_len) & (group_id % 2 == 1)
    near, far = jnp.where(swapped, before, after), jnp.where(swapped, after, before)
    stencil_hi[...], stencil_lo[...] = split(jnp.concatenate([near, far], axis=1))
    centre = split(stencil[:, group_len : 2 * group_len])
    first = 0
    for own in blocks:
        for c in range(0, own.shape[0], 2):
            result = product(centre, split(jnp.concatenate([own[c], own[c + 1]], axis=1)))
            part[first + c] = result[:, :slice_len]
            part[first + c + 1] = result[:, slice_len:]
        first += own.shape[0]


def prepare(blocks, neighbour, weight, total_k):
    comps = sum(block.shape[0] for block in blocks)
    _, group_len, slice_len = blocks[0].shape
    sides = jax.ShapeDtypeStruct((group_len, 2 * group_len), jnp.bfloat16)
    size = comps * group_len * slice_len
    return pl.pallas_call(
        lambda *refs: prepare_kernel(total_k, *refs),
        out_shape=(
            sides,
            sides,
            jax.ShapeDtypeStruct((comps, group_len, slice_len), jnp.float32),
            jax.ShapeDtypeStruct(blocks[-1].shape, jnp.float32),
        ),
        in_specs=[VMEM] * len(blocks) + [pl.BlockSpec(memory_space=pltpu.HBM)] * 2,
        out_specs=(VMEM,) * 4,
        scratch_shapes=[
            pltpu.VMEM(neighbour.shape[::-1], jnp.int32),
            pltpu.SMEM(weight.shape, jnp.float32),
            pltpu.SemaphoreType.DMA((2,)),
        ],
        compiler_params=PARAMS,
        cost_estimate=pl.CostEstimate(
            flops=6 * size * group_len, bytes_accessed=8 * size, transcendentals=0
        ),
        name="prepare",
    )(*blocks, jnp.transpose(neighbour), weight)


def smeared_pairs(first, sides, stencil_hi, stencil_lo, part):
    blocks = [block for block in sides if block is not None]
    comps, group_len, slice_len = blocks[0].shape
    start = 0 if sides[0] is not None else group_len
    at = slice(start, start + len(blocks) * group_len)
    stencil = (stencil_hi[:, at], stencil_lo[:, at])
    for c in range(0, comps, 2):
        stacked = [jnp.concatenate([block[c], block[c + 1]], axis=1) for block in blocks]
        result = product(stencil, split(jnp.concatenate(stacked, axis=0)))
        for p in range(2):
            yield c + p, part[first + c + p] + result[:, p * slice_len : (p + 1) * slice_len]


def with_sides(kernel, sides):
    def body(*refs):
        refs = list(refs)
        kernel([None if side is None else refs.pop(0) for side in sides], *refs)

    return body


def smear_cost(blocks):
    size = sum(block.size for block in blocks)
    return pl.CostEstimate(
        flops=6 * size * blocks[0].shape[1], bytes_accessed=12 * size, transcendentals=0
    )


def add_sides(first, sides, stencil_hi, stencil_lo, part, after):
    def kernel(sides, stencil_hi, stencil_lo, part, *refs):
        for c, smeared in smeared_pairs(first, sides, stencil_hi, stencil_lo, part):
            refs[-1][c] = smeared

    blocks = [block for block in sides if block is not None]
    return pl.pallas_call(
        with_sides(kernel, sides),
        out_shape=jax.ShapeDtypeStruct(blocks[0].shape, jnp.float32),
        in_specs=[VMEM] * (len(blocks) + 3) + [pl.BlockSpec(memory_space=pl.ANY)] * len(after),
        out_specs=VMEM,
        compiler_params=PARAMS,
        cost_estimate=smear_cost(blocks),
        name="add_sides",
    )(*blocks, stencil_hi, stencil_lo, part, *after)


def finish_kernel(sides, stencil_hi, stencil_lo, part, *refs):
    *ready, kept, given = refs
    chips, height, _ = kept.shape
    comps = part.shape[0]
    rows = height // comps

    def place(c, smeared):
        for m in range(2 * chips):
            out = given if m % 2 else kept
            out[m // 2, c * rows : (c + 1) * rows, :] = smeared[m * rows : (m + 1) * rows]

    first = 0
    for c, smeared in smeared_pairs(0, sides, stencil_hi, stencil_lo, part):
        place(c, smeared)
        first = c + 1
    for block in ready:
        for c in range(block.shape[0]):
            place(first + c, block[c])


def finish(sides, stencil_hi, stencil_lo, part, ready, parts):
    blocks = [block for block in sides if block is not None]
    comps, group_len, slice_len = part.shape
    shape = (parts // 2, comps * group_len // parts, slice_len)
    return pl.pallas_call(
        with_sides(finish_kernel, sides),
        out_shape=[jax.ShapeDtypeStruct(shape, jnp.float32)] * 2,
        in_specs=[VMEM] * (len(blocks) + len(ready) + 3),
        out_specs=[VMEM] * 2,
        compiler_params=PARAMS,
        cost_estimate=smear_cost(blocks),
        name="finish",
    )(*blocks, stencil_hi, stencil_lo, part, *ready)


def chip_order(parts):
    chips = parts // 2
    half = chips // 2
    return [half, *range(1, half), *range(half + 1, chips)] if chips > 1 else []


def join_kernel(own, swapped, *out):
    for chip, block in zip(chip_order(2 * own.shape[0]), out):
        block[0], block[1] = own[chip], swapped[chip]


def join(own, swapped):
    chips, height, slice_len = own.shape
    shape = jax.ShapeDtypeStruct((2, height, slice_len), jnp.float32)
    return pl.pallas_call(
        join_kernel,
        out_shape=[shape] * (chips - 1),
        in_specs=[VMEM] * 2,
        out_specs=[VMEM] * (chips - 1),
        compiler_params=PARAMS,
        name="join",
    )(own, swapped)


def paired(groups):
    return groups == 4


def halves_kernel(source, head, tail, done):
    fetches = []
    for n, half in enumerate((head, tail)):
        rows = pl.ds(n * head.shape[0], half.shape[0])
        fetches.append(pltpu.make_async_copy(source.at[rows], half, done.at[n]))
        fetches[-1].start()
    for fetch in fetches:
        fetch.wait()


def halves(source):
    shape = jax.ShapeDtypeStruct((source.shape[0] // 2,) + source.shape[1:], source.dtype)
    return pl.pallas_call(
        halves_kernel,
        out_shape=(shape, shape),
        in_specs=[pl.BlockSpec(memory_space=pltpu.HBM)],
        out_specs=(VMEM, VMEM),
        scratch_shapes=[pltpu.SemaphoreType.DMA((2,))],
        compiler_params=PARAMS,
        name="halves",
    )(source)


def hold_kernel(block, _, out):
    out[...] = block[...]


def hold(block, until):
    return pl.pallas_call(
        hold_kernel,
        out_shape=jax.ShapeDtypeStruct(block.shape, jnp.float32),
        in_specs=[VMEM, pl.BlockSpec(memory_space=pl.ANY)],
        out_specs=VMEM,
        compiler_params=PARAMS,
        name="hold",
    )(block, until)


def smear(own, neighbour, weight, groups, parts):
    total_k = groups * own.shape[1]
    if not paired(groups):
        forward = [(i, (i + 1) % groups) for i in range(groups)]
        backward = [(target, source) for source, target in forward]
        near, far = lax.ppermute(own, "kgrp", backward), lax.ppermute(own, "kgrp", forward)
        return finish((near, far), *prepare([own], neighbour, weight, total_k)[:3], [], parts)
    across = lambda block, flip: lax.ppermute(block, "kgrp", [(i, i ^ flip) for i in range(groups)])
    half = own.shape[0] // 2
    head, tail = halves(pltpu.with_memory_space_constraint(own, pltpu.HBM))
    near_head, far_tail = across(head, 1), across(tail, 3)
    hi, lo, part, late = prepare([head, tail], neighbour, weight, total_k)
    near_tail, far_head = across(late, 1), across(hold(near_head, late), 2)
    tail_part = add_sides(half, (near_tail, far_tail), hi, lo, part, [])
    return finish((near_head, far_head), hi, lo, part, [tail_part], parts)


def spread(values, shape):
    lane = lax.broadcasted_iota(jnp.int32, shape, 1)
    row = jnp.zeros(shape, jnp.float32)
    for spot, value in values:
        row = jnp.where(lane == spot, value, row)
    return row


def total(acc):
    return jnp.sum(jnp.sum(acc, axis=0, keepdims=True), axis=1, keepdims=True)


def history_kernel(
    total_rows, past_inputs, past_residuals, slots, classes, acoustic, optical, number, shift,
    aged, residuals, line, gains, shifts,
):
    first = lax.axis_index("energy") * total_rows
    row = lax.broadcasted_iota(jnp.int32, (8, LANES), 0) % total_rows
    coupling = jnp.zeros((8, LANES), jnp.float32)
    for i in range(total_rows):
        coupling = jnp.where(row == i, acoustic[classes[first + i]], coupling)
    gains[0] = coupling
    for m in range(2):
        gains[2 * m + 1] = jnp.full((8, LANES), optical[m] * (number[m] + 1.0))
        gains[2 * m + 2] = jnp.full((8, LANES), optical[m] * number[m])
        shifts[m] = jnp.full((8, LANES), shift[m], jnp.int32)
    _, rows, width = past_inputs.shape
    acc = [jnp.zeros((8, LANES), jnp.float32) for _ in PAIRS]
    for top in range(0, rows, 8):
        def column(t, acc, top=top):
            at = pl.ds(pl.multiple_of(t * LANES, LANES), LANES)
            old = []
            for j in range(HIST):
                res = past_residuals[slots[j], top : top + 8, at]
                aged[j, top : top + 8, at] = (
                    past_inputs[slots[j], top : top + 8, at] + mixing_share * res
                )
                residuals[j, top : top + 8, at] = res
                old.append(res)
            return [a + old[i - 1] * old[j - 1] for a, (i, j) in zip(acc, PAIRS)]
        acc = lax.fori_loop(0, width // LANES, column, acc, unroll=4)
    line[...] = spread([(v, total(a)) for v, a in enumerate(acc)], line.shape)


def history(past_inputs, past_residuals, scalars, rows):
    size = past_inputs.size
    return pl.pallas_call(
        lambda *refs: history_kernel(rows, *refs),
        out_shape=(
            jax.ShapeDtypeStruct(past_inputs.shape, jnp.float32),
            jax.ShapeDtypeStruct(past_inputs.shape, jnp.float32),
            jax.ShapeDtypeStruct((1, LANES), jnp.float32),
            jax.ShapeDtypeStruct((5, 8, LANES), jnp.float32),
            jax.ShapeDtypeStruct((2, 8, LANES), jnp.int32),
        ),
        in_specs=[VMEM, VMEM] + [SMEM] * 6,
        out_specs=(VMEM,) * 5,
        compiler_params=PARAMS,
        cost_estimate=pl.CostEstimate(flops=8 * size, bytes_accessed=12 * size, transcendentals=0),
        name="history",
    )(past_inputs, past_residuals, *scalars)


def residual_kernel(count, own, swapped, *refs):
    received = refs[:count]
    current, residuals, old_line, gains, shifts, fresh, lines, smeared = refs[count:]
    parts, height, slice_len = smeared.shape
    place = lax.axis_index("energy")
    smeared[place], smeared[place ^ 1] = own[0], swapped[0]
    for chip, block in zip(chip_order(parts), received):
        smeared[place ^ (2 * chip)], smeared[place ^ (2 * chip + 1)] = block[0], block[1]
    lane = lax.broadcasted_iota(jnp.int32, (8, slice_len), 1)
    coupling = gains[0]
    modes = []
    for m in range(2):
        wide = shifts[m]
        keeps = lane < slice_len - wide, lane >= wide
        modes.append((jnp.max(wide), *keeps, gains[2 * m + 1], gains[2 * m + 2]))
    zero = jnp.zeros((8, slice_len), jnp.float32)
    acc = [zero] * (HIST + 1)
    for top in range(0, height, 8):
        at = slice(top, top + 8)
        source = [smeared[e, at, :] for e in range(parts)]
        sigma = [coupling * x for x in source]
        lesser = top < height // 2
        for s, keep_up, keep_down, emitted, absorbed in modes:
            up = [pltpu.roll(x, slice_len - s, 1) for x in source] + [zero]
            down = [zero] + [pltpu.roll(x, s, 1) for x in source]
            gain_up, gain_down = (emitted, absorbed) if lesser else (absorbed, emitted)
            for e in range(parts):
                above = jnp.where(keep_up, up[e], up[e + 1])
                below = jnp.where(keep_down, down[e + 1], down[e])
                sigma[e] = sigma[e] + (gain_up * above + gain_down * below)
        for e in range(parts):
            where = (at, slice(e * slice_len, (e + 1) * slice_len))
            new = sigma[e] - current[where]
            fresh[where] = new
            acc[0] = acc[0] + new * new
            for j in range(HIST):
                acc[j + 1] = acc[j + 1] + new * residuals[(j,) + where]
    mine = jnp.concatenate([jnp.sum(a, axis=0, keepdims=True) for a in acc] + [zero[: 8 - HIST - 1]], axis=0)
    mine = jnp.sum(mine, axis=1, keepdims=True)
    spot = lax.broadcasted_iota(jnp.int32, (8, LANES), 0) + SPOTS[(0, 0)]
    mine = jnp.where(lax.broadcasted_iota(jnp.int32, (8, LANES), 1) == spot, mine, 0.0)
    mine = old_line[...] + jnp.sum(mine, axis=0, keepdims=True)
    lines[...] = jnp.broadcast_to(mine[None], lines.shape)


def residual(kept, swapped, smeared, current, residuals, old_line, gains, shifts, copies):
    return pl.pallas_call(
        lambda *refs: residual_kernel(len(smeared), *refs),
        out_shape=(
            jax.ShapeDtypeStruct(current.shape, jnp.float32),
            jax.ShapeDtypeStruct((copies, 1, LANES), jnp.float32),
        ),
        in_specs=[VMEM] * (len(smeared) + 7),
        out_specs=(VMEM, VMEM),
        scratch_shapes=[pltpu.VMEM((2 * kept.shape[0],) + kept.shape[1:], jnp.float32)],
        compiler_params=PARAMS,
        name="residual",
    )(kept, swapped, *smeared, current, residuals, old_line, gains, shifts)


def solve(products):
    prod = lambda i, j: products[(min(i, j), max(i, j))]
    n = HIST
    system = [
        [prod(i, j) - prod(i, j + 1) - prod(i + 1, j) + prod(i + 1, j + 1) for j in range(n)]
        for i in range(n)
    ]
    target = [prod(i, 0) - prod(i + 1, 0) for i in range(n)]
    trace = system[0][0]
    for i in range(1, n):
        trace = trace + system[i][i]
    ridge = ridge_share * trace / n + 1e-06
    for i in range(n):
        system[i][i] = system[i][i] + ridge
    inverse = [None] * n
    for k in range(n):
        inverse[k] = 1.0 / system[k][k]
        for i in range(k + 1, n):
            factor = system[k][i] * inverse[k]
            for j in range(i, n):
                system[i][j] = system[i][j] - factor * system[k][j]
            target[i] = target[i] - factor * target[k]
    gamma = [None] * n
    for k in range(n - 1, -1, -1):
        value = target[k]
        for j in range(k + 1, n):
            value = value - system[k][j] * gamma[j]
        gamma[k] = value * inverse[k]
    weights = [1.0 - gamma[0]]
    for j in range(1, n):
        weights.append(gamma[j - 1] - gamma[j])
    weights.append(gamma[n - 1])
    return weights


def mix_kernel(entries, lines, fresh, current, aged, out, wide, mixed_rows, done):
    summed = jnp.sum(lines[...], axis=0) / entries
    row = lax.broadcasted_iota(jnp.int32, (8, LANES), 0)
    lane = lax.broadcasted_iota(jnp.int32, (8, LANES), 1)
    for part in range(wide.shape[0]):
        own = jnp.where(lane == row + 8 * part, summed, 0.0)
        wide[part] = jnp.broadcast_to(jnp.sum(own, axis=1, keepdims=True), (8, LANES))
    products = {
        pair: jnp.broadcast_to(wide[spot // 8, spot % 8 : spot % 8 + 1, :], (8, LANES))
        for pair, spot in SPOTS.items()
    }
    weights = solve(products)
    rows, width = fresh.shape
    span = rows // done.shape[0]
    writes = []
    for part in range(done.shape[0]):
        for top in range(part * span, (part + 1) * span, 8):
            for left in range(0, width, LANES):
                at = (slice(top, top + 8), slice(left, left + LANES))
                mixed = weights[0] * (current[at] + mixing_share * fresh[at])
                for j in range(HIST):
                    mixed = mixed + weights[j + 1] * aged[(j,) + at]
                mixed_rows[at] = mixed
        at = pl.ds(part * span, span)
        writes.append(pltpu.make_async_copy(mixed_rows.at[at], out.at[at], done.at[part]))
        writes[-1].start()
    for write in writes:
        write.wait()


def mix(lines, fresh, current, aged, entries):
    return pl.pallas_call(
        lambda *refs: mix_kernel(entries, *refs),
        out_shape=jax.ShapeDtypeStruct(fresh.shape, jnp.float32),
        in_specs=[VMEM] * 4,
        out_specs=pl.BlockSpec(memory_space=pltpu.HBM),
        scratch_shapes=[
            pltpu.VMEM((3, 8, LANES), jnp.float32),
            pltpu.VMEM(fresh.shape, jnp.float32),
            pltpu.SemaphoreType.DMA((2,)),
        ],
        compiler_params=PARAMS,
        name="mix",
    )(lines, fresh, current, aged)


def per_device(
    greens,
    current,
    past_inputs,
    past_residuals,
    slot_order,
    neighbour,
    momentum_class,
    stencil_weight,
    acoustic_coupling,
    optical_coupling,
    occupation,
    phonon_shift,
):
    group_len, slice_len = greens.shape[3:]
    rows, width = current.shape[3:]
    groups = lax.axis_size("kgrp")
    parts = lax.axis_size("energy")
    own = greens.reshape(-1, group_len, slice_len)
    height = own.shape[0] * rows

    flat = current.reshape(height, width)
    old_in = past_inputs.reshape(HIST, height, width)
    old_res = past_residuals.reshape(HIST, height, width)
    scalars = (
        slot_order, momentum_class, acoustic_coupling, optical_coupling, occupation, phonon_shift
    )
    aged, residuals, old_line, gains, shifts = history(old_in, old_res, scalars, rows)
    kept, given = smear(own, neighbour, stencil_weight, groups, parts)
    meet = lambda block, m: lax.ppermute(block, "energy", [(e, e ^ m) for e in range(parts)])
    swapped = meet(given, 1)
    smeared = [meet(block, 2 * chip) for chip, block in zip(chip_order(parts), join(kept, swapped))]
    fresh, lines = residual(
        kept, swapped, smeared, flat, residuals, old_line, gains, shifts, groups * parts
    )
    lines = lax.all_to_all(lines, ("energy", "kgrp"), split_axis=0, concat_axis=0, tiled=True)
    entries = float(flat.size * groups * parts)
    return mix(lines, fresh, flat, aged, entries).reshape(current.shape)


def solution(mesh):
    return jax.shard_map(
        per_device,
        mesh=mesh,
        in_specs=(
            P(None, None, None, "kgrp", "energy"),
            P(None, None, None, ("kgrp", "energy"), None),
            P(None, None, None, None, ("kgrp", "energy"), None),
            P(None, None, None, None, ("kgrp", "energy"), None),
            P(),
            P("kgrp", None),
            P("kgrp"),
            P(),
            P(),
            P(),
            P(),
            P(),
        ),
        out_specs=P(None, None, None, ("kgrp", "energy"), None),
        check_vma=False,
    )
```

```python
import jax
import jax.numpy as jnp
from jax import lax
from jax.experimental import pallas as pl
from jax.experimental.pallas import tpu as pltpu
from jax.sharding import PartitionSpec as P

HIST = 5
LANES = 128

mixing_share = 0.5
ridge_share = 0.1

VMEM = pl.BlockSpec(memory_space=pltpu.VMEM)
SMEM = pl.BlockSpec(memory_space=pltpu.SMEM)
PARAMS = pltpu.CompilerParams(vmem_limit_bytes=16 * 1024 * 1024)

PAIRS = [(i, j) for i in range(1, HIST + 1) for j in range(i, HIST + 1)]
SPOTS = {pair: v for v, pair in enumerate(PAIRS)}
for _j in range(HIST + 1):
    SPOTS[(0, _j)] = 16 + _j


def split(value):
    high = value.astype(jnp.bfloat16)
    return high, (value - high.astype(jnp.float32)).astype(jnp.bfloat16)


def product(left, right):
    dot = lambda a, b: jnp.dot(a, b, preferred_element_type=jnp.float32)
    return dot(left[0], right[0]) + (dot(left[0], right[1]) + dot(left[1], right[0]))


def prepare_kernel(total_k, *refs):
    *blocks, neighbour_hbm, weight_hbm, stencil_hi, stencil_lo, part, late, neighbour, weight, done = refs
    fetches = [
        pltpu.make_async_copy(neighbour_hbm, neighbour, done.at[0]),
        pltpu.make_async_copy(weight_hbm, weight, done.at[1]),
    ]
    for fetch in fetches:
        fetch.start()
    late[...] = blocks[-1][...]
    _, group_len, slice_len = blocks[0].shape
    group_id = lax.axis_index("kgrp")
    parts = lax.axis_size("energy")
    rows = group_len // parts
    for fetch in fetches:
        fetch.wait()
    slots, _ = neighbour.shape
    padded = jnp.concatenate([neighbour[...], jnp.zeros((8 - slots, group_len), jnp.int32)], axis=0)
    targets = jnp.transpose(padded)
    place = lax.axis_index("energy")
    bit = 1
    while bit < parts:
        span = bit * rows
        pieces = [targets[at : at + span] for at in range(0, group_len, span)]
        flipped = [pieces[b ^ 1] for b in range(len(pieces))]
        targets = jnp.where(place & bit != 0, jnp.concatenate(flipped, axis=0), targets)
        bit *= 2
    local = targets - group_id * group_len + group_len
    local = jnp.where(local < 0, local + total_k, jnp.where(local >= total_k, local - total_k, local))
    spot = lax.broadcasted_iota(jnp.int32, (group_len, 3 * group_len), 1)
    stencil = jnp.zeros(spot.shape, jnp.float32)
    for n in range(slots):
        stencil = stencil + jnp.where(spot == local[:, n : n + 1], weight[n], 0.0)
    before, after = stencil[:, :group_len], stencil[:, 2 * group_len :]
    swapped = paired(total_k // group_len) & (group_id % 2 == 1)
    near, far = jnp.where(swapped, before, after), jnp.where(swapped, after, before)
    stencil_hi[...], stencil_lo[...] = split(jnp.concatenate([near, far], axis=1))
    centre = split(stencil[:, group_len : 2 * group_len])
    first = 0
    for own in blocks:
        for c in range(0, own.shape[0], 2):
            result = product(centre, split(jnp.concatenate([own[c], own[c + 1]], axis=1)))
            part[first + c] = result[:, :slice_len]
            part[first + c + 1] = result[:, slice_len:]
        first += own.shape[0]


def prepare(blocks, neighbour, weight, total_k):
    comps = sum(block.shape[0] for block in blocks)
    _, group_len, slice_len = blocks[0].shape
    sides = jax.ShapeDtypeStruct((group_len, 2 * group_len), jnp.bfloat16)
    size = comps * group_len * slice_len
    return pl.pallas_call(
        lambda *refs: prepare_kernel(total_k, *refs),
        out_shape=(
            sides,
            sides,
            jax.ShapeDtypeStruct((comps, group_len, slice_len), jnp.float32),
            jax.ShapeDtypeStruct(blocks[-1].shape, jnp.float32),
        ),
        in_specs=[VMEM] * len(blocks) + [pl.BlockSpec(memory_space=pltpu.HBM)] * 2,
        out_specs=(VMEM,) * 4,
        scratch_shapes=[
            pltpu.VMEM(neighbour.shape[::-1], jnp.int32),
            pltpu.SMEM(weight.shape, jnp.float32),
            pltpu.SemaphoreType.DMA((2,)),
        ],
        compiler_params=PARAMS,
        cost_estimate=pl.CostEstimate(
            flops=6 * size * group_len, bytes_accessed=8 * size, transcendentals=0
        ),
        name="prepare",
    )(*blocks, jnp.transpose(neighbour), weight)


def smeared_pairs(first, sides, stencil_hi, stencil_lo, part):
    blocks = [block for block in sides if block is not None]
    comps, group_len, slice_len = blocks[0].shape
    start = 0 if sides[0] is not None else group_len
    at = slice(start, start + len(blocks) * group_len)
    stencil = (stencil_hi[:, at], stencil_lo[:, at])
    for c in range(0, comps, 2):
        stacked = [jnp.concatenate([block[c], block[c + 1]], axis=1) for block in blocks]
        result = product(stencil, split(jnp.concatenate(stacked, axis=0)))
        for p in range(2):
            yield c + p, part[first + c + p] + result[:, p * slice_len : (p + 1) * slice_len]


def with_sides(kernel, sides):
    def body(*refs):
        refs = list(refs)
        kernel([None if side is None else refs.pop(0) for side in sides], *refs)

    return body


def smear_cost(blocks):
    size = sum(block.size for block in blocks)
    return pl.CostEstimate(
        flops=6 * size * blocks[0].shape[1], bytes_accessed=12 * size, transcendentals=0
    )


def add_sides(first, sides, stencil_hi, stencil_lo, part, after):
    def kernel(sides, stencil_hi, stencil_lo, part, *refs):
        for c, smeared in smeared_pairs(first, sides, stencil_hi, stencil_lo, part):
            refs[-1][c] = smeared

    blocks = [block for block in sides if block is not None]
    return pl.pallas_call(
        with_sides(kernel, sides),
        out_shape=jax.ShapeDtypeStruct(blocks[0].shape, jnp.float32),
        in_specs=[VMEM] * (len(blocks) + 3) + [pl.BlockSpec(memory_space=pl.ANY)] * len(after),
        out_specs=VMEM,
        compiler_params=PARAMS,
        cost_estimate=smear_cost(blocks),
        name="add_sides",
    )(*blocks, stencil_hi, stencil_lo, part, *after)


def finish_kernel(sides, stencil_hi, stencil_lo, part, *refs):
    *ready, kept, given = refs
    chips, height, _ = kept.shape
    comps = part.shape[0]
    rows = height // comps

    def place(c, smeared):
        for m in range(2 * chips):
            out = given if m % 2 else kept
            out[m // 2, c * rows : (c + 1) * rows, :] = smeared[m * rows : (m + 1) * rows]

    first = 0
    for c, smeared in smeared_pairs(0, sides, stencil_hi, stencil_lo, part):
        place(c, smeared)
        first = c + 1
    for block in ready:
        for c in range(block.shape[0]):
            place(first + c, block[c])


def finish(sides, stencil_hi, stencil_lo, part, ready, parts):
    blocks = [block for block in sides if block is not None]
    comps, group_len, slice_len = part.shape
    shape = (parts // 2, comps * group_len // parts, slice_len)
    return pl.pallas_call(
        with_sides(finish_kernel, sides),
        out_shape=[jax.ShapeDtypeStruct(shape, jnp.float32)] * 2,
        in_specs=[VMEM] * (len(blocks) + len(ready) + 3),
        out_specs=[VMEM] * 2,
        compiler_params=PARAMS,
        cost_estimate=smear_cost(blocks),
        name="finish",
    )(*blocks, stencil_hi, stencil_lo, part, *ready)


def chip_order(parts):
    chips = parts // 2
    half = chips // 2
    return [half, *range(1, half), *range(half + 1, chips)] if chips > 1 else []


def join_kernel(own, swapped, *out):
    for chip, block in zip(chip_order(2 * own.shape[0]), out):
        block[0], block[1] = own[chip], swapped[chip]


def join(own, swapped):
    chips, height, slice_len = own.shape
    shape = jax.ShapeDtypeStruct((2, height, slice_len), jnp.float32)
    return pl.pallas_call(
        join_kernel,
        out_shape=[shape] * (chips - 1),
        in_specs=[VMEM] * 2,
        out_specs=[VMEM] * (chips - 1),
        compiler_params=PARAMS,
        name="join",
    )(own, swapped)


def paired(groups):
    return groups == 4


def hold_kernel(block, _, out):
    out[...] = block[...]


def hold(block, until):
    return pl.pallas_call(
        hold_kernel,
        out_shape=jax.ShapeDtypeStruct(block.shape, jnp.float32),
        in_specs=[VMEM, pl.BlockSpec(memory_space=pl.ANY)],
        out_specs=VMEM,
        compiler_params=PARAMS,
        name="hold",
    )(block, until)


def smear(own, neighbour, weight, groups, parts):
    total_k = groups * own.shape[1]
    if not paired(groups):
        forward = [(i, (i + 1) % groups) for i in range(groups)]
        backward = [(target, source) for source, target in forward]
        near, far = lax.ppermute(own, "kgrp", backward), lax.ppermute(own, "kgrp", forward)
        return finish((near, far), *prepare([own], neighbour, weight, total_k)[:3], [], parts)
    across = lambda block, flip: lax.ppermute(block, "kgrp", [(i, i ^ flip) for i in range(groups)])
    half = own.shape[0] // 2
    head, tail = own[:half], own[half:]
    near_head, far_tail = across(head, 1), across(tail, 3)
    hi, lo, part, late = prepare([head, tail], neighbour, weight, total_k)
    near_tail, far_head = across(late, 1), across(hold(near_head, late), 2)
    tail_part = add_sides(half, (near_tail, far_tail), hi, lo, part, [])
    return finish((near_head, far_head), hi, lo, part, [tail_part], parts)


def spread(values, shape):
    lane = lax.broadcasted_iota(jnp.int32, shape, 1)
    row = jnp.zeros(shape, jnp.float32)
    for spot, value in values:
        row = jnp.where(lane == spot, value, row)
    return row


def total(acc):
    return jnp.sum(jnp.sum(acc, axis=0, keepdims=True), axis=1, keepdims=True)


def history_kernel(
    total_rows, past_inputs, past_residuals, slots, classes, acoustic, optical, number, shift,
    aged, residuals, line, gains, shifts,
):
    first = lax.axis_index("energy") * total_rows
    row = lax.broadcasted_iota(jnp.int32, (8, LANES), 0) % total_rows
    coupling = jnp.zeros((8, LANES), jnp.float32)
    for i in range(total_rows):
        coupling = jnp.where(row == i, acoustic[classes[first + i]], coupling)
    gains[0] = coupling
    for m in range(2):
        gains[2 * m + 1] = jnp.full((8, LANES), optical[m] * (number[m] + 1.0))
        gains[2 * m + 2] = jnp.full((8, LANES), optical[m] * number[m])
        shifts[m] = jnp.full((8, LANES), shift[m], jnp.int32)
    _, rows, width = past_inputs.shape
    acc = [jnp.zeros((8, LANES), jnp.float32) for _ in PAIRS]
    for top in range(0, rows, 8):
        def column(t, acc, top=top):
            at = pl.ds(pl.multiple_of(t * LANES, LANES), LANES)
            old = []
            for j in range(HIST):
                res = past_residuals[slots[j], top : top + 8, at]
                aged[j, top : top + 8, at] = (
                    past_inputs[slots[j], top : top + 8, at] + mixing_share * res
                )
                residuals[j, top : top + 8, at] = res
                old.append(res)
            return [a + old[i - 1] * old[j - 1] for a, (i, j) in zip(acc, PAIRS)]
        acc = lax.fori_loop(0, width // LANES, column, acc, unroll=4)
    line[...] = spread([(v, total(a)) for v, a in enumerate(acc)], line.shape)


def history(past_inputs, past_residuals, scalars, rows):
    size = past_inputs.size
    return pl.pallas_call(
        lambda *refs: history_kernel(rows, *refs),
        out_shape=(
            jax.ShapeDtypeStruct(past_inputs.shape, jnp.float32),
            jax.ShapeDtypeStruct(past_inputs.shape, jnp.float32),
            jax.ShapeDtypeStruct((1, LANES), jnp.float32),
            jax.ShapeDtypeStruct((5, 8, LANES), jnp.float32),
            jax.ShapeDtypeStruct((2, 8, LANES), jnp.int32),
        ),
        in_specs=[VMEM, VMEM] + [SMEM] * 6,
        out_specs=(VMEM,) * 5,
        compiler_params=PARAMS,
        cost_estimate=pl.CostEstimate(flops=8 * size, bytes_accessed=12 * size, transcendentals=0),
        name="history",
    )(past_inputs, past_residuals, *scalars)


def residual_kernel(count, own, swapped, *refs):
    received = refs[:count]
    current, residuals, old_line, gains, shifts, fresh, lines, smeared = refs[count:]
    parts, height, slice_len = smeared.shape
    place = lax.axis_index("energy")
    smeared[place], smeared[place ^ 1] = own[0], swapped[0]
    for chip, block in zip(chip_order(parts), received):
        smeared[place ^ (2 * chip)], smeared[place ^ (2 * chip + 1)] = block[0], block[1]
    lane = lax.broadcasted_iota(jnp.int32, (8, slice_len), 1)
    coupling = gains[0]
    modes = []
    for m in range(2):
        wide = shifts[m]
        keeps = lane < slice_len - wide, lane >= wide
        modes.append((jnp.max(wide), *keeps, gains[2 * m + 1], gains[2 * m + 2]))
    zero = jnp.zeros((8, slice_len), jnp.float32)
    acc = [zero] * (HIST + 1)
    for top in range(0, height, 8):
        at = slice(top, top + 8)
        source = [smeared[e, at, :] for e in range(parts)]
        sigma = [coupling * x for x in source]
        lesser = top < height // 2
        for s, keep_up, keep_down, emitted, absorbed in modes:
            up = [pltpu.roll(x, slice_len - s, 1) for x in source] + [zero]
            down = [zero] + [pltpu.roll(x, s, 1) for x in source]
            gain_up, gain_down = (emitted, absorbed) if lesser else (absorbed, emitted)
            for e in range(parts):
                above = jnp.where(keep_up, up[e], up[e + 1])
                below = jnp.where(keep_down, down[e + 1], down[e])
                sigma[e] = sigma[e] + (gain_up * above + gain_down * below)
        for e in range(parts):
            where = (at, slice(e * slice_len, (e + 1) * slice_len))
            new = sigma[e] - current[where]
            fresh[where] = current[where] + mixing_share * new
            acc[0] = acc[0] + new * new
            for j in range(HIST):
                acc[j + 1] = acc[j + 1] + new * residuals[(j,) + where]
    mine = jnp.concatenate([jnp.sum(a, axis=0, keepdims=True) for a in acc] + [zero[: 8 - HIST - 1]], axis=0)
    mine = jnp.sum(mine, axis=1, keepdims=True)
    spot = lax.broadcasted_iota(jnp.int32, (8, LANES), 0) + SPOTS[(0, 0)]
    mine = jnp.where(lax.broadcasted_iota(jnp.int32, (8, LANES), 1) == spot, mine, 0.0)
    mine = old_line[...] + jnp.sum(mine, axis=0, keepdims=True)
    lines[...] = jnp.broadcast_to(mine[None], lines.shape)


def residual(kept, swapped, smeared, current, residuals, old_line, gains, shifts, copies):
    return pl.pallas_call(
        lambda *refs: residual_kernel(len(smeared), *refs),
        out_shape=(
            jax.ShapeDtypeStruct(current.shape, jnp.float32),
            jax.ShapeDtypeStruct((copies, 1, LANES), jnp.float32),
        ),
        in_specs=[VMEM] * (len(smeared) + 7),
        out_specs=(VMEM, VMEM),
        scratch_shapes=[pltpu.VMEM((2 * kept.shape[0],) + kept.shape[1:], jnp.float32)],
        compiler_params=PARAMS,
        name="residual",
    )(kept, swapped, *smeared, current, residuals, old_line, gains, shifts)


def solve(products):
    prod = lambda i, j: products[(min(i, j), max(i, j))]
    n = HIST
    system = [
        [prod(i, j) - prod(i, j + 1) - prod(i + 1, j) + prod(i + 1, j + 1) for j in range(n)]
        for i in range(n)
    ]
    target = [prod(i, 0) - prod(i + 1, 0) for i in range(n)]
    trace = system[0][0]
    for i in range(1, n):
        trace = trace + system[i][i]
    ridge = (ridge_share / n) * trace + 1e-06
    for i in range(n):
        system[i][i] = system[i][i] + ridge
    for k in range(n):
        inverse = 1.0 / system[k][k]
        row = [system[k][j] * inverse if j > k else None for j in range(n)]
        value = target[k] * inverse
        for i in range(n):
            if i == k:
                continue
            for j in range(k + 1, n):
                system[i][j] = system[i][j] - system[i][k] * row[j]
            target[i] = target[i] - system[i][k] * value
        system[k] = row
        target[k] = value
    gamma = target
    weights = [1.0 - gamma[0]]
    for j in range(1, n):
        weights.append(gamma[j - 1] - gamma[j])
    weights.append(gamma[n - 1])
    return weights


def mix_kernel(entries, lines, fresh, aged, out, wide, mixed_rows, done):
    summed = jnp.sum(lines[...], axis=0) * (1.0 / entries)
    row = lax.broadcasted_iota(jnp.int32, (8, LANES), 0)
    lane = lax.broadcasted_iota(jnp.int32, (8, LANES), 1)
    for part in range(wide.shape[0]):
        own = jnp.where(lane == row + 8 * part, summed, 0.0)
        wide[part] = jnp.broadcast_to(jnp.sum(own, axis=1, keepdims=True), (8, LANES))
    products = {
        pair: jnp.broadcast_to(wide[spot // 8, spot % 8 : spot % 8 + 1, :], (8, LANES))
        for pair, spot in SPOTS.items()
    }
    weights = solve(products)
    rows, width = fresh.shape
    span = rows // done.shape[0]
    writes = []
    for part in range(done.shape[0]):
        for top in range(part * span, (part + 1) * span, 8):
            for left in range(0, width, LANES):
                at = (slice(top, top + 8), slice(left, left + LANES))
                mixed = weights[0] * fresh[at]
                for j in range(HIST):
                    mixed = mixed + weights[j + 1] * aged[(j,) + at]
                mixed_rows[at] = mixed
        at = pl.ds(part * span, span)
        writes.append(pltpu.make_async_copy(mixed_rows.at[at], out.at[at], done.at[part]))
        writes[-1].start()
    for write in writes:
        write.wait()


def mix(lines, fresh, aged, entries):
    return pl.pallas_call(
        lambda *refs: mix_kernel(entries, *refs),
        out_shape=jax.ShapeDtypeStruct(fresh.shape, jnp.float32),
        in_specs=[VMEM] * 3,
        out_specs=pl.BlockSpec(memory_space=pltpu.HBM),
        scratch_shapes=[
            pltpu.VMEM((3, 8, LANES), jnp.float32),
            pltpu.VMEM(fresh.shape, jnp.float32),
            pltpu.SemaphoreType.DMA((min(4, fresh.shape[0] // 8),)),
        ],
        compiler_params=PARAMS,
        name="mix",
    )(lines, fresh, aged)


def per_device(
    greens,
    current,
    past_inputs,
    past_residuals,
    slot_order,
    neighbour,
    momentum_class,
    stencil_weight,
    acoustic_coupling,
    optical_coupling,
    occupation,
    phonon_shift,
):
    group_len, slice_len = greens.shape[3:]
    rows, width = current.shape[3:]
    groups = lax.axis_size("kgrp")
    parts = lax.axis_size("energy")
    own = greens.reshape(-1, group_len, slice_len)
    height = own.shape[0] * rows

    flat = current.reshape(height, width)
    old_in = past_inputs.reshape(HIST, height, width)
    old_res = past_residuals.reshape(HIST, height, width)
    scalars = (
        slot_order, momentum_class, acoustic_coupling, optical_coupling, occupation, phonon_shift
    )
    aged, residuals, old_line, gains, shifts = history(old_in, old_res, scalars, rows)
    kept, given = smear(own, neighbour, stencil_weight, groups, parts)
    meet = lambda block, m: lax.ppermute(block, "energy", [(e, e ^ m) for e in range(parts)])
    swapped = meet(given, 1)
    smeared = [meet(block, 2 * chip) for chip, block in zip(chip_order(parts), join(kept, swapped))]
    fresh, lines = residual(
        kept, swapped, smeared, flat, residuals, old_line, gains, shifts, groups * parts
    )
    lines = lax.all_to_all(lines, ("energy", "kgrp"), split_axis=0, concat_axis=0, tiled=True)
    entries = float(flat.size * groups * parts)
    return mix(lines, fresh, aged, entries).reshape(current.shape)


def solution(mesh):
    return jax.shard_map(
        per_device,
        mesh=mesh,
        in_specs=(
            P(None, None, None, "kgrp", "energy"),
            P(None, None, None, ("kgrp", "energy"), None),
            P(None, None, None, None, ("kgrp", "energy"), None),
            P(None, None, None, None, ("kgrp", "energy"), None),
            P(),
            P("kgrp", None),
            P("kgrp"),
            P(),
            P(),
            P(),
            P(),
            P(),
        ),
        out_specs=P(None, None, None, ("kgrp", "energy"), None),
        check_vma=False,
    )
```

```python
import jax
import jax.numpy as jnp
from jax import lax
from jax.experimental import pallas as pl
from jax.experimental.pallas import tpu as pltpu
from jax.sharding import PartitionSpec as P

HIST = 5
LANES = 128

mixing_share = 0.5
ridge_share = 0.1

VMEM = pl.BlockSpec(memory_space=pltpu.VMEM)
SMEM = pl.BlockSpec(memory_space=pltpu.SMEM)
PARAMS = pltpu.CompilerParams(vmem_limit_bytes=16 * 1024 * 1024)

PAIRS = [(i, j) for i in range(1, HIST + 1) for j in range(i, HIST + 1)]
SPOTS = {pair: v for v, pair in enumerate(PAIRS)}
for _j in range(HIST + 1):
    SPOTS[(0, _j)] = 16 + _j


def split(value):
    high = value.astype(jnp.bfloat16)
    return high, (value - high.astype(jnp.float32)).astype(jnp.bfloat16)


def product(left, right):
    dot = lambda a, b: jnp.dot(a, b, preferred_element_type=jnp.float32)
    return dot(left[0], right[0]) + (dot(left[0], right[1]) + dot(left[1], right[0]))


def prepare_kernel(total_k, *refs):
    *blocks, neighbour_hbm, weight_hbm, stencil_hi, stencil_lo, part, late, neighbour, weight, done = refs
    fetches = [
        pltpu.make_async_copy(neighbour_hbm, neighbour, done.at[0]),
        pltpu.make_async_copy(weight_hbm, weight, done.at[1]),
    ]
    for fetch in fetches:
        fetch.start()
    late[...] = blocks[-1][...]
    _, group_len, slice_len = blocks[0].shape
    group_id = lax.axis_index("kgrp")
    parts = lax.axis_size("energy")
    rows = group_len // parts
    for fetch in fetches:
        fetch.wait()
    slots, _ = neighbour.shape
    padded = jnp.concatenate([neighbour[...], jnp.zeros((8 - slots, group_len), jnp.int32)], axis=0)
    targets = jnp.transpose(padded)
    place = lax.axis_index("energy")
    bit = 1
    while bit < parts:
        span = bit * rows
        pieces = [targets[at : at + span] for at in range(0, group_len, span)]
        flipped = [pieces[b ^ 1] for b in range(len(pieces))]
        targets = jnp.where(place & bit != 0, jnp.concatenate(flipped, axis=0), targets)
        bit *= 2
    local = targets - group_id * group_len + group_len
    local = jnp.where(local < 0, local + total_k, jnp.where(local >= total_k, local - total_k, local))
    spot = lax.broadcasted_iota(jnp.int32, (group_len, 3 * group_len), 1)
    stencil = jnp.zeros(spot.shape, jnp.float32)
    for n in range(slots):
        stencil = stencil + jnp.where(spot == local[:, n : n + 1], weight[n], 0.0)
    before, after = stencil[:, :group_len], stencil[:, 2 * group_len :]
    swapped = paired(total_k // group_len) & (group_id % 2 == 1)
    near, far = jnp.where(swapped, before, after), jnp.where(swapped, after, before)
    stencil_hi[...], stencil_lo[...] = split(jnp.concatenate([near, far], axis=1))
    centre = split(stencil[:, group_len : 2 * group_len])
    first = 0
    for own in blocks:
        for c in range(0, own.shape[0], 2):
            result = product(centre, split(jnp.concatenate([own[c], own[c + 1]], axis=1)))
            part[first + c] = result[:, :slice_len]
            part[first + c + 1] = result[:, slice_len:]
        first += own.shape[0]


def prepare(blocks, neighbour, weight, total_k):
    comps = sum(block.shape[0] for block in blocks)
    _, group_len, slice_len = blocks[0].shape
    sides = jax.ShapeDtypeStruct((group_len, 2 * group_len), jnp.bfloat16)
    size = comps * group_len * slice_len
    return pl.pallas_call(
        lambda *refs: prepare_kernel(total_k, *refs),
        out_shape=(
            sides,
            sides,
            jax.ShapeDtypeStruct((comps, group_len, slice_len), jnp.float32),
            jax.ShapeDtypeStruct(blocks[-1].shape, jnp.float32),
        ),
        in_specs=[VMEM] * len(blocks) + [pl.BlockSpec(memory_space=pltpu.HBM)] * 2,
        out_specs=(VMEM,) * 4,
        scratch_shapes=[
            pltpu.VMEM(neighbour.shape[::-1], jnp.int32),
            pltpu.SMEM(weight.shape, jnp.float32),
            pltpu.SemaphoreType.DMA((2,)),
        ],
        compiler_params=PARAMS,
        cost_estimate=pl.CostEstimate(
            flops=6 * size * group_len, bytes_accessed=8 * size, transcendentals=0
        ),
        name="prepare",
    )(*blocks, jnp.transpose(neighbour), weight)


def smeared_pairs(first, sides, stencil_hi, stencil_lo, part):
    blocks = [block for block in sides if block is not None]
    comps, group_len, slice_len = blocks[0].shape
    start = 0 if sides[0] is not None else group_len
    at = slice(start, start + len(blocks) * group_len)
    stencil = (stencil_hi[:, at], stencil_lo[:, at])
    for c in range(0, comps, 2):
        stacked = [jnp.concatenate([block[c], block[c + 1]], axis=1) for block in blocks]
        result = product(stencil, split(jnp.concatenate(stacked, axis=0)))
        for p in range(2):
            yield c + p, part[first + c + p] + result[:, p * slice_len : (p + 1) * slice_len]


def with_sides(kernel, sides):
    def body(*refs):
        refs = list(refs)
        kernel([None if side is None else refs.pop(0) for side in sides], *refs)

    return body


def smear_cost(blocks):
    size = sum(block.size for block in blocks)
    return pl.CostEstimate(
        flops=6 * size * blocks[0].shape[1], bytes_accessed=12 * size, transcendentals=0
    )


def add_sides(first, sides, stencil_hi, stencil_lo, part, after):
    def kernel(sides, stencil_hi, stencil_lo, part, *refs):
        for c, smeared in smeared_pairs(first, sides, stencil_hi, stencil_lo, part):
            refs[-1][c] = smeared

    blocks = [block for block in sides if block is not None]
    return pl.pallas_call(
        with_sides(kernel, sides),
        out_shape=jax.ShapeDtypeStruct(blocks[0].shape, jnp.float32),
        in_specs=[VMEM] * (len(blocks) + 3) + [pl.BlockSpec(memory_space=pl.ANY)] * len(after),
        out_specs=VMEM,
        compiler_params=PARAMS,
        cost_estimate=smear_cost(blocks),
        name="add_sides",
    )(*blocks, stencil_hi, stencil_lo, part, *after)


def finish_kernel(sides, stencil_hi, stencil_lo, part, *refs):
    *ready, kept, given = refs
    chips, height, _ = kept.shape
    comps = part.shape[0]
    rows = height // comps

    def place(c, smeared):
        for m in range(2 * chips):
            out = given if m % 2 else kept
            out[m // 2, c * rows : (c + 1) * rows, :] = smeared[m * rows : (m + 1) * rows]

    first = 0
    for c, smeared in smeared_pairs(0, sides, stencil_hi, stencil_lo, part):
        place(c, smeared)
        first = c + 1
    for block in ready:
        for c in range(block.shape[0]):
            place(first + c, block[c])


def finish(sides, stencil_hi, stencil_lo, part, ready, parts):
    blocks = [block for block in sides if block is not None]
    comps, group_len, slice_len = part.shape
    shape = (parts // 2, comps * group_len // parts, slice_len)
    return pl.pallas_call(
        with_sides(finish_kernel, sides),
        out_shape=[jax.ShapeDtypeStruct(shape, jnp.float32)] * 2,
        in_specs=[VMEM] * (len(blocks) + len(ready) + 3),
        out_specs=[VMEM] * 2,
        compiler_params=PARAMS,
        cost_estimate=smear_cost(blocks),
        name="finish",
    )(*blocks, stencil_hi, stencil_lo, part, *ready)


def chip_order(parts):
    chips = parts // 2
    half = chips // 2
    return [*range(half + 1, chips), *range(1, half), half] if chips > 1 else []


def join_kernel(own, swapped, *out):
    for chip, block in zip(chip_order(2 * own.shape[0]), out):
        block[0], block[1] = own[chip], swapped[chip]


def join(own, swapped):
    chips, height, slice_len = own.shape
    shape = jax.ShapeDtypeStruct((2, height, slice_len), jnp.float32)
    return pl.pallas_call(
        join_kernel,
        out_shape=[shape] * (chips - 1),
        in_specs=[VMEM] * 2,
        out_specs=[VMEM] * (chips - 1),
        compiler_params=PARAMS,
        name="join",
    )(own, swapped)


def paired(groups):
    return groups == 4


def hold_kernel(block, _, out):
    out[...] = block[...]


def hold(block, until):
    return pl.pallas_call(
        hold_kernel,
        out_shape=jax.ShapeDtypeStruct(block.shape, jnp.float32),
        in_specs=[VMEM, pl.BlockSpec(memory_space=pl.ANY)],
        out_specs=VMEM,
        compiler_params=PARAMS,
        name="hold",
    )(block, until)


def smear(own, neighbour, weight, groups, parts):
    total_k = groups * own.shape[1]
    if not paired(groups):
        forward = [(i, (i + 1) % groups) for i in range(groups)]
        backward = [(target, source) for source, target in forward]
        near, far = lax.ppermute(own, "kgrp", backward), lax.ppermute(own, "kgrp", forward)
        return finish((near, far), *prepare([own], neighbour, weight, total_k)[:3], [], parts)
    across = lambda block, flip: lax.ppermute(block, "kgrp", [(i, i ^ flip) for i in range(groups)])
    half = own.shape[0] // 2
    head, tail = own[:half], own[half:]
    near_head, far_tail = across(head, 1), across(tail, 3)
    hi, lo, part, late = prepare([head, tail], neighbour, weight, total_k)
    near_tail, far_head = across(late, 1), across(hold(near_head, late), 2)
    tail_part = add_sides(half, (near_tail, far_tail), hi, lo, part, [])
    return finish((near_head, far_head), hi, lo, part, [tail_part], parts)


def spread(values, shape):
    lane = lax.broadcasted_iota(jnp.int32, shape, 1)
    row = jnp.zeros(shape, jnp.float32)
    for spot, value in values:
        row = jnp.where(lane == spot, value, row)
    return row


def total(acc):
    return jnp.sum(jnp.sum(acc, axis=0, keepdims=True), axis=1, keepdims=True)


def history_kernel(
    total_rows, past_inputs, past_residuals, slots, classes, acoustic, optical, number, shift,
    aged, residuals, line, gains, shifts,
):
    first = lax.axis_index("energy") * total_rows
    row = lax.broadcasted_iota(jnp.int32, (8, LANES), 0) % total_rows
    coupling = jnp.zeros((8, LANES), jnp.float32)
    for i in range(total_rows):
        coupling = jnp.where(row == i, acoustic[classes[first + i]], coupling)
    gains[0] = coupling
    for m in range(2):
        gains[2 * m + 1] = jnp.full((8, LANES), optical[m] * (number[m] + 1.0))
        gains[2 * m + 2] = jnp.full((8, LANES), optical[m] * number[m])
        shifts[m] = jnp.full((8, LANES), shift[m], jnp.int32)
    _, rows, width = past_inputs.shape
    acc = [jnp.zeros((8, LANES), jnp.float32) for _ in PAIRS]
    for top in range(0, rows, 8):
        def column(t, acc, top=top):
            at = pl.ds(pl.multiple_of(t * LANES, LANES), LANES)
            old = []
            for j in range(HIST):
                res = past_residuals[slots[j], top : top + 8, at]
                aged[j, top : top + 8, at] = (
                    past_inputs[slots[j], top : top + 8, at] + mixing_share * res
                )
                residuals[j, top : top + 8, at] = res
                old.append(res)
            return [a + old[i - 1] * old[j - 1] for a, (i, j) in zip(acc, PAIRS)]
        acc = lax.fori_loop(0, width // LANES, column, acc, unroll=4)
    line[...] = spread([(v, total(a)) for v, a in enumerate(acc)], line.shape)


def history(past_inputs, past_residuals, scalars, rows):
    size = past_inputs.size
    return pl.pallas_call(
        lambda *refs: history_kernel(rows, *refs),
        out_shape=(
            jax.ShapeDtypeStruct(past_inputs.shape, jnp.float32),
            jax.ShapeDtypeStruct(past_inputs.shape, jnp.float32),
            jax.ShapeDtypeStruct((1, LANES), jnp.float32),
            jax.ShapeDtypeStruct((5, 8, LANES), jnp.float32),
            jax.ShapeDtypeStruct((2, 8, LANES), jnp.int32),
        ),
        in_specs=[VMEM, VMEM] + [SMEM] * 6,
        out_specs=(VMEM,) * 5,
        compiler_params=PARAMS,
        cost_estimate=pl.CostEstimate(flops=8 * size, bytes_accessed=12 * size, transcendentals=0),
        name="history",
    )(past_inputs, past_residuals, *scalars)


def residual_kernel(count, own, swapped, *refs):
    received = refs[:count]
    current, residuals, old_line, gains, shifts, fresh, lines, smeared = refs[count:]
    parts, height, slice_len = smeared.shape
    place = lax.axis_index("energy")
    smeared[place], smeared[place ^ 1] = own[0], swapped[0]
    for chip, block in zip(chip_order(parts), received):
        smeared[place ^ (2 * chip)], smeared[place ^ (2 * chip + 1)] = block[0], block[1]
    lane = lax.broadcasted_iota(jnp.int32, (8, slice_len), 1)
    coupling = gains[0]
    modes = []
    for m in range(2):
        wide = shifts[m]
        keeps = lane < slice_len - wide, lane >= wide
        modes.append((jnp.max(wide), *keeps, gains[2 * m + 1], gains[2 * m + 2]))
    zero = jnp.zeros((8, slice_len), jnp.float32)
    acc = [zero] * (HIST + 1)
    for top in range(0, height, 8):
        at = slice(top, top + 8)
        source = [smeared[e, at, :] for e in range(parts)]
        sigma = [coupling * x for x in source]
        lesser = top < height // 2
        for s, keep_up, keep_down, emitted, absorbed in modes:
            up = [pltpu.roll(x, slice_len - s, 1) for x in source] + [zero]
            down = [zero] + [pltpu.roll(x, s, 1) for x in source]
            gain_up, gain_down = (emitted, absorbed) if lesser else (absorbed, emitted)
            for e in range(parts):
                above = jnp.where(keep_up, up[e], up[e + 1])
                below = jnp.where(keep_down, down[e + 1], down[e])
                sigma[e] = sigma[e] + (gain_up * above + gain_down * below)
        for e in range(parts):
            where = (at, slice(e * slice_len, (e + 1) * slice_len))
            new = sigma[e] - current[where]
            fresh[where] = current[where] + mixing_share * new
            acc[0] = acc[0] + new * new
            for j in range(HIST):
                acc[j + 1] = acc[j + 1] + new * residuals[(j,) + where]
    mine = jnp.concatenate([jnp.sum(a, axis=0, keepdims=True) for a in acc] + [zero[: 8 - HIST - 1]], axis=0)
    mine = jnp.sum(mine, axis=1, keepdims=True)
    spot = lax.broadcasted_iota(jnp.int32, (8, LANES), 0) + SPOTS[(0, 0)]
    mine = jnp.where(lax.broadcasted_iota(jnp.int32, (8, LANES), 1) == spot, mine, 0.0)
    mine = old_line[...] + jnp.sum(mine, axis=0, keepdims=True)
    lines[...] = jnp.broadcast_to(mine[None], lines.shape)


def residual(kept, swapped, smeared, current, residuals, old_line, gains, shifts, copies):
    return pl.pallas_call(
        lambda *refs: residual_kernel(len(smeared), *refs),
        out_shape=(
            jax.ShapeDtypeStruct(current.shape, jnp.float32),
            jax.ShapeDtypeStruct((copies, 1, LANES), jnp.float32),
        ),
        in_specs=[VMEM] * (len(smeared) + 7),
        out_specs=(VMEM, VMEM),
        scratch_shapes=[pltpu.VMEM((2 * kept.shape[0],) + kept.shape[1:], jnp.float32)],
        compiler_params=PARAMS,
        name="residual",
    )(kept, swapped, *smeared, current, residuals, old_line, gains, shifts)


def solve(products):
    prod = lambda i, j: products[(min(i, j), max(i, j))]
    n = HIST
    system = [
        [prod(i, j) - prod(i, j + 1) - prod(i + 1, j) + prod(i + 1, j + 1) for j in range(n)]
        for i in range(n)
    ]
    target = [prod(i, 0) - prod(i + 1, 0) for i in range(n)]
    trace = system[0][0]
    for i in range(1, n):
        trace = trace + system[i][i]
    ridge = (ridge_share / n) * trace + 1e-06
    for i in range(n):
        system[i][i] = system[i][i] + ridge
    for k in range(n):
        inverse = 1.0 / system[k][k]
        row = [system[k][j] * inverse if j > k else None for j in range(n)]
        value = target[k] * inverse
        for i in range(n):
            if i == k:
                continue
            for j in range(k + 1, n):
                system[i][j] = system[i][j] - system[i][k] * row[j]
            target[i] = target[i] - system[i][k] * value
        system[k] = row
        target[k] = value
    gamma = target
    weights = [1.0 - gamma[0]]
    for j in range(1, n):
        weights.append(gamma[j - 1] - gamma[j])
    weights.append(gamma[n - 1])
    return weights


def mix_kernel(entries, lines, fresh, aged, out, wide, mixed_rows, done):
    summed = jnp.sum(lines[...], axis=0) * (1.0 / entries)
    row = lax.broadcasted_iota(jnp.int32, (8, LANES), 0)
    lane = lax.broadcasted_iota(jnp.int32, (8, LANES), 1)
    for part in range(wide.shape[0]):
        own = jnp.where(lane == row + 8 * part, summed, 0.0)
        wide[part] = jnp.broadcast_to(jnp.sum(own, axis=1, keepdims=True), (8, LANES))
    products = {
        pair: jnp.broadcast_to(wide[spot // 8, spot % 8 : spot % 8 + 1, :], (8, LANES))
        for pair, spot in SPOTS.items()
    }
    weights = solve(products)
    rows, width = fresh.shape
    span = rows // done.shape[0]
    writes = []
    for part in range(done.shape[0]):
        for top in range(part * span, (part + 1) * span, 8):
            for left in range(0, width, LANES):
                at = (slice(top, top + 8), slice(left, left + LANES))
                mixed = weights[0] * fresh[at]
                for j in range(HIST):
                    mixed = mixed + weights[j + 1] * aged[(j,) + at]
                mixed_rows[at] = mixed
        at = pl.ds(part * span, span)
        writes.append(pltpu.make_async_copy(mixed_rows.at[at], out.at[at], done.at[part]))
        writes[-1].start()
    for write in writes:
        write.wait()


def mix(lines, fresh, aged, entries):
    return pl.pallas_call(
        lambda *refs: mix_kernel(entries, *refs),
        out_shape=jax.ShapeDtypeStruct(fresh.shape, jnp.float32),
        in_specs=[VMEM] * 3,
        out_specs=pl.BlockSpec(memory_space=pltpu.HBM),
        scratch_shapes=[
            pltpu.VMEM((3, 8, LANES), jnp.float32),
            pltpu.VMEM(fresh.shape, jnp.float32),
            pltpu.SemaphoreType.DMA((min(4, fresh.shape[0] // 8),)),
        ],
        compiler_params=PARAMS,
        name="mix",
    )(lines, fresh, aged)


def per_device(
    greens,
    current,
    past_inputs,
    past_residuals,
    slot_order,
    neighbour,
    momentum_class,
    stencil_weight,
    acoustic_coupling,
    optical_coupling,
    occupation,
    phonon_shift,
):
    group_len, slice_len = greens.shape[3:]
    rows, width = current.shape[3:]
    groups = lax.axis_size("kgrp")
    parts = lax.axis_size("energy")
    own = greens.reshape(-1, group_len, slice_len)
    height = own.shape[0] * rows

    flat = current.reshape(height, width)
    old_in = past_inputs.reshape(HIST, height, width)
    old_res = past_residuals.reshape(HIST, height, width)
    scalars = (
        slot_order, momentum_class, acoustic_coupling, optical_coupling, occupation, phonon_shift
    )
    aged, residuals, old_line, gains, shifts = history(old_in, old_res, scalars, rows)
    kept, given = smear(own, neighbour, stencil_weight, groups, parts)
    meet = lambda block, m: lax.ppermute(block, "energy", [(e, e ^ m) for e in range(parts)])
    swapped = meet(given, 1)
    smeared = [meet(block, 2 * chip) for chip, block in zip(chip_order(parts), join(kept, swapped))]
    fresh, lines = residual(
        kept, swapped, smeared, flat, residuals, old_line, gains, shifts, groups * parts
    )
    lines = lax.all_to_all(lines, ("energy", "kgrp"), split_axis=0, concat_axis=0, tiled=True)
    entries = float(flat.size * groups * parts)
    return mix(lines, fresh, aged, entries).reshape(current.shape)


def solution(mesh):
    return jax.shard_map(
        per_device,
        mesh=mesh,
        in_specs=(
            P(None, None, None, "kgrp", "energy"),
            P(None, None, None, ("kgrp", "energy"), None),
            P(None, None, None, None, ("kgrp", "energy"), None),
            P(None, None, None, None, ("kgrp", "energy"), None),
            P(),
            P("kgrp", None),
            P("kgrp"),
            P(),
            P(),
            P(),
            P(),
            P(),
        ),
        out_specs=P(None, None, None, ("kgrp", "energy"), None),
        check_vma=False,
    )
```

```python
import jax
import jax.numpy as jnp
from jax import lax
from jax.experimental import pallas as pl
from jax.experimental.pallas import tpu as pltpu
from jax.sharding import PartitionSpec as P

HIST = 5
LANES = 128

mixing_share = 0.5
ridge_share = 0.1

VMEM = pl.BlockSpec(memory_space=pltpu.VMEM)
SMEM = pl.BlockSpec(memory_space=pltpu.SMEM)
PARAMS = pltpu.CompilerParams(vmem_limit_bytes=16 * 1024 * 1024)

PAIRS = [(i, j) for i in range(1, HIST + 1) for j in range(i, HIST + 1)]
SPOTS = {pair: v for v, pair in enumerate(PAIRS)}
for _j in range(HIST + 1):
    SPOTS[(0, _j)] = 16 + _j


def split(value):
    high = value.astype(jnp.bfloat16)
    return high, (value - high.astype(jnp.float32)).astype(jnp.bfloat16)


def product(left, right):
    dot = lambda a, b: jnp.dot(a, b, preferred_element_type=jnp.float32)
    return dot(left[0], right[0]) + (dot(left[0], right[1]) + dot(left[1], right[0]))


def prepare_kernel(total_k, *refs):
    *blocks, neighbour_hbm, weight_hbm, stencil_hi, stencil_lo, part, late, neighbour, weight, done = refs
    fetches = [
        pltpu.make_async_copy(neighbour_hbm, neighbour, done.at[0]),
        pltpu.make_async_copy(weight_hbm, weight, done.at[1]),
    ]
    for fetch in fetches:
        fetch.start()
    late[...] = blocks[-1][...]
    _, group_len, slice_len = blocks[0].shape
    group_id = lax.axis_index("kgrp")
    parts = lax.axis_size("energy")
    rows = group_len // parts
    for fetch in fetches:
        fetch.wait()
    slots, _ = neighbour.shape
    padded = jnp.concatenate([neighbour[...], jnp.zeros((8 - slots, group_len), jnp.int32)], axis=0)
    targets = jnp.transpose(padded)
    place = lax.axis_index("energy")
    bit = 1
    while bit < parts:
        span = bit * rows
        pieces = [targets[at : at + span] for at in range(0, group_len, span)]
        flipped = [pieces[b ^ 1] for b in range(len(pieces))]
        targets = jnp.where(place & bit != 0, jnp.concatenate(flipped, axis=0), targets)
        bit *= 2
    local = targets - group_id * group_len + group_len
    local = jnp.where(local < 0, local + total_k, jnp.where(local >= total_k, local - total_k, local))
    spot = lax.broadcasted_iota(jnp.int32, (group_len, 3 * group_len), 1)
    stencil = jnp.zeros(spot.shape, jnp.float32)
    for n in range(slots):
        stencil = stencil + jnp.where(spot == local[:, n : n + 1], weight[n], 0.0)
    before, after = stencil[:, :group_len], stencil[:, 2 * group_len :]
    swapped = paired(total_k // group_len) & (group_id % 2 == 1)
    near, far = jnp.where(swapped, before, after), jnp.where(swapped, after, before)
    stencil_hi[...], stencil_lo[...] = split(jnp.concatenate([near, far], axis=1))
    centre = split(stencil[:, group_len : 2 * group_len])
    first = 0
    for own in blocks:
        for c in range(0, own.shape[0], 2):
            result = product(centre, split(jnp.concatenate([own[c], own[c + 1]], axis=1)))
            part[first + c] = result[:, :slice_len]
            part[first + c + 1] = result[:, slice_len:]
        first += own.shape[0]


def prepare(blocks, neighbour, weight, total_k):
    comps = sum(block.shape[0] for block in blocks)
    _, group_len, slice_len = blocks[0].shape
    sides = jax.ShapeDtypeStruct((group_len, 2 * group_len), jnp.bfloat16)
    size = comps * group_len * slice_len
    return pl.pallas_call(
        lambda *refs: prepare_kernel(total_k, *refs),
        out_shape=(
            sides,
            sides,
            jax.ShapeDtypeStruct((comps, group_len, slice_len), jnp.float32),
            jax.ShapeDtypeStruct(blocks[-1].shape, jnp.float32),
        ),
        in_specs=[VMEM] * len(blocks) + [pl.BlockSpec(memory_space=pltpu.HBM)] * 2,
        out_specs=(VMEM,) * 4,
        scratch_shapes=[
            pltpu.VMEM(neighbour.shape[::-1], jnp.int32),
            pltpu.SMEM(weight.shape, jnp.float32),
            pltpu.SemaphoreType.DMA((2,)),
        ],
        compiler_params=PARAMS,
        cost_estimate=pl.CostEstimate(
            flops=6 * size * group_len, bytes_accessed=8 * size, transcendentals=0
        ),
        name="prepare",
    )(*blocks, jnp.transpose(neighbour), weight)


def smeared_pairs(first, sides, stencil_hi, stencil_lo, part):
    blocks = [block for block in sides if block is not None]
    comps, group_len, slice_len = blocks[0].shape
    start = 0 if sides[0] is not None else group_len
    at = slice(start, start + len(blocks) * group_len)
    stencil = (stencil_hi[:, at], stencil_lo[:, at])
    for c in range(0, comps, 2):
        stacked = [jnp.concatenate([block[c], block[c + 1]], axis=1) for block in blocks]
        result = product(stencil, split(jnp.concatenate(stacked, axis=0)))
        for p in range(2):
            yield c + p, part[first + c + p] + result[:, p * slice_len : (p + 1) * slice_len]


def with_sides(kernel, sides):
    def body(*refs):
        refs = list(refs)
        kernel([None if side is None else refs.pop(0) for side in sides], *refs)

    return body


def smear_cost(blocks):
    size = sum(block.size for block in blocks)
    return pl.CostEstimate(
        flops=6 * size * blocks[0].shape[1], bytes_accessed=12 * size, transcendentals=0
    )


def add_sides(first, sides, stencil_hi, stencil_lo, part, after):
    def kernel(sides, stencil_hi, stencil_lo, part, *refs):
        for c, smeared in smeared_pairs(first, sides, stencil_hi, stencil_lo, part):
            refs[-1][c] = smeared

    blocks = [block for block in sides if block is not None]
    return pl.pallas_call(
        with_sides(kernel, sides),
        out_shape=jax.ShapeDtypeStruct(blocks[0].shape, jnp.float32),
        in_specs=[VMEM] * (len(blocks) + 3) + [pl.BlockSpec(memory_space=pl.ANY)] * len(after),
        out_specs=VMEM,
        compiler_params=PARAMS,
        cost_estimate=smear_cost(blocks),
        name="add_sides",
    )(*blocks, stencil_hi, stencil_lo, part, *after)


def finish_kernel(sides, stencil_hi, stencil_lo, part, *refs):
    *ready, kept, given = refs
    chips, height, _ = kept.shape
    comps = part.shape[0]
    rows = height // comps

    def place(c, smeared):
        for m in range(2 * chips):
            out = given if m % 2 else kept
            out[m // 2, c * rows : (c + 1) * rows, :] = smeared[m * rows : (m + 1) * rows]

    first = 0
    for c, smeared in smeared_pairs(0, sides, stencil_hi, stencil_lo, part):
        place(c, smeared)
        first = c + 1
    for block in ready:
        for c in range(block.shape[0]):
            place(first + c, block[c])


def finish(sides, stencil_hi, stencil_lo, part, ready, parts):
    blocks = [block for block in sides if block is not None]
    comps, group_len, slice_len = part.shape
    shape = (parts // 2, comps * group_len // parts, slice_len)
    return pl.pallas_call(
        with_sides(finish_kernel, sides),
        out_shape=[jax.ShapeDtypeStruct(shape, jnp.float32)] * 2,
        in_specs=[VMEM] * (len(blocks) + len(ready) + 3),
        out_specs=[VMEM] * 2,
        compiler_params=PARAMS,
        cost_estimate=smear_cost(blocks),
        name="finish",
    )(*blocks, stencil_hi, stencil_lo, part, *ready)


def chip_order(parts):
    chips = parts // 2
    half = chips // 2
    return [*range(1, half), *range(half + 1, chips), half] if chips > 1 else []


def join_kernel(own, swapped, *out):
    for chip, block in zip(chip_order(2 * own.shape[0]), out):
        block[0], block[1] = own[chip], swapped[chip]


def join(own, swapped):
    chips, height, slice_len = own.shape
    shape = jax.ShapeDtypeStruct((2, height, slice_len), jnp.float32)
    return pl.pallas_call(
        join_kernel,
        out_shape=[shape] * (chips - 1),
        in_specs=[VMEM] * 2,
        out_specs=[VMEM] * (chips - 1),
        compiler_params=PARAMS,
        name="join",
    )(own, swapped)


def paired(groups):
    return groups == 4


def hold_kernel(block, _, out):
    out[...] = block[...]


def hold(block, until):
    return pl.pallas_call(
        hold_kernel,
        out_shape=jax.ShapeDtypeStruct(block.shape, jnp.float32),
        in_specs=[VMEM, pl.BlockSpec(memory_space=pl.ANY)],
        out_specs=VMEM,
        compiler_params=PARAMS,
        name="hold",
    )(block, until)


def smear(own, neighbour, weight, groups, parts):
    total_k = groups * own.shape[1]
    if not paired(groups):
        forward = [(i, (i + 1) % groups) for i in range(groups)]
        backward = [(target, source) for source, target in forward]
        near, far = lax.ppermute(own, "kgrp", backward), lax.ppermute(own, "kgrp", forward)
        return finish((near, far), *prepare([own], neighbour, weight, total_k)[:3], [], parts)
    across = lambda block, flip: lax.ppermute(block, "kgrp", [(i, i ^ flip) for i in range(groups)])
    half = own.shape[0] // 2
    head, tail = own[:half], own[half:]
    near_head, far_tail = across(head, 1), across(tail, 3)
    hi, lo, part, late = prepare([head, tail], neighbour, weight, total_k)
    near_tail, far_head = across(late, 1), across(hold(near_head, late), 2)
    tail_part = add_sides(half, (near_tail, far_tail), hi, lo, part, [])
    return finish((near_head, far_head), hi, lo, part, [tail_part], parts)


def spread(values, shape):
    lane = lax.broadcasted_iota(jnp.int32, shape, 1)
    row = jnp.zeros(shape, jnp.float32)
    for spot, value in values:
        row = jnp.where(lane == spot, value, row)
    return row


def total(acc):
    return jnp.sum(jnp.sum(acc, axis=0, keepdims=True), axis=1, keepdims=True)


def history_kernel(
    total_rows, past_inputs, past_residuals, slots, classes, acoustic, optical, number, shift,
    aged, residuals, line, gains, shifts,
):
    first = lax.axis_index("energy") * total_rows
    row = lax.broadcasted_iota(jnp.int32, (8, LANES), 0) % total_rows
    coupling = jnp.zeros((8, LANES), jnp.float32)
    for i in range(total_rows):
        coupling = jnp.where(row == i, acoustic[classes[first + i]], coupling)
    gains[0] = coupling
    for m in range(2):
        gains[2 * m + 1] = jnp.full((8, LANES), optical[m] * (number[m] + 1.0))
        gains[2 * m + 2] = jnp.full((8, LANES), optical[m] * number[m])
        shifts[m] = jnp.full((8, LANES), shift[m], jnp.int32)
    _, rows, width = past_inputs.shape
    acc = [jnp.zeros((8, LANES), jnp.float32) for _ in PAIRS]
    for top in range(0, rows, 8):
        def column(t, acc, top=top):
            at = pl.ds(pl.multiple_of(t * LANES, LANES), LANES)
            old = []
            for j in range(HIST):
                res = past_residuals[slots[j], top : top + 8, at]
                aged[j, top : top + 8, at] = (
                    past_inputs[slots[j], top : top + 8, at] + mixing_share * res
                )
                residuals[j, top : top + 8, at] = res
                old.append(res)
            return [a + old[i - 1] * old[j - 1] for a, (i, j) in zip(acc, PAIRS)]
        acc = lax.fori_loop(0, width // LANES, column, acc, unroll=4)
    line[...] = spread([(v, total(a)) for v, a in enumerate(acc)], line.shape)


def history(past_inputs, past_residuals, scalars, rows):
    size = past_inputs.size
    return pl.pallas_call(
        lambda *refs: history_kernel(rows, *refs),
        out_shape=(
            jax.ShapeDtypeStruct(past_inputs.shape, jnp.float32),
            jax.ShapeDtypeStruct(past_inputs.shape, jnp.float32),
            jax.ShapeDtypeStruct((1, LANES), jnp.float32),
            jax.ShapeDtypeStruct((5, 8, LANES), jnp.float32),
            jax.ShapeDtypeStruct((2, 8, LANES), jnp.int32),
        ),
        in_specs=[VMEM, VMEM] + [SMEM] * 6,
        out_specs=(VMEM,) * 5,
        compiler_params=PARAMS,
        cost_estimate=pl.CostEstimate(flops=8 * size, bytes_accessed=12 * size, transcendentals=0),
        name="history",
    )(past_inputs, past_residuals, *scalars)


def residual_kernel(count, own, swapped, *refs):
    received = refs[:count]
    current, residuals, old_line, gains, shifts, fresh, lines, smeared = refs[count:]
    parts, height, slice_len = smeared.shape
    place = lax.axis_index("energy")
    smeared[place], smeared[place ^ 1] = own[0], swapped[0]
    for chip, block in zip(chip_order(parts), received):
        smeared[place ^ (2 * chip)], smeared[place ^ (2 * chip + 1)] = block[0], block[1]
    lane = lax.broadcasted_iota(jnp.int32, (8, slice_len), 1)
    coupling = gains[0]
    modes = []
    for m in range(2):
        wide = shifts[m]
        keeps = lane < slice_len - wide, lane >= wide
        modes.append((jnp.max(wide), *keeps, gains[2 * m + 1], gains[2 * m + 2]))
    zero = jnp.zeros((8, slice_len), jnp.float32)
    acc = [zero] * (HIST + 1)
    for top in range(0, height, 8):
        at = slice(top, top + 8)
        source = [smeared[e, at, :] for e in range(parts)]
        sigma = [coupling * x for x in source]
        lesser = top < height // 2
        for s, keep_up, keep_down, emitted, absorbed in modes:
            up = [pltpu.roll(x, slice_len - s, 1) for x in source] + [zero]
            down = [zero] + [pltpu.roll(x, s, 1) for x in source]
            gain_up, gain_down = (emitted, absorbed) if lesser else (absorbed, emitted)
            for e in range(parts):
                above = jnp.where(keep_up, up[e], up[e + 1])
                below = jnp.where(keep_down, down[e + 1], down[e])
                sigma[e] = sigma[e] + (gain_up * above + gain_down * below)
        for e in range(parts):
            where = (at, slice(e * slice_len, (e + 1) * slice_len))
            new = sigma[e] - current[where]
            fresh[where] = current[where] + mixing_share * new
            acc[0] = acc[0] + new * new
            for j in range(HIST):
                acc[j + 1] = acc[j + 1] + new * residuals[(j,) + where]
    mine = jnp.concatenate([jnp.sum(a, axis=0, keepdims=True) for a in acc] + [zero[: 8 - HIST - 1]], axis=0)
    mine = jnp.sum(mine, axis=1, keepdims=True)
    spot = lax.broadcasted_iota(jnp.int32, (8, LANES), 0) + SPOTS[(0, 0)]
    mine = jnp.where(lax.broadcasted_iota(jnp.int32, (8, LANES), 1) == spot, mine, 0.0)
    mine = old_line[...] + jnp.sum(mine, axis=0, keepdims=True)
    lines[...] = jnp.broadcast_to(mine[None], lines.shape)


def residual(kept, swapped, smeared, current, residuals, old_line, gains, shifts, copies):
    return pl.pallas_call(
        lambda *refs: residual_kernel(len(smeared), *refs),
        out_shape=(
            jax.ShapeDtypeStruct(current.shape, jnp.float32),
            jax.ShapeDtypeStruct((copies, 1, LANES), jnp.float32),
        ),
        in_specs=[VMEM] * (len(smeared) + 7),
        out_specs=(VMEM, VMEM),
        scratch_shapes=[pltpu.VMEM((2 * kept.shape[0],) + kept.shape[1:], jnp.float32)],
        compiler_params=PARAMS,
        name="residual",
    )(kept, swapped, *smeared, current, residuals, old_line, gains, shifts)


def solve(products):
    prod = lambda i, j: products[(min(i, j), max(i, j))]
    n = HIST
    system = [
        [prod(i, j) - prod(i, j + 1) - prod(i + 1, j) + prod(i + 1, j + 1) for j in range(n)]
        for i in range(n)
    ]
    target = [prod(i, 0) - prod(i + 1, 0) for i in range(n)]
    trace = system[0][0]
    for i in range(1, n):
        trace = trace + system[i][i]
    ridge = (ridge_share / n) * trace + 1e-06
    for i in range(n):
        system[i][i] = system[i][i] + ridge
    for k in range(n):
        inverse = 1.0 / system[k][k]
        row = [system[k][j] * inverse if j > k else None for j in range(n)]
        value = target[k] * inverse
        for i in range(n):
            if i == k:
                continue
            for j in range(k + 1, n):
                system[i][j] = system[i][j] - system[i][k] * row[j]
            target[i] = target[i] - system[i][k] * value
        system[k] = row
        target[k] = value
    gamma = target
    weights = [1.0 - gamma[0]]
    for j in range(1, n):
        weights.append(gamma[j - 1] - gamma[j])
    weights.append(gamma[n - 1])
    return weights


def mix_kernel(entries, lines, fresh, aged, out, wide, mixed_rows, done):
    summed = jnp.sum(lines[...], axis=0) * (1.0 / entries)
    row = lax.broadcasted_iota(jnp.int32, (8, LANES), 0)
    lane = lax.broadcasted_iota(jnp.int32, (8, LANES), 1)
    for part in range(wide.shape[0]):
        own = jnp.where(lane == row + 8 * part, summed, 0.0)
        wide[part] = jnp.broadcast_to(jnp.sum(own, axis=1, keepdims=True), (8, LANES))
    products = {
        pair: jnp.broadcast_to(wide[spot // 8, spot % 8 : spot % 8 + 1, :], (8, LANES))
        for pair, spot in SPOTS.items()
    }
    weights = solve(products)
    rows, width = fresh.shape
    span = rows // done.shape[0]
    writes = []
    for part in range(done.shape[0]):
        for top in range(part * span, (part + 1) * span, 8):
            for left in range(0, width, LANES):
                at = (slice(top, top + 8), slice(left, left + LANES))
                mixed = weights[0] * fresh[at]
                for j in range(HIST):
                    mixed = mixed + weights[j + 1] * aged[(j,) + at]
                mixed_rows[at] = mixed
        at = pl.ds(part * span, span)
        writes.append(pltpu.make_async_copy(mixed_rows.at[at], out.at[at], done.at[part]))
        writes[-1].start()
    for write in writes:
        write.wait()


def mix(lines, fresh, aged, entries):
    return pl.pallas_call(
        lambda *refs: mix_kernel(entries, *refs),
        out_shape=jax.ShapeDtypeStruct(fresh.shape, jnp.float32),
        in_specs=[VMEM] * 3,
        out_specs=pl.BlockSpec(memory_space=pltpu.HBM),
        scratch_shapes=[
            pltpu.VMEM((3, 8, LANES), jnp.float32),
            pltpu.VMEM(fresh.shape, jnp.float32),
            pltpu.SemaphoreType.DMA((min(4, fresh.shape[0] // 8),)),
        ],
        compiler_params=PARAMS,
        name="mix",
    )(lines, fresh, aged)


def per_device(
    greens,
    current,
    past_inputs,
    past_residuals,
    slot_order,
    neighbour,
    momentum_class,
    stencil_weight,
    acoustic_coupling,
    optical_coupling,
    occupation,
    phonon_shift,
):
    group_len, slice_len = greens.shape[3:]
    rows, width = current.shape[3:]
    groups = lax.axis_size("kgrp")
    parts = lax.axis_size("energy")
    own = greens.reshape(-1, group_len, slice_len)
    height = own.shape[0] * rows

    flat = current.reshape(height, width)
    old_in = past_inputs.reshape(HIST, height, width)
    old_res = past_residuals.reshape(HIST, height, width)
    scalars = (
        slot_order, momentum_class, acoustic_coupling, optical_coupling, occupation, phonon_shift
    )
    aged, residuals, old_line, gains, shifts = history(old_in, old_res, scalars, rows)
    kept, given = smear(own, neighbour, stencil_weight, groups, parts)
    meet = lambda block, m: lax.ppermute(block, "energy", [(e, e ^ m) for e in range(parts)])
    swapped = meet(given, 1)
    smeared = [meet(block, 2 * chip) for chip, block in zip(chip_order(parts), join(kept, swapped))]
    fresh, lines = residual(
        kept, swapped, smeared, flat, residuals, old_line, gains, shifts, groups * parts
    )
    lines = lax.all_to_all(lines, ("energy", "kgrp"), split_axis=0, concat_axis=0, tiled=True)
    entries = float(flat.size * groups * parts)
    return mix(lines, fresh, aged, entries).reshape(current.shape)


def solution(mesh):
    return jax.shard_map(
        per_device,
        mesh=mesh,
        in_specs=(
            P(None, None, None, "kgrp", "energy"),
            P(None, None, None, ("kgrp", "energy"), None),
            P(None, None, None, None, ("kgrp", "energy"), None),
            P(None, None, None, None, ("kgrp", "energy"), None),
            P(),
            P("kgrp", None),
            P("kgrp"),
            P(),
            P(),
            P(),
            P(),
            P(),
        ),
        out_specs=P(None, None, None, ("kgrp", "energy"), None),
        check_vma=False,
    )
```

```python
import jax
import jax.numpy as jnp
from jax import lax
from jax.experimental import pallas as pl
from jax.experimental.pallas import tpu as pltpu
from jax.sharding import PartitionSpec as P

HIST = 5
LANES = 128

mixing_share = 0.5
ridge_share = 0.1

VMEM = pl.BlockSpec(memory_space=pltpu.VMEM)
SMEM = pl.BlockSpec(memory_space=pltpu.SMEM)
PARAMS = pltpu.CompilerParams(vmem_limit_bytes=16 * 1024 * 1024)

PAIRS = [(i, j) for i in range(1, HIST + 1) for j in range(i, HIST + 1)]
SPOTS = {pair: v for v, pair in enumerate(PAIRS)}
for _j in range(HIST + 1):
    SPOTS[(0, _j)] = 16 + _j


def split(value):
    high = value.astype(jnp.bfloat16)
    return high, (value - high.astype(jnp.float32)).astype(jnp.bfloat16)


def product(left, right):
    dot = lambda a, b: jnp.dot(a, b, preferred_element_type=jnp.float32)
    return dot(left[0], right[0]) + (dot(left[0], right[1]) + dot(left[1], right[0]))


def prepare_kernel(total_k, *refs):
    *blocks, neighbour_hbm, weight_hbm, stencil_hi, stencil_lo, part, late, neighbour, weight, done = refs
    fetches = [
        pltpu.make_async_copy(neighbour_hbm, neighbour, done.at[0]),
        pltpu.make_async_copy(weight_hbm, weight, done.at[1]),
    ]
    for fetch in fetches:
        fetch.start()
    late[...] = blocks[-1][...]
    _, group_len, slice_len = blocks[0].shape
    group_id = lax.axis_index("kgrp")
    parts = lax.axis_size("energy")
    rows = group_len // parts
    for fetch in fetches:
        fetch.wait()
    slots, _ = neighbour.shape
    padded = jnp.concatenate([neighbour[...], jnp.zeros((8 - slots, group_len), jnp.int32)], axis=0)
    targets = jnp.transpose(padded)
    place = lax.axis_index("energy")
    bit = 1
    while bit < parts:
        span = bit * rows
        pieces = [targets[at : at + span] for at in range(0, group_len, span)]
        flipped = [pieces[b ^ 1] for b in range(len(pieces))]
        targets = jnp.where(place & bit != 0, jnp.concatenate(flipped, axis=0), targets)
        bit *= 2
    local = targets - group_id * group_len + group_len
    local = jnp.where(local < 0, local + total_k, jnp.where(local >= total_k, local - total_k, local))
    spot = lax.broadcasted_iota(jnp.int32, (group_len, 3 * group_len), 1)
    stencil = jnp.zeros(spot.shape, jnp.float32)
    for n in range(slots):
        stencil = stencil + jnp.where(spot == local[:, n : n + 1], weight[n], 0.0)
    before, after = stencil[:, :group_len], stencil[:, 2 * group_len :]
    swapped = paired(total_k // group_len) & (group_id % 2 == 1)
    near, far = jnp.where(swapped, before, after), jnp.where(swapped, after, before)
    stencil_hi[...], stencil_lo[...] = split(jnp.concatenate([near, far], axis=1))
    centre = split(stencil[:, group_len : 2 * group_len])
    first = 0
    for own in blocks:
        for c in range(0, own.shape[0], 2):
            result = product(centre, split(jnp.concatenate([own[c], own[c + 1]], axis=1)))
            part[first + c] = result[:, :slice_len]
            part[first + c + 1] = result[:, slice_len:]
        first += own.shape[0]


def prepare(blocks, neighbour, weight, total_k):
    comps = sum(block.shape[0] for block in blocks)
    _, group_len, slice_len = blocks[0].shape
    sides = jax.ShapeDtypeStruct((group_len, 2 * group_len), jnp.bfloat16)
    size = comps * group_len * slice_len
    return pl.pallas_call(
        lambda *refs: prepare_kernel(total_k, *refs),
        out_shape=(
            sides,
            sides,
            jax.ShapeDtypeStruct((comps, group_len, slice_len), jnp.float32),
            jax.ShapeDtypeStruct(blocks[-1].shape, jnp.float32),
        ),
        in_specs=[VMEM] * len(blocks) + [pl.BlockSpec(memory_space=pltpu.HBM)] * 2,
        out_specs=(VMEM,) * 4,
        scratch_shapes=[
            pltpu.VMEM(neighbour.shape[::-1], jnp.int32),
            pltpu.SMEM(weight.shape, jnp.float32),
            pltpu.SemaphoreType.DMA((2,)),
        ],
        compiler_params=PARAMS,
        cost_estimate=pl.CostEstimate(
            flops=6 * size * group_len, bytes_accessed=8 * size, transcendentals=0
        ),
        name="prepare",
    )(*blocks, *(pltpu.with_memory_space_constraint(x, pltpu.HBM) for x in (neighbour.T, weight)))


def smeared_pairs(first, sides, stencil_hi, stencil_lo, part):
    blocks = [block for block in sides if block is not None]
    comps, group_len, slice_len = blocks[0].shape
    start = 0 if sides[0] is not None else group_len
    at = slice(start, start + len(blocks) * group_len)
    stencil = (stencil_hi[:, at], stencil_lo[:, at])
    for c in range(0, comps, 2):
        stacked = [jnp.concatenate([block[c], block[c + 1]], axis=1) for block in blocks]
        result = product(stencil, split(jnp.concatenate(stacked, axis=0)))
        for p in range(2):
            yield c + p, part[first + c + p] + result[:, p * slice_len : (p + 1) * slice_len]


def with_sides(kernel, sides):
    def body(*refs):
        refs = list(refs)
        kernel([None if side is None else refs.pop(0) for side in sides], *refs)

    return body


def smear_cost(blocks):
    size = sum(block.size for block in blocks)
    return pl.CostEstimate(
        flops=6 * size * blocks[0].shape[1], bytes_accessed=12 * size, transcendentals=0
    )


def add_sides(first, sides, stencil_hi, stencil_lo, part, after):
    def kernel(sides, stencil_hi, stencil_lo, part, *refs):
        for c, smeared in smeared_pairs(first, sides, stencil_hi, stencil_lo, part):
            refs[-1][c] = smeared

    blocks = [block for block in sides if block is not None]
    return pl.pallas_call(
        with_sides(kernel, sides),
        out_shape=jax.ShapeDtypeStruct(blocks[0].shape, jnp.float32),
        in_specs=[VMEM] * (len(blocks) + 3) + [pl.BlockSpec(memory_space=pl.ANY)] * len(after),
        out_specs=VMEM,
        compiler_params=PARAMS,
        cost_estimate=smear_cost(blocks),
        name="add_sides",
    )(*blocks, stencil_hi, stencil_lo, part, *after)


def finish_kernel(sides, stencil_hi, stencil_lo, part, *refs):
    *ready, kept, given = refs
    chips, height, _ = kept.shape
    comps = part.shape[0]
    rows = height // comps

    def place(c, smeared):
        for m in range(2 * chips):
            out = given if m % 2 else kept
            out[m // 2, c * rows : (c + 1) * rows, :] = smeared[m * rows : (m + 1) * rows]

    first = 0
    for c, smeared in smeared_pairs(0, sides, stencil_hi, stencil_lo, part):
        place(c, smeared)
        first = c + 1
    for block in ready:
        for c in range(block.shape[0]):
            place(first + c, block[c])


def finish(sides, stencil_hi, stencil_lo, part, ready, parts):
    blocks = [block for block in sides if block is not None]
    comps, group_len, slice_len = part.shape
    shape = (parts // 2, comps * group_len // parts, slice_len)
    return pl.pallas_call(
        with_sides(finish_kernel, sides),
        out_shape=[jax.ShapeDtypeStruct(shape, jnp.float32)] * 2,
        in_specs=[VMEM] * (len(blocks) + len(ready) + 3),
        out_specs=[VMEM] * 2,
        compiler_params=PARAMS,
        cost_estimate=smear_cost(blocks),
        name="finish",
    )(*blocks, stencil_hi, stencil_lo, part, *ready)


def chip_order(parts):
    chips = parts // 2
    half = chips // 2
    return [*range(half + 1, chips), *range(1, half), half] if chips > 1 else []


def join_kernel(own, swapped, *out):
    for chip, block in zip(chip_order(2 * own.shape[0]), out):
        block[0], block[1] = own[chip], swapped[chip]


def join(own, swapped):
    chips, height, slice_len = own.shape
    shape = jax.ShapeDtypeStruct((2, height, slice_len), jnp.float32)
    return pl.pallas_call(
        join_kernel,
        out_shape=[shape] * (chips - 1),
        in_specs=[VMEM] * 2,
        out_specs=[VMEM] * (chips - 1),
        compiler_params=PARAMS,
        name="join",
    )(own, swapped)


def paired(groups):
    return groups == 4


def hold_kernel(block, _, out):
    out[...] = block[...]


def hold(block, until):
    return pl.pallas_call(
        hold_kernel,
        out_shape=jax.ShapeDtypeStruct(block.shape, jnp.float32),
        in_specs=[VMEM, pl.BlockSpec(memory_space=pl.ANY)],
        out_specs=VMEM,
        compiler_params=PARAMS,
        name="hold",
    )(block, until)


def smear(own, neighbour, weight, groups, parts):
    total_k = groups * own.shape[1]
    if not paired(groups):
        forward = [(i, (i + 1) % groups) for i in range(groups)]
        backward = [(target, source) for source, target in forward]
        near, far = lax.ppermute(own, "kgrp", backward), lax.ppermute(own, "kgrp", forward)
        return finish((near, far), *prepare([own], neighbour, weight, total_k)[:3], [], parts)
    across = lambda block, flip: lax.ppermute(block, "kgrp", [(i, i ^ flip) for i in range(groups)])
    half = own.shape[0] // 2
    head, tail = own[:half], own[half:]
    near_head, far_tail = across(head, 1), across(tail, 3)
    hi, lo, part, late = prepare([head, tail], neighbour, weight, total_k)
    near_tail, far_head = across(late, 1), across(hold(near_head, late), 2)
    tail_part = add_sides(half, (near_tail, far_tail), hi, lo, part, [])
    return finish((near_head, far_head), hi, lo, part, [tail_part], parts)


def spread(values, shape):
    lane = lax.broadcasted_iota(jnp.int32, shape, 1)
    row = jnp.zeros(shape, jnp.float32)
    for spot, value in values:
        row = jnp.where(lane == spot, value, row)
    return row


def total(acc):
    return jnp.sum(jnp.sum(acc, axis=0, keepdims=True), axis=1, keepdims=True)


def history_kernel(
    total_rows, past_inputs, past_residuals, slots, classes, acoustic, optical, number, shift,
    aged, residuals, line, gains, shifts,
):
    first = lax.axis_index("energy") * total_rows
    row = lax.broadcasted_iota(jnp.int32, (8, LANES), 0) % total_rows
    coupling = jnp.zeros((8, LANES), jnp.float32)
    for i in range(total_rows):
        coupling = jnp.where(row == i, acoustic[classes[first + i]], coupling)
    gains[0] = coupling
    for m in range(2):
        gains[2 * m + 1] = jnp.full((8, LANES), optical[m] * (number[m] + 1.0))
        gains[2 * m + 2] = jnp.full((8, LANES), optical[m] * number[m])
        shifts[m] = jnp.full((8, LANES), shift[m], jnp.int32)
    _, rows, width = past_inputs.shape
    acc = [jnp.zeros((8, LANES), jnp.float32) for _ in PAIRS]
    for top in range(0, rows, 8):
        def column(t, acc, top=top):
            at = pl.ds(pl.multiple_of(t * LANES, LANES), LANES)
            old = []
            for j in range(HIST):
                res = past_residuals[slots[j], top : top + 8, at]
                aged[j, top : top + 8, at] = (
                    past_inputs[slots[j], top : top + 8, at] + mixing_share * res
                )
                residuals[j, top : top + 8, at] = res
                old.append(res)
            return [a + old[i - 1] * old[j - 1] for a, (i, j) in zip(acc, PAIRS)]
        acc = lax.fori_loop(0, width // LANES, column, acc, unroll=4)
    line[...] = spread([(v, total(a)) for v, a in enumerate(acc)], line.shape)


def history(past_inputs, past_residuals, scalars, rows):
    size = past_inputs.size
    return pl.pallas_call(
        lambda *refs: history_kernel(rows, *refs),
        out_shape=(
            jax.ShapeDtypeStruct(past_inputs.shape, jnp.float32),
            jax.ShapeDtypeStruct(past_inputs.shape, jnp.float32),
            jax.ShapeDtypeStruct((1, LANES), jnp.float32),
            jax.ShapeDtypeStruct((5, 8, LANES), jnp.float32),
            jax.ShapeDtypeStruct((2, 8, LANES), jnp.int32),
        ),
        in_specs=[VMEM, VMEM] + [SMEM] * 6,
        out_specs=(VMEM,) * 5,
        compiler_params=PARAMS,
        cost_estimate=pl.CostEstimate(flops=8 * size, bytes_accessed=12 * size, transcendentals=0),
        name="history",
    )(past_inputs, past_residuals, *scalars)


def residual_kernel(count, own, swapped, *refs):
    received = refs[:count]
    current, residuals, old_line, gains, shifts, fresh, lines, smeared = refs[count:]
    parts, height, slice_len = smeared.shape
    place = lax.axis_index("energy")
    smeared[place], smeared[place ^ 1] = own[0], swapped[0]
    for chip, block in zip(chip_order(parts), received):
        smeared[place ^ (2 * chip)], smeared[place ^ (2 * chip + 1)] = block[0], block[1]
    lane = lax.broadcasted_iota(jnp.int32, (8, slice_len), 1)
    coupling = gains[0]
    modes = []
    for m in range(2):
        wide = shifts[m]
        keeps = lane < slice_len - wide, lane >= wide
        modes.append((jnp.max(wide), *keeps, gains[2 * m + 1], gains[2 * m + 2]))
    zero = jnp.zeros((8, slice_len), jnp.float32)
    acc = [zero] * (HIST + 1)
    for top in range(0, height, 8):
        at = slice(top, top + 8)
        source = [smeared[e, at, :] for e in range(parts)]
        sigma = [coupling * x for x in source]
        lesser = top < height // 2
        for s, keep_up, keep_down, emitted, absorbed in modes:
            up = [pltpu.roll(x, slice_len - s, 1) for x in source] + [zero]
            down = [zero] + [pltpu.roll(x, s, 1) for x in source]
            gain_up, gain_down = (emitted, absorbed) if lesser else (absorbed, emitted)
            for e in range(parts):
                above = jnp.where(keep_up, up[e], up[e + 1])
                below = jnp.where(keep_down, down[e + 1], down[e])
                sigma[e] = sigma[e] + (gain_up * above + gain_down * below)
        for e in range(parts):
            where = (at, slice(e * slice_len, (e + 1) * slice_len))
            new = sigma[e] - current[where]
            fresh[where] = current[where] + mixing_share * new
            acc[0] = acc[0] + new * new
            for j in range(HIST):
                acc[j + 1] = acc[j + 1] + new * residuals[(j,) + where]
    mine = jnp.concatenate([jnp.sum(a, axis=0, keepdims=True) for a in acc] + [zero[: 8 - HIST - 1]], axis=0)
    mine = jnp.sum(mine, axis=1, keepdims=True)
    spot = lax.broadcasted_iota(jnp.int32, (8, LANES), 0) + SPOTS[(0, 0)]
    mine = jnp.where(lax.broadcasted_iota(jnp.int32, (8, LANES), 1) == spot, mine, 0.0)
    mine = old_line[...] + jnp.sum(mine, axis=0, keepdims=True)
    lines[...] = jnp.broadcast_to(mine[None], lines.shape)


def residual(kept, swapped, smeared, current, residuals, old_line, gains, shifts, copies):
    return pl.pallas_call(
        lambda *refs: residual_kernel(len(smeared), *refs),
        out_shape=(
            jax.ShapeDtypeStruct(current.shape, jnp.float32),
            jax.ShapeDtypeStruct((copies, 1, LANES), jnp.float32),
        ),
        in_specs=[VMEM] * (len(smeared) + 7),
        out_specs=(VMEM, VMEM),
        scratch_shapes=[pltpu.VMEM((2 * kept.shape[0],) + kept.shape[1:], jnp.float32)],
        compiler_params=PARAMS,
        name="residual",
    )(kept, swapped, *smeared, current, residuals, old_line, gains, shifts)


def solve(products):
    prod = lambda i, j: products[(min(i, j), max(i, j))]
    n = HIST
    system = [
        [prod(i, j) - prod(i, j + 1) - prod(i + 1, j) + prod(i + 1, j + 1) for j in range(n)]
        for i in range(n)
    ]
    target = [prod(i, 0) - prod(i + 1, 0) for i in range(n)]
    trace = system[0][0]
    for i in range(1, n):
        trace = trace + system[i][i]
    ridge = (ridge_share / n) * trace + 1e-06
    for i in range(n):
        system[i][i] = system[i][i] + ridge
    for k in range(n):
        inverse = 1.0 / system[k][k]
        row = [system[k][j] * inverse if j > k else None for j in range(n)]
        value = target[k] * inverse
        for i in range(n):
            if i == k:
                continue
            for j in range(k + 1, n):
                system[i][j] = system[i][j] - system[i][k] * row[j]
            target[i] = target[i] - system[i][k] * value
        system[k] = row
        target[k] = value
    gamma = target
    weights = [1.0 - gamma[0]]
    for j in range(1, n):
        weights.append(gamma[j - 1] - gamma[j])
    weights.append(gamma[n - 1])
    return weights


def mix_kernel(entries, lines, fresh, aged, out, wide, mixed_rows, done):
    summed = jnp.sum(lines[...], axis=0) * (1.0 / entries)
    row = lax.broadcasted_iota(jnp.int32, (8, LANES), 0)
    lane = lax.broadcasted_iota(jnp.int32, (8, LANES), 1)
    for part in range(wide.shape[0]):
        own = jnp.where(lane == row + 8 * part, summed, 0.0)
        wide[part] = jnp.broadcast_to(jnp.sum(own, axis=1, keepdims=True), (8, LANES))
    products = {
        pair: jnp.broadcast_to(wide[spot // 8, spot % 8 : spot % 8 + 1, :], (8, LANES))
        for pair, spot in SPOTS.items()
    }
    weights = solve(products)
    rows, width = fresh.shape
    span = rows // done.shape[0]
    writes = []
    for part in range(done.shape[0]):
        for top in range(part * span, (part + 1) * span, 8):
            for left in range(0, width, LANES):
                at = (slice(top, top + 8), slice(left, left + LANES))
                mixed = weights[0] * fresh[at]
                for j in range(HIST):
                    mixed = mixed + weights[j + 1] * aged[(j,) + at]
                mixed_rows[at] = mixed
        at = pl.ds(part * span, span)
        writes.append(pltpu.make_async_copy(mixed_rows.at[at], out.at[at], done.at[part]))
        writes[-1].start()
    for write in writes:
        write.wait()


def mix(lines, fresh, aged, entries):
    return pl.pallas_call(
        lambda *refs: mix_kernel(entries, *refs),
        out_shape=jax.ShapeDtypeStruct(fresh.shape, jnp.float32),
        in_specs=[VMEM] * 3,
        out_specs=pl.BlockSpec(memory_space=pltpu.HBM),
        scratch_shapes=[
            pltpu.VMEM((3, 8, LANES), jnp.float32),
            pltpu.VMEM(fresh.shape, jnp.float32),
            pltpu.SemaphoreType.DMA((min(4, fresh.shape[0] // 8),)),
        ],
        compiler_params=PARAMS,
        name="mix",
    )(lines, fresh, aged)


def per_device(
    greens,
    current,
    past_inputs,
    past_residuals,
    slot_order,
    neighbour,
    momentum_class,
    stencil_weight,
    acoustic_coupling,
    optical_coupling,
    occupation,
    phonon_shift,
):
    group_len, slice_len = greens.shape[3:]
    rows, width = current.shape[3:]
    groups = lax.axis_size("kgrp")
    parts = lax.axis_size("energy")
    own = greens.reshape(-1, group_len, slice_len)
    height = own.shape[0] * rows

    flat = current.reshape(height, width)
    old_in = past_inputs.reshape(HIST, height, width)
    old_res = past_residuals.reshape(HIST, height, width)
    scalars = (
        slot_order, momentum_class, acoustic_coupling, optical_coupling, occupation, phonon_shift
    )
    aged, residuals, old_line, gains, shifts = history(old_in, old_res, scalars, rows)
    kept, given = smear(own, neighbour, stencil_weight, groups, parts)
    meet = lambda block, m: lax.ppermute(block, "energy", [(e, e ^ m) for e in range(parts)])
    swapped = meet(given, 1)
    smeared = [meet(block, 2 * chip) for chip, block in zip(chip_order(parts), join(kept, swapped))]
    fresh, lines = residual(
        kept, swapped, smeared, flat, residuals, old_line, gains, shifts, groups * parts
    )
    lines = lax.all_to_all(lines, ("energy", "kgrp"), split_axis=0, concat_axis=0, tiled=True)
    entries = float(flat.size * groups * parts)
    return mix(lines, fresh, aged, entries).reshape(current.shape)


def solution(mesh):
    return jax.shard_map(
        per_device,
        mesh=mesh,
        in_specs=(
            P(None, None, None, "kgrp", "energy"),
            P(None, None, None, ("kgrp", "energy"), None),
            P(None, None, None, None, ("kgrp", "energy"), None),
            P(None, None, None, None, ("kgrp", "energy"), None),
            P(),
            P("kgrp", None),
            P("kgrp"),
            P(),
            P(),
            P(),
            P(),
            P(),
        ),
        out_specs=P(None, None, None, ("kgrp", "energy"), None),
        check_vma=False,
    )
```

```python
import jax
import jax.numpy as jnp
from jax import lax
from jax.experimental import pallas as pl
from jax.experimental.pallas import tpu as pltpu
from jax.sharding import PartitionSpec as P

HIST = 5
LANES = 128

mixing_share = 0.5
ridge_share = 0.1

VMEM = pl.BlockSpec(memory_space=pltpu.VMEM)
SMEM = pl.BlockSpec(memory_space=pltpu.SMEM)
PARAMS = pltpu.CompilerParams(vmem_limit_bytes=16 * 1024 * 1024)

PAIRS = [(i, j) for i in range(1, HIST + 1) for j in range(i, HIST + 1)]
SPOTS = {pair: v for v, pair in enumerate(PAIRS)}
for _j in range(HIST + 1):
    SPOTS[(0, _j)] = 16 + _j


def split(value):
    high = value.astype(jnp.bfloat16)
    return high, (value - high.astype(jnp.float32)).astype(jnp.bfloat16)


def product(left, right):
    dot = lambda a, b: jnp.dot(a, b, preferred_element_type=jnp.float32)
    return dot(left[0], right[0]) + (dot(left[0], right[1]) + dot(left[1], right[0]))


def prepare_kernel(total_k, *refs):
    *blocks, neighbour_hbm, weight_hbm, stencil_hi, stencil_lo, part, late, neighbour, weight, done = refs
    fetches = [
        pltpu.make_async_copy(neighbour_hbm, neighbour, done.at[0]),
        pltpu.make_async_copy(weight_hbm, weight, done.at[1]),
    ]
    for fetch in fetches:
        fetch.start()
    late[...] = blocks[-1][...]
    _, group_len, slice_len = blocks[0].shape
    group_id = lax.axis_index("kgrp")
    parts = lax.axis_size("energy")
    rows = group_len // parts
    for fetch in fetches:
        fetch.wait()
    slots, _ = neighbour.shape
    padded = jnp.concatenate([neighbour[...], jnp.zeros((8 - slots, group_len), jnp.int32)], axis=0)
    targets = jnp.transpose(padded)
    place = lax.axis_index("energy")
    bit = 1
    while bit < parts:
        span = bit * rows
        pieces = [targets[at : at + span] for at in range(0, group_len, span)]
        flipped = [pieces[b ^ 1] for b in range(len(pieces))]
        targets = jnp.where(place & bit != 0, jnp.concatenate(flipped, axis=0), targets)
        bit *= 2
    local = targets - group_id * group_len + group_len
    local = jnp.where(local < 0, local + total_k, jnp.where(local >= total_k, local - total_k, local))
    spot = lax.broadcasted_iota(jnp.int32, (group_len, 3 * group_len), 1)
    stencil = jnp.zeros(spot.shape, jnp.float32)
    for n in range(slots):
        stencil = stencil + jnp.where(spot == local[:, n : n + 1], weight[n], 0.0)
    before, after = stencil[:, :group_len], stencil[:, 2 * group_len :]
    swapped = paired(total_k // group_len) & (group_id % 2 == 1)
    near, far = jnp.where(swapped, before, after), jnp.where(swapped, after, before)
    stencil_hi[...], stencil_lo[...] = split(jnp.concatenate([near, far], axis=1))
    centre = split(stencil[:, group_len : 2 * group_len])
    first = 0
    for own in blocks:
        for c in range(0, own.shape[0], 2):
            result = product(centre, split(jnp.concatenate([own[c], own[c + 1]], axis=1)))
            part[first + c] = result[:, :slice_len]
            part[first + c + 1] = result[:, slice_len:]
        first += own.shape[0]


def prepare(blocks, neighbour, weight, total_k):
    comps = sum(block.shape[0] for block in blocks)
    _, group_len, slice_len = blocks[0].shape
    sides = jax.ShapeDtypeStruct((group_len, 2 * group_len), jnp.bfloat16)
    size = comps * group_len * slice_len
    return pl.pallas_call(
        lambda *refs: prepare_kernel(total_k, *refs),
        out_shape=(
            sides,
            sides,
            jax.ShapeDtypeStruct((comps, group_len, slice_len), jnp.float32),
            jax.ShapeDtypeStruct(blocks[-1].shape, jnp.float32),
        ),
        in_specs=[VMEM] * len(blocks) + [pl.BlockSpec(memory_space=pltpu.HBM)] * 2,
        out_specs=(VMEM,) * 4,
        scratch_shapes=[
            pltpu.VMEM(neighbour.shape[::-1], jnp.int32),
            pltpu.SMEM(weight.shape, jnp.float32),
            pltpu.SemaphoreType.DMA((2,)),
        ],
        compiler_params=PARAMS,
        cost_estimate=pl.CostEstimate(
            flops=6 * size * group_len, bytes_accessed=8 * size, transcendentals=0
        ),
        name="prepare",
    )(*blocks, *(pltpu.with_memory_space_constraint(x, pltpu.HBM) for x in (neighbour.T, weight)))


def smeared_pairs(first, sides, stencil_hi, stencil_lo, part):
    blocks = [block for block in sides if block is not None]
    comps, group_len, slice_len = blocks[0].shape
    start = 0 if sides[0] is not None else group_len
    at = slice(start, start + len(blocks) * group_len)
    stencil = (stencil_hi[:, at], stencil_lo[:, at])
    for c in range(0, comps, 2):
        stacked = [jnp.concatenate([block[c], block[c + 1]], axis=1) for block in blocks]
        result = product(stencil, split(jnp.concatenate(stacked, axis=0)))
        for p in range(2):
            yield c + p, part[first + c + p] + result[:, p * slice_len : (p + 1) * slice_len]


def with_sides(kernel, sides):
    def body(*refs):
        refs = list(refs)
        kernel([None if side is None else refs.pop(0) for side in sides], *refs)

    return body


def smear_cost(blocks):
    size = sum(block.size for block in blocks)
    return pl.CostEstimate(
        flops=6 * size * blocks[0].shape[1], bytes_accessed=12 * size, transcendentals=0
    )


def add_sides(first, sides, stencil_hi, stencil_lo, part, after):
    def kernel(sides, stencil_hi, stencil_lo, part, *refs):
        for c, smeared in smeared_pairs(first, sides, stencil_hi, stencil_lo, part):
            refs[-1][c] = smeared

    blocks = [block for block in sides if block is not None]
    return pl.pallas_call(
        with_sides(kernel, sides),
        out_shape=jax.ShapeDtypeStruct(blocks[0].shape, jnp.float32),
        in_specs=[VMEM] * (len(blocks) + 3) + [pl.BlockSpec(memory_space=pl.ANY)] * len(after),
        out_specs=VMEM,
        compiler_params=PARAMS,
        cost_estimate=smear_cost(blocks),
        name="add_sides",
    )(*blocks, stencil_hi, stencil_lo, part, *after)


def finish_kernel(sides, stencil_hi, stencil_lo, part, *refs):
    *ready, kept, given = refs
    chips, height, _ = kept.shape
    comps = part.shape[0]
    rows = height // comps

    def place(c, smeared):
        for m in range(2 * chips):
            out = given if m % 2 else kept
            out[m // 2, c * rows : (c + 1) * rows, :] = smeared[m * rows : (m + 1) * rows]

    first = 0
    for c, smeared in smeared_pairs(0, sides, stencil_hi, stencil_lo, part):
        place(c, smeared)
        first = c + 1
    for block in ready:
        for c in range(block.shape[0]):
            place(first + c, block[c])


def finish(sides, stencil_hi, stencil_lo, part, ready, parts):
    blocks = [block for block in sides if block is not None]
    comps, group_len, slice_len = part.shape
    shape = (parts // 2, comps * group_len // parts, slice_len)
    return pl.pallas_call(
        with_sides(finish_kernel, sides),
        out_shape=[jax.ShapeDtypeStruct(shape, jnp.float32)] * 2,
        in_specs=[VMEM] * (len(blocks) + len(ready) + 3),
        out_specs=[VMEM] * 2,
        compiler_params=PARAMS,
        cost_estimate=smear_cost(blocks),
        name="finish",
    )(*blocks, stencil_hi, stencil_lo, part, *ready)


def chip_order(parts):
    chips = parts // 2
    half = chips // 2
    return [*range(half + 1, chips), *range(1, half), half] if chips > 1 else []


def join_kernel(own, swapped, *out):
    for chip, block in zip(chip_order(2 * own.shape[0]), out):
        block[0], block[1] = own[chip], swapped[chip]


def join(own, swapped):
    chips, height, slice_len = own.shape
    shape = jax.ShapeDtypeStruct((2, height, slice_len), jnp.float32)
    return pl.pallas_call(
        join_kernel,
        out_shape=[shape] * (chips - 1),
        in_specs=[VMEM] * 2,
        out_specs=[VMEM] * (chips - 1),
        compiler_params=PARAMS,
        name="join",
    )(own, swapped)


def paired(groups):
    return groups == 4


def hold_kernel(block, _, out):
    out[...] = block[...]


def hold(block, until):
    return pl.pallas_call(
        hold_kernel,
        out_shape=jax.ShapeDtypeStruct(block.shape, jnp.float32),
        in_specs=[VMEM, pl.BlockSpec(memory_space=pl.ANY)],
        out_specs=VMEM,
        compiler_params=PARAMS,
        name="hold",
    )(block, until)


def smear(own, neighbour, weight, groups, parts):
    total_k = groups * own.shape[1]
    if not paired(groups):
        forward = [(i, (i + 1) % groups) for i in range(groups)]
        backward = [(target, source) for source, target in forward]
        near, far = lax.ppermute(own, "kgrp", backward), lax.ppermute(own, "kgrp", forward)
        return finish((near, far), *prepare([own], neighbour, weight, total_k)[:3], [], parts)
    across = lambda block, flip: lax.ppermute(block, "kgrp", [(i, i ^ flip) for i in range(groups)])
    half = own.shape[0] // 2
    head, tail = own[:half], own[half:]
    near_head = across(head, 1)
    hi, lo, part, late = prepare([head, tail], neighbour, weight, total_k)
    far_tail, near_tail, far_head = across(late, 3), across(late, 1), across(hold(near_head, late), 2)
    tail_part = add_sides(half, (near_tail, far_tail), hi, lo, part, [])
    return finish((near_head, far_head), hi, lo, part, [tail_part], parts)


def spread(values, shape):
    lane = lax.broadcasted_iota(jnp.int32, shape, 1)
    row = jnp.zeros(shape, jnp.float32)
    for spot, value in values:
        row = jnp.where(lane == spot, value, row)
    return row


def total(acc):
    return jnp.sum(jnp.sum(acc, axis=0, keepdims=True), axis=1, keepdims=True)


def history_kernel(
    total_rows, past_inputs, past_residuals, slots, classes, acoustic, optical, number, shift,
    aged, residuals, line, gains, shifts,
):
    first = lax.axis_index("energy") * total_rows
    row = lax.broadcasted_iota(jnp.int32, (8, LANES), 0) % total_rows
    coupling = jnp.zeros((8, LANES), jnp.float32)
    for i in range(total_rows):
        coupling = jnp.where(row == i, acoustic[classes[first + i]], coupling)
    gains[0] = coupling
    for m in range(2):
        gains[2 * m + 1] = jnp.full((8, LANES), optical[m] * (number[m] + 1.0))
        gains[2 * m + 2] = jnp.full((8, LANES), optical[m] * number[m])
        shifts[m] = jnp.full((8, LANES), shift[m], jnp.int32)
    _, rows, width = past_inputs.shape
    acc = [jnp.zeros((8, LANES), jnp.float32) for _ in PAIRS]
    for top in range(0, rows, 8):
        def column(t, acc, top=top):
            at = pl.ds(pl.multiple_of(t * LANES, LANES), LANES)
            old = []
            for j in range(HIST):
                res = past_residuals[slots[j], top : top + 8, at]
                aged[j, top : top + 8, at] = (
                    past_inputs[slots[j], top : top + 8, at] + mixing_share * res
                )
                residuals[j, top : top + 8, at] = res
                old.append(res)
            return [a + old[i - 1] * old[j - 1] for a, (i, j) in zip(acc, PAIRS)]
        acc = lax.fori_loop(0, width // LANES, column, acc, unroll=4)
    line[...] = spread([(v, total(a)) for v, a in enumerate(acc)], line.shape)


def history(past_inputs, past_residuals, scalars, rows):
    size = past_inputs.size
    return pl.pallas_call(
        lambda *refs: history_kernel(rows, *refs),
        out_shape=(
            jax.ShapeDtypeStruct(past_inputs.shape, jnp.float32),
            jax.ShapeDtypeStruct(past_inputs.shape, jnp.float32),
            jax.ShapeDtypeStruct((1, LANES), jnp.float32),
            jax.ShapeDtypeStruct((5, 8, LANES), jnp.float32),
            jax.ShapeDtypeStruct((2, 8, LANES), jnp.int32),
        ),
        in_specs=[VMEM, VMEM] + [SMEM] * 6,
        out_specs=(VMEM,) * 5,
        compiler_params=PARAMS,
        cost_estimate=pl.CostEstimate(flops=8 * size, bytes_accessed=12 * size, transcendentals=0),
        name="history",
    )(past_inputs, past_residuals, *scalars)


def residual_kernel(count, own, swapped, *refs):
    received = refs[:count]
    current, residuals, old_line, gains, shifts, fresh, lines, smeared = refs[count:]
    parts, height, slice_len = smeared.shape
    place = lax.axis_index("energy")
    smeared[place], smeared[place ^ 1] = own[0], swapped[0]
    for chip, block in zip(chip_order(parts), received):
        smeared[place ^ (2 * chip)], smeared[place ^ (2 * chip + 1)] = block[0], block[1]
    lane = lax.broadcasted_iota(jnp.int32, (8, slice_len), 1)
    coupling = gains[0]
    modes = []
    for m in range(2):
        wide = shifts[m]
        keeps = lane < slice_len - wide, lane >= wide
        modes.append((jnp.max(wide), *keeps, gains[2 * m + 1], gains[2 * m + 2]))
    zero = jnp.zeros((8, slice_len), jnp.float32)
    acc = [zero] * (HIST + 1)
    for top in range(0, height, 8):
        at = slice(top, top + 8)
        source = [smeared[e, at, :] for e in range(parts)]
        sigma = [coupling * x for x in source]
        lesser = top < height // 2
        for s, keep_up, keep_down, emitted, absorbed in modes:
            up = [pltpu.roll(x, slice_len - s, 1) for x in source] + [zero]
            down = [zero] + [pltpu.roll(x, s, 1) for x in source]
            gain_up, gain_down = (emitted, absorbed) if lesser else (absorbed, emitted)
            for e in range(parts):
                above = jnp.where(keep_up, up[e], up[e + 1])
                below = jnp.where(keep_down, down[e + 1], down[e])
                sigma[e] = sigma[e] + (gain_up * above + gain_down * below)
        for e in range(parts):
            where = (at, slice(e * slice_len, (e + 1) * slice_len))
            new = sigma[e] - current[where]
            fresh[where] = current[where] + mixing_share * new
            acc[0] = acc[0] + new * new
            for j in range(HIST):
                acc[j + 1] = acc[j + 1] + new * residuals[(j,) + where]
    mine = jnp.concatenate([jnp.sum(a, axis=0, keepdims=True) for a in acc] + [zero[: 8 - HIST - 1]], axis=0)
    mine = jnp.sum(mine, axis=1, keepdims=True)
    spot = lax.broadcasted_iota(jnp.int32, (8, LANES), 0) + SPOTS[(0, 0)]
    mine = jnp.where(lax.broadcasted_iota(jnp.int32, (8, LANES), 1) == spot, mine, 0.0)
    mine = old_line[...] + jnp.sum(mine, axis=0, keepdims=True)
    lines[...] = jnp.broadcast_to(mine[None], lines.shape)


def residual(kept, swapped, smeared, current, residuals, old_line, gains, shifts, copies):
    return pl.pallas_call(
        lambda *refs: residual_kernel(len(smeared), *refs),
        out_shape=(
            jax.ShapeDtypeStruct(current.shape, jnp.float32),
            jax.ShapeDtypeStruct((copies, 1, LANES), jnp.float32),
        ),
        in_specs=[VMEM] * (len(smeared) + 7),
        out_specs=(VMEM, VMEM),
        scratch_shapes=[pltpu.VMEM((2 * kept.shape[0],) + kept.shape[1:], jnp.float32)],
        compiler_params=PARAMS,
        name="residual",
    )(kept, swapped, *smeared, current, residuals, old_line, gains, shifts)


def solve(products):
    prod = lambda i, j: products[(min(i, j), max(i, j))]
    n = HIST
    system = [
        [prod(i, j) - prod(i, j + 1) - prod(i + 1, j) + prod(i + 1, j + 1) for j in range(n)]
        for i in range(n)
    ]
    target = [prod(i, 0) - prod(i + 1, 0) for i in range(n)]
    trace = system[0][0]
    for i in range(1, n):
        trace = trace + system[i][i]
    ridge = (ridge_share / n) * trace + 1e-06
    for i in range(n):
        system[i][i] = system[i][i] + ridge
    for k in range(n):
        inverse = 1.0 / system[k][k]
        row = [system[k][j] * inverse if j > k else None for j in range(n)]
        value = target[k] * inverse
        for i in range(n):
            if i == k:
                continue
            for j in range(k + 1, n):
                system[i][j] = system[i][j] - system[i][k] * row[j]
            target[i] = target[i] - system[i][k] * value
        system[k] = row
        target[k] = value
    gamma = target
    weights = [1.0 - gamma[0]]
    for j in range(1, n):
        weights.append(gamma[j - 1] - gamma[j])
    weights.append(gamma[n - 1])
    return weights


def mix_kernel(entries, lines, fresh, aged, out, wide, mixed_rows, done):
    summed = jnp.sum(lines[...], axis=0) * (1.0 / entries)
    row = lax.broadcasted_iota(jnp.int32, (8, LANES), 0)
    lane = lax.broadcasted_iota(jnp.int32, (8, LANES), 1)
    for part in range(wide.shape[0]):
        own = jnp.where(lane == row + 8 * part, summed, 0.0)
        wide[part] = jnp.broadcast_to(jnp.sum(own, axis=1, keepdims=True), (8, LANES))
    products = {
        pair: jnp.broadcast_to(wide[spot // 8, spot % 8 : spot % 8 + 1, :], (8, LANES))
        for pair, spot in SPOTS.items()
    }
    weights = solve(products)
    rows, width = fresh.shape
    span = rows // done.shape[0]
    writes = []
    for part in range(done.shape[0]):
        for top in range(part * span, (part + 1) * span, 8):
            for left in range(0, width, LANES):
                at = (slice(top, top + 8), slice(left, left + LANES))
                mixed = weights[0] * fresh[at]
                for j in range(HIST):
                    mixed = mixed + weights[j + 1] * aged[(j,) + at]
                mixed_rows[at] = mixed
        at = pl.ds(part * span, span)
        writes.append(pltpu.make_async_copy(mixed_rows.at[at], out.at[at], done.at[part]))
        writes[-1].start()
    for write in writes:
        write.wait()


def mix(lines, fresh, aged, entries):
    return pl.pallas_call(
        lambda *refs: mix_kernel(entries, *refs),
        out_shape=jax.ShapeDtypeStruct(fresh.shape, jnp.float32),
        in_specs=[VMEM] * 3,
        out_specs=pl.BlockSpec(memory_space=pltpu.HBM),
        scratch_shapes=[
            pltpu.VMEM((3, 8, LANES), jnp.float32),
            pltpu.VMEM(fresh.shape, jnp.float32),
            pltpu.SemaphoreType.DMA((min(4, fresh.shape[0] // 8),)),
        ],
        compiler_params=PARAMS,
        name="mix",
    )(lines, fresh, aged)


def per_device(
    greens,
    current,
    past_inputs,
    past_residuals,
    slot_order,
    neighbour,
    momentum_class,
    stencil_weight,
    acoustic_coupling,
    optical_coupling,
    occupation,
    phonon_shift,
):
    group_len, slice_len = greens.shape[3:]
    rows, width = current.shape[3:]
    groups = lax.axis_size("kgrp")
    parts = lax.axis_size("energy")
    own = greens.reshape(-1, group_len, slice_len)
    height = own.shape[0] * rows

    flat = current.reshape(height, width)
    old_in = past_inputs.reshape(HIST, height, width)
    old_res = past_residuals.reshape(HIST, height, width)
    scalars = (
        slot_order, momentum_class, acoustic_coupling, optical_coupling, occupation, phonon_shift
    )
    aged, residuals, old_line, gains, shifts = history(old_in, old_res, scalars, rows)
    kept, given = smear(own, neighbour, stencil_weight, groups, parts)
    meet = lambda block, m: lax.ppermute(block, "energy", [(e, e ^ m) for e in range(parts)])
    swapped = meet(given, 1)
    smeared = [meet(block, 2 * chip) for chip, block in zip(chip_order(parts), join(kept, swapped))]
    fresh, lines = residual(
        kept, swapped, smeared, flat, residuals, old_line, gains, shifts, groups * parts
    )
    lines = lax.all_to_all(lines, ("energy", "kgrp"), split_axis=0, concat_axis=0, tiled=True)
    entries = float(flat.size * groups * parts)
    return mix(lines, fresh, aged, entries).reshape(current.shape)


def solution(mesh):
    return jax.shard_map(
        per_device,
        mesh=mesh,
        in_specs=(
            P(None, None, None, "kgrp", "energy"),
            P(None, None, None, ("kgrp", "energy"), None),
            P(None, None, None, None, ("kgrp", "energy"), None),
            P(None, None, None, None, ("kgrp", "energy"), None),
            P(),
            P("kgrp", None),
            P("kgrp"),
            P(),
            P(),
            P(),
            P(),
            P(),
        ),
        out_specs=P(None, None, None, ("kgrp", "energy"), None),
        check_vma=False,
    )
```

```python
import jax
import jax.numpy as jnp
from jax import lax
from jax.experimental import pallas as pl
from jax.experimental.pallas import tpu as pltpu
from jax.sharding import PartitionSpec as P

HIST = 5
LANES = 128

mixing_share = 0.5
ridge_share = 0.1

VMEM = pl.BlockSpec(memory_space=pltpu.VMEM)
SMEM = pl.BlockSpec(memory_space=pltpu.SMEM)
PARAMS = pltpu.CompilerParams(vmem_limit_bytes=16 * 1024 * 1024)

PAIRS = [(i, j) for i in range(1, HIST + 1) for j in range(i, HIST + 1)]
SPOTS = {pair: v for v, pair in enumerate(PAIRS)}
for _j in range(HIST + 1):
    SPOTS[(0, _j)] = 16 + _j


def split(value):
    high = value.astype(jnp.bfloat16)
    return high, (value - high.astype(jnp.float32)).astype(jnp.bfloat16)


def product(left, right):
    dot = lambda a, b: jnp.dot(a, b, preferred_element_type=jnp.float32)
    return dot(left[0], right[0]) + (dot(left[0], right[1]) + dot(left[1], right[0]))


def prepare_kernel(total_k, *refs):
    *blocks, neighbour_hbm, weight_hbm, stencil_hi, stencil_lo, part, late, neighbour, weight, done = refs
    fetches = [
        pltpu.make_async_copy(neighbour_hbm, neighbour, done.at[0]),
        pltpu.make_async_copy(weight_hbm, weight, done.at[1]),
    ]
    for fetch in fetches:
        fetch.start()
    late[...] = blocks[-1][...]
    _, group_len, slice_len = blocks[0].shape
    group_id = lax.axis_index("kgrp")
    parts = lax.axis_size("energy")
    rows = group_len // parts
    for fetch in fetches:
        fetch.wait()
    slots, _ = neighbour.shape
    padded = jnp.concatenate([neighbour[...], jnp.zeros((8 - slots, group_len), jnp.int32)], axis=0)
    targets = jnp.transpose(padded)
    place = lax.axis_index("energy")
    bit = 1
    while bit < parts:
        span = bit * rows
        pieces = [targets[at : at + span] for at in range(0, group_len, span)]
        flipped = [pieces[b ^ 1] for b in range(len(pieces))]
        targets = jnp.where(place & bit != 0, jnp.concatenate(flipped, axis=0), targets)
        bit *= 2
    local = targets - group_id * group_len + group_len
    local = jnp.where(local < 0, local + total_k, jnp.where(local >= total_k, local - total_k, local))
    spot = lax.broadcasted_iota(jnp.int32, (group_len, 3 * group_len), 1)
    stencil = jnp.zeros(spot.shape, jnp.float32)
    for n in range(slots):
        stencil = stencil + jnp.where(spot == local[:, n : n + 1], weight[n], 0.0)
    before, after = stencil[:, :group_len], stencil[:, 2 * group_len :]
    swapped = paired(total_k // group_len) & (group_id % 2 == 1)
    near, far = jnp.where(swapped, before, after), jnp.where(swapped, after, before)
    stencil_hi[...], stencil_lo[...] = split(jnp.concatenate([near, far], axis=1))
    centre = split(stencil[:, group_len : 2 * group_len])
    first = 0
    for own in blocks:
        for c in range(0, own.shape[0], 2):
            result = product(centre, split(jnp.concatenate([own[c], own[c + 1]], axis=1)))
            part[first + c] = result[:, :slice_len]
            part[first + c + 1] = result[:, slice_len:]
        first += own.shape[0]


def prepare(blocks, neighbour, weight, total_k):
    comps = sum(block.shape[0] for block in blocks)
    _, group_len, slice_len = blocks[0].shape
    sides = jax.ShapeDtypeStruct((group_len, 2 * group_len), jnp.bfloat16)
    size = comps * group_len * slice_len
    return pl.pallas_call(
        lambda *refs: prepare_kernel(total_k, *refs),
        out_shape=(
            sides,
            sides,
            jax.ShapeDtypeStruct((comps, group_len, slice_len), jnp.float32),
            jax.ShapeDtypeStruct(blocks[-1].shape, jnp.float32),
        ),
        in_specs=[VMEM] * len(blocks) + [pl.BlockSpec(memory_space=pltpu.HBM)] * 2,
        out_specs=(VMEM,) * 4,
        scratch_shapes=[
            pltpu.VMEM(neighbour.shape[::-1], jnp.int32),
            pltpu.SMEM(weight.shape, jnp.float32),
            pltpu.SemaphoreType.DMA((2,)),
        ],
        compiler_params=PARAMS,
        cost_estimate=pl.CostEstimate(
            flops=6 * size * group_len, bytes_accessed=8 * size, transcendentals=0
        ),
        name="prepare",
    )(*blocks, jnp.transpose(neighbour), weight)


def smeared_pairs(first, sides, stencil_hi, stencil_lo, part):
    blocks = [block for block in sides if block is not None]
    comps, group_len, slice_len = blocks[0].shape
    start = 0 if sides[0] is not None else group_len
    at = slice(start, start + len(blocks) * group_len)
    stencil = (stencil_hi[:, at], stencil_lo[:, at])
    for c in range(0, comps, 2):
        stacked = [jnp.concatenate([block[c], block[c + 1]], axis=1) for block in blocks]
        result = product(stencil, split(jnp.concatenate(stacked, axis=0)))
        for p in range(2):
            yield c + p, part[first + c + p] + result[:, p * slice_len : (p + 1) * slice_len]


def with_sides(kernel, sides):
    def body(*refs):
        refs = list(refs)
        kernel([None if side is None else refs.pop(0) for side in sides], *refs)

    return body


def smear_cost(blocks):
    size = sum(block.size for block in blocks)
    return pl.CostEstimate(
        flops=6 * size * blocks[0].shape[1], bytes_accessed=12 * size, transcendentals=0
    )


def add_sides(first, sides, stencil_hi, stencil_lo, part, after):
    def kernel(sides, stencil_hi, stencil_lo, part, *refs):
        for c, smeared in smeared_pairs(first, sides, stencil_hi, stencil_lo, part):
            refs[-1][c] = smeared

    blocks = [block for block in sides if block is not None]
    return pl.pallas_call(
        with_sides(kernel, sides),
        out_shape=jax.ShapeDtypeStruct(blocks[0].shape, jnp.float32),
        in_specs=[VMEM] * (len(blocks) + 3) + [pl.BlockSpec(memory_space=pl.ANY)] * len(after),
        out_specs=VMEM,
        compiler_params=PARAMS,
        cost_estimate=smear_cost(blocks),
        name="add_sides",
    )(*blocks, stencil_hi, stencil_lo, part, *after)


def finish_kernel(sides, stencil_hi, stencil_lo, part, *refs):
    *ready, kept, given = refs
    chips, height, _ = kept.shape
    comps = part.shape[0]
    rows = height // comps

    def place(c, smeared):
        for m in range(2 * chips):
            out = given if m % 2 else kept
            out[m // 2, c * rows : (c + 1) * rows, :] = smeared[m * rows : (m + 1) * rows]

    first = 0
    for c, smeared in smeared_pairs(0, sides, stencil_hi, stencil_lo, part):
        place(c, smeared)
        first = c + 1
    for block in ready:
        for c in range(block.shape[0]):
            place(first + c, block[c])


def finish(sides, stencil_hi, stencil_lo, part, ready, parts):
    blocks = [block for block in sides if block is not None]
    comps, group_len, slice_len = part.shape
    shape = (parts // 2, comps * group_len // parts, slice_len)
    return pl.pallas_call(
        with_sides(finish_kernel, sides),
        out_shape=[jax.ShapeDtypeStruct(shape, jnp.float32)] * 2,
        in_specs=[VMEM] * (len(blocks) + len(ready) + 3),
        out_specs=[VMEM] * 2,
        compiler_params=PARAMS,
        cost_estimate=smear_cost(blocks),
        name="finish",
    )(*blocks, stencil_hi, stencil_lo, part, *ready)


def chip_order(parts):
    chips = parts // 2
    half = chips // 2
    return [*range(half + 1, chips), half, *range(1, half)] if chips > 1 else []


def join_kernel(own, swapped, *out):
    for chip, block in zip(chip_order(2 * own.shape[0]), out):
        block[0], block[1] = own[chip], swapped[chip]


def join(own, swapped):
    chips, height, slice_len = own.shape
    shape = jax.ShapeDtypeStruct((2, height, slice_len), jnp.float32)
    return pl.pallas_call(
        join_kernel,
        out_shape=[shape] * (chips - 1),
        in_specs=[VMEM] * 2,
        out_specs=[VMEM] * (chips - 1),
        compiler_params=PARAMS,
        name="join",
    )(own, swapped)


def paired(groups):
    return groups == 4


def hold_kernel(block, _, out):
    out[...] = block[...]


def hold(block, until):
    return pl.pallas_call(
        hold_kernel,
        out_shape=jax.ShapeDtypeStruct(block.shape, jnp.float32),
        in_specs=[VMEM, pl.BlockSpec(memory_space=pl.ANY)],
        out_specs=VMEM,
        compiler_params=PARAMS,
        name="hold",
    )(block, until)


def smear(own, neighbour, weight, groups, parts):
    total_k = groups * own.shape[1]
    if not paired(groups):
        forward = [(i, (i + 1) % groups) for i in range(groups)]
        backward = [(target, source) for source, target in forward]
        near, far = lax.ppermute(own, "kgrp", backward), lax.ppermute(own, "kgrp", forward)
        return finish((near, far), *prepare([own], neighbour, weight, total_k)[:3], [], parts)
    across = lambda block, flip: lax.ppermute(block, "kgrp", [(i, i ^ flip) for i in range(groups)])
    half = own.shape[0] // 2
    head, tail = own[:half], own[half:]
    near_head, far_tail = across(head, 1), across(tail, 3)
    hi, lo, part, late = prepare([head, tail], neighbour, weight, total_k)
    near_tail, far_head = across(late, 1), across(hold(near_head, late), 2)
    tail_part = add_sides(half, (near_tail, far_tail), hi, lo, part, [])
    return finish((near_head, far_head), hi, lo, part, [tail_part], parts)


def spread(values, shape):
    lane = lax.broadcasted_iota(jnp.int32, shape, 1)
    row = jnp.zeros(shape, jnp.float32)
    for spot, value in values:
        row = jnp.where(lane == spot, value, row)
    return row


def total(acc):
    return jnp.sum(jnp.sum(acc, axis=0, keepdims=True), axis=1, keepdims=True)


def history_kernel(
    total_rows, past_inputs, past_residuals, slots, classes, acoustic, optical, number, shift,
    aged, residuals, line, gains, shifts,
):
    first = lax.axis_index("energy") * total_rows
    row = lax.broadcasted_iota(jnp.int32, (8, LANES), 0) % total_rows
    coupling = jnp.zeros((8, LANES), jnp.float32)
    for i in range(total_rows):
        coupling = jnp.where(row == i, acoustic[classes[first + i]], coupling)
    gains[0] = coupling
    for m in range(2):
        gains[2 * m + 1] = jnp.full((8, LANES), optical[m] * (number[m] + 1.0))
        gains[2 * m + 2] = jnp.full((8, LANES), optical[m] * number[m])
        shifts[m] = jnp.full((8, LANES), shift[m], jnp.int32)
    _, rows, width = past_inputs.shape
    acc = [jnp.zeros((8, LANES), jnp.float32) for _ in PAIRS]
    for top in range(0, rows, 8):
        def column(t, acc, top=top):
            at = pl.ds(pl.multiple_of(t * LANES, LANES), LANES)
            old = []
            for j in range(HIST):
                res = past_residuals[slots[j], top : top + 8, at]
                aged[j, top : top + 8, at] = (
                    past_inputs[slots[j], top : top + 8, at] + mixing_share * res
                )
                residuals[j, top : top + 8, at] = res
                old.append(res)
            return [a + old[i - 1] * old[j - 1] for a, (i, j) in zip(acc, PAIRS)]
        acc = lax.fori_loop(0, width // LANES, column, acc, unroll=4)
    line[...] = spread([(v, total(a)) for v, a in enumerate(acc)], line.shape)


def history(past_inputs, past_residuals, scalars, rows):
    size = past_inputs.size
    return pl.pallas_call(
        lambda *refs: history_kernel(rows, *refs),
        out_shape=(
            jax.ShapeDtypeStruct(past_inputs.shape, jnp.float32),
            jax.ShapeDtypeStruct(past_inputs.shape, jnp.float32),
            jax.ShapeDtypeStruct((1, LANES), jnp.float32),
            jax.ShapeDtypeStruct((5, 8, LANES), jnp.float32),
            jax.ShapeDtypeStruct((2, 8, LANES), jnp.int32),
        ),
        in_specs=[VMEM, VMEM] + [SMEM] * 6,
        out_specs=(VMEM,) * 5,
        compiler_params=PARAMS,
        cost_estimate=pl.CostEstimate(flops=8 * size, bytes_accessed=12 * size, transcendentals=0),
        name="history",
    )(past_inputs, past_residuals, *scalars)


def residual_kernel(count, own, swapped, *refs):
    received = refs[:count]
    current, residuals, old_line, gains, shifts, fresh, lines, smeared = refs[count:]
    parts, height, slice_len = smeared.shape
    place = lax.axis_index("energy")
    smeared[place], smeared[place ^ 1] = own[0], swapped[0]
    for chip, block in zip(chip_order(parts), received):
        smeared[place ^ (2 * chip)], smeared[place ^ (2 * chip + 1)] = block[0], block[1]
    lane = lax.broadcasted_iota(jnp.int32, (8, slice_len), 1)
    coupling = gains[0]
    modes = []
    for m in range(2):
        wide = shifts[m]
        keeps = lane < slice_len - wide, lane >= wide
        modes.append((jnp.max(wide), *keeps, gains[2 * m + 1], gains[2 * m + 2]))
    zero = jnp.zeros((8, slice_len), jnp.float32)
    acc = [zero] * (HIST + 1)
    for top in range(0, height, 8):
        at = slice(top, top + 8)
        source = [smeared[e, at, :] for e in range(parts)]
        sigma = [coupling * x for x in source]
        lesser = top < height // 2
        for s, keep_up, keep_down, emitted, absorbed in modes:
            up = [pltpu.roll(x, slice_len - s, 1) for x in source] + [zero]
            down = [zero] + [pltpu.roll(x, s, 1) for x in source]
            gain_up, gain_down = (emitted, absorbed) if lesser else (absorbed, emitted)
            for e in range(parts):
                above = jnp.where(keep_up, up[e], up[e + 1])
                below = jnp.where(keep_down, down[e + 1], down[e])
                sigma[e] = sigma[e] + (gain_up * above + gain_down * below)
        for e in range(parts):
            where = (at, slice(e * slice_len, (e + 1) * slice_len))
            new = sigma[e] - current[where]
            fresh[where] = current[where] + mixing_share * new
            acc[0] = acc[0] + new * new
            for j in range(HIST):
                acc[j + 1] = acc[j + 1] + new * residuals[(j,) + where]
    mine = jnp.concatenate([jnp.sum(a, axis=0, keepdims=True) for a in acc] + [zero[: 8 - HIST - 1]], axis=0)
    mine = jnp.sum(mine, axis=1, keepdims=True)
    spot = lax.broadcasted_iota(jnp.int32, (8, LANES), 0) + SPOTS[(0, 0)]
    mine = jnp.where(lax.broadcasted_iota(jnp.int32, (8, LANES), 1) == spot, mine, 0.0)
    mine = old_line[...] + jnp.sum(mine, axis=0, keepdims=True)
    lines[...] = jnp.broadcast_to(mine[None], lines.shape)


def residual(kept, swapped, smeared, current, residuals, old_line, gains, shifts, copies):
    return pl.pallas_call(
        lambda *refs: residual_kernel(len(smeared), *refs),
        out_shape=(
            jax.ShapeDtypeStruct(current.shape, jnp.float32),
            jax.ShapeDtypeStruct((copies, 1, LANES), jnp.float32),
        ),
        in_specs=[VMEM] * (len(smeared) + 7),
        out_specs=(VMEM, VMEM),
        scratch_shapes=[pltpu.VMEM((2 * kept.shape[0],) + kept.shape[1:], jnp.float32)],
        compiler_params=PARAMS,
        name="residual",
    )(kept, swapped, *smeared, current, residuals, old_line, gains, shifts)


def solve(products):
    prod = lambda i, j: products[(min(i, j), max(i, j))]
    n = HIST
    system = [
        [prod(i, j) - prod(i, j + 1) - prod(i + 1, j) + prod(i + 1, j + 1) for j in range(n)]
        for i in range(n)
    ]
    target = [prod(i, 0) - prod(i + 1, 0) for i in range(n)]
    trace = system[0][0]
    for i in range(1, n):
        trace = trace + system[i][i]
    ridge = (ridge_share / n) * trace + 1e-06
    for i in range(n):
        system[i][i] = system[i][i] + ridge
    for k in range(n):
        inverse = 1.0 / system[k][k]
        row = [system[k][j] * inverse if j > k else None for j in range(n)]
        value = target[k] * inverse
        for i in range(n):
            if i == k:
                continue
            for j in range(k + 1, n):
                system[i][j] = system[i][j] - system[i][k] * row[j]
            target[i] = target[i] - system[i][k] * value
        system[k] = row
        target[k] = value
    gamma = target
    weights = [1.0 - gamma[0]]
    for j in range(1, n):
        weights.append(gamma[j - 1] - gamma[j])
    weights.append(gamma[n - 1])
    return weights


def mix_kernel(entries, lines, fresh, aged, out, wide, mixed_rows, done):
    summed = jnp.sum(lines[...], axis=0) * (1.0 / entries)
    row = lax.broadcasted_iota(jnp.int32, (8, LANES), 0)
    lane = lax.broadcasted_iota(jnp.int32, (8, LANES), 1)
    for part in range(wide.shape[0]):
        own = jnp.where(lane == row + 8 * part, summed, 0.0)
        wide[part] = jnp.broadcast_to(jnp.sum(own, axis=1, keepdims=True), (8, LANES))
    products = {
        pair: jnp.broadcast_to(wide[spot // 8, spot % 8 : spot % 8 + 1, :], (8, LANES))
        for pair, spot in SPOTS.items()
    }
    weights = solve(products)
    rows, width = fresh.shape
    span = rows // done.shape[0]
    writes = []
    for part in range(done.shape[0]):
        for top in range(part * span, (part + 1) * span, 8):
            for left in range(0, width, LANES):
                at = (slice(top, top + 8), slice(left, left + LANES))
                mixed = weights[0] * fresh[at]
                for j in range(HIST):
                    mixed = mixed + weights[j + 1] * aged[(j,) + at]
                mixed_rows[at] = mixed
        at = pl.ds(part * span, span)
        writes.append(pltpu.make_async_copy(mixed_rows.at[at], out.at[at], done.at[part]))
        writes[-1].start()
    for write in writes:
        write.wait()


def mix(lines, fresh, aged, entries):
    return pl.pallas_call(
        lambda *refs: mix_kernel(entries, *refs),
        out_shape=jax.ShapeDtypeStruct(fresh.shape, jnp.float32),
        in_specs=[VMEM] * 3,
        out_specs=pl.BlockSpec(memory_space=pltpu.HBM),
        scratch_shapes=[
            pltpu.VMEM((3, 8, LANES), jnp.float32),
            pltpu.VMEM(fresh.shape, jnp.float32),
            pltpu.SemaphoreType.DMA((min(4, fresh.shape[0] // 8),)),
        ],
        compiler_params=PARAMS,
        name="mix",
    )(lines, fresh, aged)


def per_device(
    greens,
    current,
    past_inputs,
    past_residuals,
    slot_order,
    neighbour,
    momentum_class,
    stencil_weight,
    acoustic_coupling,
    optical_coupling,
    occupation,
    phonon_shift,
):
    group_len, slice_len = greens.shape[3:]
    rows, width = current.shape[3:]
    groups = lax.axis_size("kgrp")
    parts = lax.axis_size("energy")
    own = greens.reshape(-1, group_len, slice_len)
    height = own.shape[0] * rows

    flat = current.reshape(height, width)
    old_in = past_inputs.reshape(HIST, height, width)
    old_res = past_residuals.reshape(HIST, height, width)
    scalars = (
        slot_order, momentum_class, acoustic_coupling, optical_coupling, occupation, phonon_shift
    )
    aged, residuals, old_line, gains, shifts = history(old_in, old_res, scalars, rows)
    kept, given = smear(own, neighbour, stencil_weight, groups, parts)
    meet = lambda block, m: lax.ppermute(block, "energy", [(e, e ^ m) for e in range(parts)])
    swapped = meet(given, 1)
    smeared = [meet(block, 2 * chip) for chip, block in zip(chip_order(parts), join(kept, swapped))]
    fresh, lines = residual(
        kept, swapped, smeared, flat, residuals, old_line, gains, shifts, groups * parts
    )
    lines = lax.all_to_all(lines, ("energy", "kgrp"), split_axis=0, concat_axis=0, tiled=True)
    entries = float(flat.size * groups * parts)
    return mix(lines, fresh, aged, entries).reshape(current.shape)


def solution(mesh):
    return jax.shard_map(
        per_device,
        mesh=mesh,
        in_specs=(
            P(None, None, None, "kgrp", "energy"),
            P(None, None, None, ("kgrp", "energy"), None),
            P(None, None, None, None, ("kgrp", "energy"), None),
            P(None, None, None, None, ("kgrp", "energy"), None),
            P(),
            P("kgrp", None),
            P("kgrp"),
            P(),
            P(),
            P(),
            P(),
            P(),
        ),
        out_specs=P(None, None, None, ("kgrp", "energy"), None),
        check_vma=False,
    )
```
